32 devices in a mesh: tm: 4 (over y, x), space: 8 (over z, core).
Axes of the slice: x: 2, y: 2, z: 4, core: 2. Of those that a mesh axis runs over, the one named last changes fastest.
Arguments:
- snapshots: float32 [128, 3, 8, 16, 128], P('tm', None, 'space'), may hold values from -6 to 6
- coeffs: float32 [128, 128], replicated, may hold values from -0.5 to 0.5
- pair_table: int32 [2048, 2], replicated, may hold values from 0 to 127
Outputs:
- tensor: float32 [2048, 128], P(('tm', 'space'))
The draws below stay inside these ranges and needn't reach their ends.
Inputs may be any that keep to these rules, and one draw needn't show every extreme that they name: `pair_table`: column 0 names the carrying mode, column 1 the carried mode.
All inputs are finite; a program needn't handle non-finite values.
Results may differ from the reference program's by a relative error of at most 0.00016.
Values sent between devices are 32-bit elements; how exact they have to be, the bound alone decides.
No kernel may reach another device: no remote copies, remote signals or barrier semaphores. Data moves between devices by JAX's collectives and lax.ppermute only.
A program may use at most 192 MiB of HBM per device.

```python
import math
import jax
import jax.numpy as jnp
from jax import lax

M = 128
NZ = 128
S = 128
NX = 8
NY = 16
PAIRS = 2048


def touch_ends(values, stream_key, least, high):
    place = [jax.random.randint(jax.random.fold_in(stream_key, axis), (), 0, length) for axis, length in enumerate(values.shape)]
    longest = values.shape.index(max(values.shape))
    neighbour = place[:longest] + [(place[longest] + 1) % values.shape[longest]] + place[longest + 1:]
    return values.at[tuple(place)].set(least).at[tuple(neighbour)].set(high)


def level_of(stream_key, shape, cuts, low, high):
    gain, own = 1.0, jax.random.fold_in(stream_key, 6)
    for position, shards_of in cuts:
        draws = jnp.exp(jax.random.uniform(jax.random.fold_in(own, position), (shards_of,), jnp.float32, low / len(cuts), high / len(cuts)))
        gain = gain * jnp.repeat(draws, shape[position] // shards_of).reshape([-1 if axis == position else 1 for axis in range(len(shape))])
    return gain


def noise(stream_key, dims, spread, reach, cuts=(), held_as=jnp.bfloat16):
    factor_of = level_of(stream_key, dims, cuts, -0.22, 0.18) if cuts else 1.0
    array = jax.random.normal(stream_key, dims, jnp.float32) * spread * factor_of
    return jnp.minimum(jnp.maximum(array, -reach), reach).astype(held_as)


def setup_inputs(seed: int = 0) -> dict:
    splits = jax.random.split(jax.random.key(seed), 4)
    snapshots = noise(splits[0], (S, 3, NX, NY, NZ), 1.0, 6.0, ((0, 4), (2, 8)), jnp.float32)
    coeffs = noise(splits[1], (S, M), S ** -0.5, 0.5, (), jnp.float32)
    pair_table = touch_ends(jax.random.randint(splits[2], (PAIRS, 2), 0, M), jax.random.fold_in(splits[2], 1), 0, M - 1).astype(jnp.int32)
    return {"snapshots": snapshots, "coeffs": coeffs, "pair_table": pair_table}


def gradient_field(mode_field):
    padded_y = jnp.pad(mode_field, ((0, 0), (0, 0), (0, 0), (1, 1), (0, 0)))
    stream_slope = (jnp.roll(mode_field, -1, 2) - jnp.roll(mode_field, 1, 2)) * 0.5
    normal_slope = (padded_y[:, :, :, 2:] - padded_y[:, :, :, :-2]) * 0.5
    span_slope = (jnp.roll(mode_field, -1, 4) - jnp.roll(mode_field, 1, 4)) * 0.5
    return jnp.stack([stream_slope, normal_slope, span_slope], axis=1)


def pair_block(pair_rows, flat_modes, flat_slopes):
    first_modes = jnp.take(flat_modes, pair_rows[:, 0], axis=0)
    second_slopes = jnp.take(flat_slopes, pair_rows[:, 1], axis=0)
    convection = jnp.einsum('bdl,bdcl->bcl', first_modes, second_slopes, precision=lax.Precision.HIGHEST)
    return jnp.einsum('bcl,kcl->bk', convection, flat_modes, precision=lax.Precision.HIGHEST)


def reference(snapshots, coeffs, pair_table):
    mode_field = jnp.einsum('sk,scxyz->kcxyz', coeffs, snapshots, precision=lax.Precision.HIGHEST)
    slopes = gradient_field(mode_field)
    flat_modes = mode_field.reshape(M, 3, -1)
    flat_slopes = slopes.reshape(M, 3, 3, -1)
    group_size = math.gcd(PAIRS, 64)
    grouped = pair_table.reshape(PAIRS // group_size, group_size, 2)

    def one_group(group_rows):
        return pair_block(group_rows, flat_modes, flat_slopes)

    result = lax.map(one_group, grouped)
    return result.reshape(PAIRS, M) * (float(NX * NY * NZ) ** -0.5)
```

```python
import functools

import jax
import jax.numpy as jnp
from jax import lax
from jax.experimental import pallas as pl
from jax.experimental.pallas import tpu as pltpu
from jax.sharding import PartitionSpec as P

F32 = jnp.float32
BF16 = jnp.bfloat16
VMEM_BYTES = 56 * 2**20


def split_high_low(values):
    high = values.astype(BF16)
    low = (values - high.astype(F32)).astype(BF16)
    return high, low


def pack_kernel(where_ref, field_ref, *out_refs, sizes):
    local_s, rows_y, block_rows, tm_count = sizes
    t = where_ref[0]
    for peer in range(tm_count):
        first_row = jnp.bitwise_xor(t, peer) * block_rows
        for row in range(block_rows + 2):
            y = first_row + row if row < block_rows else (first_row - 1 if row == block_rows else first_row + block_rows)
            inside = jnp.logical_and(y >= 0, y < rows_y)
            y = jnp.clip(y, 0, rows_y - 1)
            for c in range(3):
                slab = field_ref[pl.ds(c * rows_y + y, local_s, stride=3 * rows_y), :]
                if row >= block_rows:
                    slab = jnp.where(inside, slab, 0.0)
                out_refs[peer][row * 3 + c] = slab


def mode_weights(where_ref, coeffs_ref, local_s, tm_count):
    t = where_ref[0]
    ordered = jnp.concatenate(
        [
            coeffs_ref[pl.ds(pl.multiple_of(jnp.bitwise_xor(t, peer) * local_s, 8), local_s), :]
            for peer in range(tm_count)
        ],
        axis=0,
    )
    high, low = split_high_low(ordered.T)
    return jnp.concatenate([high, low, high, low], axis=1)


def modes_of(weights, slab):
    high, low = split_high_low(slab)
    return jnp.dot(weights, jnp.concatenate([high, high, low, low], axis=0), preferred_element_type=F32)


def store_projection(rhs_ref, place, mode_slab):
    high, low = split_high_low(mode_slab.T)
    modes = mode_slab.shape[0]
    lanes = mode_slab.shape[1]
    rhs_ref[place * lanes : (place + 1) * lanes, 0:modes] = high
    rhs_ref[place * lanes : (place + 1) * lanes, modes : 2 * modes] = low


def pair_position(where_ref, group, sizes):
    tm_count, chips, share = sizes
    t, chip, core = where_ref[0], where_ref[1], where_ref[2]
    peer, ahead = lax.div(group, chips), lax.rem(group, chips)
    to_t = jnp.bitwise_xor(t, peer)
    to_chip = lax.rem(chip + ahead, chips)
    return ((to_t * chips + to_chip) * 2 + core) * share


def project(conv_ref, lhs_ref, rhs_ref, block, places, lanes):
    for place in range(places):
        values = conv_ref[pl.ds(place, block, stride=places), :]
        high, low = split_high_low(values)
        lhs_ref[0:block, place * lanes : (place + 1) * lanes] = high
        lhs_ref[block : 2 * block, place * lanes : (place + 1) * lanes] = low
    both = jnp.dot(lhs_ref[...], rhs_ref[...], preferred_element_type=F32)
    modes = both.shape[1] // 2
    return (both[:block, :modes] + both[:block, modes:]) + (both[block:, :modes] + both[block:, modes:])


def main_kernel(
    where_ref, pairs_ref, coeffs_ref, *refs, sizes
):
    local_s, block_rows, tm_count, chips, share = sizes
    own, other = refs[:tm_count], refs[tm_count : 2 * tm_count]
    out_ref, next_ref = refs[2 * tm_count : 2 * tm_count + 2]
    field_ref, slab_ref, carry_ref, slope_ref, rhs_ref, conv_ref, lhs_ref = refs[2 * tm_count + 2 :]
    core = where_ref[2]
    modes, lanes = coeffs_ref.shape[1], own[0].shape[2]
    height = 2 * block_rows
    for peer in range(tm_count):
        rows = pl.ds(peer * local_s, local_s)
        field_ref[core, :, rows, :] = own[peer][...]
        field_ref[1 - core, :, rows, :] = other[peer][...]
    weights = mode_weights(where_ref, coeffs_ref, local_s, tm_count)

    def one_slab(index, _):
        both = jnp.concatenate([field_ref[0, index], field_ref[1, index]], axis=1)
        result = modes_of(weights, both)
        slab_ref[0, index] = result[:, :lanes]
        slab_ref[1, index] = result[:, lanes:]
        return 0

    lax.fori_loop(0, (block_rows + 2) * 3, one_slab, 0, unroll=2)
    for c in range(3):
        for row in range(block_rows):
            above = (row + 1 if row + 1 < block_rows else block_rows + 1) * 3 + c
            below = (row - 1 if row > 0 else block_rows) * 3 + c
            center = row * 3 + c
            for plane in range(2):
                place = plane * block_rows + row
                value = slab_ref[plane, center]
                other_plane = slab_ref[1 - plane, center]
                stream = other_plane * (0.5 if plane == 0 else -0.5)
                normal = (slab_ref[plane, above] - slab_ref[plane, below]) * 0.5
                span = (pltpu.roll(value, lanes - 1, 1) - pltpu.roll(value, 1, 1)) * 0.5
                carry_ref[pl.ds(c * height + place, modes, stride=3 * height), :] = value
                for d, slope in enumerate((stream, normal, span)):
                    slope_ref[pl.ds((d * 3 + c) * height + place, modes, stride=9 * height), :] = slope
                store_projection(rhs_ref, c * height + place, value)
                if plane == 1:
                    next_ref[row * 3 + c] = value
    block = conv_ref.shape[0] // (3 * height)

    def one_block(number, _):
        first = number * block

        def one_pair(q, _):
            position = pair_position(where_ref, lax.div(first + q, share), (tm_count, chips, share)) + lax.rem(
                first + q, share
            )
            i, j = pairs_ref[2 * position], pairs_ref[2 * position + 1]
            carry = carry_ref[pl.ds(pl.multiple_of(i * (3 * height), 8), 3 * height), :]
            slope = slope_ref[pl.ds(pl.multiple_of(j * (9 * height), 8), 9 * height), :]
            rows = [
                sum(
                    carry[d * height : (d + 1) * height] * slope[(d * 3 + c) * height : (d * 3 + c + 1) * height]
                    for d in range(3)
                )
                for c in range(3)
            ]
            conv_ref[pl.ds(pl.multiple_of(q * (3 * height), 8), 3 * height), :] = jnp.concatenate(rows, axis=0)
            return 0

        lax.fori_loop(0, block, one_pair, 0, unroll=8)
        out_ref[pl.ds(pl.multiple_of(first, 8), block), :] = project(
            conv_ref, lhs_ref, rhs_ref, block, 3 * height, lanes
        )
        return 0

    lax.fori_loop(0, out_ref.shape[0] // block, one_block, 0)


def edge_kernel(where_ref, pairs_ref, coeffs_ref, *refs, sizes):
    local_s, block_rows, tm_count, chips, share = sizes
    own_ref, other_ref, near_ref, partial_ref = refs[:4]
    out_ref = refs[4]
    field_ref, carry_ref, slope_ref, rhs_ref, conv_ref, lhs_ref = refs[5:]
    core = where_ref[2]
    modes, lanes = coeffs_ref.shape[1], own_ref.shape[3]
    height = 2 * block_rows
    half = tm_count // 2
    for place in range(half):
        field_ref[:, pl.ds(pl.multiple_of((core * half + place) * local_s, 8), local_s), :] = own_ref[place]
        field_ref[:, pl.ds(pl.multiple_of(((1 - core) * half + place) * local_s, 8), local_s), :] = other_ref[place]
    weights = mode_weights(where_ref, coeffs_ref, local_s, tm_count)
    for c in range(3):
        for row in range(block_rows):
            near = near_ref[row * 3 + c]
            far = modes_of(weights, field_ref[row * 3 + c])
            for place, value, across in ((row, near, far * 0.5), (block_rows + row, far, near * -0.5)):
                if c == 0:
                    carry_ref[pl.ds(place, modes, stride=height), :] = value
                slope_ref[pl.ds(c * height + place, modes, stride=3 * height), :] = across
                store_projection(rhs_ref, c * height + place, value)
    block = conv_ref.shape[0] // (3 * height)

    def one_block(number, _):
        first = number * block

        def one_pair(q, _):
            position = pair_position(where_ref, lax.div(first + q, share), (tm_count, chips, share)) + lax.rem(
                first + q, share
            )
            i, j = pairs_ref[2 * position], pairs_ref[2 * position + 1]
            carry = carry_ref[pl.ds(pl.multiple_of(i * height, 8), height), :]
            slope = slope_ref[pl.ds(pl.multiple_of(j * (3 * height), 8), 3 * height), :]
            rows = [carry * slope[c * height : (c + 1) * height] for c in range(3)]
            conv_ref[pl.ds(pl.multiple_of(q * (3 * height), 8), 3 * height), :] = jnp.concatenate(rows, axis=0)
            return 0

        lax.fori_loop(0, block, one_pair, 0, unroll=8)
        rows = pl.ds(pl.multiple_of(first, 8), block)
        out_ref[rows, :] = partial_ref[rows, :] + project(conv_ref, lhs_ref, rhs_ref, block, 3 * height, lanes)
        return 0

    lax.fori_loop(0, out_ref.shape[0] // block, one_block, 0)


def shards(snapshots, coeffs, pair_table):
    tm_count, space_count = lax.axis_size("tm"), lax.axis_size("space")
    chips = space_count // 2
    t, place = lax.axis_index("tm"), lax.axis_index("space")
    core = lax.rem(place, 2)
    where = jnp.stack([t, lax.div(place, 2), core]).astype(jnp.int32)
    local_s, _, _, rows_y, lanes = snapshots.shape
    block_rows = rows_y // tm_count
    modes = coeffs.shape[1]
    share = pair_table.shape[0] // (tm_count * space_count)
    count = tm_count * chips * share
    factor = float(space_count * rows_y * lanes) ** (-0.5)
    pairs = pair_table.reshape(-1)
    smem = pl.BlockSpec(memory_space=pltpu.SMEM)
    vmem = pl.BlockSpec(memory_space=pltpu.VMEM)
    params = pltpu.CompilerParams(vmem_limit_bytes=VMEM_BYTES)
    height = 2 * block_rows
    block = 128

    swap = [(2 * chip + c, 2 * chip + 1 - c) for chip in range(chips) for c in range(2)]

    def across(peer):
        return [(i, i ^ peer) for i in range(tm_count)]

    with jax.named_scope("pack"):
        packed = pl.pallas_call(
            functools.partial(pack_kernel, sizes=(local_s, rows_y, block_rows, tm_count)),
            out_shape=[jax.ShapeDtypeStruct(((block_rows + 2) * 3, local_s, lanes), F32)] * tm_count,
            in_specs=[smem, vmem],
            out_specs=[vmem] * tm_count,
            compiler_params=params,
        )(where, snapshots.reshape(-1, lanes))
    with jax.named_scope("to_rows"):
        own = [packed[0]] + [lax.ppermute(packed[peer], "tm", across(peer)) for peer in range(1, tm_count)]
    with jax.named_scope("to_next_chip"):
        half = tm_count // 2
        halves = [
            jnp.stack([piece[: block_rows * 3] for piece in own[c * half : (c + 1) * half]]) for c in range(2)
        ]
        ahead = [
            lax.ppermute(
                halves[c], "space", [(2 * ((chip + 1) % chips), 2 * chip + c) for chip in range(chips)]
            )
            for c in range(2)
        ]
        next_own = jnp.where(core == 0, ahead[0], ahead[1])
    with jax.named_scope("to_other_core"):
        other = [lax.ppermute(piece, "space", swap) for piece in own]
        next_other = lax.ppermute(next_own, "space", swap)
    with jax.named_scope("inner_terms"):
        sizes = (local_s, block_rows, tm_count, chips, share)
        snaps = local_s * tm_count
        partial, near = pl.pallas_call(
            functools.partial(main_kernel, sizes=sizes),
            out_shape=[
                jax.ShapeDtypeStruct((count, modes), F32),
                jax.ShapeDtypeStruct((block_rows * 3, modes, lanes), F32),
            ],
            in_specs=[smem, smem] + [vmem] * (1 + 2 * tm_count),
            out_specs=[vmem, vmem],
            scratch_shapes=[
                pltpu.VMEM((2, (block_rows + 2) * 3, snaps, lanes), F32),
                pltpu.VMEM((2, (block_rows + 2) * 3, modes, lanes), F32),
                pltpu.VMEM((modes * 3 * height, lanes), F32),
                pltpu.VMEM((modes * 9 * height, lanes), F32),
                pltpu.VMEM((3 * height * lanes, 2 * modes), BF16),
                pltpu.VMEM((block * 3 * height, lanes), F32),
                pltpu.VMEM((2 * block, 3 * height * lanes), BF16),
            ],
            compiler_params=params,
        )(where, pairs, coeffs, *own, *other)
    with jax.named_scope("edge_terms"):
        total = pl.pallas_call(
            functools.partial(edge_kernel, sizes=sizes),
            out_shape=jax.ShapeDtypeStruct((count, modes), F32),
            in_specs=[smem, smem] + [vmem] * 5,
            out_specs=vmem,
            scratch_shapes=[
                pltpu.VMEM((block_rows * 3, snaps, lanes), F32),
                pltpu.VMEM((modes * height, lanes), F32),
                pltpu.VMEM((modes * 3 * height, lanes), F32),
                pltpu.VMEM((3 * height * lanes, 2 * modes), BF16),
                pltpu.VMEM((block * 3 * height, lanes), F32),
                pltpu.VMEM((2 * block, 3 * height * lanes), BF16),
            ],
            compiler_params=params,
        )(where, pairs, coeffs, next_own, next_other, near, partial)
    with jax.named_scope("sum_over_rows"):
        blocks = total.reshape(tm_count, chips * share, modes)
        summed = blocks[0]
        for peer in range(1, tm_count):
            summed = summed + lax.ppermute(blocks[peer], "tm", across(peer))
    with jax.named_scope("sum_over_chips"):
        shares = summed.reshape(chips, share, modes)
        result = shares[0]
        for step in range(1, chips):
            shift = [
                (2 * chip + c, 2 * ((chip + step) % chips) + c) for chip in range(chips) for c in range(2)
            ]
            result = result + lax.ppermute(shares[step], "space", shift)
        return result * factor


def solution(mesh):
    placed = (P("tm", None, "space", None, None), P(), P())
    return jax.shard_map(
        shards, mesh=mesh, in_specs=placed, out_specs=P(("tm", "space"), None), check_vma=False
    )
```

```python
import functools

import jax
import jax.numpy as jnp
from jax import lax
from jax.experimental import pallas as pl
from jax.experimental.pallas import tpu as pltpu
from jax.sharding import PartitionSpec as P

F32 = jnp.float32
BF16 = jnp.bfloat16
VMEM_BYTES = 56 * 2**20


def split_high_low(values):
    high = values.astype(BF16)
    low = (values - high.astype(F32)).astype(BF16)
    return high, low


def pack_kernel(where_ref, field_ref, *out_refs, sizes):
    local_s, rows_y, block_rows, tm_count = sizes
    t = where_ref[0]
    for peer in range(tm_count):
        first_row = jnp.bitwise_xor(t, peer) * block_rows
        for row in range(block_rows + 2):
            y = first_row + row if row < block_rows else (first_row - 1 if row == block_rows else first_row + block_rows)
            inside = jnp.logical_and(y >= 0, y < rows_y)
            y = jnp.clip(y, 0, rows_y - 1)
            for c in range(3):
                slab = field_ref[pl.ds(c * rows_y + y, local_s, stride=3 * rows_y), :]
                if row >= block_rows:
                    slab = jnp.where(inside, slab, 0.0)
                out_refs[peer][row * 3 + c] = slab


def mode_weights(where_ref, coeffs_ref, local_s, tm_count):
    t = where_ref[0]
    ordered = jnp.concatenate(
        [
            coeffs_ref[pl.ds(pl.multiple_of(jnp.bitwise_xor(t, peer) * local_s, 8), local_s), :]
            for peer in range(tm_count)
        ],
        axis=0,
    )
    high, low = split_high_low(ordered.T)
    return jnp.concatenate([high, low, high, low], axis=1)


def modes_of(weights, slab):
    high, low = split_high_low(slab)
    return jnp.dot(weights, jnp.concatenate([high, high, low, low], axis=0), preferred_element_type=F32)


def store_projection(rhs_ref, place, mode_slab):
    high, low = split_high_low(mode_slab.T)
    modes = mode_slab.shape[0]
    lanes = mode_slab.shape[1]
    rhs_ref[place * lanes : (place + 1) * lanes, 0:modes] = high
    rhs_ref[place * lanes : (place + 1) * lanes, modes : 2 * modes] = low


def pair_position(where_ref, group, sizes):
    tm_count, chips, share = sizes
    t, chip, core = where_ref[0], where_ref[1], where_ref[2]
    peer, ahead = lax.div(group, chips), lax.rem(group, chips)
    to_t = jnp.bitwise_xor(t, peer)
    to_chip = lax.rem(chip + ahead, chips)
    return ((to_t * chips + to_chip) * 2 + core) * share


def project(conv_ref, lhs_ref, rhs_ref, block, places, lanes):
    for place in range(places):
        values = conv_ref[pl.ds(place, block, stride=places), :]
        high, low = split_high_low(values)
        lhs_ref[0:block, place * lanes : (place + 1) * lanes] = high
        lhs_ref[block : 2 * block, place * lanes : (place + 1) * lanes] = low
    both = jnp.dot(lhs_ref[...], rhs_ref[...], preferred_element_type=F32)
    modes = both.shape[1] // 2
    return (both[:block, :modes] + both[:block, modes:]) + (both[block:, :modes] + both[block:, modes:])


def main_kernel(
    where_ref, pairs_ref, coeffs_ref, *refs, sizes
):
    local_s, block_rows, tm_count, chips, share = sizes
    own, other = refs[:tm_count], refs[tm_count : 2 * tm_count]
    out_ref, next_ref = refs[2 * tm_count : 2 * tm_count + 2]
    field_ref, slab_ref, carry_ref, slope_ref, rhs_ref, conv_ref, lhs_ref = refs[2 * tm_count + 2 :]
    core = where_ref[2]
    modes, lanes = coeffs_ref.shape[1], own[0].shape[2]
    height = 2 * block_rows
    for peer in range(tm_count):
        rows = pl.ds(peer * local_s, local_s)
        field_ref[core, :, rows, :] = own[peer][...]
        field_ref[1 - core, :, rows, :] = other[peer][...]
    weights = mode_weights(where_ref, coeffs_ref, local_s, tm_count)

    def one_slab(index, _):
        both = jnp.concatenate([field_ref[0, index], field_ref[1, index]], axis=1)
        result = modes_of(weights, both)
        slab_ref[0, index] = result[:, :lanes]
        slab_ref[1, index] = result[:, lanes:]
        return 0

    lax.fori_loop(0, (block_rows + 2) * 3, one_slab, 0, unroll=2)
    for c in range(3):
        for row in range(block_rows):
            above = (row + 1 if row + 1 < block_rows else block_rows + 1) * 3 + c
            below = (row - 1 if row > 0 else block_rows) * 3 + c
            center = row * 3 + c
            for plane in range(2):
                place = plane * block_rows + row
                value = slab_ref[plane, center]
                other_plane = slab_ref[1 - plane, center]
                stream = other_plane * (0.5 if plane == 0 else -0.5)
                normal = (slab_ref[plane, above] - slab_ref[plane, below]) * 0.5
                span = (pltpu.roll(value, lanes - 1, 1) - pltpu.roll(value, 1, 1)) * 0.5
                carry_ref[pl.ds(c * height + place, modes, stride=3 * height), :] = value
                for d, slope in enumerate((stream, normal, span)):
                    slope_ref[pl.ds((d * 3 + c) * height + place, modes, stride=9 * height), :] = slope
                store_projection(rhs_ref, c * height + place, value)
                if plane == 1:
                    next_ref[row * 3 + c] = value
    block = conv_ref.shape[0] // (3 * height)

    def one_block(number, _):
        first = number * block

        for group in range(block // share):
            base = pair_position(where_ref, number * (block // share) + group, (tm_count, chips, share))

            def one_pair(q, _):
                position = 2 * (base + q)
                i, j = pairs_ref[position], pairs_ref[position + 1]
                carry = carry_ref[pl.ds(pl.multiple_of(i * (3 * height), 8), 3 * height), :]
                slope = slope_ref[pl.ds(pl.multiple_of(j * (9 * height), 8), 9 * height), :]
                rows = [
                    sum(
                        carry[d * height : (d + 1) * height] * slope[(d * 3 + c) * height : (d * 3 + c + 1) * height]
                        for d in range(3)
                    )
                    for c in range(3)
                ]
                target = pl.ds(pl.multiple_of((group * share + q) * (3 * height), 8), 3 * height)
                conv_ref[target, :] = jnp.concatenate(rows, axis=0)
                return 0

            lax.fori_loop(0, share, one_pair, 0, unroll=16)
        out_ref[pl.ds(pl.multiple_of(first, 8), block), :] = project(
            conv_ref, lhs_ref, rhs_ref, block, 3 * height, lanes
        )
        return 0

    lax.fori_loop(0, out_ref.shape[0] // block, one_block, 0)


def edge_kernel(where_ref, pairs_ref, coeffs_ref, *refs, sizes):
    local_s, block_rows, tm_count, chips, share = sizes
    own_ref, other_ref, near_ref, partial_ref = refs[:4]
    out_ref = refs[4]
    field_ref, carry_ref, slope_ref, rhs_ref, conv_ref, lhs_ref = refs[5:]
    core = where_ref[2]
    modes, lanes = coeffs_ref.shape[1], own_ref.shape[3]
    height = 2 * block_rows
    half = tm_count // 2
    for place in range(half):
        field_ref[:, pl.ds(pl.multiple_of((core * half + place) * local_s, 8), local_s), :] = own_ref[place]
        field_ref[:, pl.ds(pl.multiple_of(((1 - core) * half + place) * local_s, 8), local_s), :] = other_ref[place]
    weights = mode_weights(where_ref, coeffs_ref, local_s, tm_count)
    for c in range(3):
        for row in range(block_rows):
            near = near_ref[row * 3 + c]
            far = modes_of(weights, field_ref[row * 3 + c])
            for place, value, across in ((row, near, far * 0.5), (block_rows + row, far, near * -0.5)):
                if c == 0:
                    carry_ref[pl.ds(place, modes, stride=height), :] = value
                slope_ref[pl.ds(c * height + place, modes, stride=3 * height), :] = across
                store_projection(rhs_ref, c * height + place, value)
    block = conv_ref.shape[0] // (3 * height)

    def one_block(number, _):
        first = number * block

        for group in range(block // share):
            base = pair_position(where_ref, number * (block // share) + group, (tm_count, chips, share))

            def one_pair(q, _):
                position = 2 * (base + q)
                i, j = pairs_ref[position], pairs_ref[position + 1]
                carry = carry_ref[pl.ds(pl.multiple_of(i * height, 8), height), :]
                slope = slope_ref[pl.ds(pl.multiple_of(j * (3 * height), 8), 3 * height), :]
                rows = [carry * slope[c * height : (c + 1) * height] for c in range(3)]
                target = pl.ds(pl.multiple_of((group * share + q) * (3 * height), 8), 3 * height)
                conv_ref[target, :] = jnp.concatenate(rows, axis=0)
                return 0

            lax.fori_loop(0, share, one_pair, 0, unroll=16)
        rows = pl.ds(pl.multiple_of(first, 8), block)
        out_ref[rows, :] = partial_ref[rows, :] + project(conv_ref, lhs_ref, rhs_ref, block, 3 * height, lanes)
        return 0

    lax.fori_loop(0, out_ref.shape[0] // block, one_block, 0)


def shards(snapshots, coeffs, pair_table):
    tm_count, space_count = lax.axis_size("tm"), lax.axis_size("space")
    chips = space_count // 2
    t, place = lax.axis_index("tm"), lax.axis_index("space")
    core = lax.rem(place, 2)
    where = jnp.stack([t, lax.div(place, 2), core]).astype(jnp.int32)
    local_s, _, _, rows_y, lanes = snapshots.shape
    block_rows = rows_y // tm_count
    modes = coeffs.shape[1]
    share = pair_table.shape[0] // (tm_count * space_count)
    count = tm_count * chips * share
    factor = float(space_count * rows_y * lanes) ** (-0.5)
    pairs = pair_table.reshape(-1)
    smem = pl.BlockSpec(memory_space=pltpu.SMEM)
    vmem = pl.BlockSpec(memory_space=pltpu.VMEM)
    params = pltpu.CompilerParams(vmem_limit_bytes=VMEM_BYTES)
    height = 2 * block_rows
    block = 128

    swap = [(2 * chip + c, 2 * chip + 1 - c) for chip in range(chips) for c in range(2)]

    def across(peer):
        return [(i, i ^ peer) for i in range(tm_count)]

    with jax.named_scope("pack"):
        packed = pl.pallas_call(
            functools.partial(pack_kernel, sizes=(local_s, rows_y, block_rows, tm_count)),
            out_shape=[jax.ShapeDtypeStruct(((block_rows + 2) * 3, local_s, lanes), F32)] * tm_count,
            in_specs=[smem, vmem],
            out_specs=[vmem] * tm_count,
            compiler_params=params,
        )(where, snapshots.reshape(-1, lanes))
    with jax.named_scope("to_rows"):
        own = [packed[0]] + [lax.ppermute(packed[peer], "tm", across(peer)) for peer in range(1, tm_count)]
    with jax.named_scope("to_next_chip"):
        half = tm_count // 2
        halves = [
            jnp.stack([piece[: block_rows * 3] for piece in own[c * half : (c + 1) * half]]) for c in range(2)
        ]
        ahead = [
            lax.ppermute(
                halves[c], "space", [(2 * ((chip + 1) % chips), 2 * chip + c) for chip in range(chips)]
            )
            for c in range(2)
        ]
    with jax.named_scope("to_other_core"):
        other = [lax.ppermute(piece, "space", swap) for piece in own]
    with jax.named_scope("inner_terms"):
        sizes = (local_s, block_rows, tm_count, chips, share)
        snaps = local_s * tm_count
        partial, near = pl.pallas_call(
            functools.partial(main_kernel, sizes=sizes),
            out_shape=[
                jax.ShapeDtypeStruct((count, modes), F32),
                jax.ShapeDtypeStruct((block_rows * 3, modes, lanes), F32),
            ],
            in_specs=[smem, smem] + [vmem] * (1 + 2 * tm_count),
            out_specs=[vmem, vmem],
            scratch_shapes=[
                pltpu.VMEM((2, (block_rows + 2) * 3, snaps, lanes), F32),
                pltpu.VMEM((2, (block_rows + 2) * 3, modes, lanes), F32),
                pltpu.VMEM((modes * 3 * height, lanes), F32),
                pltpu.VMEM((modes * 9 * height, lanes), F32),
                pltpu.VMEM((3 * height * lanes, 2 * modes), BF16),
                pltpu.VMEM((block * 3 * height, lanes), F32),
                pltpu.VMEM((2 * block, 3 * height * lanes), BF16),
            ],
            compiler_params=params,
            cost_estimate=pl.CostEstimate(flops=30 * 10**9, bytes_accessed=10**7, transcendentals=0),
        )(where, pairs, coeffs, *own, *other)
    with jax.named_scope("next_to_other_core"):
        ahead, partial = lax.optimization_barrier((ahead, partial))
        next_own = jnp.where(core == 0, ahead[0], ahead[1])
        next_other = lax.ppermute(next_own, "space", swap)
    with jax.named_scope("edge_terms"):
        total = pl.pallas_call(
            functools.partial(edge_kernel, sizes=sizes),
            out_shape=jax.ShapeDtypeStruct((count, modes), F32),
            in_specs=[smem, smem] + [vmem] * 5,
            out_specs=vmem,
            scratch_shapes=[
                pltpu.VMEM((block_rows * 3, snaps, lanes), F32),
                pltpu.VMEM((modes * height, lanes), F32),
                pltpu.VMEM((modes * 3 * height, lanes), F32),
                pltpu.VMEM((3 * height * lanes, 2 * modes), BF16),
                pltpu.VMEM((block * 3 * height, lanes), F32),
                pltpu.VMEM((2 * block, 3 * height * lanes), BF16),
            ],
            compiler_params=params,
        )(where, pairs, coeffs, next_own, next_other, near, partial)
    with jax.named_scope("sum_over_rows"):
        blocks = total.reshape(tm_count, chips * share, modes)
        summed = blocks[0]
        for peer in range(1, tm_count):
            summed = summed + lax.ppermute(blocks[peer], "tm", across(peer))
    with jax.named_scope("sum_over_chips"):
        shares = summed.reshape(chips, share, modes)
        result = shares[0]
        for step in range(1, chips):
            shift = [
                (2 * chip + c, 2 * ((chip + step) % chips) + c) for chip in range(chips) for c in range(2)
            ]
            result = result + lax.ppermute(shares[step], "space", shift)
        return result * factor


def solution(mesh):
    placed = (P("tm", None, "space", None, None), P(), P())
    return jax.shard_map(
        shards, mesh=mesh, in_specs=placed, out_specs=P(("tm", "space"), None), check_vma=False
    )
```

```python
import functools

import jax
import jax.numpy as jnp
from jax import lax
from jax.experimental import pallas as pl
from jax.experimental.pallas import tpu as pltpu
from jax.sharding import PartitionSpec as P

F32 = jnp.float32
BF16 = jnp.bfloat16
VMEM_BYTES = 56 * 2**20


def split_high_low(values):
    high = values.astype(BF16)
    low = (values - high.astype(F32)).astype(BF16)
    return high, low


def pack_kernel(where_ref, field_ref, *out_refs, sizes):
    local_s, rows_y, block_rows, tm_count = sizes
    t = where_ref[0]
    half_s = local_s // 2
    for peer in range(tm_count):
        first_row = jnp.bitwise_xor(t, peer) * block_rows
        for row in range(block_rows + 2):
            if row < block_rows:
                y = first_row + row
            else:
                y = first_row - 1 if row == block_rows else first_row + block_rows
                inside = jnp.logical_and(y >= 0, y < rows_y)
                y = jnp.clip(y, 0, rows_y - 1)
            for c in range(3):
                slab = field_ref[pl.ds(c * rows_y + y, local_s, stride=3 * rows_y), :]
                if row < block_rows:
                    for part in range(2):
                        out_refs[tm_count + part][peer, row * 3 + c] = slab[part * half_s : (part + 1) * half_s]
                else:
                    slab = jnp.where(inside, slab, 0.0)
                out_refs[peer][row * 3 + c] = slab


def mode_weights(where_ref, coeffs_ref, local_s, tm_count):
    t = where_ref[0]
    ordered = jnp.concatenate(
        [
            coeffs_ref[pl.ds(pl.multiple_of(jnp.bitwise_xor(t, peer) * local_s, 8), local_s), :]
            for peer in range(tm_count)
        ],
        axis=0,
    )
    high, low = split_high_low(ordered.T)
    return jnp.concatenate([high, low, high, low], axis=1)


def modes_of(weights, slab):
    high, low = split_high_low(slab)
    return jnp.dot(weights, jnp.concatenate([high, high, low, low], axis=0), preferred_element_type=F32)


def store_projection(rhs_ref, place, mode_slab):
    high, low = split_high_low(mode_slab.T)
    modes, lanes = mode_slab.shape
    rhs_ref[place * lanes : (place + 1) * lanes, 0:modes] = high
    rhs_ref[place * lanes : (place + 1) * lanes, modes : 2 * modes] = low


def project(conv_ref, lhs_ref, rhs_ref, block, places, pitch, lanes):
    for place in range(places):
        values = conv_ref[pl.ds(place, block, stride=pitch), :]
        high, low = split_high_low(values)
        lhs_ref[0:block, place * lanes : (place + 1) * lanes] = high
        lhs_ref[block : 2 * block, place * lanes : (place + 1) * lanes] = low
    both = jnp.dot(lhs_ref[...], rhs_ref[...], preferred_element_type=F32)
    modes = both.shape[1] // 2
    return (both[:block, :modes] + both[:block, modes:]) + (both[block:, :modes] + both[block:, modes:])


def round_up(count):
    return -(-count // 8) * 8


def terms_kernel(where_ref, pairs_ref, coeffs_ref, *refs, sizes):
    local_s, block_rows, tm_count, chips, share = sizes
    own, other = refs[:tm_count], refs[tm_count : 2 * tm_count]
    next_own, next_other = refs[2 * tm_count : 3 * tm_count], refs[3 * tm_count]
    out_refs = refs[3 * tm_count + 1 : 4 * tm_count + 1]
    slab_ref, far_ref, carry_ref, slope_ref, rhs_ref, conv_ref, lhs_ref = refs[4 * tm_count + 1 :]
    t, chip, core = where_ref[0], where_ref[1], where_ref[2]
    modes, lanes = coeffs_ref.shape[1], own[0].shape[2]
    height = 2 * block_rows
    inner = 3 * height
    pitch = inner + round_up(3 * block_rows)
    slope_pitch = 3 * inner + round_up(3 * block_rows)
    weights = mode_weights(where_ref, coeffs_ref, local_s, tm_count)

    def one_slab(index, _):
        own_slab = jnp.concatenate([piece[index] for piece in own], axis=0)
        other_slab = jnp.concatenate([piece[index] for piece in other], axis=0)
        is_first = core == 0
        both = jnp.concatenate(
            [jnp.where(is_first, own_slab, other_slab), jnp.where(is_first, other_slab, own_slab)], axis=1
        )
        result = modes_of(weights, both)
        slab_ref[0, index] = result[:, :lanes]
        slab_ref[1, index] = result[:, lanes:]
        return 0

    lax.fori_loop(0, (block_rows + 2) * 3, one_slab, 0, unroll=3)

    def one_far(index, _):
        slabs = []
        for slab in (2 * index, 2 * index + 1):
            halves = []
            for peer in range(tm_count):
                mine, theirs = next_own[peer][slab], next_other[peer, slab]
                halves += [jnp.where(core == 0, mine, theirs), jnp.where(core == 0, theirs, mine)]
            slabs.append(jnp.concatenate(halves, axis=0))
        result = modes_of(weights, jnp.concatenate(slabs, axis=1))
        far_ref[2 * index] = result[:, :lanes]
        far_ref[2 * index + 1] = result[:, lanes:]
        return 0

    lax.fori_loop(0, block_rows * 3 // 2, one_far, 0, unroll=3)
    for c in range(3):
        for row in range(block_rows):
            above = (row + 1 if row + 1 < block_rows else block_rows + 1) * 3 + c
            below = (row - 1 if row > 0 else block_rows) * 3 + c
            center = row * 3 + c
            first, second, far = slab_ref[0, center], slab_ref[1, center], far_ref[center]
            streams = (second * 0.5, (far - first) * 0.5)
            for plane, value in enumerate((first, second)):
                place = plane * block_rows + row
                normal = (slab_ref[plane, above] - slab_ref[plane, below]) * 0.5
                span = (pltpu.roll(value, lanes - 1, 1) - pltpu.roll(value, 1, 1)) * 0.5
                carry_ref[pl.ds(c * height + place, modes, stride=pitch), :] = value
                for d, slope in enumerate((streams[plane], normal, span)):
                    slope_ref[pl.ds((d * 3 + c) * height + place, modes, stride=slope_pitch), :] = slope
                store_projection(rhs_ref, c * height + place, value)
            if c == 0:
                for copy in range(3):
                    carry_ref[pl.ds(inner + copy * block_rows + row, modes, stride=pitch), :] = far
            slope_ref[pl.ds(3 * inner + c * block_rows + row, modes, stride=slope_pitch), :] = second * -0.5
            store_projection(rhs_ref, inner + c * block_rows + row, far)
    block = chips * share
    for peer in range(tm_count):
        to_t = jnp.bitwise_xor(t, peer)
        for ahead in range(chips):
            base = ((to_t * chips + lax.rem(chip + ahead, chips)) * 2 + core) * share

            def one_pair(q, _):
                position = 2 * (base + q)
                i, j = pairs_ref[position], pairs_ref[position + 1]
                carry = carry_ref[pl.ds(pl.multiple_of(i * pitch, 8), pitch), :]
                slope = slope_ref[pl.ds(pl.multiple_of(j * slope_pitch, 8), slope_pitch), :]
                rows = [
                    sum(
                        carry[d * height : (d + 1) * height] * slope[(d * 3 + c) * height : (d * 3 + c + 1) * height]
                        for d in range(3)
                    )
                    for c in range(3)
                ]
                rows.append(carry[inner:] * slope[3 * inner :])
                target = pl.ds(pl.multiple_of((ahead * share + q) * pitch, 8), pitch)
                conv_ref[target, :] = jnp.concatenate(rows, axis=0)
                return 0

            lax.fori_loop(0, share, one_pair, 0, unroll=16)
        out_refs[peer][...] = project(conv_ref, lhs_ref, rhs_ref, block, inner + 3 * block_rows, pitch, lanes)


def in_vmem(array):
    return pltpu.with_memory_space_constraint(array, pltpu.VMEM)


def shards(snapshots, coeffs, pair_table):
    tm_count, space_count = lax.axis_size("tm"), lax.axis_size("space")
    chips = space_count // 2
    t, place = lax.axis_index("tm"), lax.axis_index("space")
    core = lax.rem(place, 2)
    where = jnp.stack([t, lax.div(place, 2), core]).astype(jnp.int32)
    local_s, _, _, rows_y, lanes = snapshots.shape
    modes = coeffs.shape[1]
    block_rows = rows_y // tm_count
    share = pair_table.shape[0] // (tm_count * space_count)
    factor = float(space_count * rows_y * lanes) ** (-0.5)
    pairs = pair_table.reshape(-1)
    smem = pl.BlockSpec(memory_space=pltpu.SMEM)
    vmem = pl.BlockSpec(memory_space=pltpu.VMEM)
    params = pltpu.CompilerParams(vmem_limit_bytes=VMEM_BYTES)
    half_s = local_s // 2
    block = chips * share
    height = 2 * block_rows
    depth = 3 * height + 3 * block_rows
    pitch = 3 * height + round_up(3 * block_rows)
    slope_pitch = 9 * height + round_up(3 * block_rows)

    swap = [(2 * chip + c, 2 * chip + 1 - c) for chip in range(chips) for c in range(2)]

    def across(peer):
        return [(i, i ^ peer) for i in range(tm_count)]

    with jax.named_scope("pack"):
        packed = pl.pallas_call(
            functools.partial(pack_kernel, sizes=(local_s, rows_y, block_rows, tm_count)),
            out_shape=[jax.ShapeDtypeStruct(((block_rows + 2) * 3, local_s, lanes), F32)] * tm_count
            + [jax.ShapeDtypeStruct((tm_count, block_rows * 3, half_s, lanes), F32)] * 2,
            in_specs=[smem, vmem],
            out_specs=[vmem] * (tm_count + 2),
            compiler_params=params,
        )(where, snapshots.reshape(-1, lanes))
    with jax.named_scope("to_chip_before"):
        ahead = [
            lax.ppermute(
                packed[tm_count + c], "space", [(2 * ((chip + 1) % chips), 2 * chip + c) for chip in range(chips)]
            )
            for c in range(2)
        ]
    with jax.named_scope("to_rows"):
        own = [packed[0]] + [lax.ppermute(packed[peer], "tm", across(peer)) for peer in range(1, tm_count)]
    with jax.named_scope("to_other_core"):
        other = [lax.ppermute(piece, "space", swap) for piece in own]
    with jax.named_scope("next_to_rows"):
        ahead, own = lax.optimization_barrier((ahead, own))
        parts = [jnp.where(core == 0, ahead[0][peer], ahead[1][peer]) for peer in range(tm_count)]
        next_own = [parts[0]] + [lax.ppermute(parts[peer], "tm", across(peer)) for peer in range(1, tm_count)]
    with jax.named_scope("next_to_other_core"):
        next_other = lax.ppermute(jnp.stack(next_own), "space", swap)
    with jax.named_scope("terms"):
        blocks = pl.pallas_call(
            functools.partial(terms_kernel, sizes=(local_s, block_rows, tm_count, chips, share)),
            out_shape=[jax.ShapeDtypeStruct((block, modes), F32)] * tm_count,
            in_specs=[smem, smem] + [vmem] * (3 * tm_count + 2),
            out_specs=[vmem] * tm_count,
            scratch_shapes=[
                pltpu.VMEM((2, (block_rows + 2) * 3, modes, lanes), F32),
                pltpu.VMEM((block_rows * 3, modes, lanes), F32),
                pltpu.VMEM((modes * pitch, lanes), F32),
                pltpu.VMEM((modes * slope_pitch, lanes), F32),
                pltpu.VMEM((depth * lanes, 2 * modes), BF16),
                pltpu.VMEM((block * pitch, lanes), F32),
                pltpu.VMEM((2 * block, depth * lanes), BF16),
            ],
            compiler_params=params,
        )(where, pairs, coeffs, *[in_vmem(piece) for piece in (*own, *other, *next_own, next_other)])
    with jax.named_scope("sum_over_rows"):
        summed = blocks[0]
        for peer in range(1, tm_count):
            summed = summed + lax.ppermute(blocks[peer], "tm", across(peer))
    with jax.named_scope("sum_over_chips"):
        shares = summed.reshape(chips, share, modes)
        result = shares[0]
        for step in range(1, chips):
            shift = [
                (2 * chip + c, 2 * ((chip + step) % chips) + c) for chip in range(chips) for c in range(2)
            ]
            result = result + lax.ppermute(shares[step], "space", shift)
        return result * factor


def solution(mesh):
    placed = (P("tm", None, "space", None, None), P(), P())
    return jax.shard_map(
        shards, mesh=mesh, in_specs=placed, out_specs=P(("tm", "space"), None), check_vma=False
    )
```

```python
import functools

import jax
import jax.numpy as jnp
from jax import lax
from jax.experimental import pallas as pl
from jax.experimental.pallas import tpu as pltpu
from jax.sharding import PartitionSpec as P

F32 = jnp.float32
BF16 = jnp.bfloat16


def split_high_low(values):
    high = values.astype(BF16)
    low = (values - high.astype(F32)).astype(BF16)
    return high, low


def pack_kernel(where_ref, field_ref, *out_refs, sizes):
    local_s, rows_y, block_rows, tm_count = sizes
    t = where_ref[0]
    half_s = local_s // 2
    for peer in range(tm_count):
        first_row = jnp.bitwise_xor(t, peer) * block_rows
        for row in range(block_rows + 2):
            if row < block_rows:
                y = first_row + row
            else:
                y = first_row - 1 if row == block_rows else first_row + block_rows
                inside = jnp.logical_and(y >= 0, y < rows_y)
                y = jnp.clip(y, 0, rows_y - 1)
            for c in range(3):
                slab = field_ref[pl.ds(c * rows_y + y, local_s, stride=3 * rows_y), :]
                if row < block_rows:
                    for part in range(2):
                        out_refs[tm_count + part][peer, row * 3 + c] = slab[part * half_s : (part + 1) * half_s]
                else:
                    slab = jnp.where(inside, slab, 0.0)
                out_refs[peer][row * 3 + c] = slab


def mode_weights(where_ref, coeffs_ref, local_s, tm_count):
    t = where_ref[0]
    ordered = jnp.concatenate(
        [
            coeffs_ref[pl.ds(pl.multiple_of(jnp.bitwise_xor(t, peer) * local_s, 8), local_s), :]
            for peer in range(tm_count)
        ],
        axis=0,
    )
    high, low = split_high_low(ordered.T)
    return jnp.concatenate([high, low, high, low], axis=1)


def modes_of(weights, slab):
    high, low = split_high_low(slab)
    return jnp.dot(weights, jnp.concatenate([high, high, low, low], axis=0), preferred_element_type=F32)


def store_projection(rhs_ref, place, mode_slab):
    high, low = split_high_low(mode_slab.T)
    modes, lanes = mode_slab.shape
    rhs_ref[place * lanes : (place + 1) * lanes, 0:modes] = high
    rhs_ref[place * lanes : (place + 1) * lanes, modes : 2 * modes] = low


def project(conv_ref, lhs_ref, rhs_ref, block, places, lanes):
    for place in range(places):
        values = conv_ref[pl.ds(place, block, stride=places), :]
        high, low = split_high_low(values)
        lhs_ref[0:block, place * lanes : (place + 1) * lanes] = high
        lhs_ref[block : 2 * block, place * lanes : (place + 1) * lanes] = low
    both = jnp.dot(lhs_ref[...], rhs_ref[...], preferred_element_type=F32)
    modes = both.shape[1] // 2
    return (both[:block, :modes] + both[:block, modes:]) + (both[block:, :modes] + both[block:, modes:])


def for_pairs_of(where_ref, pairs_ref, peer, sizes, one_pair):
    chips, share = sizes
    t, chip, core = where_ref[0], where_ref[1], where_ref[2]
    to_t = jnp.bitwise_xor(t, peer)
    for ahead in range(chips):
        base = ((to_t * chips + lax.rem(chip + ahead, chips)) * 2 + core) * share

        def one(q, _):
            one_pair(ahead * share + q, pairs_ref[0, base + q], pairs_ref[1, base + q])
            return 0

        lax.fori_loop(0, share, one, 0, unroll=16)


def inner_kernel(where_ref, pairs_ref, coeffs_ref, *refs, peers, sizes):
    local_s, block_rows, tm_count, chips, share = sizes
    own, other = refs[:tm_count], refs[tm_count : 2 * tm_count]
    near_ref, carry_ref, slope_ref, rhs_ref = refs[2 * tm_count : 2 * tm_count + 4]
    *out_refs, slab_ref, conv_ref, lhs_ref = refs[2 * tm_count + 4 :]
    core = where_ref[2]
    modes, lanes = coeffs_ref.shape[1], own[0].shape[2]
    height = 2 * block_rows
    weights = mode_weights(where_ref, coeffs_ref, local_s, tm_count)

    def one_slab(index, _):
        own_slab = jnp.concatenate([piece[index] for piece in own], axis=0)
        other_slab = jnp.concatenate([piece[index] for piece in other], axis=0)
        is_first = core == 0
        both = jnp.concatenate(
            [jnp.where(is_first, own_slab, other_slab), jnp.where(is_first, other_slab, own_slab)], axis=1
        )
        result = modes_of(weights, both)
        slab_ref[0, index] = result[:, :lanes]
        slab_ref[1, index] = result[:, lanes:]
        return 0

    lax.fori_loop(0, (block_rows + 2) * 3, one_slab, 0, unroll=3)
    for c in range(3):
        for row in range(block_rows):
            above = (row + 1 if row + 1 < block_rows else block_rows + 1) * 3 + c
            below = (row - 1 if row > 0 else block_rows) * 3 + c
            center = row * 3 + c
            for plane in range(2):
                place = plane * block_rows + row
                value = slab_ref[plane, center]
                stream = slab_ref[1 - plane, center] * (0.5 if plane == 0 else -0.5)
                normal = (slab_ref[plane, above] - slab_ref[plane, below]) * 0.5
                span = (pltpu.roll(value, lanes - 1, 1) - pltpu.roll(value, 1, 1)) * 0.5
                carry_ref[pl.ds(c * height + place, modes, stride=3 * height), :] = value
                for d, slope in enumerate((stream, normal, span)):
                    slope_ref[pl.ds((d * 3 + c) * height + place, modes, stride=9 * height), :] = slope
                store_projection(rhs_ref, c * height + place, value)
                if plane == 1:
                    near_ref[center] = value

    pairs_kernel(
        where_ref, pairs_ref, carry_ref, slope_ref, rhs_ref, *out_refs, conv_ref, lhs_ref,
        peers=peers, sizes=(height, chips, share),
    )


def pairs_kernel(where_ref, pairs_ref, carry_ref, slope_ref, rhs_ref, *refs, peers, sizes):
    *out_refs, conv_ref, lhs_ref = refs
    height, chips, share = sizes

    def one_pair(slot, i, j):
        carry = carry_ref[pl.ds(pl.multiple_of(i * (3 * height), 8), 3 * height), :]
        slope = slope_ref[pl.ds(pl.multiple_of(j * (9 * height), 8), 9 * height), :]
        rows = [
            sum(
                carry[d * height : (d + 1) * height] * slope[(d * 3 + c) * height : (d * 3 + c + 1) * height]
                for d in range(3)
            )
            for c in range(3)
        ]
        conv_ref[pl.ds(pl.multiple_of(slot * (3 * height), 8), 3 * height), :] = jnp.concatenate(rows, axis=0)

    for peer, out_ref in zip(peers, out_refs):
        for_pairs_of(where_ref, pairs_ref, peer, (chips, share), one_pair)
        out_ref[...] = project(conv_ref, lhs_ref, rhs_ref, chips * share, 3 * height, conv_ref.shape[1])


def far_kernel(where_ref, coeffs_ref, *refs, sizes):
    local_s, block_rows, tm_count = sizes
    next_own, next_other, near_ref = refs[:tm_count], refs[tm_count], refs[tm_count + 1]
    carry_ref, slope_ref, rhs_ref = refs[tm_count + 2 :]
    is_first = where_ref[2] == 0
    modes, lanes = near_ref.shape[1:]
    height = 2 * block_rows
    weights = mode_weights(where_ref, coeffs_ref, local_s, tm_count)
    for pair in range(3 * block_rows // 2):
        slabs = []
        for slab in (2 * pair, 2 * pair + 1):
            halves = []
            for peer in range(tm_count):
                mine, theirs = next_own[peer][slab], next_other[peer, slab]
                halves += [jnp.where(is_first, mine, theirs), jnp.where(is_first, theirs, mine)]
            slabs.append(jnp.concatenate(halves, axis=0))
        result = modes_of(weights, jnp.concatenate(slabs, axis=1))
        for part in range(2):
            row, c = divmod(2 * pair + part, 3)
            near, far = near_ref[2 * pair + part], result[:, part * lanes : (part + 1) * lanes]
            for place, value, across in ((row, near, far * 0.5), (block_rows + row, far, near * -0.5)):
                if c == 0:
                    carry_ref[pl.ds(place, modes, stride=height), :] = value
                slope_ref[pl.ds(c * height + place, modes, stride=3 * height), :] = across
                store_projection(rhs_ref, c * height + place, value)


def edge_kernel(
    where_ref, pairs_ref, carry_ref, slope_ref, rhs_ref, inner_ref, out_ref, conv_ref, lhs_ref, *, peer, sizes
):
    chips, share = sizes
    modes, lanes = out_ref.shape[1], carry_ref.shape[1]
    height = carry_ref.shape[0] // modes

    def one_pair(slot, i, j):
        carry = carry_ref[pl.ds(pl.multiple_of(i * height, 8), height), :]
        slope = slope_ref[pl.ds(pl.multiple_of(j * (3 * height), 8), 3 * height), :]
        rows = [carry * slope[c * height : (c + 1) * height] for c in range(3)]
        conv_ref[pl.ds(pl.multiple_of(slot * (3 * height), 8), 3 * height), :] = jnp.concatenate(rows, axis=0)

    for_pairs_of(where_ref, pairs_ref, peer, sizes, one_pair)
    out_ref[...] = inner_ref[...] + project(conv_ref, lhs_ref, rhs_ref, chips * share, 3 * height, lanes)


def vmem_limit(mebibytes):
    return pltpu.CompilerParams(vmem_limit_bytes=mebibytes * 2**20)


def in_vmem(array):
    return pltpu.with_memory_space_constraint(array, pltpu.VMEM)


def shards(snapshots, coeffs, pair_table):
    tm_count, space_count = lax.axis_size("tm"), lax.axis_size("space")
    chips = space_count // 2
    t, place = lax.axis_index("tm"), lax.axis_index("space")
    core = lax.rem(place, 2)
    where = jnp.stack([t, lax.div(place, 2), core]).astype(jnp.int32)
    local_s, _, _, rows_y, lanes = snapshots.shape
    modes = coeffs.shape[1]
    block_rows = rows_y // tm_count
    share = pair_table.shape[0] // (tm_count * space_count)
    factor = float(space_count * rows_y * lanes) ** (-0.5)
    pairs = pair_table.T
    smem = pl.BlockSpec(memory_space=pltpu.SMEM)
    vmem = pl.BlockSpec(memory_space=pltpu.VMEM)
    half_s = local_s // 2
    block = chips * share
    height = 2 * block_rows
    depth = 3 * height * lanes

    swap = [(2 * chip + c, 2 * chip + 1 - c) for chip in range(chips) for c in range(2)]

    def across(peer):
        return [(i, i ^ peer) for i in range(tm_count)]

    with jax.named_scope("pack"):
        packed = pl.pallas_call(
            functools.partial(pack_kernel, sizes=(local_s, rows_y, block_rows, tm_count)),
            out_shape=[pltpu.VMEM(((block_rows + 2) * 3, local_s, lanes), F32)] * tm_count
            + [pltpu.VMEM((tm_count, block_rows * 3, half_s, lanes), F32)] * 2,
            in_specs=[smem, vmem],
            out_specs=[vmem] * (tm_count + 2),
            compiler_params=vmem_limit(16),
        )(where, snapshots.reshape(-1, lanes))
    with jax.named_scope("to_chip_before"):
        ahead = [
            lax.ppermute(
                packed[tm_count + c], "space", [(2 * ((chip + 1) % chips), 2 * chip + c) for chip in range(chips)]
            )
            for c in range(2)
        ]
    with jax.named_scope("to_rows"):
        own = [packed[0]] + [lax.ppermute(packed[peer], "tm", across(peer)) for peer in range(1, tm_count)]
    with jax.named_scope("to_other_core"):
        other = [lax.ppermute(piece, "space", swap) for piece in own]
    with jax.named_scope("next_to_rows"):
        ahead, own, other = lax.optimization_barrier((ahead, own, other))
        parts = [jnp.where(core == 0, ahead[0][peer], ahead[1][peer]) for peer in range(tm_count)]
        next_own = [parts[0]] + [lax.ppermute(parts[peer], "tm", across(peer)) for peer in range(1, tm_count)]
    early, late = range(tm_count - 1, tm_count // 2 - 1, -1), range(tm_count // 2 - 1, -1, -1)
    work = [pltpu.VMEM((block * 3 * height, lanes), F32), pltpu.VMEM((2 * block, depth), BF16)]
    group = pltpu.VMEM((block, modes), F32)
    with jax.named_scope("inner_terms"):
        near, *inner_tables_and_early = pl.pallas_call(
            functools.partial(inner_kernel, peers=early, sizes=(local_s, block_rows, tm_count, chips, share)),
            out_shape=[
                pltpu.VMEM((block_rows * 3, modes, lanes), F32),
                pltpu.VMEM((modes * 3 * height, lanes), F32),
                pltpu.VMEM((modes * 9 * height, lanes), F32),
                pltpu.VMEM((depth, 2 * modes), BF16),
            ]
            + [group] * len(early),
            in_specs=[smem, smem] + [vmem] * (2 * tm_count + 1),
            out_specs=[vmem] * (4 + len(early)),
            scratch_shapes=[pltpu.VMEM((2, (block_rows + 2) * 3, modes, lanes), F32)] + work,
            compiler_params=vmem_limit(24),
            cost_estimate=pl.CostEstimate(flops=12 * 10**9, bytes_accessed=10**7, transcendentals=0),
        )(where, pairs, coeffs, *[in_vmem(piece) for piece in (*own, *other)])
        inner_tables, early_sums = inner_tables_and_early[:3], inner_tables_and_early[3:]
    with jax.named_scope("next_to_other_core"):
        next_own, inner_tables = lax.optimization_barrier((next_own, inner_tables))
        next_other = lax.ppermute(jnp.stack(next_own), "space", swap)
    with jax.named_scope("inner_terms"):
        late_sums = pl.pallas_call(
            functools.partial(pairs_kernel, peers=late, sizes=(height, chips, share)),
            out_shape=[group] * len(late),
            in_specs=[smem, smem] + [vmem] * 3,
            out_specs=[vmem] * len(late),
            scratch_shapes=work,
            compiler_params=vmem_limit(16),
            cost_estimate=pl.CostEstimate(flops=8 * 10**9, bytes_accessed=10**7, transcendentals=0),
        )(where, pairs, *[in_vmem(table) for table in inner_tables])
        inner = [*reversed(late_sums), *reversed(early_sums)]
    with jax.named_scope("edge_tables"):
        tables = pl.pallas_call(
            functools.partial(far_kernel, sizes=(local_s, block_rows, tm_count)),
            out_shape=[
                pltpu.VMEM((modes * height, lanes), F32),
                pltpu.VMEM((modes * 3 * height, lanes), F32),
                pltpu.VMEM((depth, 2 * modes), BF16),
            ],
            in_specs=[smem] + [vmem] * (tm_count + 3),
            out_specs=[vmem] * 3,
            compiler_params=vmem_limit(16),
        )(where, coeffs, *[in_vmem(piece) for piece in (*next_own, next_other, near)])
    sums = [None] * tm_count
    arrived = []
    for peer in reversed(range(tm_count)):
        with jax.named_scope("edge_terms"):
            sums[peer] = pl.pallas_call(
                functools.partial(edge_kernel, peer=peer, sizes=(chips, share)),
                out_shape=group,
                in_specs=[smem, smem] + [vmem] * 4,
                out_specs=vmem,
                scratch_shapes=work,
                compiler_params=vmem_limit(16),
                cost_estimate=pl.CostEstimate(flops=4 * 10**9, bytes_accessed=10**7, transcendentals=0),
            )(where, pairs, *[in_vmem(table) for table in (*tables, inner[peer])])
        with jax.named_scope("sum_over_rows"):
            if peer:
                arrived.append(lax.ppermute(sums[peer], "tm", across(peer)))
                inner[peer - 1], _ = lax.optimization_barrier((inner[peer - 1], sums[peer]))
    with jax.named_scope("sum_over_rows"):
        summed = sums[0]
        for part in arrived:
            summed = summed + part
    with jax.named_scope("sum_over_chips"):
        shares = summed.reshape(chips, share, modes)
        result = shares[0]
        for step in range(1, chips):
            shift = [
                (2 * chip + c, 2 * ((chip + step) % chips) + c) for chip in range(chips) for c in range(2)
            ]
            result = result + lax.ppermute(shares[step], "space", shift)
        return result * factor


def solution(mesh):
    placed = (P("tm", None, "space", None, None), P(), P())
    return jax.shard_map(
        shards, mesh=mesh, in_specs=placed, out_specs=P(("tm", "space"), None), check_vma=False
    )
```

```python
import functools

import jax
import jax.numpy as jnp
from jax import lax
from jax.experimental import pallas as pl
from jax.experimental.pallas import tpu as pltpu
from jax.sharding import PartitionSpec as P

F32 = jnp.float32
BF16 = jnp.bfloat16


def split_high_low(values):
    high = values.astype(BF16)
    low = (values - high.astype(F32)).astype(BF16)
    return high, low


def pack_kernel(where_ref, field_ref, *out_refs, sizes):
    local_s, rows_y, block_rows, tm_count = sizes
    t, core = where_ref[0], where_ref[2]
    half = block_rows // 2
    for peer in range(tm_count):
        first_row = jnp.bitwise_xor(t, peer) * block_rows
        for row in range(block_rows + 2):
            if row < block_rows:
                y = first_row + row
            else:
                y = first_row - 1 if row == block_rows else first_row + block_rows
                inside = jnp.logical_and(y >= 0, y < rows_y)
                y = jnp.clip(y, 0, rows_y - 1)
            for c in range(3):
                slab = field_ref[pl.ds(c * rows_y + y, local_s, stride=3 * rows_y), :]
                if row >= block_rows:
                    slab = jnp.where(inside, slab, 0.0)
                out_refs[peer][row * 3 + c] = slab
        out_refs[tm_count][peer] = out_refs[peer][pl.ds(core * (half * 3), half * 3)]


def mode_weights(where_ref, coeffs_ref, local_s, tm_count):
    t = where_ref[0]
    ordered = jnp.concatenate(
        [
            coeffs_ref[pl.ds(pl.multiple_of(jnp.bitwise_xor(t, peer) * local_s, 8), local_s), :]
            for peer in range(tm_count)
        ],
        axis=0,
    )
    high, low = split_high_low(ordered.T)
    return jnp.concatenate([high, low, high, low], axis=1)


def modes_of(weights, slab):
    high, low = split_high_low(slab)
    return jnp.dot(weights, jnp.concatenate([high, high, low, low], axis=0), preferred_element_type=F32)


def store_projection(rhs_ref, place, mode_slab):
    high, low = split_high_low(mode_slab.T)
    modes, lanes = mode_slab.shape
    rhs_ref[place * lanes : (place + 1) * lanes, 0:modes] = high
    rhs_ref[place * lanes : (place + 1) * lanes, modes : 2 * modes] = low


def project(conv_ref, rhs_ref, block, places, lanes):
    both = None
    for place in range(0, places, 2):
        highs, lows = zip(
            *(split_high_low(conv_ref[pl.ds(place + k, block, stride=places), :]) for k in range(2))
        )
        lhs = jnp.concatenate([jnp.concatenate(highs, axis=1), jnp.concatenate(lows, axis=1)], axis=0)
        part = jnp.dot(lhs, rhs_ref[place * lanes : (place + 2) * lanes, :], preferred_element_type=F32)
        both = part if both is None else both + part
    modes = both.shape[1] // 2
    return (both[:block, :modes] + both[:block, modes:]) + (both[block:, :modes] + both[block:, modes:])


def for_pairs_of(where_ref, codes_ref, peer, sizes, one_pair):
    chips, share, bits = sizes
    t, chip, core = where_ref[0], where_ref[1], where_ref[2]
    first_chip = jnp.bitwise_xor(t, peer) * chips

    def one_share(ahead, _):
        to_chip = chip + ahead
        to_chip = jnp.where(to_chip >= chips, to_chip - chips, to_chip)
        base = ((first_chip + to_chip) * 2 + core) * share

        def one(q, _):
            code = codes_ref[base + q]
            one_pair(ahead * share + q, lax.shift_right_logical(code, bits), jnp.bitwise_and(code, 2**bits - 1))
            return 0

        return lax.fori_loop(0, share, one, 0, unroll=32)

    lax.fori_loop(0, chips, one_share, 0)


def inner_kernel(where_ref, codes_ref, coeffs_ref, *refs, peers, sizes):
    local_s, block_rows, tm_count, chips, share, bits = sizes
    own, other = refs[:tm_count], refs[tm_count : 2 * tm_count]
    near_ref, carry_ref, slope_ref, rhs_ref = refs[2 * tm_count : 2 * tm_count + 4]
    *out_refs, slab_ref, conv_ref = refs[2 * tm_count + 4 :]
    core = where_ref[2]
    modes, lanes = coeffs_ref.shape[1], own[0].shape[2]
    height = 2 * block_rows
    weights = mode_weights(where_ref, coeffs_ref, local_s, tm_count)

    def one_slab(index, _):
        own_slab = jnp.concatenate([piece[index] for piece in own], axis=0)
        other_slab = jnp.concatenate([piece[index] for piece in other], axis=0)
        is_first = core == 0
        both = jnp.concatenate(
            [jnp.where(is_first, own_slab, other_slab), jnp.where(is_first, other_slab, own_slab)], axis=1
        )
        result = modes_of(weights, both)
        slab_ref[0, index] = result[:, :lanes]
        slab_ref[1, index] = result[:, lanes:]
        return 0

    lax.fori_loop(0, (block_rows + 2) * 3, one_slab, 0, unroll=3)
    for c in range(3):
        for row in range(block_rows):
            above = (row + 1 if row + 1 < block_rows else block_rows + 1) * 3 + c
            below = (row - 1 if row > 0 else block_rows) * 3 + c
            center = row * 3 + c
            for plane in range(2):
                place = plane * block_rows + row
                value = slab_ref[plane, center]
                stream = slab_ref[1 - plane, center] * (0.5 if plane == 0 else -0.5)
                normal = (slab_ref[plane, above] - slab_ref[plane, below]) * 0.5
                span = (pltpu.roll(value, lanes - 1, 1) - pltpu.roll(value, 1, 1)) * 0.5
                carry_ref[pl.ds(c * height + place, modes, stride=3 * height), :] = value
                for d, slope in enumerate((stream, normal, span)):
                    slope_ref[pl.ds((d * 3 + c) * height + place, modes, stride=9 * height), :] = slope
                store_projection(rhs_ref, c * height + place, value)
                if (plane == 1) == (row < block_rows // 2):
                    near_ref[center] = value

    pairs_kernel(
        where_ref, codes_ref, carry_ref, slope_ref, rhs_ref, *out_refs, conv_ref,
        peers=peers, sizes=(height, chips, share, bits),
    )


def pairs_kernel(where_ref, codes_ref, carry_ref, slope_ref, rhs_ref, *refs, peers, sizes):
    *out_refs, conv_ref = refs
    height, chips, share, bits = sizes

    def one_pair(slot, i, j):
        carry = carry_ref[pl.ds(pl.multiple_of(i * (3 * height), 8), 3 * height), :]
        slope = slope_ref[pl.ds(pl.multiple_of(j * (9 * height), 8), 9 * height), :]
        rows = [
            sum(
                carry[d * height : (d + 1) * height] * slope[(d * 3 + c) * height : (d * 3 + c + 1) * height]
                for d in range(3)
            )
            for c in range(3)
        ]
        conv_ref[pl.ds(pl.multiple_of(slot * (3 * height), 8), 3 * height), :] = jnp.concatenate(rows, axis=0)

    for peer, out_ref in zip(peers, out_refs):
        for_pairs_of(where_ref, codes_ref, peer, (chips, share, bits), one_pair)
        out_ref[...] = project(conv_ref, rhs_ref, chips * share, 3 * height, conv_ref.shape[1])


def far_kernel(where_ref, coeffs_ref, *refs, sizes):
    local_s, block_rows, tm_count = sizes
    next_own, next_other, near_ref = refs[:tm_count], refs[tm_count], refs[tm_count + 1]
    carry_ref, slope_ref, rhs_ref = refs[tm_count + 2 :]
    is_first = where_ref[2] == 0
    modes, lanes = near_ref.shape[1:]
    height = 2 * block_rows
    half = block_rows // 2 * 3
    weights = mode_weights(where_ref, coeffs_ref, local_s, tm_count)
    for slab in range(half):
        mine = jnp.concatenate([next_own[peer][slab] for peer in range(tm_count)], axis=0)
        theirs = jnp.concatenate([next_other[peer, slab] for peer in range(tm_count)], axis=0)
        after, before = jnp.where(is_first, theirs, mine), jnp.where(is_first, mine, theirs)
        result = modes_of(weights, jnp.concatenate([after, before], axis=1))
        row, c = divmod(slab, 3)
        edges = ((near_ref[slab], result[:, :lanes]), (result[:, lanes:], near_ref[half + slab]))
        for number, (low, high) in enumerate(edges):
            place = number * block_rows + 2 * row
            for at, value, across in ((place, low, high * 0.5), (place + 1, high, low * -0.5)):
                if c == 0:
                    carry_ref[pl.ds(at, modes, stride=height), :] = value
                slope_ref[pl.ds(c * height + at, modes, stride=3 * height), :] = across
                store_projection(rhs_ref, c * height + at, value)


def edge_kernel(
    where_ref, codes_ref, carry_ref, slope_ref, rhs_ref, inner_ref, out_ref, conv_ref, *, peer, sizes
):
    chips, share, _ = sizes
    modes, lanes = out_ref.shape[1], carry_ref.shape[1]
    height = carry_ref.shape[0] // modes

    def one_pair(slot, i, j):
        carry = carry_ref[pl.ds(pl.multiple_of(i * height, 8), height), :]
        slope = slope_ref[pl.ds(pl.multiple_of(j * (3 * height), 8), 3 * height), :]
        rows = [carry * slope[c * height : (c + 1) * height] for c in range(3)]
        conv_ref[pl.ds(pl.multiple_of(slot * (3 * height), 8), 3 * height), :] = jnp.concatenate(rows, axis=0)

    for_pairs_of(where_ref, codes_ref, peer, sizes, one_pair)
    out_ref[...] = inner_ref[...] + project(conv_ref, rhs_ref, chips * share, 3 * height, lanes)


def vmem_limit(mebibytes):
    return pltpu.CompilerParams(vmem_limit_bytes=mebibytes * 2**20)


def in_vmem(array):
    return pltpu.with_memory_space_constraint(array, pltpu.VMEM)


def shards(snapshots, coeffs, pair_table):
    tm_count, space_count = lax.axis_size("tm"), lax.axis_size("space")
    chips = space_count // 2
    t, place = lax.axis_index("tm"), lax.axis_index("space")
    core = lax.rem(place, 2)
    where = jnp.stack([t, lax.div(place, 2), core]).astype(jnp.int32)
    local_s, _, _, rows_y, lanes = snapshots.shape
    modes = coeffs.shape[1]
    block_rows = rows_y // tm_count
    share = pair_table.shape[0] // (tm_count * space_count)
    factor = float(space_count * rows_y * lanes) ** (-0.5)
    bits = modes.bit_length() - 1
    assert modes == 2**bits
    codes = pair_table[:, 0] * modes + pair_table[:, 1]
    smem = pl.BlockSpec(memory_space=pltpu.SMEM)
    vmem = pl.BlockSpec(memory_space=pltpu.VMEM)
    block = chips * share
    height = 2 * block_rows
    depth = 3 * height * lanes

    swap = [(2 * chip + c, 2 * chip + 1 - c) for chip in range(chips) for c in range(2)]

    def across(peer):
        return [(i, i ^ peer) for i in range(tm_count)]

    with jax.named_scope("pack"):
        packed = pl.pallas_call(
            functools.partial(pack_kernel, sizes=(local_s, rows_y, block_rows, tm_count)),
            out_shape=[pltpu.VMEM(((block_rows + 2) * 3, local_s, lanes), F32)] * tm_count
            + [pltpu.VMEM((tm_count, block_rows // 2 * 3, local_s, lanes), F32)],
            in_specs=[smem, vmem],
            out_specs=[vmem] * (tm_count + 1),
            compiler_params=vmem_limit(16),
        )(where, snapshots.reshape(-1, lanes))
    with jax.named_scope("to_next_plane"):
        ring = [(place, (place + (1 if place % 2 else -1)) % space_count) for place in range(space_count)]
        across_edge = lax.ppermute(packed[tm_count], "space", ring)
    with jax.named_scope("to_rows"):
        own = [packed[0]] + [lax.ppermute(packed[peer], "tm", across(peer)) for peer in range(1, tm_count)]
    with jax.named_scope("to_other_core"):
        other = [lax.ppermute(piece, "space", swap) for piece in own]
    with jax.named_scope("next_to_rows"):
        across_edge, own, other = lax.optimization_barrier((across_edge, own, other))
        parts = [across_edge[peer] for peer in range(tm_count)]
        next_own = [parts[0]] + [lax.ppermute(parts[peer], "tm", across(peer)) for peer in range(1, tm_count)]
    early, late = range(tm_count - 1, tm_count // 2 - 1, -1), range(tm_count // 2 - 1, -1, -1)
    work = [pltpu.VMEM((block * 3 * height, lanes), F32)]
    group = pltpu.VMEM((block, modes), F32)
    with jax.named_scope("inner_terms"):
        near, *inner_tables_and_early = pl.pallas_call(
            functools.partial(inner_kernel, peers=early, sizes=(local_s, block_rows, tm_count, chips, share, bits)),
            out_shape=[
                pltpu.VMEM((block_rows * 3, modes, lanes), F32),
                pltpu.VMEM((modes * 3 * height, lanes), F32),
                pltpu.VMEM((modes * 9 * height, lanes), F32),
                pltpu.VMEM((depth, 2 * modes), BF16),
            ]
            + [group] * len(early),
            in_specs=[smem, smem] + [vmem] * (2 * tm_count + 1),
            out_specs=[vmem] * (4 + len(early)),
            scratch_shapes=[pltpu.VMEM((2, (block_rows + 2) * 3, modes, lanes), F32)] + work,
            compiler_params=vmem_limit(24),
            cost_estimate=pl.CostEstimate(flops=12 * 10**9, bytes_accessed=10**7, transcendentals=0),
        )(where, codes, coeffs, *[in_vmem(piece) for piece in (*own, *other)])
        inner_tables, early_sums = inner_tables_and_early[:3], inner_tables_and_early[3:]
    with jax.named_scope("next_to_other_core"):
        next_own, inner_tables = lax.optimization_barrier((next_own, inner_tables))
        next_other = lax.ppermute(jnp.stack(next_own), "space", swap)
    with jax.named_scope("inner_terms"):
        late_sums = pl.pallas_call(
            functools.partial(pairs_kernel, peers=late, sizes=(height, chips, share, bits)),
            out_shape=[group] * len(late),
            in_specs=[smem, smem] + [vmem] * 3,
            out_specs=[vmem] * len(late),
            scratch_shapes=work,
            compiler_params=vmem_limit(16),
            cost_estimate=pl.CostEstimate(flops=8 * 10**9, bytes_accessed=10**7, transcendentals=0),
        )(where, codes, *[in_vmem(table) for table in inner_tables])
        inner = [*reversed(late_sums), *reversed(early_sums)]
    with jax.named_scope("edge_tables"):
        tables = pl.pallas_call(
            functools.partial(far_kernel, sizes=(local_s, block_rows, tm_count)),
            out_shape=[
                pltpu.VMEM((modes * height, lanes), F32),
                pltpu.VMEM((modes * 3 * height, lanes), F32),
                pltpu.VMEM((depth, 2 * modes), BF16),
            ],
            in_specs=[smem] + [vmem] * (tm_count + 3),
            out_specs=[vmem] * 3,
            compiler_params=vmem_limit(16),
        )(where, coeffs, *[in_vmem(piece) for piece in (*next_own, next_other, near)])
    sums = [None] * tm_count
    arrived = []
    for peer in reversed(range(tm_count)):
        with jax.named_scope("edge_terms"):
            sums[peer] = pl.pallas_call(
                functools.partial(edge_kernel, peer=peer, sizes=(chips, share, bits)),
                out_shape=group,
                in_specs=[smem, smem] + [vmem] * 4,
                out_specs=vmem,
                scratch_shapes=work,
                compiler_params=vmem_limit(16),
                cost_estimate=pl.CostEstimate(flops=4 * 10**9, bytes_accessed=10**7, transcendentals=0),
            )(where, codes, *[in_vmem(table) for table in (*tables, inner[peer])])
        with jax.named_scope("sum_over_rows"):
            if peer:
                arrived.append(lax.ppermute(sums[peer], "tm", across(peer)))
                inner[peer - 1], _ = lax.optimization_barrier((inner[peer - 1], sums[peer]))
    with jax.named_scope("sum_over_rows"):
        summed = sums[0]
        for part in arrived:
            summed = summed + part
    with jax.named_scope("sum_over_chips"):
        shares = summed.reshape(chips, share, modes)
        result = shares[0]
        for step in range(1, chips):
            shift = [
                (2 * chip + c, 2 * ((chip + step) % chips) + c) for chip in range(chips) for c in range(2)
            ]
            result = result + lax.ppermute(shares[step], "space", shift)
        return result * factor


def solution(mesh):
    placed = (P("tm", None, "space", None, None), P(), P())
    return jax.shard_map(
        shards, mesh=mesh, in_specs=placed, out_specs=P(("tm", "space"), None), check_vma=False
    )
```

```python
import functools

import jax
import jax.numpy as jnp
from jax import lax
from jax.experimental import pallas as pl
from jax.experimental.pallas import tpu as pltpu
from jax.sharding import PartitionSpec as P

F32 = jnp.float32
BF16 = jnp.bfloat16


def split_high_low(values):
    high = values.astype(BF16)
    low = (values - high.astype(F32)).astype(BF16)
    return high, low


def pack_kernel(where_ref, field_ref, *out_refs, sizes):
    local_s, rows_y, block_rows, tm_count = sizes
    t, core = where_ref[0], where_ref[2]
    half = block_rows // 2
    for peer in range(tm_count):
        first_row = jnp.bitwise_xor(t, peer) * block_rows
        for row in range(block_rows + 2):
            if row < block_rows:
                y = first_row + row
            else:
                y = first_row - 1 if row == block_rows else first_row + block_rows
                inside = jnp.logical_and(y >= 0, y < rows_y)
                y = jnp.clip(y, 0, rows_y - 1)
            for c in range(3):
                slab = field_ref[pl.ds(c * rows_y + y, local_s, stride=3 * rows_y), :]
                if row >= block_rows:
                    slab = jnp.where(inside, slab, 0.0)
                out_refs[peer][row * 3 + c] = slab
        out_refs[tm_count][peer] = out_refs[peer][pl.ds(core * (half * 3), half * 3)]


def mode_weights(where_ref, coeffs_ref, local_s, tm_count):
    t = where_ref[0]
    ordered = jnp.concatenate(
        [
            coeffs_ref[pl.ds(pl.multiple_of(jnp.bitwise_xor(t, peer) * local_s, 8), local_s), :]
            for peer in range(tm_count)
        ],
        axis=0,
    )
    high, low = split_high_low(ordered.T)
    return jnp.concatenate([high, low, high, low], axis=1)


def modes_of(weights, slab):
    high, low = split_high_low(slab)
    return jnp.dot(weights, jnp.concatenate([high, high, low, low], axis=0), preferred_element_type=F32)


def store_projection(rhs_ref, place, mode_slab):
    high, low = split_high_low(mode_slab.T)
    modes, lanes = mode_slab.shape
    rhs_ref[place * lanes : (place + 1) * lanes, 0:modes] = high
    rhs_ref[place * lanes : (place + 1) * lanes, modes : 2 * modes] = low


def project(conv_ref, rhs_ref, block, places, lanes):
    both = None
    for place in range(0, places, 2):
        highs, lows = zip(
            *(split_high_low(conv_ref[pl.ds(place + k, block, stride=places), :]) for k in range(2))
        )
        lhs = jnp.concatenate([jnp.concatenate(highs, axis=1), jnp.concatenate(lows, axis=1)], axis=0)
        part = jnp.dot(lhs, rhs_ref[place * lanes : (place + 2) * lanes, :], preferred_element_type=F32)
        both = part if both is None else both + part
    modes = both.shape[1] // 2
    return (both[:block, :modes] + both[:block, modes:]) + (both[block:, :modes] + both[block:, modes:])


def for_pairs_of(where_ref, codes_ref, peer, sizes, one_pair):
    chips, share, bits = sizes
    t, chip, core = where_ref[0], where_ref[1], where_ref[2]
    first_chip = jnp.bitwise_xor(t, peer) * chips

    def one_share(ahead, _):
        to_chip = chip + ahead
        to_chip = jnp.where(to_chip >= chips, to_chip - chips, to_chip)
        base = ((first_chip + to_chip) * 2 + core) * share

        def one(q, _):
            code = codes_ref[base + q]
            one_pair(ahead * share + q, lax.shift_right_logical(code, bits), jnp.bitwise_and(code, 2**bits - 1))
            return 0

        return lax.fori_loop(0, share, one, 0, unroll=32)

    lax.fori_loop(0, chips, one_share, 0)


def inner_kernel(where_ref, codes_ref, coeffs_ref, *refs, first_peer, sizes):
    local_s, block_rows, tm_count, chips, share, bits = sizes
    own, other = refs[:tm_count], refs[tm_count : 2 * tm_count]
    near_ref, carry_ref, slope_ref, rhs_ref = refs[2 * tm_count : 2 * tm_count + 4]
    out_ref, slab_ref, conv_ref = refs[2 * tm_count + 4 :]
    core = where_ref[2]
    modes, lanes = coeffs_ref.shape[1], own[0].shape[2]
    height = 2 * block_rows
    weights = mode_weights(where_ref, coeffs_ref, local_s, tm_count)

    def one_slab(index, _):
        own_slab = jnp.concatenate([piece[index] for piece in own], axis=0)
        other_slab = jnp.concatenate([piece[index] for piece in other], axis=0)
        is_first = core == 0
        both = jnp.concatenate(
            [jnp.where(is_first, own_slab, other_slab), jnp.where(is_first, other_slab, own_slab)], axis=1
        )
        result = modes_of(weights, both)
        slab_ref[0, index] = result[:, :lanes]
        slab_ref[1, index] = result[:, lanes:]
        return 0

    lax.fori_loop(0, (block_rows + 2) * 3, one_slab, 0, unroll=3)
    for c in range(3):
        for row in range(block_rows):
            above = (row + 1 if row + 1 < block_rows else block_rows + 1) * 3 + c
            below = (row - 1 if row > 0 else block_rows) * 3 + c
            center = row * 3 + c
            for plane in range(2):
                place = plane * block_rows + row
                value = slab_ref[plane, center]
                stream = slab_ref[1 - plane, center] * (0.5 if plane == 0 else -0.5)
                normal = (slab_ref[plane, above] - slab_ref[plane, below]) * 0.5
                span = (pltpu.roll(value, lanes - 1, 1) - pltpu.roll(value, 1, 1)) * 0.5
                carry_ref[pl.ds(c * height + place, modes, stride=3 * height), :] = value
                for d, slope in enumerate((stream, normal, span)):
                    slope_ref[pl.ds((d * 3 + c) * height + place, modes, stride=9 * height), :] = slope
                store_projection(rhs_ref, c * height + place, value)
                if (plane == 1) == (row < block_rows // 2):
                    near_ref[center] = value

    pairs_kernel(
        where_ref, codes_ref, carry_ref, slope_ref, rhs_ref, out_ref, conv_ref,
        first_peer=first_peer, sizes=(height, chips, share, bits),
    )


def pairs_kernel(
    where_ref, codes_ref, carry_ref, slope_ref, rhs_ref, out_ref, conv_ref, *, first_peer, sizes
):
    height, chips, share, bits = sizes

    def one_pair(slot, i, j):
        carry = carry_ref[pl.ds(pl.multiple_of(i * (3 * height), 8), 3 * height), :]
        slope = slope_ref[pl.ds(pl.multiple_of(j * (9 * height), 8), 9 * height), :]
        rows = [
            sum(
                carry[d * height : (d + 1) * height] * slope[(d * 3 + c) * height : (d * 3 + c + 1) * height]
                for d in range(3)
            )
            for c in range(3)
        ]
        conv_ref[pl.ds(pl.multiple_of(slot * (3 * height), 8), 3 * height), :] = jnp.concatenate(rows, axis=0)

    def one_peer(number, _):
        for_pairs_of(where_ref, codes_ref, first_peer + number, (chips, share, bits), one_pair)
        out_ref[number] = project(conv_ref, rhs_ref, chips * share, 3 * height, conv_ref.shape[1])
        return 0

    lax.fori_loop(0, out_ref.shape[0], one_peer, 0)


def far_kernel(where_ref, coeffs_ref, *refs, sizes):
    local_s, block_rows, tm_count = sizes
    next_own, next_other, near_ref = refs[:tm_count], refs[tm_count], refs[tm_count + 1]
    carry_ref, slope_ref, rhs_ref = refs[tm_count + 2 :]
    is_first = where_ref[2] == 0
    modes, lanes = near_ref.shape[1:]
    height = 2 * block_rows
    half = block_rows // 2 * 3
    weights = mode_weights(where_ref, coeffs_ref, local_s, tm_count)
    for slab in range(half):
        mine = jnp.concatenate([next_own[peer][slab] for peer in range(tm_count)], axis=0)
        theirs = jnp.concatenate([next_other[peer, slab] for peer in range(tm_count)], axis=0)
        after, before = jnp.where(is_first, theirs, mine), jnp.where(is_first, mine, theirs)
        result = modes_of(weights, jnp.concatenate([after, before], axis=1))
        row, c = divmod(slab, 3)
        edges = ((near_ref[slab], result[:, :lanes]), (result[:, lanes:], near_ref[half + slab]))
        for number, (low, high) in enumerate(edges):
            place = number * block_rows + 2 * row
            for at, value, across in ((place, low, high * 0.5), (place + 1, high, low * -0.5)):
                if c == 0:
                    carry_ref[pl.ds(at, modes, stride=height), :] = value
                slope_ref[pl.ds(c * height + at, modes, stride=3 * height), :] = across
                store_projection(rhs_ref, c * height + at, value)


def edge_kernel(
    where_ref, codes_ref, carry_ref, slope_ref, rhs_ref, inner_ref, *refs, peer, sizes
):
    *arrived_refs, out_ref, conv_ref = refs
    chips, share, _ = sizes
    modes, lanes = out_ref.shape[1], carry_ref.shape[1]
    height = carry_ref.shape[0] // modes

    def one_pair(slot, i, j):
        carry = carry_ref[pl.ds(pl.multiple_of(i * height, 8), height), :]
        slope = slope_ref[pl.ds(pl.multiple_of(j * (3 * height), 8), 3 * height), :]
        rows = [carry * slope[c * height : (c + 1) * height] for c in range(3)]
        conv_ref[pl.ds(pl.multiple_of(slot * (3 * height), 8), 3 * height), :] = jnp.concatenate(rows, axis=0)

    for_pairs_of(where_ref, codes_ref, peer, sizes, one_pair)
    total = inner_ref[peer % inner_ref.shape[0]]
    for arrived_ref in arrived_refs:
        total = total + arrived_ref[...]
    out_ref[...] = total + project(conv_ref, rhs_ref, chips * share, 3 * height, lanes)


def vmem_limit(mebibytes):
    return pltpu.CompilerParams(vmem_limit_bytes=mebibytes * 2**20)


def in_vmem(array):
    return pltpu.with_memory_space_constraint(array, pltpu.VMEM)


def shards(snapshots, coeffs, pair_table):
    tm_count, space_count = lax.axis_size("tm"), lax.axis_size("space")
    chips = space_count // 2
    t, place = lax.axis_index("tm"), lax.axis_index("space")
    core = lax.rem(place, 2)
    where = jnp.stack([t, lax.div(place, 2), core]).astype(jnp.int32)
    local_s, _, _, rows_y, lanes = snapshots.shape
    modes = coeffs.shape[1]
    block_rows = rows_y // tm_count
    share = pair_table.shape[0] // (tm_count * space_count)
    factor = float(space_count * rows_y * lanes) ** (-0.5)
    bits = modes.bit_length() - 1
    assert modes == 2**bits
    codes = pair_table[:, 0] * modes + pair_table[:, 1]
    smem = pl.BlockSpec(memory_space=pltpu.SMEM)
    vmem = pl.BlockSpec(memory_space=pltpu.VMEM)
    block = chips * share
    height = 2 * block_rows
    depth = 3 * height * lanes

    swap = [(2 * chip + c, 2 * chip + 1 - c) for chip in range(chips) for c in range(2)]

    def across(peer):
        return [(i, i ^ peer) for i in range(tm_count)]

    with jax.named_scope("pack"):
        packed = pl.pallas_call(
            functools.partial(pack_kernel, sizes=(local_s, rows_y, block_rows, tm_count)),
            out_shape=[pltpu.VMEM(((block_rows + 2) * 3, local_s, lanes), F32)] * tm_count
            + [pltpu.VMEM((tm_count, block_rows // 2 * 3, local_s, lanes), F32)],
            in_specs=[smem, vmem],
            out_specs=[vmem] * (tm_count + 1),
            compiler_params=vmem_limit(16),
        )(where, snapshots.reshape(-1, lanes))
    with jax.named_scope("to_next_plane"):
        ring = [(place, (place + (1 if place % 2 else -1)) % space_count) for place in range(space_count)]
        across_edge = lax.ppermute(packed[tm_count], "space", ring)
    with jax.named_scope("to_rows"):
        own = [packed[0]] + [lax.ppermute(packed[peer], "tm", across(peer)) for peer in range(1, tm_count)]
    with jax.named_scope("next_to_rows"):
        across_edge, own[:3] = lax.optimization_barrier((across_edge, own[:3]))
        parts = [across_edge[peer] for peer in range(tm_count)]
        parts, own[3:] = lax.optimization_barrier((parts, own[3:]))
        next_own = [parts[0]] + [lax.ppermute(parts[peer], "tm", across(peer)) for peer in range(1, tm_count)]
    with jax.named_scope("to_other_core"):
        other = [lax.ppermute(piece, "space", swap) for piece in own]
    early = tm_count // 2
    work = [pltpu.VMEM((block * 3 * height, lanes), F32)]
    groups = pltpu.VMEM((early, block, modes), F32)
    with jax.named_scope("inner_terms"):
        near, *inner_tables, early_sums = pl.pallas_call(
            functools.partial(inner_kernel, first_peer=early, sizes=(local_s, block_rows, tm_count, chips, share, bits)),
            out_shape=[
                pltpu.VMEM((block_rows * 3, modes, lanes), F32),
                pltpu.VMEM((modes * 3 * height, lanes), F32),
                pltpu.VMEM((modes * 9 * height, lanes), F32),
                pltpu.VMEM((depth, 2 * modes), BF16),
                groups,
            ],
            in_specs=[smem, smem] + [vmem] * (2 * tm_count + 1),
            out_specs=[vmem] * 5,
            scratch_shapes=[pltpu.VMEM((2, (block_rows + 2) * 3, modes, lanes), F32)] + work,
            compiler_params=vmem_limit(24),
            cost_estimate=pl.CostEstimate(flops=12 * 10**9, bytes_accessed=10**7, transcendentals=0),
        )(where, codes, coeffs, *[in_vmem(piece) for piece in (*own, *other)])
    with jax.named_scope("next_to_other_core"):
        next_own, inner_tables = lax.optimization_barrier((next_own, inner_tables))
        next_other = lax.ppermute(jnp.stack(next_own), "space", swap)
    with jax.named_scope("inner_terms"):
        late_sums = pl.pallas_call(
            functools.partial(pairs_kernel, first_peer=0, sizes=(height, chips, share, bits)),
            out_shape=groups,
            in_specs=[smem, smem] + [vmem] * 3,
            out_specs=vmem,
            scratch_shapes=work,
            compiler_params=vmem_limit(16),
            cost_estimate=pl.CostEstimate(flops=8 * 10**9, bytes_accessed=10**7, transcendentals=0),
        )(where, codes, *[in_vmem(table) for table in inner_tables])
    with jax.named_scope("edge_tables"):
        tables = list(pl.pallas_call(
            functools.partial(far_kernel, sizes=(local_s, block_rows, tm_count)),
            out_shape=[
                pltpu.VMEM((modes * height, lanes), F32),
                pltpu.VMEM((modes * 3 * height, lanes), F32),
                pltpu.VMEM((depth, 2 * modes), BF16),
            ],
            in_specs=[smem] + [vmem] * (tm_count + 3),
            out_specs=[vmem] * 3,
            compiler_params=vmem_limit(16),
        )(where, coeffs, *[in_vmem(piece) for piece in (*next_own, next_other, near)]))
    arrived = []
    for peer in reversed(range(tm_count)):
        with jax.named_scope("edge_terms"):
            parts = arrived[:-1] if peer == 0 else []
            summed = pl.pallas_call(
                functools.partial(edge_kernel, peer=peer, sizes=(chips, share, bits)),
                out_shape=pltpu.VMEM((block, modes), F32),
                in_specs=[smem, smem] + [vmem] * (4 + len(parts)),
                out_specs=vmem,
                scratch_shapes=work,
                compiler_params=vmem_limit(16),
                cost_estimate=pl.CostEstimate(flops=10**8, bytes_accessed=10**5, transcendentals=0),
            )(
                where,
                codes,
                *[in_vmem(table) for table in (*tables, early_sums if peer >= early else late_sums, *parts)],
            )
        with jax.named_scope("sum_over_rows"):
            if peer:
                arrived.append(lax.ppermute(summed, "tm", across(peer)))
                tables[0], _ = lax.optimization_barrier((tables[0], summed))
    with jax.named_scope("sum_over_rows"):
        summed = summed + arrived[-1]
    with jax.named_scope("sum_over_chips"):
        shares = summed.reshape(chips, share, modes)
        result = shares[0]
        for step in range(1, chips):
            shift = [
                (2 * chip + c, 2 * ((chip + step) % chips) + c) for chip in range(chips) for c in range(2)
            ]
            result = result + lax.ppermute(shares[step], "space", shift)
        return result * factor


def solution(mesh):
    placed = (P("tm", None, "space", None, None), P(), P())
    return jax.shard_map(
        shards, mesh=mesh, in_specs=placed, out_specs=P(("tm", "space"), None), check_vma=False
    )
```

```python
import functools

import jax
import jax.numpy as jnp
from jax import lax
from jax.experimental import pallas as pl
from jax.experimental.pallas import tpu as pltpu
from jax.sharding import PartitionSpec as P

F32 = jnp.float32
BF16 = jnp.bfloat16


def split_high_low(values):
    high = values.astype(BF16)
    low = (values - high.astype(F32)).astype(BF16)
    return high, low


def border_lane(rows_y, lanes, c):
    per_slab = lanes // (2 * rows_y)
    return c // per_slab, c % per_slab * 2 * rows_y


def border_slabs(rows_y, lanes):
    return border_lane(rows_y, lanes, 2)[0] + 1


def pack_kernel(where_ref, field_ref, *out_refs, sizes):
    local_s, rows_y, tm_count = sizes
    lanes = field_ref.shape[1]
    t, core = where_ref[0], where_ref[2]
    width, groups = lanes // tm_count, rows_y // tm_count
    lane = lax.broadcasted_iota(jnp.int32, (local_s, lanes), 1)
    starts = [jnp.bitwise_xor(t, peer) * width for peer in range(tm_count)]
    borders = [[jnp.zeros((local_s, lanes), F32) for _ in range(tm_count)] for _ in range(border_slabs(rows_y, lanes))]
    for c in range(3):
        slab, first_lane = border_lane(rows_y, lanes, c)

        def one_group(g, border, c=c, first_lane=first_lane):
            border = list(border)
            main = [None] * tm_count
            for q in range(tm_count):
                y = q * groups + g
                row = field_ref[pl.ds(c * rows_y + y, local_s, stride=3 * rows_y), :]
                for peer, start in enumerate(starts):
                    moved = pltpu.roll(row, jnp.bitwise_and(q * width - start, lanes - 1), 1)
                    main[peer] = moved if q == 0 else jnp.where(lane < q * width, main[peer], moved)
                    for side, column in ((0, start - 1), (1, start + width)):
                        target = first_lane + side * rows_y + y
                        moved = pltpu.roll(row, jnp.bitwise_and(target - column, lanes - 1), 1)
                        border[peer] = jnp.where(lane == target, moved, border[peer])
            for peer in range(tm_count):
                out_refs[peer][g * 3 + c] = main[peer]
            return tuple(border)

        borders[slab] = lax.fori_loop(0, groups, one_group, tuple(borders[slab]))
    half = groups // 2 * 3
    for peer in range(tm_count):
        for slab, border in enumerate(borders):
            out_refs[peer][groups * 3 + slab] = border[peer]
        out_refs[tm_count][peer] = out_refs[peer][pl.ds(core * half, half)]


def mode_weights(where_ref, coeffs_ref, local_s, tm_count):
    t = where_ref[0]
    ordered = jnp.concatenate(
        [
            coeffs_ref[pl.ds(pl.multiple_of(jnp.bitwise_xor(t, peer) * local_s, 8), local_s), :]
            for peer in range(tm_count)
        ],
        axis=0,
    )
    high, low = split_high_low(ordered.T)
    return jnp.concatenate([high, low, high, low], axis=1)


def modes_of(weights, slab):
    high, low = split_high_low(slab)
    return jnp.dot(weights, jnp.concatenate([high, high, low, low], axis=0), preferred_element_type=F32)


def store_projection(rhs_ref, place, mode_slab):
    high, low = split_high_low(mode_slab.T)
    modes, lanes = mode_slab.shape
    rhs_ref[place * lanes : (place + 1) * lanes, 0:modes] = high
    rhs_ref[place * lanes : (place + 1) * lanes, modes : 2 * modes] = low


def project(conv_ref, rhs_ref, block, places, lanes):
    both = None
    for place in range(0, places, 2):
        highs, lows = zip(
            *(split_high_low(conv_ref[pl.ds(place + k, block, stride=places), :]) for k in range(2))
        )
        lhs = jnp.concatenate([jnp.concatenate(highs, axis=1), jnp.concatenate(lows, axis=1)], axis=0)
        part = jnp.dot(lhs, rhs_ref[place * lanes : (place + 2) * lanes, :], preferred_element_type=F32)
        both = part if both is None else both + part
    modes = both.shape[1] // 2
    return (both[:block, :modes] + both[:block, modes:]) + (both[block:, :modes] + both[block:, modes:])


def for_pairs_of(where_ref, codes_ref, peer, sizes, one_pair):
    chips, share, bits = sizes
    t, chip, core = where_ref[0], where_ref[1], where_ref[2]
    first_chip = jnp.bitwise_xor(t, peer) * chips

    def one_share(ahead, _):
        to_chip = chip + ahead
        to_chip = jnp.where(to_chip >= chips, to_chip - chips, to_chip)
        base = ((first_chip + to_chip) * 2 + core) * share

        def one(q, _):
            code = codes_ref[base + q]
            one_pair(ahead * share + q, lax.shift_right_logical(code, bits), jnp.bitwise_and(code, 2**bits - 1))
            return 0

        return lax.fori_loop(0, share, one, 0, unroll=32)

    lax.fori_loop(0, chips, one_share, 0)


def inner_kernel(where_ref, codes_ref, coeffs_ref, *refs, first_peer, sizes):
    local_s, block_rows, tm_count, chips, share, bits = sizes
    own, other = refs[:tm_count], refs[tm_count : 2 * tm_count]
    near_ref, carry_ref, slope_ref, rhs_ref = refs[2 * tm_count : 2 * tm_count + 4]
    out_ref, slab_ref, conv_ref = refs[2 * tm_count + 4 :]
    core = where_ref[2]
    modes, lanes = coeffs_ref.shape[1], own[0].shape[2]
    height = 2 * block_rows
    weights = mode_weights(where_ref, coeffs_ref, local_s, tm_count)

    def one_slab(index, _):
        own_slab = jnp.concatenate([piece[index] for piece in own], axis=0)
        other_slab = jnp.concatenate([piece[index] for piece in other], axis=0)
        is_first = core == 0
        both = jnp.concatenate(
            [jnp.where(is_first, own_slab, other_slab), jnp.where(is_first, other_slab, own_slab)], axis=1
        )
        result = modes_of(weights, both)
        slab_ref[0, index] = result[:, :lanes]
        slab_ref[1, index] = result[:, lanes:]
        return 0

    slabs = own[0].shape[0]
    lax.fori_loop(0, slabs, one_slab, 0, unroll=2 if slabs % 2 == 0 else 1)
    width, rows_y = lanes // tm_count, block_rows * tm_count
    lane = lax.broadcasted_iota(jnp.int32, (1, lanes), 1)
    part, column = lax.div(lane, width), lax.rem(lane, width)
    has_border = jnp.where(column == 0, -0.5, jnp.where(column == width - 1, 0.5, 0.0))
    border_of = jnp.where(column == 0, 0, rows_y) + part * block_rows
    border_lanes = lax.broadcasted_iota(jnp.int32, (2 * lanes, lanes), 0)
    border_lanes = jnp.where(border_lanes >= lanes, border_lanes - lanes, border_lanes)
    borders = []
    for slab in range(3 * block_rows, slabs):
        both = jnp.concatenate([slab_ref[0, slab], slab_ref[1, slab]], axis=0)
        borders.append(jnp.concatenate(split_high_low(both), axis=1))
    for c in range(3):
        slab, first_lane = border_lane(rows_y, lanes, c)
        for row in range(block_rows):
            center = row * 3 + c
            pick = jnp.where(border_lanes == border_of + (first_lane + row), has_border, 0.0).astype(BF16)
            border = jnp.dot(borders[slab], pick, preferred_element_type=F32)
            for plane in range(2):
                place = plane * block_rows + row
                value = slab_ref[plane, center]
                stream = slab_ref[1 - plane, center] * (0.5 if plane == 0 else -0.5)
                if row + 1 < block_rows:
                    above = slab_ref[plane, center + 3]
                else:
                    above = pltpu.roll(slab_ref[plane, c], lanes - width, 1)
                    above = jnp.where(lane < lanes - width, above, 0.0)
                if row > 0:
                    below = slab_ref[plane, center - 3]
                else:
                    below = pltpu.roll(slab_ref[plane, 3 * (block_rows - 1) + c], width, 1)
                    below = jnp.where(lane >= width, below, 0.0)
                normal = (above - below) * 0.5
                after = jnp.where(column < width - 1, pltpu.roll(value, lanes - 1, 1), 0.0)
                before = jnp.where(column > 0, pltpu.roll(value, 1, 1), 0.0)
                span = (after - before) * 0.5 + border[plane * modes : (plane + 1) * modes]
                carry_ref[pl.ds(c * height + place, modes, stride=3 * height), :] = value
                for d, slope in enumerate((stream, normal, span)):
                    slope_ref[pl.ds((d * 3 + c) * height + place, modes, stride=9 * height), :] = slope
                store_projection(rhs_ref, c * height + place, value)
                if (plane == 1) == (row < block_rows // 2):
                    near_ref[center] = value

    pairs_kernel(
        where_ref, codes_ref, carry_ref, slope_ref, rhs_ref, out_ref, conv_ref,
        first_peer=first_peer, sizes=(height, chips, share, bits),
    )


def pairs_kernel(
    where_ref, codes_ref, carry_ref, slope_ref, rhs_ref, out_ref, conv_ref, *, first_peer, sizes
):
    height, chips, share, bits = sizes

    def one_pair(slot, i, j):
        carry = carry_ref[pl.ds(pl.multiple_of(i * (3 * height), 8), 3 * height), :]
        slope = slope_ref[pl.ds(pl.multiple_of(j * (9 * height), 8), 9 * height), :]
        rows = [
            sum(
                carry[d * height : (d + 1) * height] * slope[(d * 3 + c) * height : (d * 3 + c + 1) * height]
                for d in range(3)
            )
            for c in range(3)
        ]
        conv_ref[pl.ds(pl.multiple_of(slot * (3 * height), 8), 3 * height), :] = jnp.concatenate(rows, axis=0)

    def one_peer(number, _):
        for_pairs_of(where_ref, codes_ref, first_peer + number, (chips, share, bits), one_pair)
        out_ref[number] = project(conv_ref, rhs_ref, chips * share, 3 * height, conv_ref.shape[1])
        return 0

    lax.fori_loop(0, out_ref.shape[0], one_peer, 0)


def far_kernel(where_ref, coeffs_ref, *refs, sizes):
    local_s, block_rows, tm_count = sizes
    next_own, next_other, near_ref = refs[:tm_count], refs[tm_count], refs[tm_count + 1]
    carry_ref, slope_ref, rhs_ref = refs[tm_count + 2 :]
    is_first = where_ref[2] == 0
    modes, lanes = near_ref.shape[1:]
    height = 2 * block_rows
    half = block_rows // 2 * 3
    weights = mode_weights(where_ref, coeffs_ref, local_s, tm_count)
    for slab in range(half):
        mine = jnp.concatenate([next_own[peer][slab] for peer in range(tm_count)], axis=0)
        theirs = jnp.concatenate([next_other[peer, slab] for peer in range(tm_count)], axis=0)
        after, before = jnp.where(is_first, theirs, mine), jnp.where(is_first, mine, theirs)
        result = modes_of(weights, jnp.concatenate([after, before], axis=1))
        row, c = divmod(slab, 3)
        edges = ((near_ref[slab], result[:, :lanes]), (result[:, lanes:], near_ref[half + slab]))
        for number, (low, high) in enumerate(edges):
            place = number * block_rows + 2 * row
            for at, value, across in ((place, low, high * 0.5), (place + 1, high, low * -0.5)):
                if c == 0:
                    carry_ref[pl.ds(at, modes, stride=height), :] = value
                slope_ref[pl.ds(c * height + at, modes, stride=3 * height), :] = across
                store_projection(rhs_ref, c * height + at, value)


def edge_kernel(
    where_ref, codes_ref, carry_ref, slope_ref, rhs_ref, inner_ref, *refs, peer, sizes
):
    *arrived_refs, out_ref, conv_ref = refs
    chips, share, _ = sizes
    modes, lanes = out_ref.shape[1], carry_ref.shape[1]
    height = carry_ref.shape[0] // modes

    def one_pair(slot, i, j):
        carry = carry_ref[pl.ds(pl.multiple_of(i * height, 8), height), :]
        slope = slope_ref[pl.ds(pl.multiple_of(j * (3 * height), 8), 3 * height), :]
        rows = [carry * slope[c * height : (c + 1) * height] for c in range(3)]
        conv_ref[pl.ds(pl.multiple_of(slot * (3 * height), 8), 3 * height), :] = jnp.concatenate(rows, axis=0)

    for_pairs_of(where_ref, codes_ref, peer, sizes, one_pair)
    total = inner_ref[peer % inner_ref.shape[0]]
    for arrived_ref in arrived_refs:
        total = total + arrived_ref[...]
    out_ref[...] = total + project(conv_ref, rhs_ref, chips * share, 3 * height, lanes)


def vmem_limit(mebibytes):
    return pltpu.CompilerParams(vmem_limit_bytes=mebibytes * 2**20)


def in_vmem(array):
    return pltpu.with_memory_space_constraint(array, pltpu.VMEM)


def shards(snapshots, coeffs, pair_table):
    tm_count, space_count = lax.axis_size("tm"), lax.axis_size("space")
    chips = space_count // 2
    t, place = lax.axis_index("tm"), lax.axis_index("space")
    core = lax.rem(place, 2)
    where = jnp.stack([t, lax.div(place, 2), core]).astype(jnp.int32)
    local_s, _, _, rows_y, lanes = snapshots.shape
    modes = coeffs.shape[1]
    block_rows = rows_y // tm_count
    slabs = 3 * block_rows + border_slabs(rows_y, lanes)
    share = pair_table.shape[0] // (tm_count * space_count)
    factor = float(space_count * rows_y * lanes) ** (-0.5)
    bits = modes.bit_length() - 1
    assert modes == 2**bits
    codes = pair_table[:, 0] * modes + pair_table[:, 1]
    smem = pl.BlockSpec(memory_space=pltpu.SMEM)
    vmem = pl.BlockSpec(memory_space=pltpu.VMEM)
    block = chips * share
    height = 2 * block_rows
    depth = 3 * height * lanes

    swap = [(2 * chip + c, 2 * chip + 1 - c) for chip in range(chips) for c in range(2)]

    def across(peer):
        return [(i, i ^ peer) for i in range(tm_count)]

    with jax.named_scope("pack"):
        packed = pl.pallas_call(
            functools.partial(pack_kernel, sizes=(local_s, rows_y, tm_count)),
            out_shape=[pltpu.VMEM((slabs, local_s, lanes), F32)] * tm_count
            + [pltpu.VMEM((tm_count, block_rows // 2 * 3, local_s, lanes), F32)],
            in_specs=[smem, vmem],
            out_specs=[vmem] * (tm_count + 1),
            compiler_params=vmem_limit(16),
        )(where, snapshots.reshape(-1, lanes))
    with jax.named_scope("to_next_plane"):
        ring = [(place, (place + (1 if place % 2 else -1)) % space_count) for place in range(space_count)]
        across_edge = lax.ppermute(packed[tm_count], "space", ring)
    with jax.named_scope("to_columns"):
        own = [packed[0]] + [lax.ppermute(packed[peer], "tm", across(peer)) for peer in range(1, tm_count)]
    with jax.named_scope("to_other_core"):
        other = [lax.ppermute(piece, "space", swap) for piece in own]
    with jax.named_scope("next_to_columns"):
        across_edge, own, other = lax.optimization_barrier((across_edge, own, other))
        parts = [across_edge[peer] for peer in range(tm_count)]
        next_own = [parts[0]] + [lax.ppermute(parts[peer], "tm", across(peer)) for peer in range(1, tm_count)]
    early = tm_count // 2
    work = [pltpu.VMEM((block * 3 * height, lanes), F32)]
    groups = pltpu.VMEM((early, block, modes), F32)
    with jax.named_scope("inner_terms"):
        near, *inner_tables, early_sums = pl.pallas_call(
            functools.partial(inner_kernel, first_peer=early, sizes=(local_s, block_rows, tm_count, chips, share, bits)),
            out_shape=[
                pltpu.VMEM((block_rows * 3, modes, lanes), F32),
                pltpu.VMEM((modes * 3 * height, lanes), F32),
                pltpu.VMEM((modes * 9 * height, lanes), F32),
                pltpu.VMEM((depth, 2 * modes), BF16),
                groups,
            ],
            in_specs=[smem, smem] + [vmem] * (2 * tm_count + 1),
            out_specs=[vmem] * 5,
            scratch_shapes=[pltpu.VMEM((2, slabs, modes, lanes), F32)] + work,
            compiler_params=vmem_limit(24),
            cost_estimate=pl.CostEstimate(flops=12 * 10**9, bytes_accessed=10**7, transcendentals=0),
        )(where, codes, coeffs, *[in_vmem(piece) for piece in (*own, *other)])
    with jax.named_scope("next_to_other_core"):
        next_own, inner_tables = lax.optimization_barrier((next_own, inner_tables))
        next_other = lax.ppermute(jnp.stack(next_own), "space", swap)
    with jax.named_scope("inner_terms"):
        late_sums = pl.pallas_call(
            functools.partial(pairs_kernel, first_peer=0, sizes=(height, chips, share, bits)),
            out_shape=groups,
            in_specs=[smem, smem] + [vmem] * 3,
            out_specs=vmem,
            scratch_shapes=work,
            compiler_params=vmem_limit(16),
            cost_estimate=pl.CostEstimate(flops=8 * 10**9, bytes_accessed=10**7, transcendentals=0),
        )(where, codes, *[in_vmem(table) for table in inner_tables])
    with jax.named_scope("edge_tables"):
        tables = list(pl.pallas_call(
            functools.partial(far_kernel, sizes=(local_s, block_rows, tm_count)),
            out_shape=[
                pltpu.VMEM((modes * height, lanes), F32),
                pltpu.VMEM((modes * 3 * height, lanes), F32),
                pltpu.VMEM((depth, 2 * modes), BF16),
            ],
            in_specs=[smem] + [vmem] * (tm_count + 3),
            out_specs=[vmem] * 3,
            compiler_params=vmem_limit(16),
        )(where, coeffs, *[in_vmem(piece) for piece in (*next_own, next_other, near)]))
    arrived = []
    for peer in reversed(range(tm_count)):
        with jax.named_scope("edge_terms"):
            parts = arrived[:-1] if peer == 0 else []
            summed = pl.pallas_call(
                functools.partial(edge_kernel, peer=peer, sizes=(chips, share, bits)),
                out_shape=pltpu.VMEM((block, modes), F32),
                in_specs=[smem, smem] + [vmem] * (4 + len(parts)),
                out_specs=vmem,
                scratch_shapes=work,
                compiler_params=vmem_limit(16),
                cost_estimate=pl.CostEstimate(flops=10**8, bytes_accessed=10**5, transcendentals=0),
            )(
                where,
                codes,
                *[in_vmem(table) for table in (*tables, early_sums if peer >= early else late_sums, *parts)],
            )
        with jax.named_scope("sum_over_columns"):
            if peer:
                arrived.append(lax.ppermute(summed, "tm", across(peer)))
                if peer > early:
                    early_sums, _ = lax.optimization_barrier((early_sums, summed))
                else:
                    late_sums, _ = lax.optimization_barrier((late_sums, summed))
    with jax.named_scope("sum_over_columns"):
        summed = summed + arrived[-1]
    with jax.named_scope("sum_over_chips"):
        shares = summed.reshape(chips, share, modes)
        result = shares[0]
        for step in range(1, chips):
            shift = [
                (2 * chip + c, 2 * ((chip + step) % chips) + c) for chip in range(chips) for c in range(2)
            ]
            result = result + lax.ppermute(shares[step], "space", shift)
        return result * factor


def solution(mesh):
    placed = (P("tm", None, "space", None, None), P(), P())
    return jax.shard_map(
        shards, mesh=mesh, in_specs=placed, out_specs=P(("tm", "space"), None), check_vma=False
    )
```

```python
import functools

import jax
import jax.numpy as jnp
from jax import lax
from jax.experimental import pallas as pl
from jax.experimental.pallas import tpu as pltpu
from jax.sharding import PartitionSpec as P

F32 = jnp.float32
BF16 = jnp.bfloat16


def split_high_low(values):
    high = values.astype(BF16)
    low = (values - high.astype(F32)).astype(BF16)
    return high, low


def border_lane(rows_y, lanes, c):
    per_slab = lanes // (2 * rows_y)
    return c // per_slab, c % per_slab * 2 * rows_y


def border_slabs(rows_y, lanes):
    return border_lane(rows_y, lanes, 2)[0] + 1


def exchange_blocks(rows, lane, width, lanes):
    rows = list(rows)
    step = len(rows) // 2
    while step:
        keeps = jnp.bitwise_and(lane, step * width) == 0
        for low in range(len(rows)):
            if low & step == 0:
                first, second = rows[low], rows[low + step]
                rows[low] = jnp.where(keeps, first, pltpu.roll(second, step * width, 1))
                rows[low + step] = jnp.where(keeps, pltpu.roll(first, lanes - step * width, 1), second)
        step //= 2
    return rows


def pack_kernel(where_ref, field_ref, *refs, sizes):
    *out_refs, sorted_ref = refs
    local_s, rows_y, tm_count = sizes
    lanes = field_ref.shape[1]
    t, core = where_ref[0], where_ref[2]
    width, groups = lanes // tm_count, rows_y // tm_count
    lane = lax.broadcasted_iota(jnp.int32, (local_s, lanes), 1)
    borders = [[jnp.zeros((local_s, lanes), F32) for _ in range(tm_count)] for _ in range(border_slabs(rows_y, lanes))]
    for c in range(3):
        slab, first_lane = border_lane(rows_y, lanes, c)

        def one_group(g, border, c=c, first_lane=first_lane):
            border = list(border)
            rows = []
            for q in range(tm_count):
                y = q * groups + g
                row = field_ref[pl.ds(c * rows_y + y, local_s, stride=3 * rows_y), :]
                rows.append(row)
                for side in range(2):
                    shift = first_lane + side * (rows_y - width - 1) + y
                    moved = pltpu.roll(row, jnp.bitwise_and(shift, lanes - 1), 1)
                    for block in range(tm_count):
                        column = (block + 1) * width if side else block * width - 1
                        is_here = lane == jnp.bitwise_and(shift + column, lanes - 1)
                        border[block] = jnp.where(is_here, moved, border[block])
            for block, main in enumerate(exchange_blocks(rows, lane, width, lanes)):
                sorted_ref[block, g * 3 + c] = main
            return tuple(border)

        borders[slab] = lax.fori_loop(0, groups, one_group, tuple(borders[slab]))
    half = groups // 2 * 3
    for slab, border in enumerate(borders):
        for block in range(tm_count):
            sorted_ref[block, groups * 3 + slab] = border[block]
    for peer in range(tm_count):
        block = jnp.bitwise_xor(t, peer)
        out_refs[peer][...] = sorted_ref[block]
        out_refs[tm_count][peer] = sorted_ref[block, pl.ds(core * half, half)]


def mode_weights(where_ref, coeffs_ref, local_s, tm_count):
    t = where_ref[0]
    ordered = jnp.concatenate(
        [
            coeffs_ref[pl.ds(pl.multiple_of(jnp.bitwise_xor(t, peer) * local_s, 8), local_s), :]
            for peer in range(tm_count)
        ],
        axis=0,
    )
    high, low = split_high_low(ordered.T)
    return jnp.concatenate([high, low, high, low], axis=1)


def modes_of(weights, slab):
    high, low = split_high_low(slab)
    return jnp.dot(weights, jnp.concatenate([high, high, low, low], axis=0), preferred_element_type=F32)


def store_projection(rhs_ref, place, mode_slab):
    high, low = split_high_low(mode_slab.T)
    modes, lanes = mode_slab.shape
    rhs_ref[place * lanes : (place + 1) * lanes, 0:modes] = high
    rhs_ref[place * lanes : (place + 1) * lanes, modes : 2 * modes] = low


def project(conv_ref, rhs_ref, block, places, lanes):
    both = None
    for place in range(0, places, 2):
        highs, lows = zip(
            *(split_high_low(conv_ref[pl.ds(place + k, block, stride=places), :]) for k in range(2))
        )
        lhs = jnp.concatenate([jnp.concatenate(highs, axis=1), jnp.concatenate(lows, axis=1)], axis=0)
        part = jnp.dot(lhs, rhs_ref[place * lanes : (place + 2) * lanes, :], preferred_element_type=F32)
        both = part if both is None else both + part
    modes = both.shape[1] // 2
    return (both[:block, :modes] + both[:block, modes:]) + (both[block:, :modes] + both[block:, modes:])


def for_pairs_of(where_ref, codes_ref, peer, sizes, one_pair):
    chips, share, bits = sizes
    t, chip, core = where_ref[0], where_ref[1], where_ref[2]
    first_chip = jnp.bitwise_xor(t, peer) * chips

    def one_share(ahead, _):
        to_chip = chip + ahead
        to_chip = jnp.where(to_chip >= chips, to_chip - chips, to_chip)
        base = ((first_chip + to_chip) * 2 + core) * share

        def one(q, _):
            code = codes_ref[base + q]
            one_pair(ahead * share + q, lax.shift_right_logical(code, bits), jnp.bitwise_and(code, 2**bits - 1))
            return 0

        return lax.fori_loop(0, share, one, 0, unroll=32)

    lax.fori_loop(0, chips, one_share, 0)


def inner_kernel(where_ref, codes_ref, coeffs_ref, *refs, first_peer, sizes):
    local_s, block_rows, tm_count, chips, share, bits = sizes
    own, other = refs[:tm_count], refs[tm_count : 2 * tm_count]
    near_ref, carry_ref, slope_ref, rhs_ref = refs[2 * tm_count : 2 * tm_count + 4]
    out_ref, slab_ref, conv_ref = refs[2 * tm_count + 4 :]
    core = where_ref[2]
    modes, lanes = coeffs_ref.shape[1], own[0].shape[2]
    height = 2 * block_rows
    weights = mode_weights(where_ref, coeffs_ref, local_s, tm_count)

    def one_slab(index, _):
        own_slab = jnp.concatenate([piece[index] for piece in own], axis=0)
        other_slab = jnp.concatenate([piece[index] for piece in other], axis=0)
        is_first = core == 0
        both = jnp.concatenate(
            [jnp.where(is_first, own_slab, other_slab), jnp.where(is_first, other_slab, own_slab)], axis=1
        )
        result = modes_of(weights, both)
        slab_ref[0, index] = result[:, :lanes]
        slab_ref[1, index] = result[:, lanes:]
        return 0

    slabs = own[0].shape[0]
    lax.fori_loop(0, slabs, one_slab, 0, unroll=2 if slabs % 2 == 0 else 1)
    width, rows_y = lanes // tm_count, block_rows * tm_count
    lane = lax.broadcasted_iota(jnp.int32, (1, lanes), 1)
    part, column = lax.div(lane, width), lax.rem(lane, width)
    has_border = jnp.where(column == 0, -0.5, jnp.where(column == width - 1, 0.5, 0.0))
    t = where_ref[0]
    border_of = jnp.where(column == 0, 0, rows_y) + t * width - 1 + part * block_rows
    border_lanes = lax.broadcasted_iota(jnp.int32, (2 * lanes, lanes), 0)
    border_lanes = jnp.where(border_lanes >= lanes, border_lanes - lanes, border_lanes)
    borders = []
    for slab in range(3 * block_rows, slabs):
        both = jnp.concatenate([slab_ref[0, slab], slab_ref[1, slab]], axis=0)
        borders.append(jnp.concatenate(split_high_low(both), axis=1))
    for c in range(3):
        slab, first_lane = border_lane(rows_y, lanes, c)
        for row in range(block_rows):
            center = row * 3 + c
            if row % 2 == 0:
                picks = [
                    jnp.where(
                        border_lanes == jnp.bitwise_and(border_of + (first_lane + row + k), lanes - 1), has_border, 0.0
                    ).astype(BF16)
                    for k in range(2)
                ]
                border = jnp.dot(borders[slab], jnp.concatenate(picks, axis=1), preferred_element_type=F32)
            for plane in range(2):
                place = plane * block_rows + row
                value = slab_ref[plane, center]
                stream = slab_ref[1 - plane, center] * (0.5 if plane == 0 else -0.5)
                if row + 1 < block_rows:
                    above = slab_ref[plane, center + 3]
                else:
                    above = pltpu.roll(slab_ref[plane, c], lanes - width, 1)
                    above = jnp.where(lane < lanes - width, above, 0.0)
                if row > 0:
                    below = slab_ref[plane, center - 3]
                else:
                    below = pltpu.roll(slab_ref[plane, 3 * (block_rows - 1) + c], width, 1)
                    below = jnp.where(lane >= width, below, 0.0)
                normal = (above - below) * 0.5
                after = jnp.where(column < width - 1, pltpu.roll(value, lanes - 1, 1), 0.0)
                before = jnp.where(column > 0, pltpu.roll(value, 1, 1), 0.0)
                span = (after - before) * 0.5 + border[plane * modes : (plane + 1) * modes, row % 2 * lanes : (row % 2 + 1) * lanes]
                carry_ref[pl.ds(c * height + place, modes, stride=3 * height), :] = value
                for d, slope in enumerate((stream, normal, span)):
                    slope_ref[pl.ds((d * 3 + c) * height + place, modes, stride=9 * height), :] = slope
                store_projection(rhs_ref, c * height + place, value)
                if (plane == 1) == (row < block_rows // 2):
                    near_ref[center] = value

    pairs_kernel(
        where_ref, codes_ref, carry_ref, slope_ref, rhs_ref, out_ref, conv_ref,
        first_peer=first_peer, sizes=(height, chips, share, bits),
    )


def pairs_kernel(
    where_ref, codes_ref, carry_ref, slope_ref, rhs_ref, out_ref, conv_ref, *, first_peer, sizes
):
    height, chips, share, bits = sizes

    def one_pair(slot, i, j):
        carry = carry_ref[pl.ds(pl.multiple_of(i * (3 * height), 8), 3 * height), :]
        slope = slope_ref[pl.ds(pl.multiple_of(j * (9 * height), 8), 9 * height), :]
        rows = [
            sum(
                carry[d * height : (d + 1) * height] * slope[(d * 3 + c) * height : (d * 3 + c + 1) * height]
                for d in range(3)
            )
            for c in range(3)
        ]
        conv_ref[pl.ds(pl.multiple_of(slot * (3 * height), 8), 3 * height), :] = jnp.concatenate(rows, axis=0)

    def one_peer(number, _):
        for_pairs_of(where_ref, codes_ref, first_peer + number, (chips, share, bits), one_pair)
        out_ref[number] = project(conv_ref, rhs_ref, chips * share, 3 * height, conv_ref.shape[1])
        return 0

    lax.fori_loop(0, out_ref.shape[0], one_peer, 0)


def far_kernel(where_ref, coeffs_ref, *refs, sizes):
    local_s, block_rows, tm_count = sizes
    next_own, next_other, near_ref = refs[:tm_count], refs[tm_count], refs[tm_count + 1]
    carry_ref, slope_ref, rhs_ref = refs[tm_count + 2 :]
    is_first = where_ref[2] == 0
    modes, lanes = near_ref.shape[1:]
    height = 2 * block_rows
    half = block_rows // 2 * 3
    weights = mode_weights(where_ref, coeffs_ref, local_s, tm_count)
    for slab in range(half):
        mine = jnp.concatenate([next_own[peer][slab] for peer in range(tm_count)], axis=0)
        theirs = jnp.concatenate([next_other[peer, slab] for peer in range(tm_count)], axis=0)
        after, before = jnp.where(is_first, theirs, mine), jnp.where(is_first, mine, theirs)
        result = modes_of(weights, jnp.concatenate([after, before], axis=1))
        row, c = divmod(slab, 3)
        edges = ((near_ref[slab], result[:, :lanes]), (result[:, lanes:], near_ref[half + slab]))
        for number, (low, high) in enumerate(edges):
            place = number * block_rows + 2 * row
            for at, value, across in ((place, low, high * 0.5), (place + 1, high, low * -0.5)):
                if c == 0:
                    carry_ref[pl.ds(at, modes, stride=height), :] = value
                slope_ref[pl.ds(c * height + at, modes, stride=3 * height), :] = across
                store_projection(rhs_ref, c * height + at, value)


def edge_kernel(
    where_ref, codes_ref, carry_ref, slope_ref, rhs_ref, inner_ref, *refs, peer, sizes
):
    *arrived_refs, out_ref, conv_ref = refs
    chips, share, _ = sizes
    modes, lanes = out_ref.shape[1], carry_ref.shape[1]
    height = carry_ref.shape[0] // modes

    def one_pair(slot, i, j):
        carry = carry_ref[pl.ds(pl.multiple_of(i * height, 8), height), :]
        slope = slope_ref[pl.ds(pl.multiple_of(j * (3 * height), 8), 3 * height), :]
        rows = [carry * slope[c * height : (c + 1) * height] for c in range(3)]
        conv_ref[pl.ds(pl.multiple_of(slot * (3 * height), 8), 3 * height), :] = jnp.concatenate(rows, axis=0)

    for_pairs_of(where_ref, codes_ref, peer, sizes, one_pair)
    total = inner_ref[peer % inner_ref.shape[0]]
    for arrived_ref in arrived_refs:
        total = total + arrived_ref[...]
    out_ref[...] = total + project(conv_ref, rhs_ref, chips * share, 3 * height, lanes)


def vmem_limit(mebibytes):
    return pltpu.CompilerParams(vmem_limit_bytes=mebibytes * 2**20)


def in_vmem(array):
    return pltpu.with_memory_space_constraint(array, pltpu.VMEM)


def shards(snapshots, coeffs, pair_table):
    tm_count, space_count = lax.axis_size("tm"), lax.axis_size("space")
    chips = space_count // 2
    t, place = lax.axis_index("tm"), lax.axis_index("space")
    core = lax.rem(place, 2)
    where = jnp.stack([t, lax.div(place, 2), core]).astype(jnp.int32)
    local_s, _, _, rows_y, lanes = snapshots.shape
    modes = coeffs.shape[1]
    block_rows = rows_y // tm_count
    slabs = 3 * block_rows + border_slabs(rows_y, lanes)
    share = pair_table.shape[0] // (tm_count * space_count)
    factor = float(space_count * rows_y * lanes) ** (-0.5)
    bits = modes.bit_length() - 1
    assert modes == 2**bits
    codes = pair_table[:, 0] * modes + pair_table[:, 1]
    smem = pl.BlockSpec(memory_space=pltpu.SMEM)
    vmem = pl.BlockSpec(memory_space=pltpu.VMEM)
    block = chips * share
    height = 2 * block_rows
    depth = 3 * height * lanes

    swap = [(2 * chip + c, 2 * chip + 1 - c) for chip in range(chips) for c in range(2)]

    def across(peer):
        return [(i, i ^ peer) for i in range(tm_count)]

    with jax.named_scope("pack"):
        packed = pl.pallas_call(
            functools.partial(pack_kernel, sizes=(local_s, rows_y, tm_count)),
            out_shape=[pltpu.VMEM((slabs, local_s, lanes), F32)] * tm_count
            + [pltpu.VMEM((tm_count, block_rows // 2 * 3, local_s, lanes), F32)],
            in_specs=[smem, vmem],
            out_specs=[vmem] * (tm_count + 1),
            scratch_shapes=[pltpu.VMEM((tm_count, slabs, local_s, lanes), F32)],
            compiler_params=vmem_limit(16),
        )(where, snapshots.reshape(-1, lanes))
    with jax.named_scope("to_next_plane"):
        ring = [(place, (place + (1 if place % 2 else -1)) % space_count) for place in range(space_count)]
        across_edge = lax.ppermute(packed[tm_count], "space", ring)
    with jax.named_scope("to_columns"):
        own = [packed[0]] + [lax.ppermute(packed[peer], "tm", across(peer)) for peer in range(1, tm_count)]
    with jax.named_scope("next_to_columns"):
        across_edge, own[:3] = lax.optimization_barrier((across_edge, own[:3]))
        parts = [across_edge[peer] for peer in range(tm_count)]
        parts, own[3:] = lax.optimization_barrier((parts, own[3:]))
        next_own = [parts[0]] + [lax.ppermute(parts[peer], "tm", across(peer)) for peer in range(1, tm_count)]
    with jax.named_scope("to_other_core"):
        other = [lax.ppermute(piece, "space", swap) for piece in own]
    early = tm_count // 2
    work = [pltpu.VMEM((block * 3 * height, lanes), F32)]
    groups = pltpu.VMEM((early, block, modes), F32)
    with jax.named_scope("inner_terms"):
        near, *inner_tables, early_sums = pl.pallas_call(
            functools.partial(inner_kernel, first_peer=early, sizes=(local_s, block_rows, tm_count, chips, share, bits)),
            out_shape=[
                pltpu.VMEM((block_rows * 3, modes, lanes), F32),
                pltpu.VMEM((modes * 3 * height, lanes), F32),
                pltpu.VMEM((modes * 9 * height, lanes), F32),
                pltpu.VMEM((depth, 2 * modes), BF16),
                groups,
            ],
            in_specs=[smem, smem] + [vmem] * (2 * tm_count + 1),
            out_specs=[vmem] * 5,
            scratch_shapes=[pltpu.VMEM((2, slabs, modes, lanes), F32)] + work,
            compiler_params=vmem_limit(24),
            cost_estimate=pl.CostEstimate(flops=12 * 10**9, bytes_accessed=10**7, transcendentals=0),
        )(where, codes, coeffs, *[in_vmem(piece) for piece in (*own, *other)])
    with jax.named_scope("next_to_other_core"):
        next_own, inner_tables = lax.optimization_barrier((next_own, inner_tables))
        next_other = lax.ppermute(jnp.stack(next_own), "space", swap)
    with jax.named_scope("inner_terms"):
        late_sums = pl.pallas_call(
            functools.partial(pairs_kernel, first_peer=0, sizes=(height, chips, share, bits)),
            out_shape=groups,
            in_specs=[smem, smem] + [vmem] * 3,
            out_specs=vmem,
            scratch_shapes=work,
            compiler_params=vmem_limit(16),
            cost_estimate=pl.CostEstimate(flops=8 * 10**9, bytes_accessed=10**7, transcendentals=0),
        )(where, codes, *[in_vmem(table) for table in inner_tables])
    with jax.named_scope("edge_tables"):
        tables = list(pl.pallas_call(
            functools.partial(far_kernel, sizes=(local_s, block_rows, tm_count)),
            out_shape=[
                pltpu.VMEM((modes * height, lanes), F32),
                pltpu.VMEM((modes * 3 * height, lanes), F32),
                pltpu.VMEM((depth, 2 * modes), BF16),
            ],
            in_specs=[smem] + [vmem] * (tm_count + 3),
            out_specs=[vmem] * 3,
            compiler_params=vmem_limit(16),
        )(where, coeffs, *[in_vmem(piece) for piece in (*next_own, next_other, near)]))
    arrived = []
    for peer in reversed(range(tm_count)):
        with jax.named_scope("edge_terms"):
            parts = arrived[:-1] if peer == 0 else []
            summed = pl.pallas_call(
                functools.partial(edge_kernel, peer=peer, sizes=(chips, share, bits)),
                out_shape=pltpu.VMEM((block, modes), F32),
                in_specs=[smem, smem] + [vmem] * (4 + len(parts)),
                out_specs=vmem,
                scratch_shapes=work,
                compiler_params=vmem_limit(16),
                cost_estimate=pl.CostEstimate(flops=10**8, bytes_accessed=10**5, transcendentals=0),
            )(
                where,
                codes,
                *[in_vmem(table) for table in (*tables, early_sums if peer >= early else late_sums, *parts)],
            )
        with jax.named_scope("sum_over_columns"):
            if peer:
                arrived.append(lax.ppermute(summed, "tm", across(peer)))
                if peer > early:
                    early_sums, _ = lax.optimization_barrier((early_sums, summed))
                else:
                    late_sums, _ = lax.optimization_barrier((late_sums, summed))
    with jax.named_scope("sum_over_columns"):
        summed = summed + arrived[-1]
    with jax.named_scope("sum_over_chips"):
        shares = summed.reshape(chips, share, modes)
        result = shares[0]
        for step in range(1, chips):
            shift = [
                (2 * chip + c, 2 * ((chip + step) % chips) + c) for chip in range(chips) for c in range(2)
            ]
            result = result + lax.ppermute(shares[step], "space", shift)
        return result * factor


def solution(mesh):
    placed = (P("tm", None, "space", None, None), P(), P())
    return jax.shard_map(
        shards, mesh=mesh, in_specs=placed, out_specs=P(("tm", "space"), None), check_vma=False
    )
```

```python
import functools

import jax
import jax.numpy as jnp
from jax import lax
from jax.experimental import pallas as pl
from jax.experimental.pallas import tpu as pltpu
from jax.sharding import PartitionSpec as P

F32 = jnp.float32
BF16 = jnp.bfloat16


def split_high_low(values):
    high = values.astype(BF16)
    low = (values - high.astype(F32)).astype(BF16)
    return high, low


def border_lane(rows_y, lanes, c):
    per_slab = lanes // (2 * rows_y)
    return c // per_slab, c % per_slab * 2 * rows_y


def border_slabs(rows_y, lanes):
    return border_lane(rows_y, lanes, 2)[0] + 1


def exchange_blocks(rows, lane, width, lanes):
    rows = list(rows)
    step = len(rows) // 2
    while step:
        keeps = jnp.bitwise_and(lane, step * width) == 0
        for low in range(len(rows)):
            if low & step == 0:
                first, second = rows[low], rows[low + step]
                rows[low] = jnp.where(keeps, first, pltpu.roll(second, step * width, 1))
                rows[low + step] = jnp.where(keeps, pltpu.roll(first, lanes - step * width, 1), second)
        step //= 2
    return rows


def pack_kernel(where_ref, field_ref, *refs, sizes):
    *out_refs, sorted_ref, held_ref, sems = refs
    local_s, rows_y, tm_count = sizes
    lanes = field_ref.shape[3]
    copies = [pltpu.make_async_copy(field_ref.at[:, c], held_ref.at[c], sems.at[c]) for c in range(3)]
    for copy in copies:
        copy.start()
    rows_ref = held_ref.reshape(3 * local_s * rows_y, lanes)
    t, core = where_ref[0], where_ref[2]
    width, groups = lanes // tm_count, rows_y // tm_count
    lane = lax.broadcasted_iota(jnp.int32, (local_s, lanes), 1)
    borders = [[jnp.zeros((local_s, lanes), F32) for _ in range(tm_count)] for _ in range(border_slabs(rows_y, lanes))]
    for c in range(3):
        slab, first_lane = border_lane(rows_y, lanes, c)
        copies[c].wait()

        def one_group(g, border, c=c, first_lane=first_lane):
            border = list(border)
            rows = []
            for q in range(tm_count):
                y = q * groups + g
                row = rows_ref[pl.ds(c * local_s * rows_y + y, local_s, stride=rows_y), :]
                rows.append(row)
                for side in range(2):
                    shift = first_lane + side * (rows_y - width - 1) + y
                    moved = pltpu.roll(row, jnp.bitwise_and(shift, lanes - 1), 1)
                    for block in range(tm_count):
                        column = (block + 1) * width if side else block * width - 1
                        is_here = lane == jnp.bitwise_and(shift + column, lanes - 1)
                        border[block] = jnp.where(is_here, moved, border[block])
            for block, main in enumerate(exchange_blocks(rows, lane, width, lanes)):
                sorted_ref[block, g * 3 + c] = main
            return tuple(border)

        borders[slab] = lax.fori_loop(0, groups, one_group, tuple(borders[slab]))
    half = groups // 2 * 3
    for slab, border in enumerate(borders):
        for block in range(tm_count):
            sorted_ref[block, groups * 3 + slab] = border[block]
    for peer in range(tm_count):
        block = jnp.bitwise_xor(t, peer)
        out_refs[peer][...] = sorted_ref[block]
        out_refs[tm_count][peer] = sorted_ref[block, pl.ds(core * half, half)]


def mode_weights(where_ref, coeffs_ref, local_s, tm_count):
    t = where_ref[0]
    ordered = jnp.concatenate(
        [
            coeffs_ref[pl.ds(pl.multiple_of(jnp.bitwise_xor(t, peer) * local_s, 8), local_s), :]
            for peer in range(tm_count)
        ],
        axis=0,
    )
    high, low = split_high_low(ordered.T)
    return jnp.concatenate([high, low, high, low], axis=1)


def modes_of(weights, slab):
    high, low = split_high_low(slab)
    return jnp.dot(weights, jnp.concatenate([high, high, low, low], axis=0), preferred_element_type=F32)


def store_projection(rhs_ref, place, mode_slab):
    high, low = split_high_low(mode_slab.T)
    modes, lanes = mode_slab.shape
    rhs_ref[place * lanes : (place + 1) * lanes, 0:modes] = high
    rhs_ref[place * lanes : (place + 1) * lanes, modes : 2 * modes] = low


def project(conv_ref, rhs_ref, block, places, lanes):
    both = None
    for place in range(0, places, 2):
        highs, lows = zip(
            *(split_high_low(conv_ref[pl.ds(place + k, block, stride=places), :]) for k in range(2))
        )
        lhs = jnp.concatenate([jnp.concatenate(highs, axis=1), jnp.concatenate(lows, axis=1)], axis=0)
        part = jnp.dot(lhs, rhs_ref[place * lanes : (place + 2) * lanes, :], preferred_element_type=F32)
        both = part if both is None else both + part
    modes = both.shape[1] // 2
    return (both[:block, :modes] + both[:block, modes:]) + (both[block:, :modes] + both[block:, modes:])


def for_pairs_of(where_ref, codes_ref, peer, sizes, one_pair):
    chips, share, bits = sizes
    t, chip, core = where_ref[0], where_ref[1], where_ref[2]
    first_chip = jnp.bitwise_xor(t, peer) * chips

    def one_share(ahead, _):
        base = ((first_chip + jnp.bitwise_xor(chip, ahead)) * 2 + core) * share

        def one(q, _):
            code = codes_ref[base + q]
            one_pair(ahead * share + q, lax.shift_right_logical(code, bits), jnp.bitwise_and(code, 2**bits - 1))
            return 0

        return lax.fori_loop(0, share, one, 0, unroll=32)

    lax.fori_loop(0, chips, one_share, 0)


def inner_kernel(where_ref, codes_ref, coeffs_ref, *refs, first_peer, sizes):
    local_s, block_rows, tm_count, chips, share, bits = sizes
    own, other = refs[:tm_count], refs[tm_count : 2 * tm_count]
    near_ref, carry_ref, slope_ref, rhs_ref = refs[2 * tm_count : 2 * tm_count + 4]
    out_ref, slab_ref, conv_ref = refs[2 * tm_count + 4 :]
    core = where_ref[2]
    modes, lanes = coeffs_ref.shape[1], own[0].shape[2]
    height = 2 * block_rows
    weights = mode_weights(where_ref, coeffs_ref, local_s, tm_count)

    def one_slab(index, _):
        own_slab = jnp.concatenate([piece[index] for piece in own], axis=0)
        other_slab = jnp.concatenate([piece[index] for piece in other], axis=0)
        is_first = core == 0
        both = jnp.concatenate(
            [jnp.where(is_first, own_slab, other_slab), jnp.where(is_first, other_slab, own_slab)], axis=1
        )
        result = modes_of(weights, both)
        slab_ref[0, index] = result[:, :lanes]
        slab_ref[1, index] = result[:, lanes:]
        return 0

    slabs = own[0].shape[0]
    lax.fori_loop(0, slabs, one_slab, 0, unroll=True)
    width, rows_y = lanes // tm_count, block_rows * tm_count
    lane = lax.broadcasted_iota(jnp.int32, (1, lanes), 1)
    part, column = lax.div(lane, width), lax.rem(lane, width)
    has_border = jnp.where(column == 0, -0.5, jnp.where(column == width - 1, 0.5, 0.0))
    t = where_ref[0]
    border_of = jnp.where(column == 0, 0, rows_y) + t * width - 1 + part * block_rows
    border_lanes = lax.broadcasted_iota(jnp.int32, (2 * lanes, lanes), 0)
    border_lanes = jnp.where(border_lanes >= lanes, border_lanes - lanes, border_lanes)
    borders = []
    for slab in range(3 * block_rows, slabs):
        both = jnp.concatenate([slab_ref[0, slab], slab_ref[1, slab]], axis=0)
        borders.append(jnp.concatenate(split_high_low(both), axis=1))
    for c in range(3):
        slab, first_lane = border_lane(rows_y, lanes, c)
        for row in range(block_rows):
            center = row * 3 + c
            if row % 2 == 0:
                picks = [
                    jnp.where(
                        border_lanes == jnp.bitwise_and(border_of + (first_lane + row + k), lanes - 1), has_border, 0.0
                    ).astype(BF16)
                    for k in range(2)
                ]
                border = jnp.dot(borders[slab], jnp.concatenate(picks, axis=1), preferred_element_type=F32)
            for plane in range(2):
                place = plane * block_rows + row
                value = slab_ref[plane, center]
                stream = slab_ref[1 - plane, center] * (0.5 if plane == 0 else -0.5)
                if row + 1 < block_rows:
                    above = slab_ref[plane, center + 3]
                else:
                    above = pltpu.roll(slab_ref[plane, c], lanes - width, 1)
                    above = jnp.where(lane < lanes - width, above, 0.0)
                if row > 0:
                    below = slab_ref[plane, center - 3]
                else:
                    below = pltpu.roll(slab_ref[plane, 3 * (block_rows - 1) + c], width, 1)
                    below = jnp.where(lane >= width, below, 0.0)
                normal = (above - below) * 0.5
                after = jnp.where(column < width - 1, pltpu.roll(value, lanes - 1, 1), 0.0)
                before = jnp.where(column > 0, pltpu.roll(value, 1, 1), 0.0)
                span = (after - before) * 0.5 + border[plane * modes : (plane + 1) * modes, row % 2 * lanes : (row % 2 + 1) * lanes]
                carry_ref[pl.ds(c * height + place, modes, stride=3 * height), :] = value
                for d, slope in enumerate((stream, normal, span)):
                    slope_ref[pl.ds((d * 3 + c) * height + place, modes, stride=9 * height), :] = slope
                store_projection(rhs_ref, c * height + place, value)
                if (plane == 1) == (row < block_rows // 2):
                    near_ref[center] = value

    pairs_kernel(
        where_ref, codes_ref, carry_ref, slope_ref, rhs_ref, out_ref, conv_ref,
        first_peer=first_peer, sizes=(height, chips, share, bits),
    )


def pairs_kernel(
    where_ref, codes_ref, carry_ref, slope_ref, rhs_ref, out_ref, conv_ref, *, first_peer, sizes
):
    height, chips, share, bits = sizes

    def one_pair(slot, i, j):
        carry = carry_ref[pl.ds(pl.multiple_of(i * (3 * height), 8), 3 * height), :]
        slope = slope_ref[pl.ds(pl.multiple_of(j * (9 * height), 8), 9 * height), :]
        rows = [
            sum(
                carry[d * height : (d + 1) * height] * slope[(d * 3 + c) * height : (d * 3 + c + 1) * height]
                for d in range(3)
            )
            for c in range(3)
        ]
        conv_ref[pl.ds(pl.multiple_of(slot * (3 * height), 8), 3 * height), :] = jnp.concatenate(rows, axis=0)

    def one_peer(number, _):
        for_pairs_of(where_ref, codes_ref, first_peer + number, (chips, share, bits), one_pair)
        out_ref[number] = project(conv_ref, rhs_ref, chips * share, 3 * height, conv_ref.shape[1])
        return 0

    lax.fori_loop(0, out_ref.shape[0], one_peer, 0)


def far_kernel(where_ref, codes_ref, coeffs_ref, *refs, peer, sizes):
    local_s, block_rows, tm_count, chips, share, bits = sizes
    next_own, next_other, near_ref, inner_ref = refs[:tm_count], *refs[tm_count : tm_count + 3]
    carry_ref, slope_ref, rhs_ref, out_ref, conv_ref = refs[tm_count + 3 :]
    is_first = where_ref[2] == 0
    modes, lanes = near_ref.shape[1:]
    height = 2 * block_rows
    half = block_rows // 2 * 3
    weights = mode_weights(where_ref, coeffs_ref, local_s, tm_count)
    for slab in range(half):
        mine = jnp.concatenate([next_own[peer][slab] for peer in range(tm_count)], axis=0)
        theirs = jnp.concatenate([next_other[peer, slab] for peer in range(tm_count)], axis=0)
        after, before = jnp.where(is_first, theirs, mine), jnp.where(is_first, mine, theirs)
        result = modes_of(weights, jnp.concatenate([after, before], axis=1))
        row, c = divmod(slab, 3)
        edges = ((near_ref[slab], result[:, :lanes]), (result[:, lanes:], near_ref[half + slab]))
        for number, (low, high) in enumerate(edges):
            place = number * block_rows + 2 * row
            for at, value, across in ((place, low, high * 0.5), (place + 1, high, low * -0.5)):
                if c == 0:
                    carry_ref[pl.ds(at, modes, stride=height), :] = value
                slope_ref[pl.ds(c * height + at, modes, stride=3 * height), :] = across
                store_projection(rhs_ref, c * height + at, value)


    out_ref[...] = edge_sum(
        where_ref, codes_ref, carry_ref, slope_ref, rhs_ref, inner_ref, conv_ref, peer, (chips, share, bits)
    )


def edge_sum(where_ref, codes_ref, carry_ref, slope_ref, rhs_ref, inner_ref, conv_ref, peer, sizes):
    chips, share, _ = sizes
    modes, lanes = inner_ref.shape[2], carry_ref.shape[1]
    height = carry_ref.shape[0] // modes

    def one_pair(slot, i, j):
        carry = carry_ref[pl.ds(pl.multiple_of(i * height, 8), height), :]
        slope = slope_ref[pl.ds(pl.multiple_of(j * (3 * height), 8), 3 * height), :]
        rows = [carry * slope[c * height : (c + 1) * height] for c in range(3)]
        conv_ref[pl.ds(pl.multiple_of(slot * (3 * height), 8), 3 * height), :] = jnp.concatenate(rows, axis=0)

    for_pairs_of(where_ref, codes_ref, peer, sizes, one_pair)
    return inner_ref[peer % inner_ref.shape[0]] + project(conv_ref, rhs_ref, chips * share, 3 * height, lanes)


def edge_kernel(where_ref, codes_ref, carry_ref, slope_ref, rhs_ref, inner_ref, *refs, peer, sizes):
    *arrived_refs, out_ref, conv_ref = refs
    total = edge_sum(where_ref, codes_ref, carry_ref, slope_ref, rhs_ref, inner_ref, conv_ref, peer, sizes)
    for arrived_ref in arrived_refs:
        total = total + arrived_ref[...]
    out_ref[...] = total


def vmem_limit(mebibytes):
    return pltpu.CompilerParams(vmem_limit_bytes=mebibytes * 2**20)


def in_vmem(array):
    return pltpu.with_memory_space_constraint(array, pltpu.VMEM)


def shards(snapshots, coeffs, pair_table):
    tm_count, space_count = lax.axis_size("tm"), lax.axis_size("space")
    chips = space_count // 2
    t, place = lax.axis_index("tm"), lax.axis_index("space")
    core = lax.rem(place, 2)
    where = jnp.stack([t, lax.div(place, 2), core]).astype(jnp.int32)
    local_s, _, _, rows_y, lanes = snapshots.shape
    modes = coeffs.shape[1]
    block_rows = rows_y // tm_count
    slabs = 3 * block_rows + border_slabs(rows_y, lanes)
    share = pair_table.shape[0] // (tm_count * space_count)
    factor = float(space_count * rows_y * lanes) ** (-0.5)
    bits = modes.bit_length() - 1
    assert modes == 2**bits
    codes = pair_table[:, 0] * modes + pair_table[:, 1]
    smem = pl.BlockSpec(memory_space=pltpu.SMEM)
    vmem = pl.BlockSpec(memory_space=pltpu.VMEM)
    block = chips * share
    height = 2 * block_rows
    depth = 3 * height * lanes

    swap = [(2 * chip + c, 2 * chip + 1 - c) for chip in range(chips) for c in range(2)]

    def across(peer):
        return [(i, i ^ peer) for i in range(tm_count)]

    with jax.named_scope("pack"):
        packed = pl.pallas_call(
            functools.partial(pack_kernel, sizes=(local_s, rows_y, tm_count)),
            out_shape=[pltpu.VMEM((slabs, local_s, lanes), F32)] * tm_count
            + [pltpu.VMEM((tm_count, block_rows // 2 * 3, local_s, lanes), F32)],
            in_specs=[smem, pl.BlockSpec(memory_space=pltpu.HBM)],
            out_specs=[vmem] * (tm_count + 1),
            scratch_shapes=[
                pltpu.VMEM((tm_count, slabs, local_s, lanes), F32),
                pltpu.VMEM((3, local_s, rows_y, lanes), F32),
                pltpu.SemaphoreType.DMA((3,)),
            ],
            compiler_params=vmem_limit(16),
        )(where, pltpu.with_memory_space_constraint(snapshots.reshape(local_s, 3, rows_y, lanes), pltpu.HBM))
    with jax.named_scope("to_next_plane"):
        ring = [(place, (place + (1 if place % 2 else -1)) % space_count) for place in range(space_count)]
        across_edge = lax.ppermute(packed[tm_count], "space", ring)
    with jax.named_scope("to_columns"):
        own = [packed[0]] + [lax.ppermute(packed[peer], "tm", across(peer)) for peer in range(1, tm_count)]
    with jax.named_scope("next_to_columns"):
        across_edge, own[:3] = lax.optimization_barrier((across_edge, own[:3]))
        parts = [across_edge[peer] for peer in range(tm_count)]
        parts, own[3:] = lax.optimization_barrier((parts, own[3:]))
        next_own = [parts[0]] + [lax.ppermute(parts[peer], "tm", across(peer)) for peer in range(1, tm_count)]
    with jax.named_scope("to_other_core"):
        other = [lax.ppermute(piece, "space", swap) for piece in own]
    early = tm_count // 2
    work = [pltpu.VMEM((block * 3 * height, lanes), F32)]
    groups = pltpu.VMEM((early, block, modes), F32)
    with jax.named_scope("inner_terms"):
        near, *inner_tables, early_sums = pl.pallas_call(
            functools.partial(inner_kernel, first_peer=early, sizes=(local_s, block_rows, tm_count, chips, share, bits)),
            out_shape=[
                pltpu.VMEM((block_rows * 3, modes, lanes), F32),
                pltpu.VMEM((modes * 3 * height, lanes), F32),
                pltpu.VMEM((modes * 9 * height, lanes), F32),
                pltpu.VMEM((depth, 2 * modes), BF16),
                groups,
            ],
            in_specs=[smem, smem] + [vmem] * (2 * tm_count + 1),
            out_specs=[vmem] * 5,
            scratch_shapes=[pltpu.VMEM((2, slabs, modes, lanes), F32)] + work,
            compiler_params=vmem_limit(24),
            cost_estimate=pl.CostEstimate(flops=12 * 10**9, bytes_accessed=10**7, transcendentals=0),
        )(where, codes, coeffs, *[in_vmem(piece) for piece in (*own, *other)])
    with jax.named_scope("next_to_other_core"):
        next_own, inner_tables = lax.optimization_barrier((next_own, inner_tables))
        next_other = lax.ppermute(jnp.stack(next_own), "space", swap)
    with jax.named_scope("inner_terms"):
        late_sums = pl.pallas_call(
            functools.partial(pairs_kernel, first_peer=0, sizes=(height, chips, share, bits)),
            out_shape=groups,
            in_specs=[smem, smem] + [vmem] * 3,
            out_specs=vmem,
            scratch_shapes=work,
            compiler_params=vmem_limit(16),
            cost_estimate=pl.CostEstimate(flops=8 * 10**9, bytes_accessed=10**7, transcendentals=0),
        )(where, codes, *[in_vmem(table) for table in inner_tables])
    with jax.named_scope("edge_terms"):
        *tables, summed = pl.pallas_call(
            functools.partial(
                far_kernel, peer=tm_count - 1, sizes=(local_s, block_rows, tm_count, chips, share, bits)
            ),
            out_shape=[
                pltpu.VMEM((modes * height, lanes), F32),
                pltpu.VMEM((modes * 3 * height, lanes), F32),
                pltpu.VMEM((depth, 2 * modes), BF16),
                pltpu.VMEM((block, modes), F32),
            ],
            in_specs=[smem, smem] + [vmem] * (tm_count + 4),
            out_specs=[vmem] * 4,
            scratch_shapes=work,
            compiler_params=vmem_limit(16),
        )(where, codes, coeffs, *[in_vmem(piece) for piece in (*next_own, next_other, near, early_sums)])
    arrived = []
    for peer in reversed(range(tm_count - 1)):
        with jax.named_scope("sum_over_columns"):
            arrived.append(lax.ppermute(summed, "tm", across(peer + 1)))
            if peer >= early:
                early_sums, _ = lax.optimization_barrier((early_sums, summed))
            else:
                late_sums, _ = lax.optimization_barrier((late_sums, summed))
        with jax.named_scope("edge_terms"):
            parts = arrived[:-1] if peer == 0 else []
            summed = pl.pallas_call(
                functools.partial(edge_kernel, peer=peer, sizes=(chips, share, bits)),
                out_shape=pltpu.VMEM((block, modes), F32),
                in_specs=[smem, smem] + [vmem] * (4 + len(parts)),
                out_specs=vmem,
                scratch_shapes=work,
                compiler_params=vmem_limit(16),
                cost_estimate=pl.CostEstimate(flops=10**8, bytes_accessed=10**5, transcendentals=0),
            )(
                where,
                codes,
                *[in_vmem(table) for table in (*tables, early_sums if peer >= early else late_sums, *parts)],
            )
    with jax.named_scope("sum_over_columns"):
        summed = summed + arrived[-1]
    with jax.named_scope("sum_over_chips"):
        shares = summed.reshape(chips, share, modes)
        result = shares[0]
        for step in range(1, chips):
            pairing = [(2 * chip + c, 2 * (chip ^ step) + c) for chip in range(chips) for c in range(2)]
            result = result + lax.ppermute(shares[step], "space", pairing)
        return result * factor


def solution(mesh):
    placed = (P("tm", None, "space", None, None), P(), P())
    return jax.shard_map(
        shards, mesh=mesh, in_specs=placed, out_specs=P(("tm", "space"), None), check_vma=False
    )
```

```python
import functools

import jax
import jax.numpy as jnp
from jax import lax
from jax.experimental import pallas as pl
from jax.experimental.pallas import tpu as pltpu
from jax.sharding import PartitionSpec as P

F32 = jnp.float32
BF16 = jnp.bfloat16


def split_high_low(values):
    high = values.astype(BF16)
    low = (values - high.astype(F32)).astype(BF16)
    return high, low


def border_lane(rows_y, lanes, c):
    per_slab = lanes // (2 * rows_y)
    return c // per_slab, c % per_slab * 2 * rows_y


def border_slabs(rows_y, lanes):
    return border_lane(rows_y, lanes, 2)[0] + 1


def exchange_blocks(rows, lane, width, lanes):
    rows = list(rows)
    step = len(rows) // 2
    while step:
        keeps = jnp.bitwise_and(lane, step * width) == 0
        for low in range(len(rows)):
            if low & step == 0:
                first, second = rows[low], rows[low + step]
                rows[low] = jnp.where(keeps, first, pltpu.roll(second, step * width, 1))
                rows[low + step] = jnp.where(keeps, pltpu.roll(first, lanes - step * width, 1), second)
        step //= 2
    return rows


def pack_kernel(where_ref, field_ref, *refs, sizes):
    *out_refs, sorted_ref, held_ref, sems = refs
    local_s, rows_y, tm_count = sizes
    lanes = field_ref.shape[3]
    copies = [pltpu.make_async_copy(field_ref.at[:, c], held_ref.at[c], sems.at[c]) for c in range(3)]
    for copy in copies:
        copy.start()
    rows_ref = held_ref.reshape(3 * local_s * rows_y, lanes)
    t, core = where_ref[0], where_ref[2]
    width, groups = lanes // tm_count, rows_y // tm_count
    lane = lax.broadcasted_iota(jnp.int32, (local_s, lanes), 1)
    borders = [[jnp.zeros((local_s, lanes), F32) for _ in range(tm_count)] for _ in range(border_slabs(rows_y, lanes))]
    for c in range(3):
        slab, first_lane = border_lane(rows_y, lanes, c)
        copies[c].wait()

        def one_group(g, border, c=c, first_lane=first_lane):
            border = list(border)
            rows = []
            for q in range(tm_count):
                y = q * groups + g
                row = rows_ref[pl.ds(c * local_s * rows_y + y, local_s, stride=rows_y), :]
                rows.append(row)
                for side in range(2):
                    shift = first_lane + side * (rows_y - width - 1) + y
                    moved = pltpu.roll(row, jnp.bitwise_and(shift, lanes - 1), 1)
                    for block in range(tm_count):
                        column = (block + 1) * width if side else block * width - 1
                        is_here = lane == jnp.bitwise_and(shift + column, lanes - 1)
                        border[block] = jnp.where(is_here, moved, border[block])
            for block, main in enumerate(exchange_blocks(rows, lane, width, lanes)):
                sorted_ref[block, g * 3 + c] = main
            return tuple(border)

        borders[slab] = lax.fori_loop(0, groups, one_group, tuple(borders[slab]))
    half = groups // 2 * 3
    for slab, border in enumerate(borders):
        for block in range(tm_count):
            sorted_ref[block, groups * 3 + slab] = border[block]
    for peer in range(tm_count):
        block = jnp.bitwise_xor(t, peer)
        out_refs[peer][...] = sorted_ref[block]
        out_refs[tm_count][peer] = sorted_ref[block, pl.ds(core * half, half)]


def mode_weights(where_ref, coeffs_ref, local_s, tm_count):
    t = where_ref[0]
    ordered = jnp.concatenate(
        [
            coeffs_ref[pl.ds(pl.multiple_of(jnp.bitwise_xor(t, peer) * local_s, 8), local_s), :]
            for peer in range(tm_count)
        ],
        axis=0,
    )
    high, low = split_high_low(ordered.T)
    return jnp.concatenate([high, low, high, low], axis=1)


def modes_of(weights, slab):
    high, low = split_high_low(slab)
    return jnp.dot(weights, jnp.concatenate([high, high, low, low], axis=0), preferred_element_type=F32)


def store_projection(rhs_ref, place, mode_slab):
    high, low = split_high_low(mode_slab.T)
    modes, lanes = mode_slab.shape
    rhs_ref[place * lanes : (place + 1) * lanes, 0:modes] = high
    rhs_ref[place * lanes : (place + 1) * lanes, modes : 2 * modes] = low


def project(conv_ref, rhs_ref, block, places, lanes):
    both = None
    for place in range(0, places, 2):
        highs, lows = zip(
            *(split_high_low(conv_ref[pl.ds(place + k, block, stride=places), :]) for k in range(2))
        )
        lhs = jnp.concatenate([jnp.concatenate(highs, axis=1), jnp.concatenate(lows, axis=1)], axis=0)
        part = jnp.dot(lhs, rhs_ref[place * lanes : (place + 2) * lanes, :], preferred_element_type=F32)
        both = part if both is None else both + part
    modes = both.shape[1] // 2
    return (both[:block, :modes] + both[:block, modes:]) + (both[block:, :modes] + both[block:, modes:])


def for_pairs_of(where_ref, codes_ref, group, sizes, one_pair):
    tm_count, chips, share, bits = sizes
    t, chip, core = where_ref[0], where_ref[1], where_ref[2]
    to_chip = jnp.bitwise_xor(chip, group)

    def one_share(peer, _):
        base = ((jnp.bitwise_xor(t, peer) * chips + to_chip) * 2 + core) * share

        def one(q, _):
            code = codes_ref[base + q]
            one_pair(peer * share + q, lax.shift_right_logical(code, bits), jnp.bitwise_and(code, 2**bits - 1))
            return 0

        return lax.fori_loop(0, share, one, 0, unroll=32)

    lax.fori_loop(0, tm_count, one_share, 0)


def inner_kernel(where_ref, codes_ref, coeffs_ref, *refs, first_group, sizes):
    local_s, block_rows, tm_count, chips, share, bits = sizes
    own, other = refs[:tm_count], refs[tm_count : 2 * tm_count]
    near_ref, carry_ref, slope_ref, rhs_ref = refs[2 * tm_count : 2 * tm_count + 4]
    out_ref, slab_ref, conv_ref = refs[2 * tm_count + 4 :]
    core = where_ref[2]
    modes, lanes = coeffs_ref.shape[1], own[0].shape[2]
    height = 2 * block_rows
    weights = mode_weights(where_ref, coeffs_ref, local_s, tm_count)

    def one_slab(index, _):
        own_slab = jnp.concatenate([piece[index] for piece in own], axis=0)
        other_slab = jnp.concatenate([piece[index] for piece in other], axis=0)
        is_first = core == 0
        both = jnp.concatenate(
            [jnp.where(is_first, own_slab, other_slab), jnp.where(is_first, other_slab, own_slab)], axis=1
        )
        result = modes_of(weights, both)
        slab_ref[0, index] = result[:, :lanes]
        slab_ref[1, index] = result[:, lanes:]
        return 0

    slabs = own[0].shape[0]
    lax.fori_loop(0, slabs, one_slab, 0, unroll=True)
    width, rows_y = lanes // tm_count, block_rows * tm_count
    lane = lax.broadcasted_iota(jnp.int32, (1, lanes), 1)
    part, column = lax.div(lane, width), lax.rem(lane, width)
    has_border = jnp.where(column == 0, -0.5, jnp.where(column == width - 1, 0.5, 0.0))
    t = where_ref[0]
    border_of = jnp.where(column == 0, 0, rows_y) + t * width - 1 + part * block_rows
    border_lanes = lax.broadcasted_iota(jnp.int32, (2 * lanes, lanes), 0)
    border_lanes = jnp.where(border_lanes >= lanes, border_lanes - lanes, border_lanes)
    borders = []
    for slab in range(3 * block_rows, slabs):
        both = jnp.concatenate([slab_ref[0, slab], slab_ref[1, slab]], axis=0)
        borders.append(jnp.concatenate(split_high_low(both), axis=1))
    for c in range(3):
        slab, first_lane = border_lane(rows_y, lanes, c)
        for row in range(block_rows):
            center = row * 3 + c
            if row % 2 == 0:
                picks = [
                    jnp.where(
                        border_lanes == jnp.bitwise_and(border_of + (first_lane + row + k), lanes - 1), has_border, 0.0
                    ).astype(BF16)
                    for k in range(2)
                ]
                border = jnp.dot(borders[slab], jnp.concatenate(picks, axis=1), preferred_element_type=F32)
            for plane in range(2):
                place = plane * block_rows + row
                value = slab_ref[plane, center]
                stream = slab_ref[1 - plane, center] * (0.5 if plane == 0 else -0.5)
                if row + 1 < block_rows:
                    above = slab_ref[plane, center + 3]
                else:
                    above = pltpu.roll(slab_ref[plane, c], lanes - width, 1)
                    above = jnp.where(lane < lanes - width, above, 0.0)
                if row > 0:
                    below = slab_ref[plane, center - 3]
                else:
                    below = pltpu.roll(slab_ref[plane, 3 * (block_rows - 1) + c], width, 1)
                    below = jnp.where(lane >= width, below, 0.0)
                normal = (above - below) * 0.5
                after = jnp.where(column < width - 1, pltpu.roll(value, lanes - 1, 1), 0.0)
                before = jnp.where(column > 0, pltpu.roll(value, 1, 1), 0.0)
                span = (after - before) * 0.5 + border[plane * modes : (plane + 1) * modes, row % 2 * lanes : (row % 2 + 1) * lanes]
                carry_ref[pl.ds(c * height + place, modes, stride=3 * height), :] = value
                for d, slope in enumerate((stream, normal, span)):
                    slope_ref[pl.ds((d * 3 + c) * height + place, modes, stride=9 * height), :] = slope
                store_projection(rhs_ref, c * height + place, value)
                if (plane == 1) == (row < block_rows // 2):
                    near_ref[center] = value

    pairs_kernel(
        where_ref, codes_ref, carry_ref, slope_ref, rhs_ref, out_ref, conv_ref,
        first_group=first_group, sizes=(tm_count, chips, share, bits),
    )


def pairs_kernel(
    where_ref, codes_ref, carry_ref, slope_ref, rhs_ref, out_ref, conv_ref, *, first_group, sizes
):
    modes, lanes = out_ref.shape[2], conv_ref.shape[1]
    height = carry_ref.shape[0] // (3 * modes)

    def one_pair(slot, i, j):
        carry = carry_ref[pl.ds(pl.multiple_of(i * (3 * height), 8), 3 * height), :]
        slope = slope_ref[pl.ds(pl.multiple_of(j * (9 * height), 8), 9 * height), :]
        rows = [
            sum(
                carry[d * height : (d + 1) * height] * slope[(d * 3 + c) * height : (d * 3 + c + 1) * height]
                for d in range(3)
            )
            for c in range(3)
        ]
        conv_ref[pl.ds(pl.multiple_of(slot * (3 * height), 8), 3 * height), :] = jnp.concatenate(rows, axis=0)

    def one_group(number, _):
        for_pairs_of(where_ref, codes_ref, first_group + number, sizes, one_pair)
        out_ref[number] = project(conv_ref, rhs_ref, out_ref.shape[1], 3 * height, lanes)
        return 0

    lax.fori_loop(0, out_ref.shape[0], one_group, 0)


def far_kernel(where_ref, codes_ref, coeffs_ref, *refs, group, sizes):
    local_s, block_rows, tm_count, chips, share, bits = sizes
    next_own, next_other, near_ref, inner_ref = refs[:tm_count], *refs[tm_count : tm_count + 3]
    carry_ref, slope_ref, rhs_ref, out_ref, conv_ref = refs[tm_count + 3 :]
    is_first = where_ref[2] == 0
    modes, lanes = near_ref.shape[1:]
    height = 2 * block_rows
    half = block_rows // 2 * 3
    weights = mode_weights(where_ref, coeffs_ref, local_s, tm_count)
    for slab in range(half):
        mine = jnp.concatenate([next_own[peer][slab] for peer in range(tm_count)], axis=0)
        theirs = jnp.concatenate([next_other[peer, slab] for peer in range(tm_count)], axis=0)
        after, before = jnp.where(is_first, theirs, mine), jnp.where(is_first, mine, theirs)
        result = modes_of(weights, jnp.concatenate([after, before], axis=1))
        row, c = divmod(slab, 3)
        edges = ((near_ref[slab], result[:, :lanes]), (result[:, lanes:], near_ref[half + slab]))
        for number, (low, high) in enumerate(edges):
            place = number * block_rows + 2 * row
            for at, value, across in ((place, low, high * 0.5), (place + 1, high, low * -0.5)):
                if c == 0:
                    carry_ref[pl.ds(at, modes, stride=height), :] = value
                slope_ref[pl.ds(c * height + at, modes, stride=3 * height), :] = across
                store_projection(rhs_ref, c * height + at, value)


    out_ref[...] = edge_sum(
        where_ref, codes_ref, carry_ref, slope_ref, rhs_ref, inner_ref, conv_ref, group, (tm_count, chips, share, bits)
    )


def edge_sum(where_ref, codes_ref, carry_ref, slope_ref, rhs_ref, inner_ref, conv_ref, group, sizes):
    block, modes = inner_ref.shape[1:]
    lanes = carry_ref.shape[1]
    height = carry_ref.shape[0] // modes

    def one_pair(slot, i, j):
        carry = carry_ref[pl.ds(pl.multiple_of(i * height, 8), height), :]
        slope = slope_ref[pl.ds(pl.multiple_of(j * (3 * height), 8), 3 * height), :]
        rows = [carry * slope[c * height : (c + 1) * height] for c in range(3)]
        conv_ref[pl.ds(pl.multiple_of(slot * (3 * height), 8), 3 * height), :] = jnp.concatenate(rows, axis=0)

    for_pairs_of(where_ref, codes_ref, group, sizes, one_pair)
    return inner_ref[group % inner_ref.shape[0]] + project(conv_ref, rhs_ref, block, 3 * height, lanes)


def edge_kernel(where_ref, codes_ref, carry_ref, slope_ref, rhs_ref, inner_ref, *refs, group, sizes):
    *arrived_refs, out_ref, conv_ref = refs
    total = edge_sum(where_ref, codes_ref, carry_ref, slope_ref, rhs_ref, inner_ref, conv_ref, group, sizes)
    for arrived_ref in arrived_refs:
        total = total + arrived_ref[...]
    out_ref[...] = total


def vmem_limit(mebibytes):
    return pltpu.CompilerParams(vmem_limit_bytes=mebibytes * 2**20)


def in_vmem(array):
    return pltpu.with_memory_space_constraint(array, pltpu.VMEM)


def shards(snapshots, coeffs, pair_table):
    tm_count, space_count = lax.axis_size("tm"), lax.axis_size("space")
    chips = space_count // 2
    t, place = lax.axis_index("tm"), lax.axis_index("space")
    core = lax.rem(place, 2)
    where = jnp.stack([t, lax.div(place, 2), core]).astype(jnp.int32)
    local_s, _, _, rows_y, lanes = snapshots.shape
    modes = coeffs.shape[1]
    block_rows = rows_y // tm_count
    slabs = 3 * block_rows + border_slabs(rows_y, lanes)
    share = pair_table.shape[0] // (tm_count * space_count)
    factor = float(space_count * rows_y * lanes) ** (-0.5)
    bits = modes.bit_length() - 1
    assert modes == 2**bits
    codes = pair_table[:, 0] * modes + pair_table[:, 1]
    smem = pl.BlockSpec(memory_space=pltpu.SMEM)
    vmem = pl.BlockSpec(memory_space=pltpu.VMEM)
    block = tm_count * share
    height = 2 * block_rows
    depth = 3 * height * lanes

    swap = [(2 * chip + c, 2 * chip + 1 - c) for chip in range(chips) for c in range(2)]

    def across(peer):
        return [(i, i ^ peer) for i in range(tm_count)]

    with jax.named_scope("pack"):
        packed = pl.pallas_call(
            functools.partial(pack_kernel, sizes=(local_s, rows_y, tm_count)),
            out_shape=[pltpu.VMEM((slabs, local_s, lanes), F32)] * tm_count
            + [pltpu.VMEM((tm_count, block_rows // 2 * 3, local_s, lanes), F32)],
            in_specs=[smem, pl.BlockSpec(memory_space=pltpu.HBM)],
            out_specs=[vmem] * (tm_count + 1),
            scratch_shapes=[
                pltpu.VMEM((tm_count, slabs, local_s, lanes), F32),
                pltpu.VMEM((3, local_s, rows_y, lanes), F32),
                pltpu.SemaphoreType.DMA((3,)),
            ],
            compiler_params=vmem_limit(16),
        )(where, pltpu.with_memory_space_constraint(snapshots.reshape(local_s, 3, rows_y, lanes), pltpu.HBM))
    with jax.named_scope("to_next_plane"):
        ring = [(place, (place + (1 if place % 2 else -1)) % space_count) for place in range(space_count)]
        across_edge = lax.ppermute(packed[tm_count], "space", ring)
    with jax.named_scope("to_columns"):
        own = [packed[0]] + [lax.ppermute(packed[peer], "tm", across(peer)) for peer in range(1, tm_count)]
    with jax.named_scope("next_to_columns"):
        across_edge, own[:3] = lax.optimization_barrier((across_edge, own[:3]))
        parts = [across_edge[peer] for peer in range(tm_count)]
        parts, own[3:] = lax.optimization_barrier((parts, own[3:]))
        next_own = [parts[0]] + [lax.ppermute(parts[peer], "tm", across(peer)) for peer in range(1, tm_count)]
    with jax.named_scope("to_other_core"):
        other = [lax.ppermute(piece, "space", swap) for piece in own]
    early = chips // 2
    work = [pltpu.VMEM((block * 3 * height, lanes), F32)]
    groups = pltpu.VMEM((early, block, modes), F32)
    with jax.named_scope("inner_terms"):
        near, *inner_tables, early_sums = pl.pallas_call(
            functools.partial(inner_kernel, first_group=early, sizes=(local_s, block_rows, tm_count, chips, share, bits)),
            out_shape=[
                pltpu.VMEM((block_rows * 3, modes, lanes), F32),
                pltpu.VMEM((modes * 3 * height, lanes), F32),
                pltpu.VMEM((modes * 9 * height, lanes), F32),
                pltpu.VMEM((depth, 2 * modes), BF16),
                groups,
            ],
            in_specs=[smem, smem] + [vmem] * (2 * tm_count + 1),
            out_specs=[vmem] * 5,
            scratch_shapes=[pltpu.VMEM((2, slabs, modes, lanes), F32)] + work,
            compiler_params=vmem_limit(24),
            cost_estimate=pl.CostEstimate(flops=12 * 10**9, bytes_accessed=10**7, transcendentals=0),
        )(where, codes, coeffs, *[in_vmem(piece) for piece in (*own, *other)])
    with jax.named_scope("next_to_other_core"):
        next_own, inner_tables = lax.optimization_barrier((next_own, inner_tables))
        next_other = lax.ppermute(jnp.stack(next_own), "space", swap)
    with jax.named_scope("inner_terms"):
        late_sums = pl.pallas_call(
            functools.partial(pairs_kernel, first_group=0, sizes=(tm_count, chips, share, bits)),
            out_shape=groups,
            in_specs=[smem, smem] + [vmem] * 3,
            out_specs=vmem,
            scratch_shapes=work,
            compiler_params=vmem_limit(16),
            cost_estimate=pl.CostEstimate(flops=8 * 10**9, bytes_accessed=10**7, transcendentals=0),
        )(where, codes, *[in_vmem(table) for table in inner_tables])
    with jax.named_scope("edge_terms"):
        *tables, summed = pl.pallas_call(
            functools.partial(
                far_kernel, group=chips - 1, sizes=(local_s, block_rows, tm_count, chips, share, bits)
            ),
            out_shape=[
                pltpu.VMEM((modes * height, lanes), F32),
                pltpu.VMEM((modes * 3 * height, lanes), F32),
                pltpu.VMEM((depth, 2 * modes), BF16),
                pltpu.VMEM((block, modes), F32),
            ],
            in_specs=[smem, smem] + [vmem] * (tm_count + 4),
            out_specs=[vmem] * 4,
            scratch_shapes=work,
            compiler_params=vmem_limit(16),
        )(where, codes, coeffs, *[in_vmem(piece) for piece in (*next_own, next_other, near, early_sums)])
    arrived = []
    for group in reversed(range(chips - 1)):
        with jax.named_scope("sum_over_chips"):
            pairing = [(2 * chip + c, 2 * (chip ^ (group + 1)) + c) for chip in range(chips) for c in range(2)]
            arrived.append(lax.ppermute(summed, "space", pairing))
            if group >= early:
                early_sums, _ = lax.optimization_barrier((early_sums, summed))
            else:
                late_sums, _ = lax.optimization_barrier((late_sums, summed))
        with jax.named_scope("edge_terms"):
            parts = arrived[:-1] if group == 0 else []
            summed = pl.pallas_call(
                functools.partial(edge_kernel, group=group, sizes=(tm_count, chips, share, bits)),
                out_shape=pltpu.VMEM((block, modes), F32),
                in_specs=[smem, smem] + [vmem] * (4 + len(parts)),
                out_specs=vmem,
                scratch_shapes=work,
                compiler_params=vmem_limit(16),
                cost_estimate=pl.CostEstimate(flops=10**8, bytes_accessed=10**5, transcendentals=0),
            )(
                where,
                codes,
                *[in_vmem(table) for table in (*tables, early_sums if group >= early else late_sums, *parts)],
            )
    with jax.named_scope("sum_over_chips"):
        shares = (summed + arrived[-1]).reshape(tm_count, share, modes)
    with jax.named_scope("sum_over_columns"):
        result = shares[0]
        for peer in range(1, tm_count):
            result = result + lax.ppermute(shares[peer], "tm", across(peer))
        return result * factor


def solution(mesh):
    placed = (P("tm", None, "space", None, None), P(), P())
    return jax.shard_map(
        shards, mesh=mesh, in_specs=placed, out_specs=P(("tm", "space"), None), check_vma=False
    )
```

```python
import functools

import jax
import jax.numpy as jnp
from jax import lax
from jax.experimental import pallas as pl
from jax.experimental.pallas import tpu as pltpu
from jax.sharding import PartitionSpec as P

F32 = jnp.float32
BF16 = jnp.bfloat16


def place_of_device():
    place = lax.axis_index("space")
    return lax.axis_index("tm"), lax.shift_right_logical(place, 1), jnp.bitwise_and(place, 1)


def split_high_low(values):
    high = values.astype(BF16)
    low = (values - high.astype(F32)).astype(BF16)
    return high, low


def border_lane(rows_y, lanes, c):
    per_slab = lanes // (2 * rows_y)
    return c // per_slab, c % per_slab * 2 * rows_y


def border_slabs(rows_y, lanes):
    return border_lane(rows_y, lanes, 2)[0] + 1


def exchange_blocks(rows, lane, width, lanes):
    rows = list(rows)
    step = len(rows) // 2
    while step:
        keeps = jnp.bitwise_and(lane, step * width) == 0
        for low in range(len(rows)):
            if low & step == 0:
                first, second = rows[low], rows[low + step]
                rows[low] = jnp.where(keeps, first, pltpu.roll(second, step * width, 1))
                rows[low + step] = jnp.where(keeps, pltpu.roll(first, lanes - step * width, 1), second)
        step //= 2
    return rows


def pack_kernel(field_ref, *refs, sizes):
    *out_refs, sorted_ref, held_ref, sems = refs
    local_s, rows_y, tm_count = sizes
    lanes = field_ref.shape[3]
    copies = [pltpu.make_async_copy(field_ref.at[:, c], held_ref.at[c], sems.at[c]) for c in range(3)]
    for copy in copies:
        copy.start()
    rows_ref = held_ref.reshape(3 * local_s * rows_y, lanes)
    t, _, core = place_of_device()
    width, groups = lanes // tm_count, rows_y // tm_count
    lane = lax.broadcasted_iota(jnp.int32, (local_s, lanes), 1)
    borders = [[jnp.zeros((local_s, lanes), F32) for _ in range(tm_count)] for _ in range(border_slabs(rows_y, lanes))]
    for c in range(3):
        slab, first_lane = border_lane(rows_y, lanes, c)
        copies[c].wait()

        def one_group(g, border, c=c, first_lane=first_lane):
            border = list(border)
            rows = []
            for q in range(tm_count):
                y = q * groups + g
                row = rows_ref[pl.ds(c * local_s * rows_y + y, local_s, stride=rows_y), :]
                rows.append(row)
                for side in range(2):
                    shift = first_lane + side * (rows_y - width - 1) + y
                    moved = pltpu.roll(row, jnp.bitwise_and(shift, lanes - 1), 1)
                    for block in range(tm_count):
                        column = (block + 1) * width if side else block * width - 1
                        is_here = lane == jnp.bitwise_and(shift + column, lanes - 1)
                        border[block] = jnp.where(is_here, moved, border[block])
            for block, main in enumerate(exchange_blocks(rows, lane, width, lanes)):
                sorted_ref[block, g * 3 + c] = main
            return tuple(border)

        borders[slab] = lax.fori_loop(0, groups, one_group, tuple(borders[slab]))
    half = groups // 2 * 3
    for slab, border in enumerate(borders):
        for block in range(tm_count):
            sorted_ref[block, groups * 3 + slab] = border[block]
    for peer in range(tm_count):
        block = jnp.bitwise_xor(t, peer)
        out_refs[peer][...] = sorted_ref[block]
        out_refs[tm_count][peer] = sorted_ref[block, pl.ds(core * half, half)]


def mode_weights(coeffs_ref, local_s, tm_count):
    t, _, _ = place_of_device()
    ordered = jnp.concatenate(
        [
            coeffs_ref[pl.ds(pl.multiple_of(jnp.bitwise_xor(t, peer) * local_s, 8), local_s), :]
            for peer in range(tm_count)
        ],
        axis=0,
    )
    high, low = split_high_low(ordered.T)
    return jnp.concatenate([high, low, high, low], axis=1)


def modes_of(weights, slab):
    high, low = split_high_low(slab)
    return jnp.dot(weights, jnp.concatenate([high, high, low, low], axis=0), preferred_element_type=F32)


def store_projection(rhs_ref, place, mode_slab):
    high, low = split_high_low(mode_slab.T)
    modes, lanes = mode_slab.shape
    rhs_ref[place * lanes : (place + 1) * lanes, 0:modes] = high
    rhs_ref[place * lanes : (place + 1) * lanes, modes : 2 * modes] = low


def project(conv_ref, rhs_ref, block, places, lanes):
    both = None
    for place in range(0, places, 2):
        highs, lows = zip(
            *(split_high_low(conv_ref[pl.ds(place + k, block, stride=places), :]) for k in range(2))
        )
        lhs = jnp.concatenate([jnp.concatenate(highs, axis=1), jnp.concatenate(lows, axis=1)], axis=0)
        part = jnp.dot(lhs, rhs_ref[place * lanes : (place + 2) * lanes, :], preferred_element_type=F32)
        both = part if both is None else both + part
    modes = both.shape[1] // 2
    return (both[:block, :modes] + both[:block, modes:]) + (both[block:, :modes] + both[block:, modes:])


def for_pairs_of(codes_ref, peer, sizes, one_pair):
    chips, share, bits = sizes
    t, chip, core = place_of_device()
    first_chip = jnp.bitwise_xor(t, peer) * chips

    def one_share(ahead, _):
        base = ((first_chip + jnp.bitwise_xor(chip, ahead)) * 2 + core) * share

        def one(q, _):
            code = codes_ref[base + q]
            one_pair(ahead * share + q, lax.shift_right_logical(code, bits), jnp.bitwise_and(code, 2**bits - 1))
            return 0

        return lax.fori_loop(0, share, one, 0, unroll=32)

    lax.fori_loop(0, chips, one_share, 0)


def copy_of_codes(codes_ref, held_codes_ref, sem):
    copy = pltpu.make_async_copy(codes_ref, held_codes_ref, sem)
    copy.start()
    return copy


def inner_kernel(codes_ref, coeffs_ref, *refs, first_peer, sizes):
    local_s, block_rows, tm_count, chips, share, bits = sizes
    own, other = refs[:tm_count], refs[tm_count : 2 * tm_count]
    near_ref, carry_ref, slope_ref, rhs_ref, out_ref, conv_ref, slab_ref, held_codes_ref, sem = refs[2 * tm_count :]
    codes = copy_of_codes(codes_ref, held_codes_ref, sem)
    t, _, core = place_of_device()
    modes, lanes = coeffs_ref.shape[1], own[0].shape[2]
    height = 2 * block_rows
    weights = mode_weights(coeffs_ref, local_s, tm_count)

    def one_slab(index, _):
        own_slab = jnp.concatenate([piece[index] for piece in own], axis=0)
        other_slab = jnp.concatenate([piece[index] for piece in other], axis=0)
        is_first = core == 0
        both = jnp.concatenate(
            [jnp.where(is_first, own_slab, other_slab), jnp.where(is_first, other_slab, own_slab)], axis=1
        )
        result = modes_of(weights, both)
        slab_ref[0, index] = result[:, :lanes]
        slab_ref[1, index] = result[:, lanes:]
        return 0

    slabs = own[0].shape[0]
    lax.fori_loop(0, slabs, one_slab, 0, unroll=True)
    width, rows_y = lanes // tm_count, block_rows * tm_count
    lane = lax.broadcasted_iota(jnp.int32, (1, lanes), 1)
    part, column = lax.div(lane, width), lax.rem(lane, width)
    has_border = jnp.where(column == 0, -0.5, jnp.where(column == width - 1, 0.5, 0.0))
    border_of = jnp.where(column == 0, 0, rows_y) + t * width - 1 + part * block_rows
    border_lanes = lax.broadcasted_iota(jnp.int32, (2 * lanes, lanes), 0)
    border_lanes = jnp.where(border_lanes >= lanes, border_lanes - lanes, border_lanes)
    borders = []
    for slab in range(3 * block_rows, slabs):
        both = jnp.concatenate([slab_ref[0, slab], slab_ref[1, slab]], axis=0)
        borders.append(jnp.concatenate(split_high_low(both), axis=1))
    for c in range(3):
        slab, first_lane = border_lane(rows_y, lanes, c)
        for row in range(block_rows):
            center = row * 3 + c
            if row % 2 == 0:
                picks = [
                    jnp.where(
                        border_lanes == jnp.bitwise_and(border_of + (first_lane + row + k), lanes - 1), has_border, 0.0
                    ).astype(BF16)
                    for k in range(2)
                ]
                border = jnp.dot(borders[slab], jnp.concatenate(picks, axis=1), preferred_element_type=F32)
            for plane in range(2):
                place = plane * block_rows + row
                value = slab_ref[plane, center]
                stream = slab_ref[1 - plane, center] * (0.5 if plane == 0 else -0.5)
                if row + 1 < block_rows:
                    above = slab_ref[plane, center + 3]
                else:
                    above = pltpu.roll(slab_ref[plane, c], lanes - width, 1)
                    above = jnp.where(lane < lanes - width, above, 0.0)
                if row > 0:
                    below = slab_ref[plane, center - 3]
                else:
                    below = pltpu.roll(slab_ref[plane, 3 * (block_rows - 1) + c], width, 1)
                    below = jnp.where(lane >= width, below, 0.0)
                normal = (above - below) * 0.5
                after = jnp.where(column < width - 1, pltpu.roll(value, lanes - 1, 1), 0.0)
                before = jnp.where(column > 0, pltpu.roll(value, 1, 1), 0.0)
                span = (after - before) * 0.5 + border[plane * modes : (plane + 1) * modes, row % 2 * lanes : (row % 2 + 1) * lanes]
                carry_ref[pl.ds(c * height + place, modes, stride=3 * height), :] = value
                for d, slope in enumerate((stream, normal, span)):
                    slope_ref[pl.ds((d * 3 + c) * height + place, modes, stride=9 * height), :] = slope
                store_projection(rhs_ref, c * height + place, value)
                if (plane == 1) == (row < block_rows // 2):
                    near_ref[center] = value

    codes.wait()

    def one_peer(number, _):
        pick_inner(held_codes_ref, carry_ref, slope_ref, conv_ref, first_peer + number, (chips, share, bits))
        out_ref[number] = project(conv_ref, rhs_ref, chips * share, 3 * height, lanes)
        return 0

    lax.fori_loop(0, out_ref.shape[0], one_peer, 0)
    pick_inner(held_codes_ref, carry_ref, slope_ref, conv_ref, 0, (chips, share, bits))


def pick_inner(codes_ref, carry_ref, slope_ref, conv_ref, peer, sizes):
    places = conv_ref.shape[0] // (sizes[0] * sizes[1])
    height = places // 3

    def one_pair(slot, i, j):
        carry = carry_ref[pl.ds(pl.multiple_of(i * places, 8), places), :]
        slope = slope_ref[pl.ds(pl.multiple_of(j * (3 * places), 8), 3 * places), :]
        rows = [
            sum(
                carry[d * height : (d + 1) * height] * slope[(d * 3 + c) * height : (d * 3 + c + 1) * height]
                for d in range(3)
            )
            for c in range(3)
        ]
        conv_ref[pl.ds(pl.multiple_of(slot * places, 8), places), :] = jnp.concatenate(rows, axis=0)

    for_pairs_of(codes_ref, peer, sizes, one_pair)


def rest_kernel(
    codes_ref, carry_ref, slope_ref, rhs_ref, picked_ref, out_ref, conv_ref, held_codes_ref, sem, *, sizes
):
    chips, share, _ = sizes
    codes = copy_of_codes(codes_ref, held_codes_ref, sem)
    block, lanes = chips * share, conv_ref.shape[1]
    places = conv_ref.shape[0] // block
    out_ref[0] = project(picked_ref, rhs_ref, block, places, lanes)
    codes.wait()

    def one_peer(peer, _):
        pick_inner(held_codes_ref, carry_ref, slope_ref, conv_ref, peer, sizes)
        out_ref[peer] = project(conv_ref, rhs_ref, block, places, lanes)
        return 0

    lax.fori_loop(1, out_ref.shape[0], one_peer, 0)


def far_kernel(codes_ref, coeffs_ref, *refs, peer, sizes):
    local_s, block_rows, tm_count, chips, share, bits = sizes
    next_own, next_other, near_ref, inner_ref = refs[:tm_count], *refs[tm_count : tm_count + 3]
    carry_ref, slope_ref, rhs_ref, out_ref, conv_ref, held_codes_ref, sem = refs[tm_count + 3 :]
    codes = copy_of_codes(codes_ref, held_codes_ref, sem)
    _, _, core = place_of_device()
    is_first = core == 0
    modes, lanes = near_ref.shape[1:]
    height = 2 * block_rows
    half = block_rows // 2 * 3
    weights = mode_weights(coeffs_ref, local_s, tm_count)
    for slab in range(half):
        mine = jnp.concatenate([next_own[peer][slab] for peer in range(tm_count)], axis=0)
        theirs = jnp.concatenate([next_other[peer, slab] for peer in range(tm_count)], axis=0)
        after, before = jnp.where(is_first, theirs, mine), jnp.where(is_first, mine, theirs)
        result = modes_of(weights, jnp.concatenate([after, before], axis=1))
        row, c = divmod(slab, 3)
        edges = ((near_ref[slab], result[:, :lanes]), (result[:, lanes:], near_ref[half + slab]))
        for number, (low, high) in enumerate(edges):
            place = number * block_rows + 2 * row
            for at, value, across in ((place, low, high * 0.5), (place + 1, high, low * -0.5)):
                if c == 0:
                    carry_ref[pl.ds(at, modes, stride=height), :] = value
                slope_ref[pl.ds(c * height + at, modes, stride=3 * height), :] = across
                store_projection(rhs_ref, c * height + at, value)


    codes.wait()
    pick_edge(held_codes_ref, carry_ref, slope_ref, conv_ref, peer, (chips, share, bits))
    out_ref[...] = edge_sum(conv_ref, rhs_ref, inner_ref, peer)
    pick_edge(held_codes_ref, carry_ref, slope_ref, conv_ref, peer - 1, (chips, share, bits))


def pick_edge(codes_ref, carry_ref, slope_ref, conv_ref, peer, sizes):
    places = conv_ref.shape[0] // (sizes[0] * sizes[1])
    height = places // 3

    def one_pair(slot, i, j):
        carry = carry_ref[pl.ds(pl.multiple_of(i * height, 8), height), :]
        slope = slope_ref[pl.ds(pl.multiple_of(j * places, 8), places), :]
        rows = [carry * slope[c * height : (c + 1) * height] for c in range(3)]
        conv_ref[pl.ds(pl.multiple_of(slot * places, 8), places), :] = jnp.concatenate(rows, axis=0)

    for_pairs_of(codes_ref, peer, sizes, one_pair)


def edge_sum(picked_ref, rhs_ref, inner_ref, peer):
    block = inner_ref.shape[1]
    places = picked_ref.shape[0] // block
    return inner_ref[peer % inner_ref.shape[0]] + project(picked_ref, rhs_ref, block, places, picked_ref.shape[1])


def edge_kernel(
    codes_ref, carry_ref, slope_ref, rhs_ref, inner_ref, picked_ref, out_ref, conv_ref, held_codes_ref, sem, *,
    peer, sizes
):
    codes = copy_of_codes(codes_ref, held_codes_ref, sem)
    out_ref[...] = edge_sum(picked_ref, rhs_ref, inner_ref, peer)
    codes.wait()
    pick_edge(held_codes_ref, carry_ref, slope_ref, conv_ref, peer - 1, sizes)


def last_edge_kernel(rhs_ref, inner_ref, picked_ref, *refs):
    *arrived_refs, out_ref = refs
    total = edge_sum(picked_ref, rhs_ref, inner_ref, 0)
    for arrived_ref in arrived_refs:
        total = total + arrived_ref[...]
    out_ref[...] = total


def vmem_limit(mebibytes):
    return pltpu.CompilerParams(vmem_limit_bytes=mebibytes * 2**20)


def in_vmem(array):
    return pltpu.with_memory_space_constraint(array, pltpu.VMEM)


def shards(snapshots, coeffs, pair_table):
    tm_count, space_count = lax.axis_size("tm"), lax.axis_size("space")
    chips = space_count // 2
    local_s, _, _, rows_y, lanes = snapshots.shape
    modes = coeffs.shape[1]
    block_rows = rows_y // tm_count
    slabs = 3 * block_rows + border_slabs(rows_y, lanes)
    share = pair_table.shape[0] // (tm_count * space_count)
    factor = float(space_count * rows_y * lanes) ** (-0.5)
    bits = modes.bit_length() - 1
    assert modes == 2**bits
    codes = in_vmem(pair_table[:, 0] * modes + pair_table[:, 1])
    vmem = pl.BlockSpec(memory_space=pltpu.VMEM)
    block = chips * share
    height = 2 * block_rows
    depth = 3 * height * lanes

    swap = [(2 * chip + c, 2 * chip + 1 - c) for chip in range(chips) for c in range(2)]

    def across(peer):
        return [(i, i ^ peer) for i in range(tm_count)]

    with jax.named_scope("pack"):
        packed = pl.pallas_call(
            functools.partial(pack_kernel, sizes=(local_s, rows_y, tm_count)),
            out_shape=[pltpu.VMEM((slabs, local_s, lanes), F32)] * tm_count
            + [pltpu.VMEM((tm_count, block_rows // 2 * 3, local_s, lanes), F32)],
            in_specs=[pl.BlockSpec(memory_space=pltpu.HBM)],
            out_specs=[vmem] * (tm_count + 1),
            scratch_shapes=[
                pltpu.VMEM((tm_count, slabs, local_s, lanes), F32),
                pltpu.VMEM((3, local_s, rows_y, lanes), F32),
                pltpu.SemaphoreType.DMA((3,)),
            ],
            compiler_params=vmem_limit(16),
        )(pltpu.with_memory_space_constraint(snapshots.reshape(local_s, 3, rows_y, lanes), pltpu.HBM))
    with jax.named_scope("to_next_plane"):
        ring = [(place, (place + (1 if place % 2 else -1)) % space_count) for place in range(space_count)]
        across_edge = lax.ppermute(packed[tm_count], "space", ring)
    with jax.named_scope("to_columns"):
        own = [packed[0]] + [lax.ppermute(packed[peer], "tm", across(peer)) for peer in range(1, tm_count)]
    with jax.named_scope("next_to_columns"):
        across_edge, own[:3] = lax.optimization_barrier((across_edge, own[:3]))
        parts = [across_edge[peer] for peer in range(tm_count)]
        parts, own[3:] = lax.optimization_barrier((parts, own[3:]))
        next_own = [parts[0]] + [lax.ppermute(parts[peer], "tm", across(peer)) for peer in range(1, tm_count)]
    with jax.named_scope("to_other_core"):
        other = [lax.ppermute(piece, "space", swap) for piece in own]
    early = tm_count // 2
    picked = pltpu.VMEM((block * 3 * height, lanes), F32)
    held_codes = [pltpu.SMEM(codes.shape, jnp.int32), pltpu.SemaphoreType.DMA]
    groups = pltpu.VMEM((early, block, modes), F32)
    with jax.named_scope("inner_terms"):
        near, *inner_tables, early_sums, first_picked = pl.pallas_call(
            functools.partial(inner_kernel, first_peer=early, sizes=(local_s, block_rows, tm_count, chips, share, bits)),
            out_shape=[
                pltpu.VMEM((block_rows * 3, modes, lanes), F32),
                pltpu.VMEM((modes * 3 * height, lanes), F32),
                pltpu.VMEM((modes * 9 * height, lanes), F32),
                pltpu.VMEM((depth, 2 * modes), BF16),
                groups,
                picked,
            ],
            in_specs=[vmem] * (2 * tm_count + 2),
            out_specs=[vmem] * 6,
            scratch_shapes=[pltpu.VMEM((2, slabs, modes, lanes), F32)] + held_codes,
            compiler_params=vmem_limit(24),
            cost_estimate=pl.CostEstimate(flops=12 * 10**9, bytes_accessed=10**7, transcendentals=0),
        )(codes, coeffs, *[in_vmem(piece) for piece in (*own, *other)])
    with jax.named_scope("next_to_other_core"):
        next_own, inner_tables = lax.optimization_barrier((next_own, inner_tables))
        next_other = lax.ppermute(jnp.stack(next_own), "space", swap)
    with jax.named_scope("inner_terms"):
        late_sums = pl.pallas_call(
            functools.partial(rest_kernel, sizes=(chips, share, bits)),
            out_shape=groups,
            in_specs=[vmem] * 5,
            out_specs=vmem,
            scratch_shapes=[picked] + held_codes,
            compiler_params=vmem_limit(16),
            cost_estimate=pl.CostEstimate(flops=8 * 10**9, bytes_accessed=10**7, transcendentals=0),
        )(codes, *[in_vmem(table) for table in (*inner_tables, first_picked)])
    with jax.named_scope("edge_terms"):
        *tables, summed, next_picked = pl.pallas_call(
            functools.partial(
                far_kernel, peer=tm_count - 1, sizes=(local_s, block_rows, tm_count, chips, share, bits)
            ),
            out_shape=[
                pltpu.VMEM((modes * height, lanes), F32),
                pltpu.VMEM((modes * 3 * height, lanes), F32),
                pltpu.VMEM((depth, 2 * modes), BF16),
                pltpu.VMEM((block, modes), F32),
                picked,
            ],
            in_specs=[vmem] * (tm_count + 5),
            out_specs=[vmem] * 5,
            scratch_shapes=held_codes,
            compiler_params=vmem_limit(16),
        )(codes, coeffs, *[in_vmem(piece) for piece in (*next_own, next_other, near, early_sums)])
    arrived = []
    for peer in reversed(range(tm_count - 1)):
        with jax.named_scope("sum_over_columns"):
            arrived.append(lax.ppermute(summed, "tm", across(peer + 1)))
            if peer >= early:
                early_sums, _ = lax.optimization_barrier((early_sums, summed))
            else:
                late_sums, _ = lax.optimization_barrier((late_sums, summed))
        with jax.named_scope("edge_terms"):
            inner_sums = early_sums if peer >= early else late_sums
            if peer:
                summed, next_picked = pl.pallas_call(
                    functools.partial(edge_kernel, peer=peer, sizes=(chips, share, bits)),
                    out_shape=[pltpu.VMEM((block, modes), F32), picked],
                    in_specs=[vmem] * 6,
                    out_specs=[vmem] * 2,
                    scratch_shapes=held_codes,
                    compiler_params=vmem_limit(16),
                    cost_estimate=pl.CostEstimate(flops=10**8, bytes_accessed=10**5, transcendentals=0),
                )(codes, *[in_vmem(table) for table in (*tables, inner_sums, next_picked)])
            else:
                summed = pl.pallas_call(
                    last_edge_kernel,
                    out_shape=pltpu.VMEM((block, modes), F32),
                    in_specs=[vmem] * (2 + len(arrived)),
                    out_specs=vmem,
                    compiler_params=vmem_limit(16),
                    cost_estimate=pl.CostEstimate(flops=10**8, bytes_accessed=10**5, transcendentals=0),
                )(*[in_vmem(table) for table in (tables[2], inner_sums, next_picked, *arrived[:-1])])
    with jax.named_scope("sum_over_columns"):
        summed = summed + arrived[-1]
    with jax.named_scope("sum_over_chips"):
        shares = summed.reshape(chips, share, modes)
        result = shares[0]
        for step in range(1, chips):
            pairing = [(2 * chip + c, 2 * (chip ^ step) + c) for chip in range(chips) for c in range(2)]
            result = result + lax.ppermute(shares[step], "space", pairing)
        return result * factor


def solution(mesh):
    placed = (P("tm", None, "space", None, None), P(), P())
    return jax.shard_map(
        shards, mesh=mesh, in_specs=placed, out_specs=P(("tm", "space"), None), check_vma=False
    )
```

```python
import functools

import jax
import jax.numpy as jnp
from jax import lax
from jax.experimental import pallas as pl
from jax.experimental.pallas import tpu as pltpu
from jax.sharding import PartitionSpec as P

F32 = jnp.float32
BF16 = jnp.bfloat16


def place_of_device():
    place = lax.axis_index("space")
    return lax.axis_index("tm"), lax.shift_right_logical(place, 1), jnp.bitwise_and(place, 1)


def split_high_low(values):
    high = values.astype(BF16)
    low = (values - high.astype(F32)).astype(BF16)
    return high, low


def border_lane(rows_y, lanes, c):
    per_slab = lanes // (2 * rows_y)
    return c // per_slab, c % per_slab * 2 * rows_y


def border_slabs(rows_y, lanes):
    return border_lane(rows_y, lanes, 2)[0] + 1


def exchange_blocks(rows, lane, width, lanes):
    rows = list(rows)
    step = len(rows) // 2
    while step:
        keeps = jnp.bitwise_and(lane, step * width) == 0
        for low in range(len(rows)):
            if low & step == 0:
                first, second = rows[low], rows[low + step]
                rows[low] = jnp.where(keeps, first, pltpu.roll(second, step * width, 1))
                rows[low + step] = jnp.where(keeps, pltpu.roll(first, lanes - step * width, 1), second)
        step //= 2
    return rows


def pack_kernel(field_ref, pairs_ref, coeffs_ref, *refs, sizes):
    *out_refs, codes_ref, held_coeffs_ref, sorted_ref, held_ref, held_pairs_ref, sems = refs
    local_s, rows_y, tm_count = sizes
    lanes = field_ref.shape[3]
    copies = [pltpu.make_async_copy(field_ref.at[:, c], held_ref.at[c], sems.at[c]) for c in range(3)]
    copies.append(pltpu.make_async_copy(pairs_ref, held_pairs_ref, sems.at[3]))
    copies.append(pltpu.make_async_copy(coeffs_ref, held_coeffs_ref, sems.at[4]))
    for copy in copies:
        copy.start()
    rows_ref = held_ref.reshape(3 * local_s * rows_y, lanes)
    t, _, core = place_of_device()
    width, groups = lanes // tm_count, rows_y // tm_count
    lane = lax.broadcasted_iota(jnp.int32, (local_s, lanes), 1)
    borders = [[jnp.zeros((local_s, lanes), F32) for _ in range(tm_count)] for _ in range(border_slabs(rows_y, lanes))]
    for c in range(3):
        slab, first_lane = border_lane(rows_y, lanes, c)
        copies[c].wait()

        def one_group(g, border, c=c, first_lane=first_lane):
            border = list(border)
            rows = []
            for q in range(tm_count):
                y = q * groups + g
                row = rows_ref[pl.ds(c * local_s * rows_y + y, local_s, stride=rows_y), :]
                rows.append(row)
                for side in range(2):
                    shift = first_lane + side * (rows_y - width - 1) + y
                    moved = pltpu.roll(row, jnp.bitwise_and(shift, lanes - 1), 1)
                    for block in range(tm_count):
                        column = (block + 1) * width if side else block * width - 1
                        is_here = lane == jnp.bitwise_and(shift + column, lanes - 1)
                        border[block] = jnp.where(is_here, moved, border[block])
            for block, main in enumerate(exchange_blocks(rows, lane, width, lanes)):
                sorted_ref[block, g * 3 + c] = main
            return tuple(border)

        borders[slab] = lax.fori_loop(0, groups, one_group, tuple(borders[slab]))
    half = groups // 2 * 3
    for slab, border in enumerate(borders):
        for block in range(tm_count):
            sorted_ref[block, groups * 3 + slab] = border[block]
    for peer in range(tm_count):
        block = jnp.bitwise_xor(t, peer)
        out_refs[peer][...] = sorted_ref[block]
        out_refs[tm_count][peer] = sorted_ref[block, pl.ds(core * half, half)]
    copies[3].wait()
    copies[4].wait()
    for row in range(codes_ref.shape[0]):
        here = pl.ds(row * lanes, lanes)
        first, second = held_pairs_ref[0:1, here], held_pairs_ref[1:2, here]
        codes_ref[row : row + 1, :] = first * held_coeffs_ref.shape[1] + second


def mode_weights(coeffs_ref, local_s, tm_count):
    t, _, _ = place_of_device()
    ordered = jnp.concatenate(
        [
            coeffs_ref[pl.ds(pl.multiple_of(jnp.bitwise_xor(t, peer) * local_s, 8), local_s), :]
            for peer in range(tm_count)
        ],
        axis=0,
    )
    high, low = split_high_low(ordered.T)
    return jnp.concatenate([high, low, high, low], axis=1)


def modes_of(weights, slab):
    high, low = split_high_low(slab)
    return jnp.dot(weights, jnp.concatenate([high, high, low, low], axis=0), preferred_element_type=F32)


def store_projection(rhs_ref, place, mode_slab):
    high, low = split_high_low(mode_slab.T)
    modes, lanes = mode_slab.shape
    rhs_ref[place * lanes : (place + 1) * lanes, 0:modes] = high
    rhs_ref[place * lanes : (place + 1) * lanes, modes : 2 * modes] = low


def project(conv_ref, rhs_ref, block, places, lanes):
    both = None
    for place in range(0, places, 2):
        highs, lows = zip(
            *(split_high_low(conv_ref[pl.ds(place + k, block, stride=places), :]) for k in range(2))
        )
        lhs = jnp.concatenate([jnp.concatenate(highs, axis=1), jnp.concatenate(lows, axis=1)], axis=0)
        part = jnp.dot(lhs, rhs_ref[place * lanes : (place + 2) * lanes, :], preferred_element_type=F32)
        both = part if both is None else both + part
    modes = both.shape[1] // 2
    return (both[:block, :modes] + both[:block, modes:]) + (both[block:, :modes] + both[block:, modes:])


def for_pairs_of(codes_ref, peer, sizes, one_pair):
    chips, share, bits = sizes
    t, chip, core = place_of_device()
    first_chip = jnp.bitwise_xor(t, peer) * chips
    assert codes_ref.shape[1] % share == 0

    def one_share(ahead, _):
        base = ((first_chip + jnp.bitwise_xor(chip, ahead)) * 2 + core) * share
        row, first = lax.div(base, codes_ref.shape[1]), lax.rem(base, codes_ref.shape[1])

        def one(q, _):
            code = codes_ref[row, first + q]
            one_pair(ahead * share + q, lax.shift_right_logical(code, bits), jnp.bitwise_and(code, 2**bits - 1))
            return 0

        return lax.fori_loop(0, share, one, 0, unroll=32)

    lax.fori_loop(0, chips, one_share, 0)


def copy_of_codes(codes_ref, held_codes_ref, sem):
    copy = pltpu.make_async_copy(codes_ref, held_codes_ref, sem)
    copy.start()
    return copy


def inner_kernel(codes_ref, coeffs_ref, *refs, first_peer, sizes):
    local_s, block_rows, tm_count, chips, share, bits = sizes
    own, other = refs[:tm_count], refs[tm_count : 2 * tm_count]
    near_ref, carry_ref, slope_ref, rhs_ref, out_ref, conv_ref, slab_ref, held_codes_ref, sem = refs[2 * tm_count :]
    codes = copy_of_codes(codes_ref, held_codes_ref, sem)
    t, _, core = place_of_device()
    modes, lanes = coeffs_ref.shape[1], own[0].shape[2]
    height = 2 * block_rows
    weights = mode_weights(coeffs_ref, local_s, tm_count)

    def one_slab(index, _):
        own_slab = jnp.concatenate([piece[index] for piece in own], axis=0)
        other_slab = jnp.concatenate([piece[index] for piece in other], axis=0)
        is_first = core == 0
        both = jnp.concatenate(
            [jnp.where(is_first, own_slab, other_slab), jnp.where(is_first, other_slab, own_slab)], axis=1
        )
        result = modes_of(weights, both)
        slab_ref[0, index] = result[:, :lanes]
        slab_ref[1, index] = result[:, lanes:]
        return 0

    slabs = own[0].shape[0]
    lax.fori_loop(0, slabs, one_slab, 0, unroll=True)
    width, rows_y = lanes // tm_count, block_rows * tm_count
    lane = lax.broadcasted_iota(jnp.int32, (1, lanes), 1)
    part, column = lax.div(lane, width), lax.rem(lane, width)
    has_border = jnp.where(column == 0, -0.5, jnp.where(column == width - 1, 0.5, 0.0))
    border_of = jnp.where(column == 0, 0, rows_y) + t * width - 1 + part * block_rows
    border_lanes = lax.broadcasted_iota(jnp.int32, (2 * lanes, lanes), 0)
    border_lanes = jnp.where(border_lanes >= lanes, border_lanes - lanes, border_lanes)
    borders = []
    for slab in range(3 * block_rows, slabs):
        both = jnp.concatenate([slab_ref[0, slab], slab_ref[1, slab]], axis=0)
        borders.append(jnp.concatenate(split_high_low(both), axis=1))
    for c in range(3):
        slab, first_lane = border_lane(rows_y, lanes, c)
        for row in range(block_rows):
            center = row * 3 + c
            if row % 2 == 0:
                picks = [
                    jnp.where(
                        border_lanes == jnp.bitwise_and(border_of + (first_lane + row + k), lanes - 1), has_border, 0.0
                    ).astype(BF16)
                    for k in range(2)
                ]
                border = jnp.dot(borders[slab], jnp.concatenate(picks, axis=1), preferred_element_type=F32)
            for plane in range(2):
                place = plane * block_rows + row
                value = slab_ref[plane, center]
                stream = slab_ref[1 - plane, center] * (0.5 if plane == 0 else -0.5)
                if row + 1 < block_rows:
                    above = slab_ref[plane, center + 3]
                else:
                    above = pltpu.roll(slab_ref[plane, c], lanes - width, 1)
                    above = jnp.where(lane < lanes - width, above, 0.0)
                if row > 0:
                    below = slab_ref[plane, center - 3]
                else:
                    below = pltpu.roll(slab_ref[plane, 3 * (block_rows - 1) + c], width, 1)
                    below = jnp.where(lane >= width, below, 0.0)
                normal = (above - below) * 0.5
                after = jnp.where(column < width - 1, pltpu.roll(value, lanes - 1, 1), 0.0)
                before = jnp.where(column > 0, pltpu.roll(value, 1, 1), 0.0)
                span = (after - before) * 0.5 + border[plane * modes : (plane + 1) * modes, row % 2 * lanes : (row % 2 + 1) * lanes]
                carry_ref[pl.ds(c * height + place, modes, stride=3 * height), :] = value
                for d, slope in enumerate((stream, normal, span)):
                    slope_ref[pl.ds((d * 3 + c) * height + place, modes, stride=9 * height), :] = slope
                store_projection(rhs_ref, c * height + place, value)
                if (plane == 1) == (row < block_rows // 2):
                    near_ref[center] = value

    codes.wait()

    pick_inner(held_codes_ref, carry_ref, slope_ref, conv_ref, first_peer, (chips, share, bits))

    def one_peer(number, _):
        out_ref[number] = project(conv_ref, rhs_ref, chips * share, 3 * height, lanes)
        following = lax.rem(first_peer + number + 1, tm_count)
        pick_inner(held_codes_ref, carry_ref, slope_ref, conv_ref, following, (chips, share, bits))
        return 0

    lax.fori_loop(0, out_ref.shape[0], one_peer, 0)


def pick_inner(codes_ref, carry_ref, slope_ref, conv_ref, peer, sizes):
    places = conv_ref.shape[0] // (sizes[0] * sizes[1])
    height = places // 3

    def one_pair(slot, i, j):
        carry = carry_ref[pl.ds(pl.multiple_of(i * places, 8), places), :]
        slope = slope_ref[pl.ds(pl.multiple_of(j * (3 * places), 8), 3 * places), :]
        rows = [
            sum(
                carry[d * height : (d + 1) * height] * slope[(d * 3 + c) * height : (d * 3 + c + 1) * height]
                for d in range(3)
            )
            for c in range(3)
        ]
        conv_ref[pl.ds(pl.multiple_of(slot * places, 8), places), :] = jnp.concatenate(rows, axis=0)

    for_pairs_of(codes_ref, peer, sizes, one_pair)


def rest_kernel(
    codes_ref, carry_ref, slope_ref, rhs_ref, picked_ref, out_ref, conv_ref, held_codes_ref, sem, *, sizes
):
    del picked_ref
    chips, share, _ = sizes
    codes = copy_of_codes(codes_ref, held_codes_ref, sem)
    block, lanes = chips * share, conv_ref.shape[1]
    places = conv_ref.shape[0] // block

    def one_peer(peer, _):
        out_ref[peer] = project(conv_ref, rhs_ref, block, places, lanes)

        @pl.when(peer == 0)
        def _():
            codes.wait()

        @pl.when(peer + 1 < out_ref.shape[0])
        def _():
            pick_inner(held_codes_ref, carry_ref, slope_ref, conv_ref, peer + 1, sizes)

        return 0

    lax.fori_loop(0, out_ref.shape[0], one_peer, 0)


def far_kernel(codes_ref, coeffs_ref, *refs, peer, sizes):
    local_s, block_rows, tm_count, chips, share, bits = sizes
    next_own, next_other, near_ref, inner_ref = refs[:tm_count], *refs[tm_count : tm_count + 3]
    carry_ref, slope_ref, rhs_ref, out_ref, conv_ref, held_codes_ref, sem = refs[tm_count + 3 :]
    codes = copy_of_codes(codes_ref, held_codes_ref, sem)
    _, _, core = place_of_device()
    is_first = core == 0
    modes, lanes = near_ref.shape[1:]
    height = 2 * block_rows
    half = block_rows // 2 * 3
    weights = mode_weights(coeffs_ref, local_s, tm_count)
    for slab in range(half):
        mine = jnp.concatenate([next_own[peer][slab] for peer in range(tm_count)], axis=0)
        theirs = jnp.concatenate([next_other[peer, slab] for peer in range(tm_count)], axis=0)
        after, before = jnp.where(is_first, theirs, mine), jnp.where(is_first, mine, theirs)
        result = modes_of(weights, jnp.concatenate([after, before], axis=1))
        row, c = divmod(slab, 3)
        edges = ((near_ref[slab], result[:, :lanes]), (result[:, lanes:], near_ref[half + slab]))
        for number, (low, high) in enumerate(edges):
            place = number * block_rows + 2 * row
            for at, value, across in ((place, low, high * 0.5), (place + 1, high, low * -0.5)):
                if c == 0:
                    carry_ref[pl.ds(at, modes, stride=height), :] = value
                slope_ref[pl.ds(c * height + at, modes, stride=3 * height), :] = across
                store_projection(rhs_ref, c * height + at, value)


    codes.wait()
    pick_edge(held_codes_ref, carry_ref, slope_ref, conv_ref, peer, (chips, share, bits))
    out_ref[...] = edge_sum(conv_ref, rhs_ref, inner_ref, peer)
    pick_edge(held_codes_ref, carry_ref, slope_ref, conv_ref, peer - 1, (chips, share, bits))


def pick_edge(codes_ref, carry_ref, slope_ref, conv_ref, peer, sizes):
    places = conv_ref.shape[0] // (sizes[0] * sizes[1])
    height = places // 3

    def one_pair(slot, i, j):
        carry = carry_ref[pl.ds(pl.multiple_of(i * height, 8), height), :]
        slope = slope_ref[pl.ds(pl.multiple_of(j * places, 8), places), :]
        rows = [carry * slope[c * height : (c + 1) * height] for c in range(3)]
        conv_ref[pl.ds(pl.multiple_of(slot * places, 8), places), :] = jnp.concatenate(rows, axis=0)

    for_pairs_of(codes_ref, peer, sizes, one_pair)


def edge_sum(picked_ref, rhs_ref, inner_ref, peer):
    block = inner_ref.shape[1]
    places = picked_ref.shape[0] // block
    return inner_ref[peer % inner_ref.shape[0]] + project(picked_ref, rhs_ref, block, places, picked_ref.shape[1])


def edge_kernel(
    codes_ref, carry_ref, slope_ref, rhs_ref, inner_ref, picked_ref, out_ref, conv_ref, held_codes_ref, sem, *,
    peer, sizes
):
    codes = copy_of_codes(codes_ref, held_codes_ref, sem)
    out_ref[...] = edge_sum(picked_ref, rhs_ref, inner_ref, peer)
    codes.wait()
    pick_edge(held_codes_ref, carry_ref, slope_ref, conv_ref, peer - 1, sizes)


def picked_edge_kernel(rhs_ref, inner_ref, picked_ref, out_ref, *, peer):
    out_ref[...] = edge_sum(picked_ref, rhs_ref, inner_ref, peer)


def own_edge_kernel(codes_ref, carry_ref, slope_ref, rhs_ref, inner_ref, *refs, sizes):
    *arrived_refs, out_ref, conv_ref, held_codes_ref, sem = refs
    copy_of_codes(codes_ref, held_codes_ref, sem).wait()
    pick_edge(held_codes_ref, carry_ref, slope_ref, conv_ref, 0, sizes)
    total = edge_sum(conv_ref, rhs_ref, inner_ref, 0)
    for arrived_ref in arrived_refs:
        total = total + arrived_ref[...]
    out_ref[...] = total


def vmem_limit(mebibytes):
    return pltpu.CompilerParams(vmem_limit_bytes=mebibytes * 2**20)


def in_vmem(array):
    return pltpu.with_memory_space_constraint(array, pltpu.VMEM)


def shards(snapshots, coeffs, pair_table):
    tm_count, space_count = lax.axis_size("tm"), lax.axis_size("space")
    chips = space_count // 2
    local_s, _, _, rows_y, lanes = snapshots.shape
    modes = coeffs.shape[1]
    block_rows = rows_y // tm_count
    slabs = 3 * block_rows + border_slabs(rows_y, lanes)
    share = pair_table.shape[0] // (tm_count * space_count)
    factor = float(space_count * rows_y * lanes) ** (-0.5)
    bits = modes.bit_length() - 1
    assert modes == 2**bits
    vmem = pl.BlockSpec(memory_space=pltpu.VMEM)
    block = chips * share
    height = 2 * block_rows
    depth = 3 * height * lanes

    swap = [(2 * chip + c, 2 * chip + 1 - c) for chip in range(chips) for c in range(2)]

    def across(peer):
        return [(i, i ^ peer) for i in range(tm_count)]

    with jax.named_scope("pack"):
        *packed, codes, held_coeffs = pl.pallas_call(
            functools.partial(pack_kernel, sizes=(local_s, rows_y, tm_count)),
            out_shape=[pltpu.VMEM((slabs, local_s, lanes), F32)] * tm_count
            + [
                pltpu.VMEM((tm_count, block_rows // 2 * 3, local_s, lanes), F32),
                pltpu.VMEM((pair_table.shape[0] // lanes, lanes), jnp.int32),
                pltpu.VMEM(coeffs.shape, F32),
            ],
            in_specs=[pl.BlockSpec(memory_space=pltpu.HBM)] * 3,
            out_specs=[vmem] * (tm_count + 3),
            scratch_shapes=[
                pltpu.VMEM((tm_count, slabs, local_s, lanes), F32),
                pltpu.VMEM((3, local_s, rows_y, lanes), F32),
                pltpu.VMEM((2, pair_table.shape[0]), jnp.int32),
                pltpu.SemaphoreType.DMA((5,)),
            ],
            compiler_params=vmem_limit(16),
        )(
            *[
                pltpu.with_memory_space_constraint(array, pltpu.HBM)
                for array in (snapshots.reshape(local_s, 3, rows_y, lanes), pair_table.T, coeffs)
            ]
        )
        codes, coeffs = in_vmem(codes), in_vmem(held_coeffs)
    with jax.named_scope("to_next_plane"):
        ring = [(place, (place + (1 if place % 2 else -1)) % space_count) for place in range(space_count)]
        across_edge = lax.ppermute(packed[tm_count], "space", ring)
    with jax.named_scope("to_columns"):
        own = [packed[0]] + [lax.ppermute(packed[peer], "tm", across(peer)) for peer in range(1, tm_count)]
    with jax.named_scope("next_to_columns"):
        across_edge, own[:3] = lax.optimization_barrier((across_edge, own[:3]))
        parts = [across_edge[peer] for peer in range(tm_count)]
        parts, own[3:] = lax.optimization_barrier((parts, own[3:]))
        next_own = [parts[0]] + [lax.ppermute(parts[peer], "tm", across(peer)) for peer in range(1, tm_count)]
    with jax.named_scope("to_other_core"):
        other = [lax.ppermute(piece, "space", swap) for piece in own]
    early = tm_count // 2
    picked = pltpu.VMEM((block * 3 * height, lanes), F32)
    held_codes = [pltpu.SMEM(codes.shape, jnp.int32), pltpu.SemaphoreType.DMA]
    groups = pltpu.VMEM((early, block, modes), F32)
    with jax.named_scope("inner_terms"):
        near, *inner_tables, early_sums, first_picked = pl.pallas_call(
            functools.partial(inner_kernel, first_peer=early, sizes=(local_s, block_rows, tm_count, chips, share, bits)),
            out_shape=[
                pltpu.VMEM((block_rows * 3, modes, lanes), F32),
                pltpu.VMEM((modes * 3 * height, lanes), F32),
                pltpu.VMEM((modes * 9 * height, lanes), F32),
                pltpu.VMEM((depth, 2 * modes), BF16),
                groups,
                picked,
            ],
            in_specs=[vmem] * (2 * tm_count + 2),
            out_specs=[vmem] * 6,
            scratch_shapes=[pltpu.VMEM((2, slabs, modes, lanes), F32)] + held_codes,
            compiler_params=vmem_limit(24),
            cost_estimate=pl.CostEstimate(flops=12 * 10**9, bytes_accessed=10**7, transcendentals=0),
        )(codes, coeffs, *[in_vmem(piece) for piece in (*own, *other)])
    with jax.named_scope("next_to_other_core"):
        next_own, inner_tables = lax.optimization_barrier((next_own, inner_tables))
        next_other = lax.ppermute(jnp.stack(next_own), "space", swap)
    with jax.named_scope("inner_terms"):
        late_sums, _ = pl.pallas_call(
            functools.partial(rest_kernel, sizes=(chips, share, bits)),
            out_shape=[groups, picked],
            in_specs=[vmem] * 5,
            out_specs=[vmem] * 2,
            input_output_aliases={4: 1},
            scratch_shapes=held_codes,
            compiler_params=vmem_limit(16),
            cost_estimate=pl.CostEstimate(flops=8 * 10**9, bytes_accessed=10**7, transcendentals=0),
        )(codes, *[in_vmem(table) for table in (*inner_tables, first_picked)])
    with jax.named_scope("edge_terms"):
        *tables, summed, next_picked = pl.pallas_call(
            functools.partial(
                far_kernel, peer=tm_count - 1, sizes=(local_s, block_rows, tm_count, chips, share, bits)
            ),
            out_shape=[
                pltpu.VMEM((modes * height, lanes), F32),
                pltpu.VMEM((modes * 3 * height, lanes), F32),
                pltpu.VMEM((depth, 2 * modes), BF16),
                pltpu.VMEM((block, modes), F32),
                picked,
            ],
            in_specs=[vmem] * (tm_count + 5),
            out_specs=[vmem] * 5,
            scratch_shapes=held_codes,
            compiler_params=vmem_limit(16),
        )(codes, coeffs, *[in_vmem(piece) for piece in (*next_own, next_other, near, early_sums)])
    arrived, taken = [], 2
    for peer in reversed(range(tm_count - 1)):
        with jax.named_scope("sum_over_columns"):
            arrived.append(lax.ppermute(summed, "tm", across(peer + 1)))
            if peer >= early:
                early_sums, _ = lax.optimization_barrier((early_sums, summed))
            else:
                late_sums, _ = lax.optimization_barrier((late_sums, summed))
        with jax.named_scope("edge_terms"):
            inner_sums = early_sums if peer >= early else late_sums
            edge_cost = pl.CostEstimate(flops=10**8, bytes_accessed=10**5, transcendentals=0)
            if peer > 1:
                summed, next_picked = pl.pallas_call(
                    functools.partial(edge_kernel, peer=peer, sizes=(chips, share, bits)),
                    out_shape=[pltpu.VMEM((block, modes), F32), picked],
                    in_specs=[vmem] * 6,
                    out_specs=[vmem] * 2,
                    scratch_shapes=held_codes,
                    compiler_params=vmem_limit(16),
                    cost_estimate=edge_cost,
                )(codes, *[in_vmem(table) for table in (*tables, inner_sums, next_picked)])
            elif peer:
                summed = pl.pallas_call(
                    functools.partial(picked_edge_kernel, peer=peer),
                    out_shape=pltpu.VMEM((block, modes), F32),
                    in_specs=[vmem] * 3,
                    out_specs=vmem,
                    compiler_params=vmem_limit(16),
                    cost_estimate=edge_cost,
                )(*[in_vmem(table) for table in (tables[2], inner_sums, next_picked)])
            else:
                summed = pl.pallas_call(
                    functools.partial(own_edge_kernel, sizes=(chips, share, bits)),
                    out_shape=pltpu.VMEM((block, modes), F32),
                    in_specs=[vmem] * (5 + taken),
                    out_specs=vmem,
                    scratch_shapes=[picked] + held_codes,
                    compiler_params=vmem_limit(16),
                    cost_estimate=edge_cost,
                )(codes, *[in_vmem(table) for table in (*tables, inner_sums, *arrived[:taken])])
    with jax.named_scope("sum_over_columns"):
        for part in arrived[taken:]:
            summed = summed + part
    with jax.named_scope("sum_over_chips"):
        shares = summed.reshape(chips, share, modes)
        result = shares[0]
        for step in range(1, chips):
            pairing = [(2 * chip + c, 2 * (chip ^ step) + c) for chip in range(chips) for c in range(2)]
            result = result + lax.ppermute(shares[step], "space", pairing)
        return result * factor


def solution(mesh):
    placed = (P("tm", None, "space", None, None), P(), P())
    return jax.shard_map(
        shards, mesh=mesh, in_specs=placed, out_specs=P(("tm", "space"), None), check_vma=False
    )
```

```python
import functools

import jax
import jax.numpy as jnp
from jax import lax
from jax.experimental import pallas as pl
from jax.experimental.pallas import tpu as pltpu
from jax.sharding import PartitionSpec as P

F32 = jnp.float32
BF16 = jnp.bfloat16


def place_of_device():
    place = lax.axis_index("space")
    return lax.axis_index("tm"), lax.shift_right_logical(place, 1), jnp.bitwise_and(place, 1)


def split_high_low(values):
    high = values.astype(BF16)
    low = (values - high.astype(F32)).astype(BF16)
    return high, low


def border_lane(rows_y, lanes, c):
    per_slab = lanes // (2 * rows_y)
    return c // per_slab, c % per_slab * 2 * rows_y


def border_slabs(rows_y, lanes):
    return border_lane(rows_y, lanes, 2)[0] + 1


def exchange_blocks(rows, lane, width, lanes):
    rows = list(rows)
    step = len(rows) // 2
    while step:
        keeps = jnp.bitwise_and(lane, step * width) == 0
        for low in range(len(rows)):
            if low & step == 0:
                first, second = rows[low], rows[low + step]
                rows[low] = jnp.where(keeps, first, pltpu.roll(second, step * width, 1))
                rows[low + step] = jnp.where(keeps, pltpu.roll(first, lanes - step * width, 1), second)
        step //= 2
    return rows


def pack_kernel(field_ref, pairs_ref, coeffs_ref, *refs, sizes):
    *out_refs, codes_ref, held_coeffs_ref, sorted_ref, held_ref, held_pairs_ref, sems = refs
    local_s, rows_y, tm_count = sizes
    lanes = field_ref.shape[3]
    copies = [pltpu.make_async_copy(field_ref.at[:, c], held_ref.at[c], sems.at[c]) for c in range(3)]
    copies.append(pltpu.make_async_copy(pairs_ref, held_pairs_ref, sems.at[3]))
    copies.append(pltpu.make_async_copy(coeffs_ref, held_coeffs_ref, sems.at[4]))
    for copy in copies:
        copy.start()
    rows_ref = held_ref.reshape(3 * local_s * rows_y, lanes)
    t, _, core = place_of_device()
    width, groups = lanes // tm_count, rows_y // tm_count
    lane = lax.broadcasted_iota(jnp.int32, (local_s, lanes), 1)
    borders = [[jnp.zeros((local_s, lanes), F32) for _ in range(tm_count)] for _ in range(border_slabs(rows_y, lanes))]
    for c in range(3):
        slab, first_lane = border_lane(rows_y, lanes, c)
        copies[c].wait()

        def one_group(g, border, c=c, first_lane=first_lane):
            border = list(border)
            rows = []
            for q in range(tm_count):
                y = q * groups + g
                row = rows_ref[pl.ds(c * local_s * rows_y + y, local_s, stride=rows_y), :]
                rows.append(row)
                for side in range(2):
                    shift = first_lane + side * (rows_y - width - 1) + y
                    moved = pltpu.roll(row, jnp.bitwise_and(shift, lanes - 1), 1)
                    for block in range(tm_count):
                        column = (block + 1) * width if side else block * width - 1
                        is_here = lane == jnp.bitwise_and(shift + column, lanes - 1)
                        border[block] = jnp.where(is_here, moved, border[block])
            for block, main in enumerate(exchange_blocks(rows, lane, width, lanes)):
                sorted_ref[block, g * 3 + c] = main
            return tuple(border)

        borders[slab] = lax.fori_loop(0, groups, one_group, tuple(borders[slab]))
    half = groups // 2 * 3
    for slab, border in enumerate(borders):
        for block in range(tm_count):
            sorted_ref[block, groups * 3 + slab] = border[block]
    for peer in range(tm_count):
        block = jnp.bitwise_xor(t, peer)
        out_refs[peer][...] = sorted_ref[block]
        out_refs[tm_count][peer] = sorted_ref[block, pl.ds(core * half, half)]
    copies[3].wait()
    copies[4].wait()
    for first in range(0, codes_ref.shape[0], lanes):
        here = pl.ds(first, lanes)
        codes_ref[here] = held_pairs_ref[0, here] * held_coeffs_ref.shape[1] + held_pairs_ref[1, here]


def mode_weights(coeffs_ref, local_s, tm_count):
    t, _, _ = place_of_device()
    ordered = jnp.concatenate(
        [
            coeffs_ref[pl.ds(pl.multiple_of(jnp.bitwise_xor(t, peer) * local_s, 8), local_s), :]
            for peer in range(tm_count)
        ],
        axis=0,
    )
    high, low = split_high_low(ordered.T)
    return jnp.concatenate([high, low, high, low], axis=1)


def modes_of(weights, slab):
    high, low = split_high_low(slab)
    return jnp.dot(weights, jnp.concatenate([high, high, low, low], axis=0), preferred_element_type=F32)


def store_projection(rhs_ref, place, mode_slab):
    high, low = split_high_low(mode_slab.T)
    modes, lanes = mode_slab.shape
    rhs_ref[place * lanes : (place + 1) * lanes, 0:modes] = high
    rhs_ref[place * lanes : (place + 1) * lanes, modes : 2 * modes] = low


def project(conv_ref, rhs_ref, block, places, lanes):
    both = None
    for place in range(0, places, 2):
        highs, lows = zip(
            *(split_high_low(conv_ref[pl.ds(place + k, block, stride=places), :]) for k in range(2))
        )
        lhs = jnp.concatenate([jnp.concatenate(highs, axis=1), jnp.concatenate(lows, axis=1)], axis=0)
        part = jnp.dot(lhs, rhs_ref[place * lanes : (place + 2) * lanes, :], preferred_element_type=F32)
        both = part if both is None else both + part
    modes = both.shape[1] // 2
    return (both[:block, :modes] + both[:block, modes:]) + (both[block:, :modes] + both[block:, modes:])


def for_pairs_of(codes_ref, peer, sizes, one_pair):
    chips, share, bits = sizes
    t, chip, core = place_of_device()
    first_chip = jnp.bitwise_xor(t, peer) * chips

    def one_share(ahead, _):
        base = ((first_chip + jnp.bitwise_xor(chip, ahead)) * 2 + core) * share

        def one(q, _):
            code = codes_ref[base + q]
            one_pair(ahead * share + q, lax.shift_right_logical(code, bits), jnp.bitwise_and(code, 2**bits - 1))
            return 0

        return lax.fori_loop(0, share, one, 0, unroll=32)

    lax.fori_loop(0, chips, one_share, 0)


def copy_of_codes(codes_ref, held_codes_ref, sem):
    copy = pltpu.make_async_copy(codes_ref, held_codes_ref, sem)
    copy.start()
    return copy


def inner_kernel(codes_ref, coeffs_ref, *refs, first_peer, sizes):
    local_s, block_rows, tm_count, chips, share, bits = sizes
    own, other = refs[:tm_count], refs[tm_count : 2 * tm_count]
    near_ref, carry_ref, slope_ref, rhs_ref, out_ref, conv_ref, slab_ref, held_codes_ref, sem = refs[2 * tm_count :]
    codes = copy_of_codes(codes_ref, held_codes_ref, sem)
    t, _, core = place_of_device()
    modes, lanes = coeffs_ref.shape[1], own[0].shape[2]
    height = 2 * block_rows
    weights = mode_weights(coeffs_ref, local_s, tm_count)

    def one_slab(index, _):
        own_slab = jnp.concatenate([piece[index] for piece in own], axis=0)
        other_slab = jnp.concatenate([piece[index] for piece in other], axis=0)
        is_first = core == 0
        both = jnp.concatenate(
            [jnp.where(is_first, own_slab, other_slab), jnp.where(is_first, other_slab, own_slab)], axis=1
        )
        result = modes_of(weights, both)
        slab_ref[0, index] = result[:, :lanes]
        slab_ref[1, index] = result[:, lanes:]
        return 0

    slabs = own[0].shape[0]
    lax.fori_loop(0, slabs, one_slab, 0, unroll=True)
    width, rows_y = lanes // tm_count, block_rows * tm_count
    lane = lax.broadcasted_iota(jnp.int32, (1, lanes), 1)
    part, column = lax.div(lane, width), lax.rem(lane, width)
    has_border = jnp.where(column == 0, -0.5, jnp.where(column == width - 1, 0.5, 0.0))
    border_of = jnp.where(column == 0, 0, rows_y) + t * width - 1 + part * block_rows
    border_lanes = lax.broadcasted_iota(jnp.int32, (2 * lanes, lanes), 0)
    border_lanes = jnp.where(border_lanes >= lanes, border_lanes - lanes, border_lanes)
    borders = []
    for slab in range(3 * block_rows, slabs):
        both = jnp.concatenate([slab_ref[0, slab], slab_ref[1, slab]], axis=0)
        borders.append(jnp.concatenate(split_high_low(both), axis=1))
    for c in range(3):
        slab, first_lane = border_lane(rows_y, lanes, c)
        for row in range(block_rows):
            center = row * 3 + c
            if row % 2 == 0:
                picks = [
                    jnp.where(
                        border_lanes == jnp.bitwise_and(border_of + (first_lane + row + k), lanes - 1), has_border, 0.0
                    ).astype(BF16)
                    for k in range(2)
                ]
                border = jnp.dot(borders[slab], jnp.concatenate(picks, axis=1), preferred_element_type=F32)
            for plane in range(2):
                place = plane * block_rows + row
                value = slab_ref[plane, center]
                stream = slab_ref[1 - plane, center] * (0.5 if plane == 0 else -0.5)
                if row + 1 < block_rows:
                    above = slab_ref[plane, center + 3]
                else:
                    above = pltpu.roll(slab_ref[plane, c], lanes - width, 1)
                    above = jnp.where(lane < lanes - width, above, 0.0)
                if row > 0:
                    below = slab_ref[plane, center - 3]
                else:
                    below = pltpu.roll(slab_ref[plane, 3 * (block_rows - 1) + c], width, 1)
                    below = jnp.where(lane >= width, below, 0.0)
                normal = (above - below) * 0.5
                after = jnp.where(column < width - 1, pltpu.roll(value, lanes - 1, 1), 0.0)
                before = jnp.where(column > 0, pltpu.roll(value, 1, 1), 0.0)
                span = (after - before) * 0.5 + border[plane * modes : (plane + 1) * modes, row % 2 * lanes : (row % 2 + 1) * lanes]
                carry_ref[pl.ds(c * height + place, modes, stride=3 * height), :] = value
                for d, slope in enumerate((stream, normal, span)):
                    slope_ref[pl.ds((d * 3 + c) * height + place, modes, stride=9 * height), :] = slope
                store_projection(rhs_ref, c * height + place, value)
                if (plane == 1) == (row < block_rows // 2):
                    near_ref[center] = value

    codes.wait()

    pick_inner(held_codes_ref, carry_ref, slope_ref, conv_ref, first_peer, (chips, share, bits))

    def one_peer(number, _):
        out_ref[number] = project(conv_ref, rhs_ref, chips * share, 3 * height, lanes)
        following = lax.rem(first_peer + number + 1, tm_count)
        pick_inner(held_codes_ref, carry_ref, slope_ref, conv_ref, following, (chips, share, bits))
        return 0

    lax.fori_loop(0, out_ref.shape[0], one_peer, 0)


def pick_inner(codes_ref, carry_ref, slope_ref, conv_ref, peer, sizes):
    places = conv_ref.shape[0] // (sizes[0] * sizes[1])
    height = places // 3

    def one_pair(slot, i, j):
        carry = carry_ref[pl.ds(pl.multiple_of(i * places, 8), places), :]
        slope = slope_ref[pl.ds(pl.multiple_of(j * (3 * places), 8), 3 * places), :]
        rows = [
            sum(
                carry[d * height : (d + 1) * height] * slope[(d * 3 + c) * height : (d * 3 + c + 1) * height]
                for d in range(3)
            )
            for c in range(3)
        ]
        conv_ref[pl.ds(pl.multiple_of(slot * places, 8), places), :] = jnp.concatenate(rows, axis=0)

    for_pairs_of(codes_ref, peer, sizes, one_pair)


def rest_kernel(
    codes_ref, carry_ref, slope_ref, rhs_ref, picked_ref, out_ref, conv_ref, held_codes_ref, sem, *, sizes
):
    del picked_ref
    chips, share, _ = sizes
    codes = copy_of_codes(codes_ref, held_codes_ref, sem)
    block, lanes = chips * share, conv_ref.shape[1]
    places = conv_ref.shape[0] // block

    def one_peer(peer, _):
        out_ref[peer] = project(conv_ref, rhs_ref, block, places, lanes)

        @pl.when(peer == 0)
        def _():
            codes.wait()

        @pl.when(peer + 1 < out_ref.shape[0])
        def _():
            pick_inner(held_codes_ref, carry_ref, slope_ref, conv_ref, peer + 1, sizes)

        return 0

    lax.fori_loop(0, out_ref.shape[0], one_peer, 0)


def far_kernel(codes_ref, coeffs_ref, *refs, peer, sizes):
    local_s, block_rows, tm_count, chips, share, bits = sizes
    next_own, next_other, near_ref, inner_ref = refs[:tm_count], *refs[tm_count : tm_count + 3]
    carry_ref, slope_ref, rhs_ref, out_ref, conv_ref, held_codes_ref, sem = refs[tm_count + 3 :]
    codes = copy_of_codes(codes_ref, held_codes_ref, sem)
    _, _, core = place_of_device()
    is_first = core == 0
    modes, lanes = near_ref.shape[1:]
    height = 2 * block_rows
    half = block_rows // 2 * 3
    weights = mode_weights(coeffs_ref, local_s, tm_count)
    for slab in range(half):
        mine = jnp.concatenate([next_own[peer][slab] for peer in range(tm_count)], axis=0)
        theirs = jnp.concatenate([next_other[peer, slab] for peer in range(tm_count)], axis=0)
        after, before = jnp.where(is_first, theirs, mine), jnp.where(is_first, mine, theirs)
        result = modes_of(weights, jnp.concatenate([after, before], axis=1))
        row, c = divmod(slab, 3)
        edges = ((near_ref[slab], result[:, :lanes]), (result[:, lanes:], near_ref[half + slab]))
        for number, (low, high) in enumerate(edges):
            place = number * block_rows + 2 * row
            for at, value, across in ((place, low, high * 0.5), (place + 1, high, low * -0.5)):
                if c == 0:
                    carry_ref[pl.ds(at, modes, stride=height), :] = value
                slope_ref[pl.ds(c * height + at, modes, stride=3 * height), :] = across
                store_projection(rhs_ref, c * height + at, value)


    codes.wait()
    pick_edge(held_codes_ref, carry_ref, slope_ref, conv_ref, peer, (chips, share, bits))
    out_ref[...] = edge_sum(conv_ref, rhs_ref, inner_ref, peer)
    pick_edge(held_codes_ref, carry_ref, slope_ref, conv_ref, peer - 1, (chips, share, bits))


def pick_edge(codes_ref, carry_ref, slope_ref, conv_ref, peer, sizes):
    places = conv_ref.shape[0] // (sizes[0] * sizes[1])
    height = places // 3

    def one_pair(slot, i, j):
        carry = carry_ref[pl.ds(pl.multiple_of(i * height, 8), height), :]
        slope = slope_ref[pl.ds(pl.multiple_of(j * places, 8), places), :]
        rows = [carry * slope[c * height : (c + 1) * height] for c in range(3)]
        conv_ref[pl.ds(pl.multiple_of(slot * places, 8), places), :] = jnp.concatenate(rows, axis=0)

    for_pairs_of(codes_ref, peer, sizes, one_pair)


def edge_sum(picked_ref, rhs_ref, inner_ref, peer):
    block = inner_ref.shape[1]
    places = picked_ref.shape[0] // block
    return inner_ref[peer % inner_ref.shape[0]] + project(picked_ref, rhs_ref, block, places, picked_ref.shape[1])


def edge_kernel(
    codes_ref, carry_ref, slope_ref, rhs_ref, inner_ref, picked_ref, out_ref, conv_ref, held_codes_ref, sem, *,
    peer, sizes
):
    codes = copy_of_codes(codes_ref, held_codes_ref, sem)
    out_ref[...] = edge_sum(picked_ref, rhs_ref, inner_ref, peer)
    codes.wait()
    pick_edge(held_codes_ref, carry_ref, slope_ref, conv_ref, peer - 1, sizes)


def picked_edge_kernel(rhs_ref, inner_ref, picked_ref, out_ref, *, peer):
    out_ref[...] = edge_sum(picked_ref, rhs_ref, inner_ref, peer)


def own_edge_kernel(codes_ref, carry_ref, slope_ref, rhs_ref, inner_ref, *refs, sizes):
    *arrived_refs, out_ref, conv_ref, held_codes_ref, sem = refs
    copy_of_codes(codes_ref, held_codes_ref, sem).wait()
    pick_edge(held_codes_ref, carry_ref, slope_ref, conv_ref, 0, sizes)
    total = edge_sum(conv_ref, rhs_ref, inner_ref, 0)
    for arrived_ref in arrived_refs:
        total = total + arrived_ref[...]
    out_ref[...] = total


def vmem_limit(mebibytes):
    return pltpu.CompilerParams(vmem_limit_bytes=mebibytes * 2**20)


def in_vmem(array):
    return pltpu.with_memory_space_constraint(array, pltpu.VMEM)


def shards(snapshots, coeffs, pair_table):
    tm_count, space_count = lax.axis_size("tm"), lax.axis_size("space")
    chips = space_count // 2
    local_s, _, _, rows_y, lanes = snapshots.shape
    modes = coeffs.shape[1]
    block_rows = rows_y // tm_count
    slabs = 3 * block_rows + border_slabs(rows_y, lanes)
    share = pair_table.shape[0] // (tm_count * space_count)
    factor = float(space_count * rows_y * lanes) ** (-0.5)
    bits = modes.bit_length() - 1
    assert modes == 2**bits
    vmem = pl.BlockSpec(memory_space=pltpu.VMEM)
    block = chips * share
    height = 2 * block_rows
    depth = 3 * height * lanes

    swap = [(2 * chip + c, 2 * chip + 1 - c) for chip in range(chips) for c in range(2)]

    def across(peer):
        return [(i, i ^ peer) for i in range(tm_count)]

    with jax.named_scope("pack"):
        *packed, codes, held_coeffs = pl.pallas_call(
            functools.partial(pack_kernel, sizes=(local_s, rows_y, tm_count)),
            out_shape=[pltpu.VMEM((slabs, local_s, lanes), F32)] * tm_count
            + [
                pltpu.VMEM((tm_count, block_rows // 2 * 3, local_s, lanes), F32),
                pltpu.VMEM((pair_table.shape[0],), jnp.int32),
                pltpu.VMEM(coeffs.shape, F32),
            ],
            in_specs=[pl.BlockSpec(memory_space=pltpu.HBM)] * 3,
            out_specs=[vmem] * (tm_count + 3),
            scratch_shapes=[
                pltpu.VMEM((tm_count, slabs, local_s, lanes), F32),
                pltpu.VMEM((3, local_s, rows_y, lanes), F32),
                pltpu.VMEM((2, pair_table.shape[0]), jnp.int32),
                pltpu.SemaphoreType.DMA((5,)),
            ],
            compiler_params=vmem_limit(16),
        )(
            *[
                pltpu.with_memory_space_constraint(array, pltpu.HBM)
                for array in (snapshots.reshape(local_s, 3, rows_y, lanes), pair_table.T, coeffs)
            ]
        )
        codes, coeffs = in_vmem(codes), in_vmem(held_coeffs)
    with jax.named_scope("to_next_plane"):
        ring = [(place, (place + (1 if place % 2 else -1)) % space_count) for place in range(space_count)]
        across_edge = lax.ppermute(packed[tm_count], "space", ring)
    with jax.named_scope("to_columns"):
        own = [packed[0]] + [lax.ppermute(packed[peer], "tm", across(peer)) for peer in range(1, tm_count)]
    with jax.named_scope("next_to_columns"):
        across_edge, own[:3] = lax.optimization_barrier((across_edge, own[:3]))
        parts = [across_edge[peer] for peer in range(tm_count)]
        parts, own[3:] = lax.optimization_barrier((parts, own[3:]))
        next_own = [parts[0]] + [lax.ppermute(parts[peer], "tm", across(peer)) for peer in range(1, tm_count)]
    with jax.named_scope("to_other_core"):
        other = [lax.ppermute(piece, "space", swap) for piece in own]
    early = tm_count // 2
    picked = pltpu.VMEM((block * 3 * height, lanes), F32)
    held_codes = [pltpu.SMEM(codes.shape, jnp.int32), pltpu.SemaphoreType.DMA]
    groups = pltpu.VMEM((early, block, modes), F32)
    with jax.named_scope("inner_terms"):
        near, *inner_tables, early_sums, first_picked = pl.pallas_call(
            functools.partial(inner_kernel, first_peer=early, sizes=(local_s, block_rows, tm_count, chips, share, bits)),
            out_shape=[
                pltpu.VMEM((block_rows * 3, modes, lanes), F32),
                pltpu.VMEM((modes * 3 * height, lanes), F32),
                pltpu.VMEM((modes * 9 * height, lanes), F32),
                pltpu.VMEM((depth, 2 * modes), BF16),
                groups,
                picked,
            ],
            in_specs=[vmem] * (2 * tm_count + 2),
            out_specs=[vmem] * 6,
            scratch_shapes=[pltpu.VMEM((2, slabs, modes, lanes), F32)] + held_codes,
            compiler_params=vmem_limit(24),
            cost_estimate=pl.CostEstimate(flops=12 * 10**9, bytes_accessed=10**7, transcendentals=0),
        )(codes, coeffs, *[in_vmem(piece) for piece in (*own, *other)])
    with jax.named_scope("next_to_other_core"):
        next_own, inner_tables = lax.optimization_barrier((next_own, inner_tables))
        next_other = lax.ppermute(jnp.stack(next_own), "space", swap)
    with jax.named_scope("inner_terms"):
        late_sums, _ = pl.pallas_call(
            functools.partial(rest_kernel, sizes=(chips, share, bits)),
            out_shape=[groups, picked],
            in_specs=[vmem] * 5,
            out_specs=[vmem] * 2,
            input_output_aliases={4: 1},
            scratch_shapes=held_codes,
            compiler_params=vmem_limit(16),
            cost_estimate=pl.CostEstimate(flops=8 * 10**9, bytes_accessed=10**7, transcendentals=0),
        )(codes, *[in_vmem(table) for table in (*inner_tables, first_picked)])
    with jax.named_scope("edge_terms"):
        *tables, summed, next_picked = pl.pallas_call(
            functools.partial(
                far_kernel, peer=tm_count - 1, sizes=(local_s, block_rows, tm_count, chips, share, bits)
            ),
            out_shape=[
                pltpu.VMEM((modes * height, lanes), F32),
                pltpu.VMEM((modes * 3 * height, lanes), F32),
                pltpu.VMEM((depth, 2 * modes), BF16),
                pltpu.VMEM((block, modes), F32),
                picked,
            ],
            in_specs=[vmem] * (tm_count + 5),
            out_specs=[vmem] * 5,
            scratch_shapes=held_codes,
            compiler_params=vmem_limit(16),
        )(codes, coeffs, *[in_vmem(piece) for piece in (*next_own, next_other, near, early_sums)])
    arrived, taken = [], 2
    for peer in reversed(range(tm_count - 1)):
        with jax.named_scope("sum_over_columns"):
            arrived.append(lax.ppermute(summed, "tm", across(peer + 1)))
            if peer >= early:
                early_sums, _ = lax.optimization_barrier((early_sums, summed))
            else:
                late_sums, _ = lax.optimization_barrier((late_sums, summed))
        with jax.named_scope("edge_terms"):
            inner_sums = early_sums if peer >= early else late_sums
            edge_cost = pl.CostEstimate(flops=10**8, bytes_accessed=10**5, transcendentals=0)
            if peer > 1:
                summed, next_picked = pl.pallas_call(
                    functools.partial(edge_kernel, peer=peer, sizes=(chips, share, bits)),
                    out_shape=[pltpu.VMEM((block, modes), F32), picked],
                    in_specs=[vmem] * 6,
                    out_specs=[vmem] * 2,
                    scratch_shapes=held_codes,
                    compiler_params=vmem_limit(16),
                    cost_estimate=edge_cost,
                )(codes, *[in_vmem(table) for table in (*tables, inner_sums, next_picked)])
            elif peer:
                summed = pl.pallas_call(
                    functools.partial(picked_edge_kernel, peer=peer),
                    out_shape=pltpu.VMEM((block, modes), F32),
                    in_specs=[vmem] * 3,
                    out_specs=vmem,
                    compiler_params=vmem_limit(16),
                    cost_estimate=edge_cost,
                )(*[in_vmem(table) for table in (tables[2], inner_sums, next_picked)])
            else:
                summed = pl.pallas_call(
                    functools.partial(own_edge_kernel, sizes=(chips, share, bits)),
                    out_shape=pltpu.VMEM((block, modes), F32),
                    in_specs=[vmem] * (5 + taken),
                    out_specs=vmem,
                    scratch_shapes=[picked] + held_codes,
                    compiler_params=vmem_limit(16),
                    cost_estimate=edge_cost,
                )(codes, *[in_vmem(table) for table in (*tables, inner_sums, *arrived[:taken])])
    with jax.named_scope("sum_over_columns"):
        for part in arrived[taken:]:
            summed = summed + part
    with jax.named_scope("sum_over_chips"):
        shares = summed.reshape(chips, share, modes)
        result = shares[0]
        for step in range(1, chips):
            pairing = [(2 * chip + c, 2 * (chip ^ step) + c) for chip in range(chips) for c in range(2)]
            result = result + lax.ppermute(shares[step], "space", pairing)
        return result * factor


def solution(mesh):
    placed = (P("tm", None, "space", None, None), P(), P())
    return jax.shard_map(
        shards, mesh=mesh, in_specs=placed, out_specs=P(("tm", "space"), None), check_vma=False
    )
```

```python
import functools

import jax
import jax.numpy as jnp
from jax import lax
from jax.experimental import pallas as pl
from jax.experimental.pallas import tpu as pltpu
from jax.sharding import PartitionSpec as P

F32 = jnp.float32
BF16 = jnp.bfloat16


def place_of_device():
    place = lax.axis_index("space")
    return lax.axis_index("tm"), lax.shift_right_logical(place, 1), jnp.bitwise_and(place, 1)


def split_high_low(values):
    high = values.astype(BF16)
    low = (values - high.astype(F32)).astype(BF16)
    return high, low


def border_layout(rows_y, lanes, width):
    per_run = (width + 1) // rows_y
    if per_run:
        run = width + 1 + per_run * rows_y
        firsts = [c // per_run * run + c % per_run * rows_y for c in range(3)]
        if firsts[2] + width + 1 + rows_y <= lanes:
            return [(0, first) for first in firsts], width + 1, 1
    per_slab = lanes // (2 * rows_y)
    places = [(c // per_slab, c % per_slab * 2 * rows_y) for c in range(3)]
    return places, rows_y, places[2][0] + 1


def exchange_blocks(rows, lane, width, lanes):
    rows = list(rows)
    step = len(rows) // 2
    while step:
        keeps = jnp.bitwise_and(lane, step * width) == 0
        for low in range(len(rows)):
            if low & step == 0:
                first, second = rows[low], rows[low + step]
                rows[low] = jnp.where(keeps, first, pltpu.roll(second, step * width, 1))
                rows[low + step] = jnp.where(keeps, pltpu.roll(first, lanes - step * width, 1), second)
        step //= 2
    return rows


def pack_kernel(field_ref, pairs_ref, coeffs_ref, *refs, sizes):
    *out_refs, codes_ref, held_coeffs_ref, sorted_ref, held_ref, held_pairs_ref, sems = refs
    local_s, rows_y, tm_count = sizes
    lanes = field_ref.shape[3]
    copies = [pltpu.make_async_copy(field_ref.at[:, c], held_ref.at[c], sems.at[c]) for c in range(3)]
    copies.append(pltpu.make_async_copy(pairs_ref, held_pairs_ref, sems.at[3]))
    copies.append(pltpu.make_async_copy(coeffs_ref, held_coeffs_ref, sems.at[4]))
    for copy in copies:
        copy.start()
    rows_ref = held_ref.reshape(3 * local_s * rows_y, lanes)
    t, _, core = place_of_device()
    width, groups = lanes // tm_count, rows_y // tm_count
    lane = lax.broadcasted_iota(jnp.int32, (local_s, lanes), 1)
    places, offset, border_slabs = border_layout(rows_y, lanes, width)
    borders = [[jnp.zeros((local_s, lanes), F32) for _ in range(tm_count)] for _ in range(border_slabs)]
    for c, (slab, first_lane) in enumerate(places):
        copies[c].wait()

        def one_group(g, border, c=c, first_lane=first_lane):
            border = list(border)
            rows = []
            for q in range(tm_count):
                y = q * groups + g
                row = rows_ref[pl.ds(c * local_s * rows_y + y, local_s, stride=rows_y), :]
                rows.append(row)
                before = first_lane + y
                after = before + offset - (width + 1)
                moved = pltpu.roll(row, jnp.bitwise_and(before, lanes - 1), 1)
                moved_after = moved if offset == width + 1 else pltpu.roll(row, jnp.bitwise_and(after, lanes - 1), 1)
                for block in range(tm_count):
                    at_before = lane == jnp.bitwise_and(before + block * width - 1, lanes - 1)
                    at_after = lane == jnp.bitwise_and(after + (block + 1) * width, lanes - 1)
                    if moved is moved_after:
                        border[block] = jnp.where(jnp.logical_or(at_before, at_after), moved, border[block])
                    else:
                        border[block] = jnp.where(at_before, moved, jnp.where(at_after, moved_after, border[block]))
            for block, main in enumerate(exchange_blocks(rows, lane, width, lanes)):
                sorted_ref[block, g * 3 + c] = main
            return tuple(border)

        borders[slab] = lax.fori_loop(0, groups, one_group, tuple(borders[slab]))
    half = groups // 2 * 3
    for slab, border in enumerate(borders):
        for block in range(tm_count):
            sorted_ref[block, groups * 3 + slab] = border[block]
    for peer in range(tm_count):
        block = jnp.bitwise_xor(t, peer)
        out_refs[peer][...] = sorted_ref[block]
        out_refs[tm_count][peer] = sorted_ref[block, pl.ds(core * half, half)]
    copies[3].wait()
    copies[4].wait()
    for first in range(0, codes_ref.shape[0], lanes):
        here = pl.ds(first, lanes)
        codes_ref[here] = held_pairs_ref[0, here] * held_coeffs_ref.shape[1] + held_pairs_ref[1, here]


def mode_weights(coeffs_ref, local_s, tm_count):
    t, _, _ = place_of_device()
    ordered = jnp.concatenate(
        [
            coeffs_ref[pl.ds(pl.multiple_of(jnp.bitwise_xor(t, peer) * local_s, 8), local_s), :]
            for peer in range(tm_count)
        ],
        axis=0,
    )
    high, low = split_high_low(ordered.T)
    return jnp.concatenate([high, low, high, low], axis=1)


def modes_of(weights, slab):
    high, low = split_high_low(slab)
    return jnp.dot(weights, jnp.concatenate([high, high, low, low], axis=0), preferred_element_type=F32)


def store_projection(rhs_ref, place, mode_slab):
    high, low = split_high_low(mode_slab.T)
    modes, lanes = mode_slab.shape
    rhs_ref[place * lanes : (place + 1) * lanes, 0:modes] = high
    rhs_ref[place * lanes : (place + 1) * lanes, modes : 2 * modes] = low


def project(conv_ref, rhs_ref, block, places, lanes):
    both = None
    for place in range(0, places, 2):
        highs, lows = zip(
            *(split_high_low(conv_ref[pl.ds(place + k, block, stride=places), :]) for k in range(2))
        )
        lhs = jnp.concatenate([jnp.concatenate(highs, axis=1), jnp.concatenate(lows, axis=1)], axis=0)
        part = jnp.dot(lhs, rhs_ref[place * lanes : (place + 2) * lanes, :], preferred_element_type=F32)
        both = part if both is None else both + part
    modes = both.shape[1] // 2
    return (both[:block, :modes] + both[:block, modes:]) + (both[block:, :modes] + both[block:, modes:])


def for_pairs_of(codes_ref, peer, sizes, one_pair):
    chips, share, bits = sizes
    t, chip, core = place_of_device()
    first_chip = jnp.bitwise_xor(t, peer) * chips

    def one_share(ahead, _):
        base = ((first_chip + jnp.bitwise_xor(chip, ahead)) * 2 + core) * share

        def one(q, _):
            code = codes_ref[base + q]
            one_pair(ahead * share + q, lax.shift_right_logical(code, bits), jnp.bitwise_and(code, 2**bits - 1))
            return 0

        return lax.fori_loop(0, share, one, 0, unroll=True)

    lax.fori_loop(0, chips, one_share, 0)


def copy_of_codes(codes_ref, held_codes_ref, sem):
    copy = pltpu.make_async_copy(codes_ref, held_codes_ref, sem)
    copy.start()
    return copy


def inner_kernel(codes_ref, coeffs_ref, *refs, first_peer, sizes):
    local_s, block_rows, tm_count, chips, share, bits = sizes
    own, other = refs[:tm_count], refs[tm_count : 2 * tm_count]
    near_ref, carry_ref, slope_ref, rhs_ref, out_ref, conv_ref, slab_ref, held_codes_ref, sem = refs[2 * tm_count :]
    codes = copy_of_codes(codes_ref, held_codes_ref, sem)
    t, _, core = place_of_device()
    modes, lanes = coeffs_ref.shape[1], own[0].shape[2]
    height = 2 * block_rows
    weights = mode_weights(coeffs_ref, local_s, tm_count)

    def one_slab(index, _):
        own_slab = jnp.concatenate([piece[index] for piece in own], axis=0)
        other_slab = jnp.concatenate([piece[index] for piece in other], axis=0)
        is_first = core == 0
        both = jnp.concatenate(
            [jnp.where(is_first, own_slab, other_slab), jnp.where(is_first, other_slab, own_slab)], axis=1
        )
        result = modes_of(weights, both)
        slab_ref[0, index] = result[:, :lanes]
        slab_ref[1, index] = result[:, lanes:]
        return 0

    slabs = own[0].shape[0]
    lax.fori_loop(0, slabs, one_slab, 0, unroll=True)
    width, rows_y = lanes // tm_count, block_rows * tm_count
    lane = lax.broadcasted_iota(jnp.int32, (1, lanes), 1)
    part, column = lax.div(lane, width), lax.rem(lane, width)
    has_border = jnp.where(column == 0, -0.5, jnp.where(column == width - 1, 0.5, 0.0))
    places, offset, _ = border_layout(rows_y, lanes, width)
    border_of = jnp.where(column == 0, 0, offset) + t * width - 1 + part * block_rows
    border_lanes = lax.broadcasted_iota(jnp.int32, (2 * lanes, lanes), 0)
    border_lanes = jnp.where(border_lanes >= lanes, border_lanes - lanes, border_lanes)
    borders = []
    for slab in range(3 * block_rows, slabs):
        both = jnp.concatenate([slab_ref[0, slab], slab_ref[1, slab]], axis=0)
        borders.append(jnp.concatenate(split_high_low(both), axis=1))
    for c, (slab, first_lane) in enumerate(places):
        for row in range(block_rows):
            center = row * 3 + c
            if row % 2 == 0:
                picks = [
                    jnp.where(
                        border_lanes == jnp.bitwise_and(border_of + (first_lane + row + k), lanes - 1), has_border, 0.0
                    ).astype(BF16)
                    for k in range(2)
                ]
                border = jnp.dot(borders[slab], jnp.concatenate(picks, axis=1), preferred_element_type=F32)
            for plane in range(2):
                place = plane * block_rows + row
                value = slab_ref[plane, center]
                stream = slab_ref[1 - plane, center] * (0.5 if plane == 0 else -0.5)
                if row + 1 < block_rows:
                    above = slab_ref[plane, center + 3]
                else:
                    above = pltpu.roll(slab_ref[plane, c], lanes - width, 1)
                    above = jnp.where(lane < lanes - width, above, 0.0)
                if row > 0:
                    below = slab_ref[plane, center - 3]
                else:
                    below = pltpu.roll(slab_ref[plane, 3 * (block_rows - 1) + c], width, 1)
                    below = jnp.where(lane >= width, below, 0.0)
                normal = (above - below) * 0.5
                after = jnp.where(column < width - 1, pltpu.roll(value, lanes - 1, 1), 0.0)
                before = jnp.where(column > 0, pltpu.roll(value, 1, 1), 0.0)
                span = (after - before) * 0.5 + border[plane * modes : (plane + 1) * modes, row % 2 * lanes : (row % 2 + 1) * lanes]
                carry_ref[pl.ds(c * height + place, modes, stride=3 * height), :] = value
                for d, slope in enumerate((stream, normal, span)):
                    slope_ref[pl.ds((d * 3 + c) * height + place, modes, stride=9 * height), :] = slope
                store_projection(rhs_ref, c * height + place, value)
                if (plane == 1) == (row < block_rows // 2):
                    near_ref[center] = value

    codes.wait()

    def one_peer(number, _):
        @pl.when(number > 0)
        def _():
            out_ref[number - 1] = project(conv_ref, rhs_ref, chips * share, 3 * height, lanes)

        following = lax.rem(first_peer + number, tm_count)
        pick_inner(held_codes_ref, carry_ref, slope_ref, conv_ref, following, (chips, share, bits))
        return 0

    lax.fori_loop(0, out_ref.shape[0] + 1, one_peer, 0)


def pick_inner(codes_ref, carry_ref, slope_ref, conv_ref, peer, sizes):
    places = conv_ref.shape[0] // (sizes[0] * sizes[1])
    height = places // 3

    def one_pair(slot, i, j):
        carry = carry_ref[pl.ds(pl.multiple_of(i * places, 8), places), :]
        slope = slope_ref[pl.ds(pl.multiple_of(j * (3 * places), 8), 3 * places), :]
        rows = [
            sum(
                carry[d * height : (d + 1) * height] * slope[(d * 3 + c) * height : (d * 3 + c + 1) * height]
                for d in range(3)
            )
            for c in range(3)
        ]
        conv_ref[pl.ds(pl.multiple_of(slot * places, 8), places), :] = jnp.concatenate(rows, axis=0)

    for_pairs_of(codes_ref, peer, sizes, one_pair)


def rest_kernel(
    codes_ref, carry_ref, slope_ref, rhs_ref, picked_ref, out_ref, conv_ref, held_codes_ref, sem, *, sizes
):
    del picked_ref
    chips, share, _ = sizes
    codes = copy_of_codes(codes_ref, held_codes_ref, sem)
    block, lanes = chips * share, conv_ref.shape[1]
    places = conv_ref.shape[0] // block

    def one_peer(peer, _):
        out_ref[peer] = project(conv_ref, rhs_ref, block, places, lanes)

        @pl.when(peer == 0)
        def _():
            codes.wait()

        @pl.when(peer + 1 < out_ref.shape[0])
        def _():
            pick_inner(held_codes_ref, carry_ref, slope_ref, conv_ref, peer + 1, sizes)

        return 0

    lax.fori_loop(0, out_ref.shape[0], one_peer, 0)


def far_kernel(codes_ref, coeffs_ref, *refs, peer, sizes):
    local_s, block_rows, tm_count, chips, share, bits = sizes
    next_own, next_other, near_ref, inner_ref = refs[:tm_count], *refs[tm_count : tm_count + 3]
    carry_ref, slope_ref, rhs_ref, out_ref, conv_ref, held_codes_ref, sem = refs[tm_count + 3 :]
    codes = copy_of_codes(codes_ref, held_codes_ref, sem)
    _, _, core = place_of_device()
    is_first = core == 0
    modes, lanes = near_ref.shape[1:]
    height = 2 * block_rows
    half = block_rows // 2 * 3
    weights = mode_weights(coeffs_ref, local_s, tm_count)
    for slab in range(half):
        mine = jnp.concatenate([next_own[peer][slab] for peer in range(tm_count)], axis=0)
        theirs = jnp.concatenate([next_other[peer, slab] for peer in range(tm_count)], axis=0)
        after, before = jnp.where(is_first, theirs, mine), jnp.where(is_first, mine, theirs)
        result = modes_of(weights, jnp.concatenate([after, before], axis=1))
        row, c = divmod(slab, 3)
        edges = ((near_ref[slab], result[:, :lanes]), (result[:, lanes:], near_ref[half + slab]))
        for number, (low, high) in enumerate(edges):
            place = number * block_rows + 2 * row
            for at, value, across in ((place, low, high * 0.5), (place + 1, high, low * -0.5)):
                if c == 0:
                    carry_ref[pl.ds(at, modes, stride=height), :] = value
                slope_ref[pl.ds(c * height + at, modes, stride=3 * height), :] = across
                store_projection(rhs_ref, c * height + at, value)


    codes.wait()
    pick_edge(held_codes_ref, carry_ref, slope_ref, conv_ref, peer, (chips, share, bits))
    out_ref[...] = edge_sum(conv_ref, rhs_ref, inner_ref, peer)
    pick_edge(held_codes_ref, carry_ref, slope_ref, conv_ref, peer - 1, (chips, share, bits))


def pick_edge(codes_ref, carry_ref, slope_ref, conv_ref, peer, sizes):
    places = conv_ref.shape[0] // (sizes[0] * sizes[1])
    height = places // 3

    def one_pair(slot, i, j):
        carry = carry_ref[pl.ds(pl.multiple_of(i * height, 8), height), :]
        slope = slope_ref[pl.ds(pl.multiple_of(j * places, 8), places), :]
        rows = [carry * slope[c * height : (c + 1) * height] for c in range(3)]
        conv_ref[pl.ds(pl.multiple_of(slot * places, 8), places), :] = jnp.concatenate(rows, axis=0)

    for_pairs_of(codes_ref, peer, sizes, one_pair)


def edge_sum(picked_ref, rhs_ref, inner_ref, peer):
    block = inner_ref.shape[1]
    places = picked_ref.shape[0] // block
    return inner_ref[peer % inner_ref.shape[0]] + project(picked_ref, rhs_ref, block, places, picked_ref.shape[1])


def edge_kernel(
    codes_ref, carry_ref, slope_ref, rhs_ref, inner_ref, picked_ref, out_ref, conv_ref, held_codes_ref, sem, *,
    peer, sizes
):
    codes = copy_of_codes(codes_ref, held_codes_ref, sem)
    out_ref[...] = edge_sum(picked_ref, rhs_ref, inner_ref, peer)
    codes.wait()
    pick_edge(held_codes_ref, carry_ref, slope_ref, conv_ref, peer - 1, sizes)


def own_edge_kernel(rhs_ref, inner_ref, picked_ref, *refs):
    *arrived_refs, out_ref = refs
    total = edge_sum(picked_ref, rhs_ref, inner_ref, 0)
    for arrived_ref in arrived_refs:
        total = total + arrived_ref[...]
    out_ref[...] = total


def vmem_limit(mebibytes):
    return pltpu.CompilerParams(vmem_limit_bytes=mebibytes * 2**20)


def in_vmem(array):
    return pltpu.with_memory_space_constraint(array, pltpu.VMEM)


def shards(snapshots, coeffs, pair_table):
    tm_count, space_count = lax.axis_size("tm"), lax.axis_size("space")
    chips = space_count // 2
    local_s, _, _, rows_y, lanes = snapshots.shape
    modes = coeffs.shape[1]
    block_rows = rows_y // tm_count
    slabs = 3 * block_rows + border_layout(rows_y, lanes, lanes // tm_count)[2]
    share = pair_table.shape[0] // (tm_count * space_count)
    factor = float(space_count * rows_y * lanes) ** (-0.5)
    bits = modes.bit_length() - 1
    assert modes == 2**bits
    vmem = pl.BlockSpec(memory_space=pltpu.VMEM)
    block = chips * share
    height = 2 * block_rows
    depth = 3 * height * lanes

    swap = [(2 * chip + c, 2 * chip + 1 - c) for chip in range(chips) for c in range(2)]

    def across(peer):
        return [(i, i ^ peer) for i in range(tm_count)]

    with jax.named_scope("pack"):
        *packed, codes, held_coeffs = pl.pallas_call(
            functools.partial(pack_kernel, sizes=(local_s, rows_y, tm_count)),
            out_shape=[pltpu.VMEM((slabs, local_s, lanes), F32)] * tm_count
            + [
                pltpu.VMEM((tm_count, block_rows // 2 * 3, local_s, lanes), F32),
                pltpu.VMEM((pair_table.shape[0],), jnp.int32),
                pltpu.VMEM(coeffs.shape, F32),
            ],
            in_specs=[pl.BlockSpec(memory_space=pltpu.HBM)] * 3,
            out_specs=[vmem] * (tm_count + 3),
            scratch_shapes=[
                pltpu.VMEM((tm_count, slabs, local_s, lanes), F32),
                pltpu.VMEM((3, local_s, rows_y, lanes), F32),
                pltpu.VMEM((2, pair_table.shape[0]), jnp.int32),
                pltpu.SemaphoreType.DMA((5,)),
            ],
            compiler_params=vmem_limit(16),
        )(
            *[
                pltpu.with_memory_space_constraint(array, pltpu.HBM)
                for array in (snapshots.reshape(local_s, 3, rows_y, lanes), pair_table.T, coeffs)
            ]
        )
        codes, coeffs = in_vmem(codes), in_vmem(held_coeffs)
    with jax.named_scope("to_next_plane"):
        ring = [(place, (place + (1 if place % 2 else -1)) % space_count) for place in range(space_count)]
        across_edge = lax.ppermute(packed[tm_count], "space", ring)
    with jax.named_scope("to_columns"):
        own = [packed[0]] + [lax.ppermute(packed[peer], "tm", across(peer)) for peer in range(1, tm_count)]
    with jax.named_scope("next_to_columns"):
        across_edge, own[:3] = lax.optimization_barrier((across_edge, own[:3]))
        parts = [across_edge[peer] for peer in range(tm_count)]
        parts, own[3:] = lax.optimization_barrier((parts, own[3:]))
        next_own = [parts[0]] + [lax.ppermute(parts[peer], "tm", across(peer)) for peer in range(1, tm_count)]
    with jax.named_scope("to_other_core"):
        other = [lax.ppermute(piece, "space", swap) for piece in own]
    early = tm_count // 2
    picked = pltpu.VMEM((block * 3 * height, lanes), F32)
    held_codes = [pltpu.SMEM(codes.shape, jnp.int32), pltpu.SemaphoreType.DMA]
    groups = pltpu.VMEM((early, block, modes), F32)
    with jax.named_scope("inner_terms"):
        near, *inner_tables, early_sums, first_picked = pl.pallas_call(
            functools.partial(inner_kernel, first_peer=early, sizes=(local_s, block_rows, tm_count, chips, share, bits)),
            out_shape=[
                pltpu.VMEM((block_rows * 3, modes, lanes), F32),
                pltpu.VMEM((modes * 3 * height, lanes), F32),
                pltpu.VMEM((modes * 9 * height, lanes), F32),
                pltpu.VMEM((depth, 2 * modes), BF16),
                groups,
                picked,
            ],
            in_specs=[vmem] * (2 * tm_count + 2),
            out_specs=[vmem] * 6,
            scratch_shapes=[pltpu.VMEM((2, slabs, modes, lanes), F32)] + held_codes,
            compiler_params=vmem_limit(24),
            cost_estimate=pl.CostEstimate(flops=12 * 10**9, bytes_accessed=10**7, transcendentals=0),
        )(codes, coeffs, *[in_vmem(piece) for piece in (*own, *other)])
    with jax.named_scope("next_to_other_core"):
        next_own, inner_tables = lax.optimization_barrier((next_own, inner_tables))
        next_other = lax.ppermute(jnp.stack(next_own), "space", swap)
    with jax.named_scope("inner_terms"):
        late_sums, _ = pl.pallas_call(
            functools.partial(rest_kernel, sizes=(chips, share, bits)),
            out_shape=[groups, picked],
            in_specs=[vmem] * 5,
            out_specs=[vmem] * 2,
            input_output_aliases={4: 1},
            scratch_shapes=held_codes,
            compiler_params=vmem_limit(16),
            cost_estimate=pl.CostEstimate(flops=8 * 10**9, bytes_accessed=10**7, transcendentals=0),
        )(codes, *[in_vmem(table) for table in (*inner_tables, first_picked)])
    with jax.named_scope("edge_terms"):
        *tables, summed, next_picked = pl.pallas_call(
            functools.partial(
                far_kernel, peer=tm_count - 1, sizes=(local_s, block_rows, tm_count, chips, share, bits)
            ),
            out_shape=[
                pltpu.VMEM((modes * height, lanes), F32),
                pltpu.VMEM((modes * 3 * height, lanes), F32),
                pltpu.VMEM((depth, 2 * modes), BF16),
                pltpu.VMEM((block, modes), F32),
                picked,
            ],
            in_specs=[vmem] * (tm_count + 5),
            out_specs=[vmem] * 5,
            scratch_shapes=held_codes,
            compiler_params=vmem_limit(16),
        )(codes, coeffs, *[in_vmem(piece) for piece in (*next_own, next_other, near, early_sums)])
    arrived, taken = [], 2
    for peer in reversed(range(tm_count - 1)):
        with jax.named_scope("sum_over_columns"):
            arrived.append(lax.ppermute(summed, "tm", across(peer + 1)))
            if peer >= early:
                early_sums, _ = lax.optimization_barrier((early_sums, summed))
            else:
                late_sums, _ = lax.optimization_barrier((late_sums, summed))
        with jax.named_scope("edge_terms"):
            inner_sums = early_sums if peer >= early else late_sums
            edge_cost = pl.CostEstimate(flops=10**8, bytes_accessed=10**5, transcendentals=0)
            if peer:
                summed, next_picked = pl.pallas_call(
                    functools.partial(edge_kernel, peer=peer, sizes=(chips, share, bits)),
                    out_shape=[pltpu.VMEM((block, modes), F32), picked],
                    in_specs=[vmem] * 6,
                    out_specs=[vmem] * 2,
                    scratch_shapes=held_codes,
                    compiler_params=vmem_limit(16),
                    cost_estimate=edge_cost,
                )(codes, *[in_vmem(table) for table in (*tables, inner_sums, next_picked)])
            else:
                summed = pl.pallas_call(
                    own_edge_kernel,
                    out_shape=pltpu.VMEM((block, modes), F32),
                    in_specs=[vmem] * (3 + taken),
                    out_specs=vmem,
                    compiler_params=vmem_limit(16),
                    cost_estimate=edge_cost,
                )(*[in_vmem(table) for table in (tables[2], inner_sums, next_picked, *arrived[:taken])])
    with jax.named_scope("sum_over_columns"):
        for part in arrived[taken:]:
            summed = summed + part
    with jax.named_scope("sum_over_chips"):
        shares = summed.reshape(chips, share, modes)
        result = shares[0]
        for step in range(1, chips):
            pairing = [(2 * chip + c, 2 * (chip ^ step) + c) for chip in range(chips) for c in range(2)]
            result = result + lax.ppermute(shares[step], "space", pairing)
        return result * factor


def solution(mesh):
    placed = (P("tm", None, "space", None, None), P(), P())
    return jax.shard_map(
        shards, mesh=mesh, in_specs=placed, out_specs=P(("tm", "space"), None), check_vma=False
    )
```

```python
import functools

import jax
import jax.numpy as jnp
from jax import lax
from jax.experimental import pallas as pl
from jax.experimental.pallas import tpu as pltpu
from jax.sharding import PartitionSpec as P

F32 = jnp.float32
BF16 = jnp.bfloat16


def place_of_device():
    place = lax.axis_index("space")
    return lax.axis_index("tm"), lax.shift_right_logical(place, 1), jnp.bitwise_and(place, 1)


def split_high_low(values):
    high = values.astype(BF16)
    low = (values - high.astype(F32)).astype(BF16)
    return high, low


def border_layout(rows_y, lanes, width):
    per_run = (width + 1) // rows_y
    if per_run:
        run = width + 1 + per_run * rows_y
        firsts = [c // per_run * run + c % per_run * rows_y for c in range(3)]
        if firsts[2] + width + 1 + rows_y <= lanes:
            return [(0, first) for first in firsts], width + 1, 1
    per_slab = lanes // (2 * rows_y)
    places = [(c // per_slab, c % per_slab * 2 * rows_y) for c in range(3)]
    return places, rows_y, places[2][0] + 1


def exchange_blocks(rows, lane, width, lanes):
    rows = list(rows)
    step = len(rows) // 2
    while step:
        keeps = jnp.bitwise_and(lane, step * width) == 0
        for low in range(len(rows)):
            if low & step == 0:
                first, second = rows[low], rows[low + step]
                rows[low] = jnp.where(keeps, first, pltpu.roll(second, step * width, 1))
                rows[low + step] = jnp.where(keeps, pltpu.roll(first, lanes - step * width, 1), second)
        step //= 2
    return rows


def pack_kernel(field_ref, pairs_ref, coeffs_ref, *refs, sizes):
    *out_refs, codes_ref, held_coeffs_ref, sorted_ref, held_ref, held_pairs_ref, sems = refs
    local_s, rows_y, tm_count = sizes
    lanes = field_ref.shape[3]
    copies = [pltpu.make_async_copy(field_ref.at[:, c], held_ref.at[c], sems.at[c]) for c in range(3)]
    copies.append(pltpu.make_async_copy(pairs_ref, held_pairs_ref, sems.at[3]))
    copies.append(pltpu.make_async_copy(coeffs_ref, held_coeffs_ref, sems.at[4]))
    for copy in copies:
        copy.start()
    rows_ref = held_ref.reshape(3 * local_s * rows_y, lanes)
    t, _, core = place_of_device()
    width, groups = lanes // tm_count, rows_y // tm_count
    lane = lax.broadcasted_iota(jnp.int32, (local_s, lanes), 1)
    places, offset, border_slabs = border_layout(rows_y, lanes, width)
    borders = [[jnp.zeros((local_s, lanes), F32) for _ in range(tm_count)] for _ in range(border_slabs)]
    for c, (slab, first_lane) in enumerate(places):
        copies[c].wait()

        def one_group(g, border, c=c, first_lane=first_lane):
            border = list(border)
            rows = []
            for q in range(tm_count):
                y = q * groups + g
                row = rows_ref[pl.ds(c * local_s * rows_y + y, local_s, stride=rows_y), :]
                rows.append(row)
                before = first_lane + y
                after = before + offset - (width + 1)
                moved = pltpu.roll(row, jnp.bitwise_and(before, lanes - 1), 1)
                moved_after = moved if offset == width + 1 else pltpu.roll(row, jnp.bitwise_and(after, lanes - 1), 1)
                for block in range(tm_count):
                    at_before = lane == jnp.bitwise_and(before + block * width - 1, lanes - 1)
                    at_after = lane == jnp.bitwise_and(after + (block + 1) * width, lanes - 1)
                    if moved is moved_after:
                        border[block] = jnp.where(jnp.logical_or(at_before, at_after), moved, border[block])
                    else:
                        border[block] = jnp.where(at_before, moved, jnp.where(at_after, moved_after, border[block]))
            for block, main in enumerate(exchange_blocks(rows, lane, width, lanes)):
                sorted_ref[block, g * 3 + c] = main
            return tuple(border)

        borders[slab] = lax.fori_loop(0, groups, one_group, tuple(borders[slab]))
    half = groups // 2 * 3
    for slab, border in enumerate(borders):
        for block in range(tm_count):
            sorted_ref[block, groups * 3 + slab] = border[block]
    for peer in range(tm_count):
        block = jnp.bitwise_xor(t, peer)
        out_refs[peer][...] = sorted_ref[block]
        out_refs[tm_count][peer] = sorted_ref[peer, pl.ds(core * half, half)]
    copies[3].wait()
    copies[4].wait()
    for first in range(0, codes_ref.shape[0], lanes):
        here = pl.ds(first, lanes)
        codes_ref[here] = held_pairs_ref[0, here] * held_coeffs_ref.shape[1] + held_pairs_ref[1, here]


def mode_weights(coeffs):
    high, low = split_high_low(coeffs.T)
    return jnp.concatenate([high, low, high, low], axis=1)


def modes_of(weights, slab):
    high, low = split_high_low(slab)
    return jnp.dot(weights, jnp.concatenate([high, high, low, low], axis=0), preferred_element_type=F32)


def store_projection(rhs_ref, place, mode_slab):
    high, low = split_high_low(mode_slab.T)
    modes, lanes = mode_slab.shape
    rhs_ref[place * lanes : (place + 1) * lanes, 0:modes] = high
    rhs_ref[place * lanes : (place + 1) * lanes, modes : 2 * modes] = low


def project(conv_ref, rhs_ref, block, places, lanes):
    both = None
    for place in range(0, places, 2):
        highs, lows = zip(
            *(split_high_low(conv_ref[pl.ds(place + k, block, stride=places), :]) for k in range(2))
        )
        lhs = jnp.concatenate([jnp.concatenate(highs, axis=1), jnp.concatenate(lows, axis=1)], axis=0)
        part = jnp.dot(lhs, rhs_ref[place * lanes : (place + 2) * lanes, :], preferred_element_type=F32)
        both = part if both is None else both + part
    modes = both.shape[1] // 2
    return (both[:block, :modes] + both[:block, modes:]) + (both[block:, :modes] + both[block:, modes:])


def for_pairs_of(codes_ref, peer, sizes, one_pair):
    chips, share, bits = sizes
    t, chip, core = place_of_device()
    first_chip = jnp.bitwise_xor(t, peer) * chips

    def one_share(ahead, _):
        base = ((first_chip + jnp.bitwise_xor(chip, ahead)) * 2 + core) * share

        def one(q, _):
            code = codes_ref[base + q]
            one_pair(ahead * share + q, lax.shift_right_logical(code, bits), jnp.bitwise_and(code, 2**bits - 1))
            return 0

        return lax.fori_loop(0, share, one, 0, unroll=True)

    lax.fori_loop(0, chips, one_share, 0)


def copy_of_codes(codes_ref, held_codes_ref, sem):
    copy = pltpu.make_async_copy(codes_ref, held_codes_ref, sem)
    copy.start()
    return copy


def inner_kernel(codes_ref, coeffs_ref, *refs, first_peer, sizes):
    local_s, block_rows, tm_count, chips, share, bits = sizes
    own, other = refs[:tm_count], refs[tm_count : 2 * tm_count]
    near_ref, carry_ref, slope_ref, rhs_ref, out_ref, conv_ref, slab_ref, held_codes_ref, sem = refs[2 * tm_count :]
    codes = copy_of_codes(codes_ref, held_codes_ref, sem)
    t, _, core = place_of_device()
    modes, lanes = coeffs_ref.shape[1], own[0].shape[2]
    height = 2 * block_rows
    blocks = [pl.ds(pl.multiple_of(jnp.bitwise_xor(t, peer) * local_s, 8), local_s) for peer in range(tm_count)]
    weights = mode_weights(jnp.concatenate([coeffs_ref[rows, :] for rows in blocks], axis=0))

    def one_slab(index, _):
        own_slab = jnp.concatenate([piece[index] for piece in own], axis=0)
        other_slab = jnp.concatenate([piece[index] for piece in other], axis=0)
        is_first = core == 0
        both = jnp.concatenate(
            [jnp.where(is_first, own_slab, other_slab), jnp.where(is_first, other_slab, own_slab)], axis=1
        )
        result = modes_of(weights, both)
        slab_ref[0, index] = result[:, :lanes]
        slab_ref[1, index] = result[:, lanes:]
        return 0

    slabs = own[0].shape[0]
    lax.fori_loop(0, slabs, one_slab, 0, unroll=True)
    width, rows_y = lanes // tm_count, block_rows * tm_count
    lane = lax.broadcasted_iota(jnp.int32, (1, lanes), 1)
    part, column = lax.div(lane, width), lax.rem(lane, width)
    has_border = jnp.where(column == 0, -0.5, jnp.where(column == width - 1, 0.5, 0.0))
    places, offset, _ = border_layout(rows_y, lanes, width)
    border_of = jnp.where(column == 0, 0, offset) + t * width - 1 + part * block_rows
    border_lanes = lax.broadcasted_iota(jnp.int32, (2 * lanes, lanes), 0)
    border_lanes = jnp.where(border_lanes >= lanes, border_lanes - lanes, border_lanes)
    borders = []
    for slab in range(3 * block_rows, slabs):
        both = jnp.concatenate([slab_ref[0, slab], slab_ref[1, slab]], axis=0)
        borders.append(jnp.concatenate(split_high_low(both), axis=1))
    for c, (slab, first_lane) in enumerate(places):
        for row in range(block_rows):
            center = row * 3 + c
            if row % 2 == 0:
                picks = [
                    jnp.where(
                        border_lanes == jnp.bitwise_and(border_of + (first_lane + row + k), lanes - 1), has_border, 0.0
                    ).astype(BF16)
                    for k in range(2)
                ]
                border = jnp.dot(borders[slab], jnp.concatenate(picks, axis=1), preferred_element_type=F32)
            for plane in range(2):
                place = plane * block_rows + row
                value = slab_ref[plane, center]
                stream = slab_ref[1 - plane, center] * (0.5 if plane == 0 else -0.5)
                if row + 1 < block_rows:
                    above = slab_ref[plane, center + 3]
                else:
                    above = pltpu.roll(slab_ref[plane, c], lanes - width, 1)
                    above = jnp.where(lane < lanes - width, above, 0.0)
                if row > 0:
                    below = slab_ref[plane, center - 3]
                else:
                    below = pltpu.roll(slab_ref[plane, 3 * (block_rows - 1) + c], width, 1)
                    below = jnp.where(lane >= width, below, 0.0)
                normal = (above - below) * 0.5
                after = jnp.where(column < width - 1, pltpu.roll(value, lanes - 1, 1), 0.0)
                before = jnp.where(column > 0, pltpu.roll(value, 1, 1), 0.0)
                span = (after - before) * 0.5 + border[plane * modes : (plane + 1) * modes, row % 2 * lanes : (row % 2 + 1) * lanes]
                carry_ref[pl.ds(c * height + place, modes, stride=3 * height), :] = value
                for d, slope in enumerate((stream, normal, span)):
                    slope_ref[pl.ds((d * 3 + c) * height + place, modes, stride=9 * height), :] = slope
                store_projection(rhs_ref, c * height + place, value)
                if (plane == 1) == (row < block_rows // 2):
                    near_ref[center] = value

    codes.wait()

    def one_peer(number, _):
        @pl.when(number > 0)
        def _():
            out_ref[number - 1] = project(conv_ref, rhs_ref, chips * share, 3 * height, lanes)

        following = lax.rem(first_peer + number, tm_count)
        pick_inner(held_codes_ref, carry_ref, slope_ref, conv_ref, following, (chips, share, bits))
        return 0

    lax.fori_loop(0, out_ref.shape[0] + 1, one_peer, 0)


def pick_inner(codes_ref, carry_ref, slope_ref, conv_ref, peer, sizes):
    places = conv_ref.shape[0] // (sizes[0] * sizes[1])
    height = places // 3

    def one_pair(slot, i, j):
        carry = carry_ref[pl.ds(pl.multiple_of(i * places, 8), places), :]
        slope = slope_ref[pl.ds(pl.multiple_of(j * (3 * places), 8), 3 * places), :]
        rows = [
            sum(
                carry[d * height : (d + 1) * height] * slope[(d * 3 + c) * height : (d * 3 + c + 1) * height]
                for d in range(3)
            )
            for c in range(3)
        ]
        conv_ref[pl.ds(pl.multiple_of(slot * places, 8), places), :] = jnp.concatenate(rows, axis=0)

    for_pairs_of(codes_ref, peer, sizes, one_pair)


def rest_kernel(
    codes_ref, carry_ref, slope_ref, rhs_ref, picked_ref, out_ref, conv_ref, held_codes_ref, sem, *, sizes
):
    del picked_ref
    chips, share, _ = sizes
    codes = copy_of_codes(codes_ref, held_codes_ref, sem)
    block, lanes = chips * share, conv_ref.shape[1]
    places = conv_ref.shape[0] // block

    def one_peer(peer, _):
        out_ref[peer] = project(conv_ref, rhs_ref, block, places, lanes)

        @pl.when(peer == 0)
        def _():
            codes.wait()

        @pl.when(peer + 1 < out_ref.shape[0])
        def _():
            pick_inner(held_codes_ref, carry_ref, slope_ref, conv_ref, peer + 1, sizes)

        return 0

    lax.fori_loop(0, out_ref.shape[0], one_peer, 0)


def far_kernel(codes_ref, coeffs_ref, *refs, peer, sizes):
    local_s, block_rows, tm_count, chips, share, bits = sizes
    next_own, next_other, near_ref, inner_ref = refs[:4]
    carry_ref, slope_ref, rhs_ref, out_ref, conv_ref, held_codes_ref, sem = refs[4:]
    codes = copy_of_codes(codes_ref, held_codes_ref, sem)
    _, _, core = place_of_device()
    is_first = core == 0
    modes, lanes = near_ref.shape[1:]
    height = 2 * block_rows
    half = block_rows // 2 * 3
    weights = mode_weights(coeffs_ref[...])
    for slab in range(half):
        mine = jnp.concatenate([next_own[peer, slab] for peer in range(tm_count)], axis=0)
        theirs = jnp.concatenate([next_other[peer, slab] for peer in range(tm_count)], axis=0)
        after, before = jnp.where(is_first, theirs, mine), jnp.where(is_first, mine, theirs)
        result = modes_of(weights, jnp.concatenate([after, before], axis=1))
        row, c = divmod(slab, 3)
        edges = ((near_ref[slab], result[:, :lanes]), (result[:, lanes:], near_ref[half + slab]))
        for number, (low, high) in enumerate(edges):
            place = number * block_rows + 2 * row
            for at, value, across in ((place, low, high * 0.5), (place + 1, high, low * -0.5)):
                if c == 0:
                    carry_ref[pl.ds(at, modes, stride=height), :] = value
                slope_ref[pl.ds(c * height + at, modes, stride=3 * height), :] = across
                store_projection(rhs_ref, c * height + at, value)


    codes.wait()
    pick_edge(held_codes_ref, carry_ref, slope_ref, conv_ref, peer, (chips, share, bits))
    out_ref[...] = edge_sum(conv_ref, rhs_ref, inner_ref, peer)
    pick_edge(held_codes_ref, carry_ref, slope_ref, conv_ref, peer - 1, (chips, share, bits))


def pick_edge(codes_ref, carry_ref, slope_ref, conv_ref, peer, sizes):
    places = conv_ref.shape[0] // (sizes[0] * sizes[1])
    height = places // 3

    def one_pair(slot, i, j):
        carry = carry_ref[pl.ds(pl.multiple_of(i * height, 8), height), :]
        slope = slope_ref[pl.ds(pl.multiple_of(j * places, 8), places), :]
        rows = [carry * slope[c * height : (c + 1) * height] for c in range(3)]
        conv_ref[pl.ds(pl.multiple_of(slot * places, 8), places), :] = jnp.concatenate(rows, axis=0)

    for_pairs_of(codes_ref, peer, sizes, one_pair)


def edge_sum(picked_ref, rhs_ref, inner_ref, peer):
    block = inner_ref.shape[1]
    places = picked_ref.shape[0] // block
    return inner_ref[peer % inner_ref.shape[0]] + project(picked_ref, rhs_ref, block, places, picked_ref.shape[1])


def edge_kernel(
    codes_ref, carry_ref, slope_ref, rhs_ref, inner_ref, picked_ref, out_ref, conv_ref, held_codes_ref, sem, *,
    peer, sizes
):
    codes = copy_of_codes(codes_ref, held_codes_ref, sem)
    out_ref[...] = edge_sum(picked_ref, rhs_ref, inner_ref, peer)
    codes.wait()
    pick_edge(held_codes_ref, carry_ref, slope_ref, conv_ref, peer - 1, sizes)


def own_edge_kernel(rhs_ref, inner_ref, picked_ref, *refs):
    *arrived_refs, out_ref = refs
    total = edge_sum(picked_ref, rhs_ref, inner_ref, 0)
    for arrived_ref in arrived_refs:
        total = total + arrived_ref[...]
    out_ref[...] = total


def vmem_limit(mebibytes):
    return pltpu.CompilerParams(vmem_limit_bytes=mebibytes * 2**20)


def in_vmem(array):
    return pltpu.with_memory_space_constraint(array, pltpu.VMEM)


def shards(snapshots, coeffs, pair_table):
    tm_count, space_count = lax.axis_size("tm"), lax.axis_size("space")
    chips = space_count // 2
    local_s, _, _, rows_y, lanes = snapshots.shape
    modes = coeffs.shape[1]
    block_rows = rows_y // tm_count
    slabs = 3 * block_rows + border_layout(rows_y, lanes, lanes // tm_count)[2]
    share = pair_table.shape[0] // (tm_count * space_count)
    factor = float(space_count * rows_y * lanes) ** (-0.5)
    bits = modes.bit_length() - 1
    assert modes == 2**bits
    vmem = pl.BlockSpec(memory_space=pltpu.VMEM)
    block = chips * share
    height = 2 * block_rows
    depth = 3 * height * lanes

    swap = [(2 * chip + c, 2 * chip + 1 - c) for chip in range(chips) for c in range(2)]

    def across(peer):
        return [(i, i ^ peer) for i in range(tm_count)]

    with jax.named_scope("pack"):
        *packed, codes, held_coeffs = pl.pallas_call(
            functools.partial(pack_kernel, sizes=(local_s, rows_y, tm_count)),
            out_shape=[pltpu.VMEM((slabs, local_s, lanes), F32)] * tm_count
            + [
                pltpu.VMEM((tm_count, block_rows // 2 * 3, local_s, lanes), F32),
                pltpu.VMEM((pair_table.shape[0],), jnp.int32),
                pltpu.VMEM(coeffs.shape, F32),
            ],
            in_specs=[pl.BlockSpec(memory_space=pltpu.HBM)] * 3,
            out_specs=[vmem] * (tm_count + 3),
            scratch_shapes=[
                pltpu.VMEM((tm_count, slabs, local_s, lanes), F32),
                pltpu.VMEM((3, local_s, rows_y, lanes), F32),
                pltpu.VMEM((2, pair_table.shape[0]), jnp.int32),
                pltpu.SemaphoreType.DMA((5,)),
            ],
            compiler_params=vmem_limit(16),
        )(
            *[
                pltpu.with_memory_space_constraint(array, pltpu.HBM)
                for array in (snapshots.reshape(local_s, 3, rows_y, lanes), pair_table.T, coeffs)
            ]
        )
        codes, coeffs = in_vmem(codes), in_vmem(held_coeffs)
    with jax.named_scope("to_next_plane"):
        ring = [(place, (place + (1 if place % 2 else -1)) % space_count) for place in range(space_count)]
        across_edge = lax.ppermute(packed[tm_count], "space", ring)
    with jax.named_scope("to_columns"):
        own = [packed[0]] + [lax.ppermute(packed[peer], "tm", across(peer)) for peer in range(1, tm_count)]
    with jax.named_scope("next_to_columns"):
        across_edge, own[:3] = lax.optimization_barrier((across_edge, own[:3]))
        next_own = lax.all_to_all(across_edge, "tm", 0, 0, tiled=True)
    with jax.named_scope("to_other_core"):
        other = [lax.ppermute(piece, "space", swap) for piece in own]
    early = tm_count // 2
    picked = pltpu.VMEM((block * 3 * height, lanes), F32)
    held_codes = [pltpu.SMEM(codes.shape, jnp.int32), pltpu.SemaphoreType.DMA]
    groups = pltpu.VMEM((early, block, modes), F32)
    with jax.named_scope("inner_terms"):
        near, *inner_tables, early_sums, first_picked = pl.pallas_call(
            functools.partial(inner_kernel, first_peer=early, sizes=(local_s, block_rows, tm_count, chips, share, bits)),
            out_shape=[
                pltpu.VMEM((block_rows * 3, modes, lanes), F32),
                pltpu.VMEM((modes * 3 * height, lanes), F32),
                pltpu.VMEM((modes * 9 * height, lanes), F32),
                pltpu.VMEM((depth, 2 * modes), BF16),
                groups,
                picked,
            ],
            in_specs=[vmem] * (2 * tm_count + 2),
            out_specs=[vmem] * 6,
            scratch_shapes=[pltpu.VMEM((2, slabs, modes, lanes), F32)] + held_codes,
            compiler_params=vmem_limit(24),
            cost_estimate=pl.CostEstimate(flops=12 * 10**9, bytes_accessed=10**7, transcendentals=0),
        )(codes, coeffs, *[in_vmem(piece) for piece in (*own, *other)])
    with jax.named_scope("next_to_other_core"):
        next_own, inner_tables = lax.optimization_barrier((next_own, inner_tables))
        next_other = lax.ppermute(next_own, "space", swap)
    with jax.named_scope("inner_terms"):
        late_sums, _ = pl.pallas_call(
            functools.partial(rest_kernel, sizes=(chips, share, bits)),
            out_shape=[groups, picked],
            in_specs=[vmem] * 5,
            out_specs=[vmem] * 2,
            input_output_aliases={4: 1},
            scratch_shapes=held_codes,
            compiler_params=vmem_limit(16),
            cost_estimate=pl.CostEstimate(flops=8 * 10**9, bytes_accessed=10**7, transcendentals=0),
        )(codes, *[in_vmem(table) for table in (*inner_tables, first_picked)])
    with jax.named_scope("edge_terms"):
        *tables, summed, next_picked = pl.pallas_call(
            functools.partial(
                far_kernel, peer=tm_count - 1, sizes=(local_s, block_rows, tm_count, chips, share, bits)
            ),
            out_shape=[
                pltpu.VMEM((modes * height, lanes), F32),
                pltpu.VMEM((modes * 3 * height, lanes), F32),
                pltpu.VMEM((depth, 2 * modes), BF16),
                pltpu.VMEM((block, modes), F32),
                picked,
            ],
            in_specs=[vmem] * 6,
            out_specs=[vmem] * 5,
            scratch_shapes=held_codes,
            compiler_params=vmem_limit(16),
        )(codes, coeffs, *[in_vmem(piece) for piece in (next_own, next_other, near, early_sums)])
    arrived, taken = [], 2
    for peer in reversed(range(tm_count - 1)):
        with jax.named_scope("sum_over_columns"):
            arrived.append(lax.ppermute(summed, "tm", across(peer + 1)))
            if peer >= early:
                early_sums, _ = lax.optimization_barrier((early_sums, summed))
            else:
                late_sums, _ = lax.optimization_barrier((late_sums, summed))
        with jax.named_scope("edge_terms"):
            inner_sums = early_sums if peer >= early else late_sums
            edge_cost = pl.CostEstimate(flops=10**8, bytes_accessed=10**5, transcendentals=0)
            if peer:
                summed, next_picked = pl.pallas_call(
                    functools.partial(edge_kernel, peer=peer, sizes=(chips, share, bits)),
                    out_shape=[pltpu.VMEM((block, modes), F32), picked],
                    in_specs=[vmem] * 6,
                    out_specs=[vmem] * 2,
                    scratch_shapes=held_codes,
                    compiler_params=vmem_limit(16),
                    cost_estimate=edge_cost,
                )(codes, *[in_vmem(table) for table in (*tables, inner_sums, next_picked)])
            else:
                summed = pl.pallas_call(
                    own_edge_kernel,
                    out_shape=pltpu.VMEM((block, modes), F32),
                    in_specs=[vmem] * (3 + taken),
                    out_specs=vmem,
                    compiler_params=vmem_limit(16),
                    cost_estimate=edge_cost,
                )(*[in_vmem(table) for table in (tables[2], inner_sums, next_picked, *arrived[:taken])])
    with jax.named_scope("sum_over_columns"):
        for part in arrived[taken:]:
            summed = summed + part
    with jax.named_scope("sum_over_chips"):
        shares = summed.reshape(chips, share, modes)
        result = shares[0]
        for step in range(1, chips):
            pairing = [(2 * chip + c, 2 * (chip ^ step) + c) for chip in range(chips) for c in range(2)]
            result = result + lax.ppermute(shares[step], "space", pairing)
        return result * factor


def solution(mesh):
    placed = (P("tm", None, "space", None, None), P(), P())
    return jax.shard_map(
        shards, mesh=mesh, in_specs=placed, out_specs=P(("tm", "space"), None), check_vma=False
    )
```

```python
import functools

import jax
import jax.numpy as jnp
from jax import lax
from jax.experimental import pallas as pl
from jax.experimental.pallas import tpu as pltpu
from jax.sharding import PartitionSpec as P

F32 = jnp.float32
BF16 = jnp.bfloat16


def place_of_device():
    place = lax.axis_index("space")
    return lax.axis_index("tm"), lax.shift_right_logical(place, 1), jnp.bitwise_and(place, 1)


def split_high_low(values):
    high = values.astype(BF16)
    low = (values - high.astype(F32)).astype(BF16)
    return high, low


def border_layout(rows_y, lanes, width):
    per_run = (width + 1) // rows_y
    if per_run:
        run = width + 1 + per_run * rows_y
        firsts = [c // per_run * run + c % per_run * rows_y for c in range(3)]
        if firsts[2] + width + 1 + rows_y <= lanes:
            return [(0, first) for first in firsts], width + 1, 1
    per_slab = lanes // (2 * rows_y)
    places = [(c // per_slab, c % per_slab * 2 * rows_y) for c in range(3)]
    return places, rows_y, places[2][0] + 1


def exchange_blocks(rows, lane, width, lanes):
    rows = list(rows)
    step = len(rows) // 2
    while step:
        keeps = jnp.bitwise_and(lane, step * width) == 0
        for low in range(len(rows)):
            if low & step == 0:
                first, second = rows[low], rows[low + step]
                rows[low] = jnp.where(keeps, first, pltpu.roll(second, step * width, 1))
                rows[low + step] = jnp.where(keeps, pltpu.roll(first, lanes - step * width, 1), second)
        step //= 2
    return rows


def pack_kernel(field_ref, pairs_ref, coeffs_ref, *refs, sizes):
    *out_refs, codes_ref, held_coeffs_ref, sorted_ref, held_ref, held_pairs_ref, sems = refs
    local_s, rows_y, tm_count = sizes
    lanes = field_ref.shape[3]
    copies = [pltpu.make_async_copy(field_ref.at[:, c], held_ref.at[c], sems.at[c]) for c in range(3)]
    copies.append(pltpu.make_async_copy(pairs_ref, held_pairs_ref, sems.at[3]))
    copies.append(pltpu.make_async_copy(coeffs_ref, held_coeffs_ref, sems.at[4]))
    for copy in copies:
        copy.start()
    rows_ref = held_ref.reshape(3 * local_s * rows_y, lanes)
    t, _, core = place_of_device()
    width, groups = lanes // tm_count, rows_y // tm_count
    lane = lax.broadcasted_iota(jnp.int32, (local_s, lanes), 1)
    places, offset, border_slabs = border_layout(rows_y, lanes, width)
    borders = [[jnp.zeros((local_s, lanes), F32) for _ in range(tm_count)] for _ in range(border_slabs)]
    for c, (slab, first_lane) in enumerate(places):
        copies[c].wait()

        def one_group(g, border, c=c, first_lane=first_lane):
            border = list(border)
            rows = []
            for q in range(tm_count):
                y = q * groups + g
                row = rows_ref[pl.ds(c * local_s * rows_y + y, local_s, stride=rows_y), :]
                rows.append(row)
                before = first_lane + y
                after = before + offset - (width + 1)
                moved = pltpu.roll(row, jnp.bitwise_and(before, lanes - 1), 1)
                moved_after = moved if offset == width + 1 else pltpu.roll(row, jnp.bitwise_and(after, lanes - 1), 1)
                for block in range(tm_count):
                    at_before = lane == jnp.bitwise_and(before + block * width - 1, lanes - 1)
                    at_after = lane == jnp.bitwise_and(after + (block + 1) * width, lanes - 1)
                    if moved is moved_after:
                        border[block] = jnp.where(jnp.logical_or(at_before, at_after), moved, border[block])
                    else:
                        border[block] = jnp.where(at_before, moved, jnp.where(at_after, moved_after, border[block]))
            for block, main in enumerate(exchange_blocks(rows, lane, width, lanes)):
                sorted_ref[block, g * 3 + c] = main
            return tuple(border)

        borders[slab] = lax.fori_loop(0, groups, one_group, tuple(borders[slab]), unroll=True)
    half = groups // 2 * 3
    for slab, border in enumerate(borders):
        for block in range(tm_count):
            sorted_ref[block, groups * 3 + slab] = border[block]
    for peer in range(tm_count):
        block = jnp.bitwise_xor(t, peer)
        out_refs[peer][...] = sorted_ref[block]
        out_refs[tm_count][peer] = sorted_ref[block, pl.ds(core * half, half)]
    copies[3].wait()
    copies[4].wait()
    for first in range(0, codes_ref.shape[0], lanes):
        here = pl.ds(first, lanes)
        codes_ref[here] = held_pairs_ref[0, here] * held_coeffs_ref.shape[1] + held_pairs_ref[1, here]


def mode_weights(coeffs_ref, local_s, tm_count):
    t, _, _ = place_of_device()
    ordered = jnp.concatenate(
        [
            coeffs_ref[pl.ds(pl.multiple_of(jnp.bitwise_xor(t, peer) * local_s, 8), local_s), :]
            for peer in range(tm_count)
        ],
        axis=0,
    )
    high, low = split_high_low(ordered.T)
    return jnp.concatenate([high, low, high, low], axis=1)


def modes_of(weights, slab):
    high, low = split_high_low(slab)
    return jnp.dot(weights, jnp.concatenate([high, high, low, low], axis=0), preferred_element_type=F32)


def store_projection(rhs_ref, place, mode_slab):
    high, low = split_high_low(mode_slab.T)
    modes, lanes = mode_slab.shape
    rhs_ref[place * lanes : (place + 1) * lanes, 0:modes] = high
    rhs_ref[place * lanes : (place + 1) * lanes, modes : 2 * modes] = low


def project(conv_ref, rhs_ref, block, places, lanes):
    both = None
    for place in range(0, places, 2):
        highs, lows = zip(
            *(split_high_low(conv_ref[pl.ds(place + k, block, stride=places), :]) for k in range(2))
        )
        lhs = jnp.concatenate([jnp.concatenate(highs, axis=1), jnp.concatenate(lows, axis=1)], axis=0)
        part = jnp.dot(lhs, rhs_ref[place * lanes : (place + 2) * lanes, :], preferred_element_type=F32)
        both = part if both is None else both + part
    modes = both.shape[1] // 2
    return (both[:block, :modes] + both[:block, modes:]) + (both[block:, :modes] + both[block:, modes:])


def for_pairs_of(codes_ref, peer, sizes, one_pair):
    chips, share, bits = sizes
    t, chip, core = place_of_device()
    first_chip = jnp.bitwise_xor(t, peer) * chips

    def one_share(ahead, _):
        base = ((first_chip + jnp.bitwise_xor(chip, ahead)) * 2 + core) * share

        def one(q, _):
            code = codes_ref[base + q]
            one_pair(ahead * share + q, lax.shift_right_logical(code, bits), jnp.bitwise_and(code, 2**bits - 1))
            return 0

        return lax.fori_loop(0, share, one, 0, unroll=True)

    lax.fori_loop(0, chips, one_share, 0)


def copy_of_codes(codes_ref, held_codes_ref, sem):
    copy = pltpu.make_async_copy(codes_ref, held_codes_ref, sem)
    copy.start()
    return copy


def inner_kernel(codes_ref, coeffs_ref, *refs, first_peer, sizes):
    local_s, block_rows, tm_count, chips, share, bits = sizes
    own, other = refs[:tm_count], refs[tm_count : 2 * tm_count]
    near_ref, carry_ref, slope_ref, rhs_ref, out_ref, conv_ref, slab_ref, held_codes_ref, sem = refs[2 * tm_count :]
    codes = copy_of_codes(codes_ref, held_codes_ref, sem)
    t, _, core = place_of_device()
    modes, lanes = coeffs_ref.shape[1], own[0].shape[2]
    height = 2 * block_rows
    weights = mode_weights(coeffs_ref, local_s, tm_count)

    def one_slab(index, _):
        own_slab = jnp.concatenate([piece[index] for piece in own], axis=0)
        other_slab = jnp.concatenate([piece[index] for piece in other], axis=0)
        is_first = core == 0
        both = jnp.concatenate(
            [jnp.where(is_first, own_slab, other_slab), jnp.where(is_first, other_slab, own_slab)], axis=1
        )
        result = modes_of(weights, both)
        slab_ref[0, index] = result[:, :lanes]
        slab_ref[1, index] = result[:, lanes:]
        return 0

    slabs = own[0].shape[0]
    lax.fori_loop(0, slabs, one_slab, 0, unroll=True)
    width, rows_y = lanes // tm_count, block_rows * tm_count
    lane = lax.broadcasted_iota(jnp.int32, (1, lanes), 1)
    part, column = lax.div(lane, width), lax.rem(lane, width)
    has_border = jnp.where(column == 0, -0.5, jnp.where(column == width - 1, 0.5, 0.0))
    places, offset, _ = border_layout(rows_y, lanes, width)
    border_of = jnp.where(column == 0, 0, offset) + t * width - 1 + part * block_rows
    border_lanes = lax.broadcasted_iota(jnp.int32, (2 * lanes, lanes), 0)
    border_lanes = jnp.where(border_lanes >= lanes, border_lanes - lanes, border_lanes)
    borders = []
    for slab in range(3 * block_rows, slabs):
        both = jnp.concatenate([slab_ref[0, slab], slab_ref[1, slab]], axis=0)
        borders.append(jnp.concatenate(split_high_low(both), axis=1))
    for c, (slab, first_lane) in enumerate(places):
        for row in range(block_rows):
            center = row * 3 + c
            if row % 2 == 0:
                picks = [
                    jnp.where(
                        border_lanes == jnp.bitwise_and(border_of + (first_lane + row + k), lanes - 1), has_border, 0.0
                    ).astype(BF16)
                    for k in range(2)
                ]
                border = jnp.dot(borders[slab], jnp.concatenate(picks, axis=1), preferred_element_type=F32)
            for plane in range(2):
                place = plane * block_rows + row
                value = slab_ref[plane, center]
                stream = slab_ref[1 - plane, center] * (0.5 if plane == 0 else -0.5)
                if row + 1 < block_rows:
                    above = slab_ref[plane, center + 3]
                else:
                    above = pltpu.roll(slab_ref[plane, c], lanes - width, 1)
                    above = jnp.where(lane < lanes - width, above, 0.0)
                if row > 0:
                    below = slab_ref[plane, center - 3]
                else:
                    below = pltpu.roll(slab_ref[plane, 3 * (block_rows - 1) + c], width, 1)
                    below = jnp.where(lane >= width, below, 0.0)
                normal = (above - below) * 0.5
                after = jnp.where(column < width - 1, pltpu.roll(value, lanes - 1, 1), 0.0)
                before = jnp.where(column > 0, pltpu.roll(value, 1, 1), 0.0)
                span = (after - before) * 0.5 + border[plane * modes : (plane + 1) * modes, row % 2 * lanes : (row % 2 + 1) * lanes]
                carry_ref[pl.ds(c * height + place, modes, stride=3 * height), :] = value
                for d, slope in enumerate((stream, normal, span)):
                    slope_ref[pl.ds((d * 3 + c) * height + place, modes, stride=9 * height), :] = slope
                store_projection(rhs_ref, c * height + place, value)
                if (plane == 1) == (row < block_rows // 2):
                    near_ref[center] = value

    codes.wait()

    def one_peer(number, _):
        @pl.when(number > 0)
        def _():
            out_ref[number - 1] = project(conv_ref, rhs_ref, chips * share, 3 * height, lanes)

        following = lax.rem(first_peer + number, tm_count)
        pick_inner(held_codes_ref, carry_ref, slope_ref, conv_ref, following, (chips, share, bits))
        return 0

    lax.fori_loop(0, out_ref.shape[0] + 1, one_peer, 0)


def pick_inner(codes_ref, carry_ref, slope_ref, conv_ref, peer, sizes):
    places = conv_ref.shape[0] // (sizes[0] * sizes[1])
    height = places // 3

    def one_pair(slot, i, j):
        carry = carry_ref[pl.ds(pl.multiple_of(i * places, 8), places), :]
        slope = slope_ref[pl.ds(pl.multiple_of(j * (3 * places), 8), 3 * places), :]
        rows = [
            sum(
                carry[d * height : (d + 1) * height] * slope[(d * 3 + c) * height : (d * 3 + c + 1) * height]
                for d in range(3)
            )
            for c in range(3)
        ]
        conv_ref[pl.ds(pl.multiple_of(slot * places, 8), places), :] = jnp.concatenate(rows, axis=0)

    for_pairs_of(codes_ref, peer, sizes, one_pair)


def rest_kernel(
    codes_ref, carry_ref, slope_ref, rhs_ref, picked_ref, out_ref, conv_ref, held_codes_ref, sem, *, sizes
):
    del picked_ref
    chips, share, _ = sizes
    codes = copy_of_codes(codes_ref, held_codes_ref, sem)
    block, lanes = chips * share, conv_ref.shape[1]
    places = conv_ref.shape[0] // block

    def one_peer(peer, _):
        out_ref[peer] = project(conv_ref, rhs_ref, block, places, lanes)

        @pl.when(peer == 0)
        def _():
            codes.wait()

        @pl.when(peer + 1 < out_ref.shape[0])
        def _():
            pick_inner(held_codes_ref, carry_ref, slope_ref, conv_ref, peer + 1, sizes)

        return 0

    lax.fori_loop(0, out_ref.shape[0], one_peer, 0)


def far_kernel(codes_ref, coeffs_ref, *refs, peer, sizes):
    local_s, block_rows, tm_count, chips, share, bits = sizes
    next_own, next_other, near_ref, inner_ref = refs[:tm_count], *refs[tm_count : tm_count + 3]
    carry_ref, slope_ref, rhs_ref, out_ref, conv_ref, held_codes_ref, sem = refs[tm_count + 3 :]
    codes = copy_of_codes(codes_ref, held_codes_ref, sem)
    _, _, core = place_of_device()
    is_first = core == 0
    modes, lanes = near_ref.shape[1:]
    height = 2 * block_rows
    half = block_rows // 2 * 3
    weights = mode_weights(coeffs_ref, local_s, tm_count)
    for slab in range(half):
        mine = jnp.concatenate([next_own[peer][slab] for peer in range(tm_count)], axis=0)
        theirs = jnp.concatenate([next_other[peer, slab] for peer in range(tm_count)], axis=0)
        after, before = jnp.where(is_first, theirs, mine), jnp.where(is_first, mine, theirs)
        result = modes_of(weights, jnp.concatenate([after, before], axis=1))
        row, c = divmod(slab, 3)
        edges = ((near_ref[slab], result[:, :lanes]), (result[:, lanes:], near_ref[half + slab]))
        for number, (low, high) in enumerate(edges):
            place = number * block_rows + 2 * row
            for at, value, across in ((place, low, high * 0.5), (place + 1, high, low * -0.5)):
                if c == 0:
                    carry_ref[pl.ds(at, modes, stride=height), :] = value
                slope_ref[pl.ds(c * height + at, modes, stride=3 * height), :] = across
                store_projection(rhs_ref, c * height + at, value)


    codes.wait()
    pick_edge(held_codes_ref, carry_ref, slope_ref, conv_ref, peer, (chips, share, bits))
    out_ref[...] = edge_sum(conv_ref, rhs_ref, inner_ref, peer)
    pick_edge(held_codes_ref, carry_ref, slope_ref, conv_ref, peer - 1, (chips, share, bits))


def pick_edge(codes_ref, carry_ref, slope_ref, conv_ref, peer, sizes):
    places = conv_ref.shape[0] // (sizes[0] * sizes[1])
    height = places // 3

    def one_pair(slot, i, j):
        carry = carry_ref[pl.ds(pl.multiple_of(i * height, 8), height), :]
        slope = slope_ref[pl.ds(pl.multiple_of(j * places, 8), places), :]
        rows = [carry * slope[c * height : (c + 1) * height] for c in range(3)]
        conv_ref[pl.ds(pl.multiple_of(slot * places, 8), places), :] = jnp.concatenate(rows, axis=0)

    for_pairs_of(codes_ref, peer, sizes, one_pair)


def edge_sum(picked_ref, rhs_ref, inner_ref, peer):
    block = inner_ref.shape[1]
    places = picked_ref.shape[0] // block
    return inner_ref[peer % inner_ref.shape[0]] + project(picked_ref, rhs_ref, block, places, picked_ref.shape[1])


def edge_kernel(
    codes_ref, carry_ref, slope_ref, rhs_ref, inner_ref, picked_ref, out_ref, conv_ref, held_codes_ref, sem, *,
    peer, sizes
):
    codes = copy_of_codes(codes_ref, held_codes_ref, sem)
    out_ref[...] = edge_sum(picked_ref, rhs_ref, inner_ref, peer)
    codes.wait()
    pick_edge(held_codes_ref, carry_ref, slope_ref, conv_ref, peer - 1, sizes)


def own_edge_kernel(rhs_ref, inner_ref, picked_ref, *refs):
    *arrived_refs, out_ref = refs
    total = edge_sum(picked_ref, rhs_ref, inner_ref, 0)
    for arrived_ref in arrived_refs:
        total = total + arrived_ref[...]
    out_ref[...] = total


def vmem_limit(mebibytes):
    return pltpu.CompilerParams(vmem_limit_bytes=mebibytes * 2**20)


def in_vmem(array):
    return pltpu.with_memory_space_constraint(array, pltpu.VMEM)


def shards(snapshots, coeffs, pair_table):
    tm_count, space_count = lax.axis_size("tm"), lax.axis_size("space")
    chips = space_count // 2
    local_s, _, _, rows_y, lanes = snapshots.shape
    modes = coeffs.shape[1]
    block_rows = rows_y // tm_count
    slabs = 3 * block_rows + border_layout(rows_y, lanes, lanes // tm_count)[2]
    share = pair_table.shape[0] // (tm_count * space_count)
    factor = float(space_count * rows_y * lanes) ** (-0.5)
    bits = modes.bit_length() - 1
    assert modes == 2**bits
    vmem = pl.BlockSpec(memory_space=pltpu.VMEM)
    block = chips * share
    height = 2 * block_rows
    depth = 3 * height * lanes

    swap = [(2 * chip + c, 2 * chip + 1 - c) for chip in range(chips) for c in range(2)]

    def across(peer):
        return [(i, i ^ peer) for i in range(tm_count)]

    with jax.named_scope("pack"):
        *packed, codes, held_coeffs = pl.pallas_call(
            functools.partial(pack_kernel, sizes=(local_s, rows_y, tm_count)),
            out_shape=[pltpu.VMEM((slabs, local_s, lanes), F32)] * tm_count
            + [
                pltpu.VMEM((tm_count, block_rows // 2 * 3, local_s, lanes), F32),
                pltpu.VMEM((pair_table.shape[0],), jnp.int32),
                pltpu.VMEM(coeffs.shape, F32),
            ],
            in_specs=[pl.BlockSpec(memory_space=pltpu.HBM)] * 3,
            out_specs=[vmem] * (tm_count + 3),
            scratch_shapes=[
                pltpu.VMEM((tm_count, slabs, local_s, lanes), F32),
                pltpu.VMEM((3, local_s, rows_y, lanes), F32),
                pltpu.VMEM((2, pair_table.shape[0]), jnp.int32),
                pltpu.SemaphoreType.DMA((5,)),
            ],
            compiler_params=vmem_limit(16),
        )(
            *[
                pltpu.with_memory_space_constraint(array, pltpu.HBM)
                for array in (snapshots.reshape(local_s, 3, rows_y, lanes), pair_table.T, coeffs)
            ]
        )
        codes, coeffs = in_vmem(codes), in_vmem(held_coeffs)
    with jax.named_scope("to_next_plane"):
        ring = [(place, (place + (1 if place % 2 else -1)) % space_count) for place in range(space_count)]
        across_edge = lax.ppermute(packed[tm_count], "space", ring)
    with jax.named_scope("to_columns"):
        own = [packed[0]] + [lax.ppermute(packed[peer], "tm", across(peer)) for peer in range(1, tm_count)]
    with jax.named_scope("next_to_columns"):
        across_edge, own[:3] = lax.optimization_barrier((across_edge, own[:3]))
        parts = [across_edge[peer] for peer in range(tm_count)]
        parts, own[3:] = lax.optimization_barrier((parts, own[3:]))
        next_own = [parts[0]] + [lax.ppermute(parts[peer], "tm", across(peer)) for peer in range(1, tm_count)]
    with jax.named_scope("to_other_core"):
        other = [lax.ppermute(piece, "space", swap) for piece in own]
    early = tm_count // 2
    picked = pltpu.VMEM((block * 3 * height, lanes), F32)
    held_codes = [pltpu.SMEM(codes.shape, jnp.int32), pltpu.SemaphoreType.DMA]
    groups = pltpu.VMEM((early, block, modes), F32)
    with jax.named_scope("inner_terms"):
        near, *inner_tables, early_sums, first_picked = pl.pallas_call(
            functools.partial(inner_kernel, first_peer=early, sizes=(local_s, block_rows, tm_count, chips, share, bits)),
            out_shape=[
                pltpu.VMEM((block_rows * 3, modes, lanes), F32),
                pltpu.VMEM((modes * 3 * height, lanes), F32),
                pltpu.VMEM((modes * 9 * height, lanes), F32),
                pltpu.VMEM((depth, 2 * modes), BF16),
                groups,
                picked,
            ],
            in_specs=[vmem] * (2 * tm_count + 2),
            out_specs=[vmem] * 6,
            scratch_shapes=[pltpu.VMEM((2, slabs, modes, lanes), F32)] + held_codes,
            compiler_params=vmem_limit(24),
            cost_estimate=pl.CostEstimate(flops=12 * 10**9, bytes_accessed=10**7, transcendentals=0),
        )(codes, coeffs, *[in_vmem(piece) for piece in (*own, *other)])
    with jax.named_scope("next_to_other_core"):
        next_own, inner_tables = lax.optimization_barrier((next_own, inner_tables))
        next_other = lax.ppermute(jnp.stack(next_own), "space", swap)
    with jax.named_scope("inner_terms"):
        late_sums, _ = pl.pallas_call(
            functools.partial(rest_kernel, sizes=(chips, share, bits)),
            out_shape=[groups, picked],
            in_specs=[vmem] * 5,
            out_specs=[vmem] * 2,
            input_output_aliases={4: 1},
            scratch_shapes=held_codes,
            compiler_params=vmem_limit(16),
            cost_estimate=pl.CostEstimate(flops=8 * 10**9, bytes_accessed=10**7, transcendentals=0),
        )(codes, *[in_vmem(table) for table in (*inner_tables, first_picked)])
    with jax.named_scope("edge_terms"):
        *tables, summed, next_picked = pl.pallas_call(
            functools.partial(
                far_kernel, peer=tm_count - 1, sizes=(local_s, block_rows, tm_count, chips, share, bits)
            ),
            out_shape=[
                pltpu.VMEM((modes * height, lanes), F32),
                pltpu.VMEM((modes * 3 * height, lanes), F32),
                pltpu.VMEM((depth, 2 * modes), BF16),
                pltpu.VMEM((block, modes), F32),
                picked,
            ],
            in_specs=[vmem] * (tm_count + 5),
            out_specs=[vmem] * 5,
            scratch_shapes=held_codes,
            compiler_params=vmem_limit(16),
        )(codes, coeffs, *[in_vmem(piece) for piece in (*next_own, next_other, near, early_sums)])
    arrived, taken = [], 2
    for peer in reversed(range(tm_count - 1)):
        with jax.named_scope("sum_over_columns"):
            arrived.append(lax.ppermute(summed, "tm", across(peer + 1)))
            if peer >= early:
                early_sums, _ = lax.optimization_barrier((early_sums, summed))
            else:
                late_sums, _ = lax.optimization_barrier((late_sums, summed))
        with jax.named_scope("edge_terms"):
            inner_sums = early_sums if peer >= early else late_sums
            edge_cost = pl.CostEstimate(flops=10**8, bytes_accessed=10**5, transcendentals=0)
            if peer:
                summed, next_picked = pl.pallas_call(
                    functools.partial(edge_kernel, peer=peer, sizes=(chips, share, bits)),
                    out_shape=[pltpu.VMEM((block, modes), F32), picked],
                    in_specs=[vmem] * 6,
                    out_specs=[vmem] * 2,
                    scratch_shapes=held_codes,
                    compiler_params=vmem_limit(16),
                    cost_estimate=edge_cost,
                )(codes, *[in_vmem(table) for table in (*tables, inner_sums, next_picked)])
            else:
                summed = pl.pallas_call(
                    own_edge_kernel,
                    out_shape=pltpu.VMEM((block, modes), F32),
                    in_specs=[vmem] * (3 + taken),
                    out_specs=vmem,
                    compiler_params=vmem_limit(16),
                    cost_estimate=edge_cost,
                )(*[in_vmem(table) for table in (tables[2], inner_sums, next_picked, *arrived[:taken])])
    with jax.named_scope("sum_over_columns"):
        for part in arrived[taken:]:
            summed = summed + part
    with jax.named_scope("sum_over_chips"):
        shares = summed.reshape(chips, share, modes)
        result = shares[0]
        for step in range(1, chips):
            pairing = [(2 * chip + c, 2 * (chip ^ step) + c) for chip in range(chips) for c in range(2)]
            result = result + lax.ppermute(shares[step], "space", pairing)
        return result * factor


def solution(mesh):
    placed = (P("tm", None, "space", None, None), P(), P())
    return jax.shard_map(
        shards, mesh=mesh, in_specs=placed, out_specs=P(("tm", "space"), None), check_vma=False
    )
```

```python
import functools
import itertools
import math

import jax
import jax.numpy as jnp
from jax import lax
from jax.experimental import pallas as pl
from jax.experimental.pallas import tpu as pltpu
from jax.sharding import PartitionSpec as P

F32 = jnp.float32
BF16 = jnp.bfloat16


def place_of_device():
    place = lax.axis_index("space")
    return lax.axis_index("tm"), lax.shift_right_logical(place, 1), jnp.bitwise_and(place, 1)


def split_high_low(values):
    high = values.astype(BF16)
    low = (values - high.astype(F32)).astype(BF16)
    return high, low


def border_layout(rows_y, lanes, width):
    per_run = (width + 1) // rows_y
    if per_run:
        run = width + 1 + per_run * rows_y
        firsts = [c // per_run * run + c % per_run * rows_y for c in range(3)]
        if firsts[2] + width + 1 + rows_y <= lanes:
            return [(0, first) for first in firsts], width + 1, 1
    per_slab = lanes // (2 * rows_y)
    places = [(c // per_slab, c % per_slab * 2 * rows_y) for c in range(3)]
    return places, rows_y, places[2][0] + 1


def exchange_blocks(rows, lane, width, lanes):
    rows = list(rows)
    step = len(rows) // 2
    while step:
        keeps = jnp.bitwise_and(lane, step * width) == 0
        for low in range(len(rows)):
            if low & step == 0:
                first, second = rows[low], rows[low + step]
                rows[low] = jnp.where(keeps, first, pltpu.roll(second, step * width, 1))
                rows[low + step] = jnp.where(keeps, pltpu.roll(first, lanes - step * width, 1), second)
        step //= 2
    return rows


def pack_kernel(field_ref, pairs_ref, coeffs_ref, *refs, sizes):
    *out_refs, codes_ref, held_coeffs_ref, sorted_ref, held_ref, held_pairs_ref, sems = refs
    local_s, rows_y, tm_count = sizes
    lanes = field_ref.shape[3]
    copies = [pltpu.make_async_copy(field_ref.at[:, c], held_ref.at[c], sems.at[c]) for c in range(3)]
    copies.append(pltpu.make_async_copy(pairs_ref, held_pairs_ref, sems.at[3]))
    copies.append(pltpu.make_async_copy(coeffs_ref, held_coeffs_ref, sems.at[4]))
    for copy in copies:
        copy.start()
    rows_ref = held_ref.reshape(3 * local_s * rows_y, lanes)
    t, _, core = place_of_device()
    width, groups = lanes // tm_count, rows_y // tm_count
    lane = lax.broadcasted_iota(jnp.int32, (local_s, lanes), 1)
    places, offset, border_slabs = border_layout(rows_y, lanes, width)
    borders = [[jnp.zeros((local_s, lanes), F32) for _ in range(tm_count)] for _ in range(border_slabs)]
    for c, (slab, first_lane) in enumerate(places):
        copies[c].wait()

        def one_group(g, border, c=c, first_lane=first_lane):
            border = list(border)
            rows = []
            for q in range(tm_count):
                y = q * groups + g
                row = rows_ref[pl.ds(c * local_s * rows_y + y, local_s, stride=rows_y), :]
                rows.append(row)
                before = first_lane + y
                after = before + offset - (width + 1)
                moved = pltpu.roll(row, jnp.bitwise_and(before, lanes - 1), 1)
                moved_after = moved if offset == width + 1 else pltpu.roll(row, jnp.bitwise_and(after, lanes - 1), 1)
                for block in range(tm_count):
                    at_before = lane == jnp.bitwise_and(before + block * width - 1, lanes - 1)
                    at_after = lane == jnp.bitwise_and(after + (block + 1) * width, lanes - 1)
                    if moved is moved_after:
                        border[block] = jnp.where(jnp.logical_or(at_before, at_after), moved, border[block])
                    else:
                        border[block] = jnp.where(at_before, moved, jnp.where(at_after, moved_after, border[block]))
            for block, main in enumerate(exchange_blocks(rows, lane, width, lanes)):
                sorted_ref[block, g * 3 + c] = main
            return tuple(border)

        borders[slab] = lax.fori_loop(0, groups, one_group, tuple(borders[slab]), unroll=True)
    half = groups // 2 * 3
    for slab, border in enumerate(borders):
        for block in range(tm_count):
            sorted_ref[block, groups * 3 + slab] = border[block]
    for peer in range(tm_count):
        block = jnp.bitwise_xor(t, peer)
        out_refs[peer][...] = sorted_ref[block]
        out_refs[tm_count][peer] = sorted_ref[block, pl.ds(core * half, half)]
    copies[3].wait()
    copies[4].wait()
    for first in range(0, codes_ref.shape[0], lanes):
        here = pl.ds(first, lanes)
        codes_ref[here] = held_pairs_ref[0, here] * held_coeffs_ref.shape[1] + held_pairs_ref[1, here]


def mode_weights(coeffs_ref, local_s, tm_count):
    t, _, _ = place_of_device()
    ordered = jnp.concatenate(
        [
            coeffs_ref[pl.ds(pl.multiple_of(jnp.bitwise_xor(t, peer) * local_s, 8), local_s), :]
            for peer in range(tm_count)
        ],
        axis=0,
    )
    high, low = split_high_low(ordered.T)
    return jnp.concatenate([high, low, high, low], axis=1)


def modes_of(weights, slab):
    high, low = split_high_low(slab)
    return jnp.dot(weights, jnp.concatenate([high, high, low, low], axis=0), preferred_element_type=F32)


def store_projection(rhs_ref, place, mode_slab):
    high, low = split_high_low(mode_slab.T)
    modes, lanes = mode_slab.shape
    rhs_ref[place * lanes : (place + 1) * lanes, 0:modes] = high
    rhs_ref[place * lanes : (place + 1) * lanes, modes : 2 * modes] = low


def project(conv_ref, rhs_ref, block, places, lanes):
    both = None
    for place in range(0, places, 2):
        highs, lows = zip(
            *(split_high_low(conv_ref[pl.ds(place + k, block, stride=places), :]) for k in range(2))
        )
        lhs = jnp.concatenate([jnp.concatenate(highs, axis=1), jnp.concatenate(lows, axis=1)], axis=0)
        part = jnp.dot(lhs, rhs_ref[place * lanes : (place + 2) * lanes, :], preferred_element_type=F32)
        both = part if both is None else both + part
    modes = both.shape[1] // 2
    return (both[:block, :modes] + both[:block, modes:]) + (both[block:, :modes] + both[block:, modes:])


def for_pairs_of(codes_ref, peer, sizes, one_pair):
    chips, share, bits = sizes
    t, chip, core = place_of_device()
    first_chip = jnp.bitwise_xor(t, peer) * chips

    def one_share(ahead, _):
        base = ((first_chip + jnp.bitwise_xor(chip, ahead)) * 2 + core) * share

        def one(q, _):
            code = codes_ref[base + q]
            one_pair(ahead * share + q, lax.shift_right_logical(code, bits), jnp.bitwise_and(code, 2**bits - 1))
            return 0

        return lax.fori_loop(0, share, one, 0, unroll=True)

    lax.fori_loop(0, chips, one_share, 0)


def copy_of_codes(codes_ref, held_codes_ref, sem):
    copy = pltpu.make_async_copy(codes_ref, held_codes_ref, sem)
    copy.start()
    return copy


def inner_kernel(codes_ref, coeffs_ref, *refs, first_peer, sizes):
    local_s, block_rows, tm_count, chips, share, bits = sizes
    own, other = refs[:tm_count], refs[tm_count : 2 * tm_count]
    near_ref, carry_ref, slope_ref, rhs_ref, out_ref, conv_ref, slab_ref, held_codes_ref, sem = refs[2 * tm_count :]
    codes = copy_of_codes(codes_ref, held_codes_ref, sem)
    t, _, core = place_of_device()
    modes, lanes = coeffs_ref.shape[1], own[0].shape[2]
    height = 2 * block_rows
    weights = mode_weights(coeffs_ref, local_s, tm_count)

    def one_slab(index, _):
        own_slab = jnp.concatenate([piece[index] for piece in own], axis=0)
        other_slab = jnp.concatenate([piece[index] for piece in other], axis=0)
        is_first = core == 0
        both = jnp.concatenate(
            [jnp.where(is_first, own_slab, other_slab), jnp.where(is_first, other_slab, own_slab)], axis=1
        )
        result = modes_of(weights, both)
        slab_ref[0, index] = result[:, :lanes]
        slab_ref[1, index] = result[:, lanes:]
        return 0

    slabs = own[0].shape[0]
    lax.fori_loop(0, slabs, one_slab, 0, unroll=True)
    width, rows_y = lanes // tm_count, block_rows * tm_count
    lane = lax.broadcasted_iota(jnp.int32, (1, lanes), 1)
    part, column = lax.div(lane, width), lax.rem(lane, width)
    has_border = jnp.where(column == 0, -0.5, jnp.where(column == width - 1, 0.5, 0.0))
    places, offset, _ = border_layout(rows_y, lanes, width)
    border_of = jnp.where(column == 0, 0, offset) + t * width - 1 + part * block_rows
    border_lanes = lax.broadcasted_iota(jnp.int32, (2 * lanes, lanes), 0)
    border_lanes = jnp.where(border_lanes >= lanes, border_lanes - lanes, border_lanes)
    borders = []
    for slab in range(3 * block_rows, slabs):
        both = jnp.concatenate([slab_ref[0, slab], slab_ref[1, slab]], axis=0)
        borders.append(jnp.concatenate(split_high_low(both), axis=1))
    some = math.gcd(modes, 32)
    for c, (slab, first_lane) in enumerate(places):
        for row in range(block_rows):
            center = row * 3 + c
            if row % 2 == 0:
                picks = [
                    jnp.where(
                        border_lanes == jnp.bitwise_and(border_of + (first_lane + row + k), lanes - 1), has_border, 0.0
                    ).astype(BF16)
                    for k in range(2)
                ]
                border = jnp.dot(borders[slab], jnp.concatenate(picks, axis=1), preferred_element_type=F32)
            for plane, first in itertools.product(range(2), range(0, modes, some)):
                place = plane * block_rows + row
                here = pl.ds(first, some)
                value = slab_ref[plane, center, here, :]
                stream = slab_ref[1 - plane, center, here, :] * (0.5 if plane == 0 else -0.5)
                if row + 1 < block_rows:
                    above = slab_ref[plane, center + 3, here, :]
                else:
                    above = pltpu.roll(slab_ref[plane, c, here, :], lanes - width, 1)
                    above = jnp.where(lane < lanes - width, above, 0.0)
                if row > 0:
                    below = slab_ref[plane, center - 3, here, :]
                else:
                    below = pltpu.roll(slab_ref[plane, 3 * (block_rows - 1) + c, here, :], width, 1)
                    below = jnp.where(lane >= width, below, 0.0)
                normal = (above - below) * 0.5
                after = jnp.where(column < width - 1, pltpu.roll(value, lanes - 1, 1), 0.0)
                before = jnp.where(column > 0, pltpu.roll(value, 1, 1), 0.0)
                beside = border[plane * modes + first :, row % 2 * lanes :][:some, :lanes]
                span = (after - before) * 0.5 + beside
                carry_ref[pl.ds(first * (3 * height) + c * height + place, some, stride=3 * height), :] = value
                for d, slope in enumerate((stream, normal, span)):
                    start = first * (9 * height) + (d * 3 + c) * height + place
                    slope_ref[pl.ds(start, some, stride=9 * height), :] = slope
                if (plane == 1) == (row < block_rows // 2):
                    near_ref[center, here, :] = value
            for plane in range(2):
                store_projection(rhs_ref, c * height + plane * block_rows + row, slab_ref[plane, center])
    codes.wait()

    def one_peer(number, _):
        @pl.when(number > 0)
        def _():
            out_ref[number - 1] = project(conv_ref, rhs_ref, chips * share, 3 * height, lanes)

        following = lax.rem(first_peer + number, tm_count)
        pick_inner(held_codes_ref, carry_ref, slope_ref, conv_ref, following, (chips, share, bits))
        return 0

    lax.fori_loop(0, out_ref.shape[0] + 1, one_peer, 0)


def pick_inner(codes_ref, carry_ref, slope_ref, conv_ref, peer, sizes):
    places = conv_ref.shape[0] // (sizes[0] * sizes[1])
    height = places // 3

    def one_pair(slot, i, j):
        carry = carry_ref[pl.ds(pl.multiple_of(i * places, 8), places), :]
        slope = slope_ref[pl.ds(pl.multiple_of(j * (3 * places), 8), 3 * places), :]
        rows = [
            sum(
                carry[d * height : (d + 1) * height] * slope[(d * 3 + c) * height : (d * 3 + c + 1) * height]
                for d in range(3)
            )
            for c in range(3)
        ]
        conv_ref[pl.ds(pl.multiple_of(slot * places, 8), places), :] = jnp.concatenate(rows, axis=0)

    for_pairs_of(codes_ref, peer, sizes, one_pair)


def rest_kernel(
    codes_ref, carry_ref, slope_ref, rhs_ref, picked_ref, out_ref, conv_ref, held_codes_ref, sem, *, sizes
):
    del picked_ref
    chips, share, _ = sizes
    codes = copy_of_codes(codes_ref, held_codes_ref, sem)
    block, lanes = chips * share, conv_ref.shape[1]
    places = conv_ref.shape[0] // block

    def one_peer(peer, _):
        out_ref[peer] = project(conv_ref, rhs_ref, block, places, lanes)

        @pl.when(peer == 0)
        def _():
            codes.wait()

        @pl.when(peer + 1 < out_ref.shape[0])
        def _():
            pick_inner(held_codes_ref, carry_ref, slope_ref, conv_ref, peer + 1, sizes)

        return 0

    lax.fori_loop(0, out_ref.shape[0], one_peer, 0)


def far_kernel(codes_ref, coeffs_ref, *refs, peer, sizes):
    local_s, block_rows, tm_count, chips, share, bits = sizes
    next_own, next_other, near_ref, inner_ref = refs[:tm_count], *refs[tm_count : tm_count + 3]
    carry_ref, slope_ref, rhs_ref, out_ref, conv_ref, held_codes_ref, sem = refs[tm_count + 3 :]
    codes = copy_of_codes(codes_ref, held_codes_ref, sem)
    _, _, core = place_of_device()
    is_first = core == 0
    modes, lanes = near_ref.shape[1:]
    height = 2 * block_rows
    half = block_rows // 2 * 3
    weights = mode_weights(coeffs_ref, local_s, tm_count)
    for slab in range(half):
        mine = jnp.concatenate([next_own[peer][slab] for peer in range(tm_count)], axis=0)
        theirs = jnp.concatenate([next_other[peer, slab] for peer in range(tm_count)], axis=0)
        after, before = jnp.where(is_first, theirs, mine), jnp.where(is_first, mine, theirs)
        result = modes_of(weights, jnp.concatenate([after, before], axis=1))
        row, c = divmod(slab, 3)
        edges = ((near_ref[slab], result[:, :lanes]), (result[:, lanes:], near_ref[half + slab]))
        for number, (low, high) in enumerate(edges):
            place = number * block_rows + 2 * row
            for at, value, across in ((place, low, high * 0.5), (place + 1, high, low * -0.5)):
                if c == 0:
                    carry_ref[pl.ds(at, modes, stride=height), :] = value
                slope_ref[pl.ds(c * height + at, modes, stride=3 * height), :] = across
                store_projection(rhs_ref, c * height + at, value)


    codes.wait()
    pick_edge(held_codes_ref, carry_ref, slope_ref, conv_ref, peer, (chips, share, bits))
    out_ref[...] = edge_sum(conv_ref, rhs_ref, inner_ref, peer)
    pick_edge(held_codes_ref, carry_ref, slope_ref, conv_ref, peer - 1, (chips, share, bits))


def pick_edge(codes_ref, carry_ref, slope_ref, conv_ref, peer, sizes):
    places = conv_ref.shape[0] // (sizes[0] * sizes[1])
    height = places // 3

    def one_pair(slot, i, j):
        carry = carry_ref[pl.ds(pl.multiple_of(i * height, 8), height), :]
        slope = slope_ref[pl.ds(pl.multiple_of(j * places, 8), places), :]
        rows = [carry * slope[c * height : (c + 1) * height] for c in range(3)]
        conv_ref[pl.ds(pl.multiple_of(slot * places, 8), places), :] = jnp.concatenate(rows, axis=0)

    for_pairs_of(codes_ref, peer, sizes, one_pair)


def edge_sum(picked_ref, rhs_ref, inner_ref, peer):
    block = inner_ref.shape[1]
    places = picked_ref.shape[0] // block
    return inner_ref[peer % inner_ref.shape[0]] + project(picked_ref, rhs_ref, block, places, picked_ref.shape[1])


def edge_kernel(
    codes_ref, carry_ref, slope_ref, rhs_ref, inner_ref, picked_ref, out_ref, conv_ref, held_codes_ref, sem, *,
    peer, sizes
):
    codes = copy_of_codes(codes_ref, held_codes_ref, sem)
    out_ref[...] = edge_sum(picked_ref, rhs_ref, inner_ref, peer)
    codes.wait()
    pick_edge(held_codes_ref, carry_ref, slope_ref, conv_ref, peer - 1, sizes)


def own_edge_kernel(rhs_ref, inner_ref, picked_ref, *refs):
    *arrived_refs, out_ref = refs
    total = edge_sum(picked_ref, rhs_ref, inner_ref, 0)
    for arrived_ref in arrived_refs:
        total = total + arrived_ref[...]
    out_ref[...] = total


def vmem_limit(mebibytes):
    return pltpu.CompilerParams(vmem_limit_bytes=mebibytes * 2**20)


def in_vmem(array):
    return pltpu.with_memory_space_constraint(array, pltpu.VMEM)


def shards(snapshots, coeffs, pair_table):
    tm_count, space_count = lax.axis_size("tm"), lax.axis_size("space")
    chips = space_count // 2
    local_s, _, _, rows_y, lanes = snapshots.shape
    modes = coeffs.shape[1]
    block_rows = rows_y // tm_count
    slabs = 3 * block_rows + border_layout(rows_y, lanes, lanes // tm_count)[2]
    share = pair_table.shape[0] // (tm_count * space_count)
    factor = float(space_count * rows_y * lanes) ** (-0.5)
    bits = modes.bit_length() - 1
    assert modes == 2**bits
    vmem = pl.BlockSpec(memory_space=pltpu.VMEM)
    block = chips * share
    height = 2 * block_rows
    depth = 3 * height * lanes

    swap = [(2 * chip + c, 2 * chip + 1 - c) for chip in range(chips) for c in range(2)]

    def across(peer):
        return [(i, i ^ peer) for i in range(tm_count)]

    with jax.named_scope("pack"):
        *packed, codes, held_coeffs = pl.pallas_call(
            functools.partial(pack_kernel, sizes=(local_s, rows_y, tm_count)),
            out_shape=[pltpu.VMEM((slabs, local_s, lanes), F32)] * tm_count
            + [
                pltpu.VMEM((tm_count, block_rows // 2 * 3, local_s, lanes), F32),
                pltpu.VMEM((pair_table.shape[0],), jnp.int32),
                pltpu.VMEM(coeffs.shape, F32),
            ],
            in_specs=[pl.BlockSpec(memory_space=pltpu.HBM)] * 3,
            out_specs=[vmem] * (tm_count + 3),
            scratch_shapes=[
                pltpu.VMEM((tm_count, slabs, local_s, lanes), F32),
                pltpu.VMEM((3, local_s, rows_y, lanes), F32),
                pltpu.VMEM((2, pair_table.shape[0]), jnp.int32),
                pltpu.SemaphoreType.DMA((5,)),
            ],
            compiler_params=vmem_limit(16),
        )(
            *[
                pltpu.with_memory_space_constraint(array, pltpu.HBM)
                for array in (snapshots.reshape(local_s, 3, rows_y, lanes), pair_table.T, coeffs)
            ]
        )
        codes, coeffs = in_vmem(codes), in_vmem(held_coeffs)
    with jax.named_scope("to_next_plane"):
        ring = [(place, (place + (1 if place % 2 else -1)) % space_count) for place in range(space_count)]
        across_edge = lax.ppermute(packed[tm_count], "space", ring)
    with jax.named_scope("to_columns"):
        own = [packed[0]] + [lax.ppermute(packed[peer], "tm", across(peer)) for peer in range(1, tm_count)]
    with jax.named_scope("next_to_columns"):
        across_edge, own[:3] = lax.optimization_barrier((across_edge, own[:3]))
        parts = [across_edge[peer] for peer in range(tm_count)]
        parts, own[3:] = lax.optimization_barrier((parts, own[3:]))
        next_own = [parts[0]] + [lax.ppermute(parts[peer], "tm", across(peer)) for peer in range(1, tm_count)]
    with jax.named_scope("to_other_core"):
        other = [lax.ppermute(piece, "space", swap) for piece in own]
    early = tm_count // 2
    picked = pltpu.VMEM((block * 3 * height, lanes), F32)
    held_codes = [pltpu.SMEM(codes.shape, jnp.int32), pltpu.SemaphoreType.DMA]
    groups = pltpu.VMEM((early, block, modes), F32)
    with jax.named_scope("inner_terms"):
        near, *inner_tables, early_sums, first_picked = pl.pallas_call(
            functools.partial(inner_kernel, first_peer=early, sizes=(local_s, block_rows, tm_count, chips, share, bits)),
            out_shape=[
                pltpu.VMEM((block_rows * 3, modes, lanes), F32),
                pltpu.VMEM((modes * 3 * height, lanes), F32),
                pltpu.VMEM((modes * 9 * height, lanes), F32),
                pltpu.VMEM((depth, 2 * modes), BF16),
                groups,
                picked,
            ],
            in_specs=[vmem] * (2 * tm_count + 2),
            out_specs=[vmem] * 6,
            scratch_shapes=[pltpu.VMEM((2, slabs, modes, lanes), F32)] + held_codes,
            compiler_params=vmem_limit(24),
            cost_estimate=pl.CostEstimate(flops=12 * 10**9, bytes_accessed=10**7, transcendentals=0),
        )(codes, coeffs, *[in_vmem(piece) for piece in (*own, *other)])
    with jax.named_scope("next_to_other_core"):
        next_own, inner_tables = lax.optimization_barrier((next_own, inner_tables))
        next_other = lax.ppermute(jnp.stack(next_own), "space", swap)
    with jax.named_scope("inner_terms"):
        late_sums, _ = pl.pallas_call(
            functools.partial(rest_kernel, sizes=(chips, share, bits)),
            out_shape=[groups, picked],
            in_specs=[vmem] * 5,
            out_specs=[vmem] * 2,
            input_output_aliases={4: 1},
            scratch_shapes=held_codes,
            compiler_params=vmem_limit(16),
            cost_estimate=pl.CostEstimate(flops=8 * 10**9, bytes_accessed=10**7, transcendentals=0),
        )(codes, *[in_vmem(table) for table in (*inner_tables, first_picked)])
    with jax.named_scope("edge_terms"):
        *tables, summed, next_picked = pl.pallas_call(
            functools.partial(
                far_kernel, peer=tm_count - 1, sizes=(local_s, block_rows, tm_count, chips, share, bits)
            ),
            out_shape=[
                pltpu.VMEM((modes * height, lanes), F32),
                pltpu.VMEM((modes * 3 * height, lanes), F32),
                pltpu.VMEM((depth, 2 * modes), BF16),
                pltpu.VMEM((block, modes), F32),
                picked,
            ],
            in_specs=[vmem] * (tm_count + 5),
            out_specs=[vmem] * 5,
            scratch_shapes=held_codes,
            compiler_params=vmem_limit(16),
        )(codes, coeffs, *[in_vmem(piece) for piece in (*next_own, next_other, near, early_sums)])
    arrived, taken = [], 2
    for peer in reversed(range(tm_count - 1)):
        with jax.named_scope("sum_over_columns"):
            arrived.append(lax.ppermute(summed, "tm", across(peer + 1)))
            if peer >= early:
                early_sums, _ = lax.optimization_barrier((early_sums, summed))
            else:
                late_sums, _ = lax.optimization_barrier((late_sums, summed))
        with jax.named_scope("edge_terms"):
            inner_sums = early_sums if peer >= early else late_sums
            edge_cost = pl.CostEstimate(flops=10**8, bytes_accessed=10**5, transcendentals=0)
            if peer:
                summed, next_picked = pl.pallas_call(
                    functools.partial(edge_kernel, peer=peer, sizes=(chips, share, bits)),
                    out_shape=[pltpu.VMEM((block, modes), F32), picked],
                    in_specs=[vmem] * 6,
                    out_specs=[vmem] * 2,
                    scratch_shapes=held_codes,
                    compiler_params=vmem_limit(16),
                    cost_estimate=edge_cost,
                )(codes, *[in_vmem(table) for table in (*tables, inner_sums, next_picked)])
            else:
                summed = pl.pallas_call(
                    own_edge_kernel,
                    out_shape=pltpu.VMEM((block, modes), F32),
                    in_specs=[vmem] * (3 + taken),
                    out_specs=vmem,
                    compiler_params=vmem_limit(16),
                    cost_estimate=edge_cost,
                )(*[in_vmem(table) for table in (tables[2], inner_sums, next_picked, *arrived[:taken])])
    with jax.named_scope("sum_over_columns"):
        for part in arrived[taken:]:
            summed = summed + part
    with jax.named_scope("sum_over_chips"):
        shares = summed.reshape(chips, share, modes)
        parts = None
        for step in reversed(range(1, chips)):
            pairing = [(2 * chip + c, 2 * (chip ^ step) + c) for chip in range(chips) for c in range(2)]
            part = lax.ppermute(shares[step], "space", pairing)
            parts = part if parts is None else part + parts
        result = shares[0] + parts
        return result * factor


def solution(mesh):
    placed = (P("tm", None, "space", None, None), P(), P())
    return jax.shard_map(
        shards, mesh=mesh, in_specs=placed, out_specs=P(("tm", "space"), None), check_vma=False
    )
```

```python
import functools
import itertools
import math

import jax
import jax.numpy as jnp
from jax import lax
from jax.experimental import pallas as pl
from jax.experimental.pallas import tpu as pltpu
from jax.sharding import PartitionSpec as P

F32 = jnp.float32
BF16 = jnp.bfloat16


def place_of_device():
    place = lax.axis_index("space")
    return lax.axis_index("tm"), lax.shift_right_logical(place, 1), jnp.bitwise_and(place, 1)


def split_high_low(values):
    high = values.astype(BF16)
    low = (values - high.astype(F32)).astype(BF16)
    return high, low


def border_layout(rows_y, lanes, width):
    per_run = (width + 1) // rows_y
    if per_run:
        run = width + 1 + per_run * rows_y
        firsts = [c // per_run * run + c % per_run * rows_y for c in range(3)]
        if firsts[2] + width + 1 + rows_y <= lanes:
            return [(0, first) for first in firsts], width + 1, 1
    per_slab = lanes // (2 * rows_y)
    places = [(c // per_slab, c % per_slab * 2 * rows_y) for c in range(3)]
    return places, rows_y, places[2][0] + 1


def exchange_blocks(rows, lane, width, lanes):
    rows = list(rows)
    step = len(rows) // 2
    while step:
        keeps = jnp.bitwise_and(lane, step * width) == 0
        for low in range(len(rows)):
            if low & step == 0:
                first, second = rows[low], rows[low + step]
                rows[low] = jnp.where(keeps, first, pltpu.roll(second, step * width, 1))
                rows[low + step] = jnp.where(keeps, pltpu.roll(first, lanes - step * width, 1), second)
        step //= 2
    return rows


def pack_kernel(field_ref, pairs_ref, coeffs_ref, *refs, sizes):
    *out_refs, codes_ref, held_coeffs_ref, sorted_ref, held_ref, held_pairs_ref, sems = refs
    local_s, rows_y, tm_count = sizes
    lanes = field_ref.shape[3]
    copies = [pltpu.make_async_copy(field_ref.at[:, c], held_ref.at[c], sems.at[c]) for c in range(3)]
    copies.append(pltpu.make_async_copy(pairs_ref, held_pairs_ref, sems.at[3]))
    copies.append(pltpu.make_async_copy(coeffs_ref, held_coeffs_ref, sems.at[4]))
    for copy in copies:
        copy.start()
    rows_ref = held_ref.reshape(3 * local_s * rows_y, lanes)
    t, _, core = place_of_device()
    width, groups = lanes // tm_count, rows_y // tm_count
    lane = lax.broadcasted_iota(jnp.int32, (local_s, lanes), 1)
    places, offset, border_slabs = border_layout(rows_y, lanes, width)
    borders = [[jnp.zeros((local_s, lanes), F32) for _ in range(tm_count)] for _ in range(border_slabs)]
    for c, (slab, first_lane) in enumerate(places):
        copies[c].wait()

        def one_group(g, border, c=c, first_lane=first_lane):
            border = list(border)
            rows = []
            for q in range(tm_count):
                y = q * groups + g
                row = rows_ref[pl.ds(c * local_s * rows_y + y, local_s, stride=rows_y), :]
                rows.append(row)
                before = first_lane + y
                after = before + offset - (width + 1)
                moved = pltpu.roll(row, jnp.bitwise_and(before, lanes - 1), 1)
                moved_after = moved if offset == width + 1 else pltpu.roll(row, jnp.bitwise_and(after, lanes - 1), 1)
                for block in range(tm_count):
                    at_before = lane == jnp.bitwise_and(before + block * width - 1, lanes - 1)
                    at_after = lane == jnp.bitwise_and(after + (block + 1) * width, lanes - 1)
                    if moved is moved_after:
                        border[block] = jnp.where(jnp.logical_or(at_before, at_after), moved, border[block])
                    else:
                        border[block] = jnp.where(at_before, moved, jnp.where(at_after, moved_after, border[block]))
            for block, main in enumerate(exchange_blocks(rows, lane, width, lanes)):
                sorted_ref[block, g * 3 + c] = main
            return tuple(border)

        borders[slab] = lax.fori_loop(0, groups, one_group, tuple(borders[slab]), unroll=True)
    half = groups // 2 * 3
    for slab, border in enumerate(borders):
        for block in range(tm_count):
            sorted_ref[block, groups * 3 + slab] = border[block]
    for peer in range(tm_count):
        block = jnp.bitwise_xor(t, peer)
        out_refs[peer][...] = sorted_ref[block]
        out_refs[tm_count][peer] = sorted_ref[block, pl.ds(core * half, half)]
    copies[3].wait()
    copies[4].wait()
    for first in range(0, codes_ref.shape[0], lanes):
        here = pl.ds(first, lanes)
        codes_ref[here] = held_pairs_ref[0, here] * held_coeffs_ref.shape[1] + held_pairs_ref[1, here]


def mode_weights(coeffs_ref, local_s, tm_count):
    t, _, _ = place_of_device()
    ordered = jnp.concatenate(
        [
            coeffs_ref[pl.ds(pl.multiple_of(jnp.bitwise_xor(t, peer) * local_s, 8), local_s), :]
            for peer in range(tm_count)
        ],
        axis=0,
    )
    high, low = split_high_low(ordered.T)
    return jnp.concatenate([high, low, high, low], axis=1)


def modes_of(weights, slab):
    high, low = split_high_low(slab)
    return jnp.dot(weights, jnp.concatenate([high, high, low, low], axis=0), preferred_element_type=F32)


def store_projection(rhs_ref, place, mode_slab):
    high, low = split_high_low(mode_slab.T)
    modes, lanes = mode_slab.shape
    rhs_ref[place * lanes : (place + 1) * lanes, 0:modes] = high
    rhs_ref[place * lanes : (place + 1) * lanes, modes : 2 * modes] = low


def project(conv_ref, rhs_ref, block, places, lanes):
    both = None
    for place in range(0, places, 2):
        highs, lows = zip(
            *(split_high_low(conv_ref[pl.ds(place + k, block, stride=places), :]) for k in range(2))
        )
        lhs = jnp.concatenate([jnp.concatenate(highs, axis=1), jnp.concatenate(lows, axis=1)], axis=0)
        part = jnp.dot(lhs, rhs_ref[place * lanes : (place + 2) * lanes, :], preferred_element_type=F32)
        both = part if both is None else both + part
    modes = both.shape[1] // 2
    return (both[:block, :modes] + both[:block, modes:]) + (both[block:, :modes] + both[block:, modes:])


def for_pairs_of(codes_ref, peer, sizes, one_pair):
    chips, share, bits = sizes
    t, chip, core = place_of_device()
    first_chip = jnp.bitwise_xor(t, peer) * chips

    def one_share(ahead, _):
        base = ((first_chip + jnp.bitwise_xor(chip, ahead)) * 2 + core) * share

        def one(q, _):
            code = codes_ref[base + q]
            one_pair(ahead * share + q, lax.shift_right_logical(code, bits), jnp.bitwise_and(code, 2**bits - 1))
            return 0

        return lax.fori_loop(0, share, one, 0, unroll=True)

    lax.fori_loop(0, chips, one_share, 0)


def copy_of_codes(codes_ref, held_codes_ref, sem):
    copy = pltpu.make_async_copy(codes_ref, held_codes_ref, sem)
    copy.start()
    return copy


def inner_kernel(codes_ref, coeffs_ref, *refs, first_peer, sizes):
    local_s, block_rows, tm_count, chips, share, bits = sizes
    own, other = refs[:tm_count], refs[tm_count : 2 * tm_count]
    near_ref, carry_ref, slope_ref, rhs_ref, out_ref, conv_ref, slab_ref, held_codes_ref, sem = refs[2 * tm_count :]
    codes = copy_of_codes(codes_ref, held_codes_ref, sem)
    t, _, core = place_of_device()
    modes, lanes = coeffs_ref.shape[1], own[0].shape[2]
    height = 2 * block_rows
    weights = mode_weights(coeffs_ref, local_s, tm_count)

    def one_slab(index, _):
        own_slab = jnp.concatenate([piece[index] for piece in own], axis=0)
        other_slab = jnp.concatenate([piece[index] for piece in other], axis=0)
        is_first = core == 0
        both = jnp.concatenate(
            [jnp.where(is_first, own_slab, other_slab), jnp.where(is_first, other_slab, own_slab)], axis=1
        )
        result = modes_of(weights, both)
        slab_ref[0, index] = result[:, :lanes]
        slab_ref[1, index] = result[:, lanes:]
        return 0

    slabs = own[0].shape[0]
    lax.fori_loop(0, slabs, one_slab, 0, unroll=True)
    width, rows_y = lanes // tm_count, block_rows * tm_count
    lane = lax.broadcasted_iota(jnp.int32, (1, lanes), 1)
    part, column = lax.div(lane, width), lax.rem(lane, width)
    has_border = jnp.where(column == 0, -0.5, jnp.where(column == width - 1, 0.5, 0.0))
    places, offset, _ = border_layout(rows_y, lanes, width)
    border_of = jnp.where(column == 0, 0, offset) + t * width - 1 + part * block_rows
    border_lanes = lax.broadcasted_iota(jnp.int32, (2 * lanes, lanes), 0)
    border_lanes = jnp.where(border_lanes >= lanes, border_lanes - lanes, border_lanes)
    borders = []
    for slab in range(3 * block_rows, slabs):
        both = jnp.concatenate([slab_ref[0, slab], slab_ref[1, slab]], axis=0)
        borders.append(jnp.concatenate(split_high_low(both), axis=1))
    some = math.gcd(modes, 32)
    for c, (slab, first_lane) in enumerate(places):
        for row in range(block_rows):
            center = row * 3 + c
            if row % 2 == 0:
                picks = [
                    jnp.where(
                        border_lanes == jnp.bitwise_and(border_of + (first_lane + row + k), lanes - 1), has_border, 0.0
                    ).astype(BF16)
                    for k in range(2)
                ]
                border = jnp.dot(borders[slab], jnp.concatenate(picks, axis=1), preferred_element_type=F32)
            for plane, first in itertools.product(range(2), range(0, modes, some)):
                place = plane * block_rows + row
                here = pl.ds(first, some)
                value = slab_ref[plane, center, here, :]
                stream = slab_ref[1 - plane, center, here, :] * (0.5 if plane == 0 else -0.5)
                if row + 1 < block_rows:
                    above = slab_ref[plane, center + 3, here, :]
                else:
                    above = pltpu.roll(slab_ref[plane, c, here, :], lanes - width, 1)
                    above = jnp.where(lane < lanes - width, above, 0.0)
                if row > 0:
                    below = slab_ref[plane, center - 3, here, :]
                else:
                    below = pltpu.roll(slab_ref[plane, 3 * (block_rows - 1) + c, here, :], width, 1)
                    below = jnp.where(lane >= width, below, 0.0)
                normal = (above - below) * 0.5
                after = jnp.where(column < width - 1, pltpu.roll(value, lanes - 1, 1), 0.0)
                before = jnp.where(column > 0, pltpu.roll(value, 1, 1), 0.0)
                beside = border[plane * modes + first :, row % 2 * lanes :][:some, :lanes]
                span = (after - before) * 0.5 + beside
                carry_ref[pl.ds(first * (3 * height) + c * height + place, some, stride=3 * height), :] = value
                for d, slope in enumerate((stream, normal, span)):
                    start = first * (9 * height) + (d * 3 + c) * height + place
                    slope_ref[pl.ds(start, some, stride=9 * height), :] = slope
                if (plane == 1) == (row < block_rows // 2):
                    near_ref[center, here, :] = value
            for plane in range(2):
                store_projection(rhs_ref, c * height + plane * block_rows + row, slab_ref[plane, center])
    codes.wait()

    def one_peer(number, _):
        @pl.when(number > 0)
        def _():
            out_ref[number - 1] = project(conv_ref, rhs_ref, chips * share, 3 * height, lanes)

        following = lax.rem(first_peer + number, tm_count)
        pick_inner(held_codes_ref, carry_ref, slope_ref, conv_ref, following, (chips, share, bits))
        return 0

    lax.fori_loop(0, out_ref.shape[0] + 1, one_peer, 0)


def pick_inner(codes_ref, carry_ref, slope_ref, conv_ref, peer, sizes):
    places = conv_ref.shape[0] // (sizes[0] * sizes[1])
    height = places // 3

    def one_pair(slot, i, j):
        carry = carry_ref[pl.ds(pl.multiple_of(i * places, 8), places), :]
        slope = slope_ref[pl.ds(pl.multiple_of(j * (3 * places), 8), 3 * places), :]
        rows = [
            sum(
                carry[d * height : (d + 1) * height] * slope[(d * 3 + c) * height : (d * 3 + c + 1) * height]
                for d in range(3)
            )
            for c in range(3)
        ]
        conv_ref[pl.ds(pl.multiple_of(slot * places, 8), places), :] = jnp.concatenate(rows, axis=0)

    for_pairs_of(codes_ref, peer, sizes, one_pair)


def rest_kernel(
    codes_ref, carry_ref, slope_ref, rhs_ref, picked_ref, out_ref, conv_ref, held_codes_ref, sem, *, sizes
):
    del picked_ref
    chips, share, _ = sizes
    codes = copy_of_codes(codes_ref, held_codes_ref, sem)
    block, lanes = chips * share, conv_ref.shape[1]
    places = conv_ref.shape[0] // block

    def one_peer(peer, _):
        out_ref[peer] = project(conv_ref, rhs_ref, block, places, lanes)

        @pl.when(peer == 0)
        def _():
            codes.wait()

        @pl.when(peer + 1 < out_ref.shape[0])
        def _():
            pick_inner(held_codes_ref, carry_ref, slope_ref, conv_ref, peer + 1, sizes)

        return 0

    lax.fori_loop(0, out_ref.shape[0], one_peer, 0)


def far_kernel(codes_ref, coeffs_ref, *refs, peer, sizes):
    local_s, block_rows, tm_count, chips, share, bits = sizes
    next_own, next_other, near_ref, inner_ref = refs[:tm_count], *refs[tm_count : tm_count + 3]
    carry_ref, slope_ref, rhs_ref, out_ref, conv_ref, held_codes_ref, sem = refs[tm_count + 3 :]
    codes = copy_of_codes(codes_ref, held_codes_ref, sem)
    _, _, core = place_of_device()
    is_first = core == 0
    modes, lanes = near_ref.shape[1:]
    height = 2 * block_rows
    half = block_rows // 2 * 3
    some = math.gcd(modes, 32)
    weights = mode_weights(coeffs_ref, local_s, tm_count)
    for slab in range(half):
        mine = jnp.concatenate([next_own[peer][slab] for peer in range(tm_count)], axis=0)
        theirs = jnp.concatenate([next_other[peer, slab] for peer in range(tm_count)], axis=0)
        after, before = jnp.where(is_first, theirs, mine), jnp.where(is_first, mine, theirs)
        result = modes_of(weights, jnp.concatenate([after, before], axis=1))
        row, c = divmod(slab, 3)
        edges = ((near_ref[slab], result[:, :lanes]), (result[:, lanes:], near_ref[half + slab]))
        for number, (low, high) in enumerate(edges):
            place = number * block_rows + 2 * row
            for first in range(0, modes, some):
                one, two = low[first : first + some], high[first : first + some]
                for at, value, across in ((place, one, two * 0.5), (place + 1, two, one * -0.5)):
                    if c == 0:
                        carry_ref[pl.ds(first * height + at, some, stride=height), :] = value
                    start = first * (3 * height) + c * height + at
                    slope_ref[pl.ds(start, some, stride=3 * height), :] = across
            store_projection(rhs_ref, c * height + place, low)
            store_projection(rhs_ref, c * height + place + 1, high)
    codes.wait()
    pick_edge(held_codes_ref, carry_ref, slope_ref, conv_ref, peer, (chips, share, bits))
    out_ref[...] = edge_sum(conv_ref, rhs_ref, inner_ref, peer)
    pick_edge(held_codes_ref, carry_ref, slope_ref, conv_ref, peer - 1, (chips, share, bits))


def pick_edge(codes_ref, carry_ref, slope_ref, conv_ref, peer, sizes):
    places = conv_ref.shape[0] // (sizes[0] * sizes[1])
    height = places // 3

    def one_pair(slot, i, j):
        carry = carry_ref[pl.ds(pl.multiple_of(i * height, 8), height), :]
        slope = slope_ref[pl.ds(pl.multiple_of(j * places, 8), places), :]
        rows = [carry * slope[c * height : (c + 1) * height] for c in range(3)]
        conv_ref[pl.ds(pl.multiple_of(slot * places, 8), places), :] = jnp.concatenate(rows, axis=0)

    for_pairs_of(codes_ref, peer, sizes, one_pair)


def edge_sum(picked_ref, rhs_ref, inner_ref, peer):
    block = inner_ref.shape[1]
    places = picked_ref.shape[0] // block
    return inner_ref[peer % inner_ref.shape[0]] + project(picked_ref, rhs_ref, block, places, picked_ref.shape[1])


def edge_kernel(
    codes_ref, carry_ref, slope_ref, rhs_ref, inner_ref, picked_ref, out_ref, conv_ref, held_codes_ref, sem, *,
    peer, sizes
):
    codes = copy_of_codes(codes_ref, held_codes_ref, sem)
    out_ref[...] = edge_sum(picked_ref, rhs_ref, inner_ref, peer)
    codes.wait()
    pick_edge(held_codes_ref, carry_ref, slope_ref, conv_ref, peer - 1, sizes)


def picked_edge_kernel(rhs_ref, inner_ref, picked_ref, out_ref, *, peer):
    out_ref[...] = edge_sum(picked_ref, rhs_ref, inner_ref, peer)


def own_edge_kernel(
    codes_ref, carry_ref, slope_ref, rhs_ref, inner_ref, after_ref, out_ref, conv_ref, held_codes_ref, sem, *, sizes
):
    del after_ref
    copy_of_codes(codes_ref, held_codes_ref, sem).wait()
    pick_edge(held_codes_ref, carry_ref, slope_ref, conv_ref, 0, sizes)
    out_ref[...] = edge_sum(conv_ref, rhs_ref, inner_ref, 0)


def add_kernel(own_ref, *refs):
    *arrived_refs, out_ref = refs
    total = own_ref[...]
    for arrived_ref in arrived_refs:
        total = total + arrived_ref[...]
    out_ref[...] = total


def vmem_limit(mebibytes):
    return pltpu.CompilerParams(vmem_limit_bytes=mebibytes * 2**20)


def in_vmem(array):
    return pltpu.with_memory_space_constraint(array, pltpu.VMEM)


def shards(snapshots, coeffs, pair_table):
    tm_count, space_count = lax.axis_size("tm"), lax.axis_size("space")
    chips = space_count // 2
    local_s, _, _, rows_y, lanes = snapshots.shape
    modes = coeffs.shape[1]
    block_rows = rows_y // tm_count
    slabs = 3 * block_rows + border_layout(rows_y, lanes, lanes // tm_count)[2]
    share = pair_table.shape[0] // (tm_count * space_count)
    factor = float(space_count * rows_y * lanes) ** (-0.5)
    bits = modes.bit_length() - 1
    assert modes == 2**bits
    vmem = pl.BlockSpec(memory_space=pltpu.VMEM)
    block = chips * share
    height = 2 * block_rows
    depth = 3 * height * lanes

    swap = [(2 * chip + c, 2 * chip + 1 - c) for chip in range(chips) for c in range(2)]

    def across(peer):
        return [(i, i ^ peer) for i in range(tm_count)]

    with jax.named_scope("pack"):
        *packed, codes, held_coeffs = pl.pallas_call(
            functools.partial(pack_kernel, sizes=(local_s, rows_y, tm_count)),
            out_shape=[pltpu.VMEM((slabs, local_s, lanes), F32)] * tm_count
            + [
                pltpu.VMEM((tm_count, block_rows // 2 * 3, local_s, lanes), F32),
                pltpu.VMEM((pair_table.shape[0],), jnp.int32),
                pltpu.VMEM(coeffs.shape, F32),
            ],
            in_specs=[pl.BlockSpec(memory_space=pltpu.HBM)] * 3,
            out_specs=[vmem] * (tm_count + 3),
            scratch_shapes=[
                pltpu.VMEM((tm_count, slabs, local_s, lanes), F32),
                pltpu.VMEM((3, local_s, rows_y, lanes), F32),
                pltpu.VMEM((2, pair_table.shape[0]), jnp.int32),
                pltpu.SemaphoreType.DMA((5,)),
            ],
            compiler_params=vmem_limit(16),
        )(
            *[
                pltpu.with_memory_space_constraint(array, pltpu.HBM)
                for array in (snapshots.reshape(local_s, 3, rows_y, lanes), pair_table.T, coeffs)
            ]
        )
        codes, coeffs = in_vmem(codes), in_vmem(held_coeffs)
    with jax.named_scope("to_next_plane"):
        ring = [(place, (place + (1 if place % 2 else -1)) % space_count) for place in range(space_count)]
        across_edge = lax.ppermute(packed[tm_count], "space", ring)
    with jax.named_scope("to_columns"):
        own = [packed[0]] + [lax.ppermute(packed[peer], "tm", across(peer)) for peer in range(1, tm_count)]
    with jax.named_scope("next_to_columns"):
        across_edge, own[:3] = lax.optimization_barrier((across_edge, own[:3]))
        parts = [across_edge[peer] for peer in range(tm_count)]
        parts, own[3:] = lax.optimization_barrier((parts, own[3:]))
        next_own = [parts[0]] + [lax.ppermute(parts[peer], "tm", across(peer)) for peer in range(1, tm_count)]
    with jax.named_scope("to_other_core"):
        other = [lax.ppermute(piece, "space", swap) for piece in own]
    early = tm_count // 2
    picked = pltpu.VMEM((block * 3 * height, lanes), F32)
    held_codes = [pltpu.SMEM(codes.shape, jnp.int32), pltpu.SemaphoreType.DMA]
    groups = pltpu.VMEM((early, block, modes), F32)
    with jax.named_scope("inner_terms"):
        near, *inner_tables, early_sums, first_picked = pl.pallas_call(
            functools.partial(inner_kernel, first_peer=early, sizes=(local_s, block_rows, tm_count, chips, share, bits)),
            out_shape=[
                pltpu.VMEM((block_rows * 3, modes, lanes), F32),
                pltpu.VMEM((modes * 3 * height, lanes), F32),
                pltpu.VMEM((modes * 9 * height, lanes), F32),
                pltpu.VMEM((depth, 2 * modes), BF16),
                groups,
                picked,
            ],
            in_specs=[vmem] * (2 * tm_count + 2),
            out_specs=[vmem] * 6,
            scratch_shapes=[pltpu.VMEM((2, slabs, modes, lanes), F32)] + held_codes,
            compiler_params=vmem_limit(24),
            cost_estimate=pl.CostEstimate(flops=12 * 10**9, bytes_accessed=10**7, transcendentals=0),
        )(codes, coeffs, *[in_vmem(piece) for piece in (*own, *other)])
    with jax.named_scope("next_to_other_core"):
        next_own, inner_tables = lax.optimization_barrier((next_own, inner_tables))
        next_other = lax.ppermute(jnp.stack(next_own), "space", swap)
    with jax.named_scope("inner_terms"):
        late_sums, _ = pl.pallas_call(
            functools.partial(rest_kernel, sizes=(chips, share, bits)),
            out_shape=[groups, picked],
            in_specs=[vmem] * 5,
            out_specs=[vmem] * 2,
            input_output_aliases={4: 1},
            scratch_shapes=held_codes,
            compiler_params=vmem_limit(16),
            cost_estimate=pl.CostEstimate(flops=8 * 10**9, bytes_accessed=10**7, transcendentals=0),
        )(codes, *[in_vmem(table) for table in (*inner_tables, first_picked)])
    with jax.named_scope("edge_terms"):
        *tables, summed, next_picked = pl.pallas_call(
            functools.partial(
                far_kernel, peer=tm_count - 1, sizes=(local_s, block_rows, tm_count, chips, share, bits)
            ),
            out_shape=[
                pltpu.VMEM((modes * height, lanes), F32),
                pltpu.VMEM((modes * 3 * height, lanes), F32),
                pltpu.VMEM((depth, 2 * modes), BF16),
                pltpu.VMEM((block, modes), F32),
                picked,
            ],
            in_specs=[vmem] * (tm_count + 5),
            out_specs=[vmem] * 5,
            scratch_shapes=held_codes,
            compiler_params=vmem_limit(16),
        )(codes, coeffs, *[in_vmem(piece) for piece in (*next_own, next_other, near, early_sums)])
    arrived, taken = [], 2
    for peer in reversed(range(tm_count - 1)):
        with jax.named_scope("sum_over_columns"):
            arrived.append(lax.ppermute(summed, "tm", across(peer + 1)))
            if peer >= early:
                early_sums, _ = lax.optimization_barrier((early_sums, summed))
            else:
                late_sums, _ = lax.optimization_barrier((late_sums, summed))
        with jax.named_scope("edge_terms"):
            inner_sums = early_sums if peer >= early else late_sums
            edge_cost = pl.CostEstimate(flops=10**8, bytes_accessed=10**5, transcendentals=0)
            if peer > 1:
                summed, next_picked = pl.pallas_call(
                    functools.partial(edge_kernel, peer=peer, sizes=(chips, share, bits)),
                    out_shape=[pltpu.VMEM((block, modes), F32), picked],
                    in_specs=[vmem] * 6,
                    out_specs=[vmem] * 2,
                    scratch_shapes=held_codes,
                    compiler_params=vmem_limit(16),
                    cost_estimate=edge_cost,
                )(codes, *[in_vmem(table) for table in (*tables, inner_sums, next_picked)])
            elif peer:
                summed = pl.pallas_call(
                    functools.partial(picked_edge_kernel, peer=peer),
                    out_shape=pltpu.VMEM((block, modes), F32),
                    in_specs=[vmem] * 3,
                    out_specs=vmem,
                    compiler_params=vmem_limit(16),
                    cost_estimate=edge_cost,
                )(*[in_vmem(table) for table in (tables[2], inner_sums, next_picked)])
            else:
                summed = pl.pallas_call(
                    functools.partial(own_edge_kernel, sizes=(chips, share, bits)),
                    out_shape=pltpu.VMEM((block, modes), F32),
                    in_specs=[vmem] * 6,
                    out_specs=vmem,
                    scratch_shapes=[picked] + held_codes,
                    compiler_params=vmem_limit(16),
                    cost_estimate=edge_cost,
                )(codes, *[in_vmem(table) for table in (*tables, inner_sums, summed)])
                summed = pl.pallas_call(
                    add_kernel,
                    out_shape=pltpu.VMEM((block, modes), F32),
                    in_specs=[vmem] * (1 + taken),
                    out_specs=vmem,
                )(*[in_vmem(table) for table in (summed, *arrived[:taken])])
    with jax.named_scope("sum_over_columns"):
        for part in arrived[taken:]:
            summed = summed + part
    with jax.named_scope("sum_over_chips"):
        shares = summed.reshape(chips, share, modes)
        parts = None
        for step in reversed(range(1, chips)):
            pairing = [(2 * chip + c, 2 * (chip ^ step) + c) for chip in range(chips) for c in range(2)]
            part = lax.ppermute(shares[step], "space", pairing)
            parts = part if parts is None else part + parts
        result = shares[0] + parts
        return result * factor


def solution(mesh):
    placed = (P("tm", None, "space", None, None), P(), P())
    return jax.shard_map(
        shards, mesh=mesh, in_specs=placed, out_specs=P(("tm", "space"), None), check_vma=False
    )
```

```python
import functools
import itertools
import math

import jax
import jax.numpy as jnp
from jax import lax
from jax.experimental import pallas as pl
from jax.experimental.pallas import tpu as pltpu
from jax.sharding import PartitionSpec as P

F32 = jnp.float32
BF16 = jnp.bfloat16


def place_of_device():
    place = lax.axis_index("space")
    return lax.axis_index("tm"), lax.shift_right_logical(place, 1), jnp.bitwise_and(place, 1)


def split_high_low(values):
    high = values.astype(BF16)
    low = (values - high.astype(F32)).astype(BF16)
    return high, low


def border_layout(rows_y, lanes, width):
    per_run = (width + 1) // rows_y
    if per_run:
        run = width + 1 + per_run * rows_y
        firsts = [c // per_run * run + c % per_run * rows_y for c in range(3)]
        if firsts[2] + width + 1 + rows_y <= lanes:
            return [(0, first) for first in firsts], width + 1, 1
    per_slab = lanes // (2 * rows_y)
    places = [(c // per_slab, c % per_slab * 2 * rows_y) for c in range(3)]
    return places, rows_y, places[2][0] + 1


def exchange_blocks(rows, lane, width, lanes):
    rows = list(rows)
    step = len(rows) // 2
    while step:
        keeps = jnp.bitwise_and(lane, step * width) == 0
        for low in range(len(rows)):
            if low & step == 0:
                first, second = rows[low], rows[low + step]
                rows[low] = jnp.where(keeps, first, pltpu.roll(second, step * width, 1))
                rows[low + step] = jnp.where(keeps, pltpu.roll(first, lanes - step * width, 1), second)
        step //= 2
    return rows


def pack_kernel(field_ref, pairs_ref, coeffs_ref, *refs, sizes):
    *out_refs, codes_ref, held_coeffs_ref, sorted_ref, held_ref, held_pairs_ref, sems = refs
    local_s, rows_y, tm_count = sizes
    lanes = field_ref.shape[3]
    copies = [pltpu.make_async_copy(field_ref.at[:, c], held_ref.at[c], sems.at[c]) for c in range(3)]
    copies.append(pltpu.make_async_copy(pairs_ref, held_pairs_ref, sems.at[3]))
    copies.append(pltpu.make_async_copy(coeffs_ref, held_coeffs_ref, sems.at[4]))
    for copy in copies:
        copy.start()
    rows_ref = held_ref.reshape(3 * local_s * rows_y, lanes)
    t, _, core = place_of_device()
    width, groups = lanes // tm_count, rows_y // tm_count
    lane = lax.broadcasted_iota(jnp.int32, (local_s, lanes), 1)
    places, offset, border_slabs = border_layout(rows_y, lanes, width)
    borders = [[jnp.zeros((local_s, lanes), F32) for _ in range(tm_count)] for _ in range(border_slabs)]
    for c, (slab, first_lane) in enumerate(places):
        copies[c].wait()

        def one_group(g, border, c=c, first_lane=first_lane):
            border = list(border)
            rows = []
            for q in range(tm_count):
                y = q * groups + g
                row = rows_ref[pl.ds(c * local_s * rows_y + y, local_s, stride=rows_y), :]
                rows.append(row)
                before = first_lane + y
                after = before + offset - (width + 1)
                moved = pltpu.roll(row, jnp.bitwise_and(before, lanes - 1), 1)
                moved_after = moved if offset == width + 1 else pltpu.roll(row, jnp.bitwise_and(after, lanes - 1), 1)
                for block in range(tm_count):
                    at_before = lane == jnp.bitwise_and(before + block * width - 1, lanes - 1)
                    at_after = lane == jnp.bitwise_and(after + (block + 1) * width, lanes - 1)
                    if moved is moved_after:
                        border[block] = jnp.where(jnp.logical_or(at_before, at_after), moved, border[block])
                    else:
                        border[block] = jnp.where(at_before, moved, jnp.where(at_after, moved_after, border[block]))
            for block, main in enumerate(exchange_blocks(rows, lane, width, lanes)):
                sorted_ref[block, g * 3 + c] = main
            return tuple(border)

        borders[slab] = lax.fori_loop(0, groups, one_group, tuple(borders[slab]), unroll=True)
    half = groups // 2 * 3
    for slab, border in enumerate(borders):
        for block in range(tm_count):
            sorted_ref[block, groups * 3 + slab] = border[block]
    for peer in range(tm_count):
        block = jnp.bitwise_xor(t, peer)
        out_refs[peer][...] = sorted_ref[block]
        out_refs[tm_count][peer] = sorted_ref[block, pl.ds(core * half, half)]
    copies[3].wait()
    copies[4].wait()
    for first in range(0, codes_ref.shape[0], lanes):
        here = pl.ds(first, lanes)
        codes_ref[here] = held_pairs_ref[0, here] * held_coeffs_ref.shape[1] + held_pairs_ref[1, here]


def mode_weights(coeffs_ref, local_s, tm_count):
    t, _, _ = place_of_device()
    ordered = jnp.concatenate(
        [
            coeffs_ref[pl.ds(pl.multiple_of(jnp.bitwise_xor(t, peer) * local_s, 8), local_s), :]
            for peer in range(tm_count)
        ],
        axis=0,
    )
    high, low = split_high_low(ordered.T)
    return jnp.concatenate([high, low, high, low], axis=1)


def modes_of(weights, slab):
    high, low = split_high_low(slab)
    return jnp.dot(weights, jnp.concatenate([high, high, low, low], axis=0), preferred_element_type=F32)


def store_projection(rhs_ref, place, mode_slab):
    high, low = split_high_low(mode_slab.T)
    modes, lanes = mode_slab.shape
    rhs_ref[place * lanes : (place + 1) * lanes, 0:modes] = high
    rhs_ref[place * lanes : (place + 1) * lanes, modes : 2 * modes] = low


def project(conv_ref, rhs_ref, block, places, lanes):
    both = None
    for place in range(0, places, 2):
        highs, lows = zip(
            *(split_high_low(conv_ref[pl.ds(place + k, block, stride=places), :]) for k in range(2))
        )
        lhs = jnp.concatenate([jnp.concatenate(highs, axis=1), jnp.concatenate(lows, axis=1)], axis=0)
        part = jnp.dot(lhs, rhs_ref[place * lanes : (place + 2) * lanes, :], preferred_element_type=F32)
        both = part if both is None else both + part
    modes = both.shape[1] // 2
    return (both[:block, :modes] + both[:block, modes:]) + (both[block:, :modes] + both[block:, modes:])


def for_pairs_of(codes_ref, peer, sizes, one_pair):
    chips, share, bits = sizes
    t, chip, core = place_of_device()
    first_chip = jnp.bitwise_xor(t, peer) * chips

    def one_share(ahead, _):
        base = ((first_chip + jnp.bitwise_xor(chip, ahead)) * 2 + core) * share

        def one(q, _):
            code = codes_ref[base + q]
            one_pair(ahead * share + q, lax.shift_right_logical(code, bits), jnp.bitwise_and(code, 2**bits - 1))
            return 0

        return lax.fori_loop(0, share, one, 0, unroll=True)

    lax.fori_loop(0, chips, one_share, 0)


def copy_of_codes(codes_ref, held_codes_ref, sem):
    copy = pltpu.make_async_copy(codes_ref, held_codes_ref, sem)
    copy.start()
    return copy


def inner_kernel(codes_ref, coeffs_ref, *refs, first_peer, sizes):
    local_s, block_rows, tm_count, chips, share, bits = sizes
    own, other = refs[:tm_count], refs[tm_count : 2 * tm_count]
    near_ref, carry_ref, slope_ref, rhs_ref, out_ref, conv_ref, slab_ref, held_codes_ref, sem = refs[2 * tm_count :]
    codes = copy_of_codes(codes_ref, held_codes_ref, sem)
    t, _, core = place_of_device()
    modes, lanes = coeffs_ref.shape[1], own[0].shape[2]
    height = 2 * block_rows
    weights = mode_weights(coeffs_ref, local_s, tm_count)

    def one_slab(index, _):
        own_slab = jnp.concatenate([piece[index] for piece in own], axis=0)
        other_slab = jnp.concatenate([piece[index] for piece in other], axis=0)
        is_first = core == 0
        both = jnp.concatenate(
            [jnp.where(is_first, own_slab, other_slab), jnp.where(is_first, other_slab, own_slab)], axis=1
        )
        result = modes_of(weights, both)
        slab_ref[0, index] = result[:, :lanes]
        slab_ref[1, index] = result[:, lanes:]
        return 0

    slabs = own[0].shape[0]
    lax.fori_loop(0, slabs, one_slab, 0, unroll=True)
    width, rows_y = lanes // tm_count, block_rows * tm_count
    lane = lax.broadcasted_iota(jnp.int32, (1, lanes), 1)
    part, column = lax.div(lane, width), lax.rem(lane, width)
    has_border = jnp.where(column == 0, -0.5, jnp.where(column == width - 1, 0.5, 0.0))
    places, offset, _ = border_layout(rows_y, lanes, width)
    border_of = jnp.where(column == 0, 0, offset) + t * width - 1 + part * block_rows
    border_lanes = lax.broadcasted_iota(jnp.int32, (2 * lanes, lanes), 0)
    border_lanes = jnp.where(border_lanes >= lanes, border_lanes - lanes, border_lanes)
    borders = []
    for slab in range(3 * block_rows, slabs):
        both = jnp.concatenate([slab_ref[0, slab], slab_ref[1, slab]], axis=0)
        borders.append(jnp.concatenate(split_high_low(both), axis=1))
    some = math.gcd(modes, 32)
    for c, (slab, first_lane) in enumerate(places):
        for row in range(block_rows):
            center = row * 3 + c
            if row % 2 == 0:
                picks = [
                    jnp.where(
                        border_lanes == jnp.bitwise_and(border_of + (first_lane + row + k), lanes - 1), has_border, 0.0
                    ).astype(BF16)
                    for k in range(2)
                ]
                border = jnp.dot(borders[slab], jnp.concatenate(picks, axis=1), preferred_element_type=F32)
            for plane, first in itertools.product(range(2), range(0, modes, some)):
                place = plane * block_rows + row
                here = pl.ds(first, some)
                value = slab_ref[plane, center, here, :]
                stream = slab_ref[1 - plane, center, here, :] * (0.5 if plane == 0 else -0.5)
                if row + 1 < block_rows:
                    above = slab_ref[plane, center + 3, here, :]
                else:
                    above = pltpu.roll(slab_ref[plane, c, here, :], lanes - width, 1)
                    above = jnp.where(lane < lanes - width, above, 0.0)
                if row > 0:
                    below = slab_ref[plane, center - 3, here, :]
                else:
                    below = pltpu.roll(slab_ref[plane, 3 * (block_rows - 1) + c, here, :], width, 1)
                    below = jnp.where(lane >= width, below, 0.0)
                normal = (above - below) * 0.5
                after = jnp.where(column < width - 1, pltpu.roll(value, lanes - 1, 1), 0.0)
                before = jnp.where(column > 0, pltpu.roll(value, 1, 1), 0.0)
                beside = border[plane * modes + first :, row % 2 * lanes :][:some, :lanes]
                span = (after - before) * 0.5 + beside
                carry_ref[pl.ds(first * (3 * height) + c * height + place, some, stride=3 * height), :] = value
                for d, slope in enumerate((stream, normal, span)):
                    start = first * (9 * height) + (d * 3 + c) * height + place
                    slope_ref[pl.ds(start, some, stride=9 * height), :] = slope
                if (plane == 1) == (row < block_rows // 2):
                    near_ref[center, here, :] = value
            for plane in range(2):
                store_projection(rhs_ref, c * height + plane * block_rows + row, slab_ref[plane, center])
    codes.wait()

    def one_peer(number, _):
        @pl.when(number > 0)
        def _():
            out_ref[number - 1] = project(conv_ref, rhs_ref, chips * share, 3 * height, lanes)

        following = lax.rem(first_peer + number, tm_count)
        pick_inner(held_codes_ref, carry_ref, slope_ref, conv_ref, following, (chips, share, bits))
        return 0

    lax.fori_loop(0, out_ref.shape[0] + 1, one_peer, 0)


def pick_inner(codes_ref, carry_ref, slope_ref, conv_ref, peer, sizes):
    places = conv_ref.shape[0] // (sizes[0] * sizes[1])
    height = places // 3

    def one_pair(slot, i, j):
        carry = carry_ref[pl.ds(pl.multiple_of(i * places, 8), places), :]
        slope = slope_ref[pl.ds(pl.multiple_of(j * (3 * places), 8), 3 * places), :]
        rows = [
            sum(
                carry[d * height : (d + 1) * height] * slope[(d * 3 + c) * height : (d * 3 + c + 1) * height]
                for d in range(3)
            )
            for c in range(3)
        ]
        conv_ref[pl.ds(pl.multiple_of(slot * places, 8), places), :] = jnp.concatenate(rows, axis=0)

    for_pairs_of(codes_ref, peer, sizes, one_pair)


def rest_kernel(
    codes_ref, carry_ref, slope_ref, rhs_ref, picked_ref, out_ref, conv_ref, held_codes_ref, sem, *, sizes
):
    del picked_ref
    chips, share, _ = sizes
    codes = copy_of_codes(codes_ref, held_codes_ref, sem)
    block, lanes = chips * share, conv_ref.shape[1]
    places = conv_ref.shape[0] // block

    def one_peer(peer, _):
        out_ref[peer] = project(conv_ref, rhs_ref, block, places, lanes)

        @pl.when(peer == 0)
        def _():
            codes.wait()

        @pl.when(peer + 1 < out_ref.shape[0])
        def _():
            pick_inner(held_codes_ref, carry_ref, slope_ref, conv_ref, peer + 1, sizes)

        return 0

    lax.fori_loop(0, out_ref.shape[0], one_peer, 0)


def far_kernel(codes_ref, coeffs_ref, *refs, peer, sizes):
    local_s, block_rows, tm_count, chips, share, bits = sizes
    next_own, next_other, near_ref, inner_ref = refs[:tm_count], *refs[tm_count : tm_count + 3]
    carry_ref, slope_ref, rhs_ref, out_ref, conv_ref, held_codes_ref, sem = refs[tm_count + 3 :]
    codes = copy_of_codes(codes_ref, held_codes_ref, sem)
    _, _, core = place_of_device()
    is_first = core == 0
    modes, lanes = near_ref.shape[1:]
    height = 2 * block_rows
    half = block_rows // 2 * 3
    some = math.gcd(modes, 32)
    weights = mode_weights(coeffs_ref, local_s, tm_count)
    for slab in range(half):
        mine = jnp.concatenate([next_own[peer][slab] for peer in range(tm_count)], axis=0)
        theirs = jnp.concatenate([next_other[peer, slab] for peer in range(tm_count)], axis=0)
        after, before = jnp.where(is_first, theirs, mine), jnp.where(is_first, mine, theirs)
        result = modes_of(weights, jnp.concatenate([after, before], axis=1))
        row, c = divmod(slab, 3)
        edges = ((near_ref[slab], result[:, :lanes]), (result[:, lanes:], near_ref[half + slab]))
        for number, (low, high) in enumerate(edges):
            place = number * block_rows + 2 * row
            for first in range(0, modes, some):
                one, two = low[first : first + some], high[first : first + some]
                for at, value, across in ((place, one, two * 0.5), (place + 1, two, one * -0.5)):
                    if c == 0:
                        carry_ref[pl.ds(first * height + at, some, stride=height), :] = value
                    start = first * (3 * height) + c * height + at
                    slope_ref[pl.ds(start, some, stride=3 * height), :] = across
            store_projection(rhs_ref, c * height + place, low)
            store_projection(rhs_ref, c * height + place + 1, high)
    codes.wait()
    pick_edge(held_codes_ref, carry_ref, slope_ref, conv_ref, peer, (chips, share, bits))
    out_ref[...] = edge_sum(conv_ref, rhs_ref, inner_ref, peer)
    pick_edge(held_codes_ref, carry_ref, slope_ref, conv_ref, peer - 1, (chips, share, bits))


def pick_edge(codes_ref, carry_ref, slope_ref, conv_ref, peer, sizes):
    places = conv_ref.shape[0] // (sizes[0] * sizes[1])
    height = places // 3

    def one_pair(slot, i, j):
        carry = carry_ref[pl.ds(pl.multiple_of(i * height, 8), height), :]
        slope = slope_ref[pl.ds(pl.multiple_of(j * places, 8), places), :]
        rows = [carry * slope[c * height : (c + 1) * height] for c in range(3)]
        conv_ref[pl.ds(pl.multiple_of(slot * places, 8), places), :] = jnp.concatenate(rows, axis=0)

    for_pairs_of(codes_ref, peer, sizes, one_pair)


def edge_sum(picked_ref, rhs_ref, inner_ref, peer):
    block = inner_ref.shape[1]
    places = picked_ref.shape[0] // block
    return inner_ref[peer % inner_ref.shape[0]] + project(picked_ref, rhs_ref, block, places, picked_ref.shape[1])


def edge_kernel(
    codes_ref, carry_ref, slope_ref, rhs_ref, inner_ref, picked_ref, out_ref, conv_ref, held_codes_ref, sem, *,
    peer, sizes
):
    codes = copy_of_codes(codes_ref, held_codes_ref, sem)
    out_ref[...] = edge_sum(picked_ref, rhs_ref, inner_ref, peer)
    codes.wait()
    pick_edge(held_codes_ref, carry_ref, slope_ref, conv_ref, peer - 1, sizes)


def picked_edge_kernel(rhs_ref, inner_ref, picked_ref, out_ref, *, peer):
    out_ref[...] = edge_sum(picked_ref, rhs_ref, inner_ref, peer)


def own_edge_kernel(
    codes_ref, carry_ref, slope_ref, rhs_ref, inner_ref, after_ref, out_ref, conv_ref, held_codes_ref, sem, *, sizes
):
    del after_ref
    copy_of_codes(codes_ref, held_codes_ref, sem).wait()
    pick_edge(held_codes_ref, carry_ref, slope_ref, conv_ref, 0, sizes)
    out_ref[...] = edge_sum(conv_ref, rhs_ref, inner_ref, 0)


def add_kernel(own_ref, *refs):
    *arrived_refs, out_ref = refs
    total = own_ref[...]
    for arrived_ref in arrived_refs:
        total = total + arrived_ref[...]
    out_ref[...] = total


def vmem_limit(mebibytes):
    return pltpu.CompilerParams(vmem_limit_bytes=mebibytes * 2**20)


def in_vmem(array):
    return pltpu.with_memory_space_constraint(array, pltpu.VMEM)


def shards(snapshots, coeffs, pair_table):
    tm_count, space_count = lax.axis_size("tm"), lax.axis_size("space")
    chips = space_count // 2
    local_s, _, _, rows_y, lanes = snapshots.shape
    modes = coeffs.shape[1]
    block_rows = rows_y // tm_count
    slabs = 3 * block_rows + border_layout(rows_y, lanes, lanes // tm_count)[2]
    share = pair_table.shape[0] // (tm_count * space_count)
    factor = float(space_count * rows_y * lanes) ** (-0.5)
    bits = modes.bit_length() - 1
    assert modes == 2**bits
    vmem = pl.BlockSpec(memory_space=pltpu.VMEM)
    block = chips * share
    height = 2 * block_rows
    depth = 3 * height * lanes

    swap = [(2 * chip + c, 2 * chip + 1 - c) for chip in range(chips) for c in range(2)]

    def across(peer):
        return [(i, i ^ peer) for i in range(tm_count)]

    with jax.named_scope("pack"):
        *packed, codes, held_coeffs = pl.pallas_call(
            functools.partial(pack_kernel, sizes=(local_s, rows_y, tm_count)),
            out_shape=[pltpu.VMEM((slabs, local_s, lanes), F32)] * tm_count
            + [
                pltpu.VMEM((tm_count, block_rows // 2 * 3, local_s, lanes), F32),
                pltpu.VMEM((pair_table.shape[0],), jnp.int32),
                pltpu.VMEM(coeffs.shape, F32),
            ],
            in_specs=[pl.BlockSpec(memory_space=pltpu.HBM)] * 3,
            out_specs=[vmem] * (tm_count + 3),
            scratch_shapes=[
                pltpu.VMEM((tm_count, slabs, local_s, lanes), F32),
                pltpu.VMEM((3, local_s, rows_y, lanes), F32),
                pltpu.VMEM((2, pair_table.shape[0]), jnp.int32),
                pltpu.SemaphoreType.DMA((5,)),
            ],
            compiler_params=vmem_limit(16),
        )(
            *[
                pltpu.with_memory_space_constraint(array, pltpu.HBM)
                for array in (snapshots.reshape(local_s, 3, rows_y, lanes), pair_table.T, coeffs)
            ]
        )
        codes, coeffs = in_vmem(codes), in_vmem(held_coeffs)
    with jax.named_scope("to_next_plane"):
        ring = [(place, (place + (1 if place % 2 else -1)) % space_count) for place in range(space_count)]
        across_edge = lax.ppermute(packed[tm_count], "space", ring)
    with jax.named_scope("to_columns"):
        own = [packed[0]] + [lax.ppermute(packed[peer], "tm", across(peer)) for peer in range(1, tm_count)]
    with jax.named_scope("next_to_columns"):
        early_other = [lax.ppermute(piece, "space", swap) for piece in own[:3]]
        across_edge, own[:3] = lax.optimization_barrier((across_edge, own[:3]))
        parts = [across_edge[peer] for peer in range(tm_count)]
        parts, own[3:] = lax.optimization_barrier((parts, own[3:]))
        next_own = [parts[0]] + [lax.ppermute(parts[peer], "tm", across(peer)) for peer in range(1, tm_count)]
    with jax.named_scope("to_other_core"):
        other = early_other + [lax.ppermute(piece, "space", swap) for piece in own[3:]]
    early = tm_count // 2
    picked = pltpu.VMEM((block * 3 * height, lanes), F32)
    held_codes = [pltpu.SMEM(codes.shape, jnp.int32), pltpu.SemaphoreType.DMA]
    groups = pltpu.VMEM((early, block, modes), F32)
    with jax.named_scope("inner_terms"):
        near, *inner_tables, early_sums, first_picked = pl.pallas_call(
            functools.partial(inner_kernel, first_peer=early, sizes=(local_s, block_rows, tm_count, chips, share, bits)),
            out_shape=[
                pltpu.VMEM((block_rows * 3, modes, lanes), F32),
                pltpu.VMEM((modes * 3 * height, lanes), F32),
                pltpu.VMEM((modes * 9 * height, lanes), F32),
                pltpu.VMEM((depth, 2 * modes), BF16),
                groups,
                picked,
            ],
            in_specs=[vmem] * (2 * tm_count + 2),
            out_specs=[vmem] * 6,
            scratch_shapes=[pltpu.VMEM((2, slabs, modes, lanes), F32)] + held_codes,
            compiler_params=vmem_limit(24),
            cost_estimate=pl.CostEstimate(flops=12 * 10**9, bytes_accessed=10**7, transcendentals=0),
        )(codes, coeffs, *[in_vmem(piece) for piece in (*own, *other)])
    with jax.named_scope("next_to_other_core"):
        next_own, inner_tables = lax.optimization_barrier((next_own, inner_tables))
        next_other = lax.ppermute(jnp.stack(next_own), "space", swap)
    with jax.named_scope("inner_terms"):
        late_sums, _ = pl.pallas_call(
            functools.partial(rest_kernel, sizes=(chips, share, bits)),
            out_shape=[groups, picked],
            in_specs=[vmem] * 5,
            out_specs=[vmem] * 2,
            input_output_aliases={4: 1},
            scratch_shapes=held_codes,
            compiler_params=vmem_limit(16),
            cost_estimate=pl.CostEstimate(flops=8 * 10**9, bytes_accessed=10**7, transcendentals=0),
        )(codes, *[in_vmem(table) for table in (*inner_tables, first_picked)])
    with jax.named_scope("edge_terms"):
        *tables, summed, next_picked = pl.pallas_call(
            functools.partial(
                far_kernel, peer=tm_count - 1, sizes=(local_s, block_rows, tm_count, chips, share, bits)
            ),
            out_shape=[
                pltpu.VMEM((modes * height, lanes), F32),
                pltpu.VMEM((modes * 3 * height, lanes), F32),
                pltpu.VMEM((depth, 2 * modes), BF16),
                pltpu.VMEM((block, modes), F32),
                picked,
            ],
            in_specs=[vmem] * (tm_count + 5),
            out_specs=[vmem] * 5,
            scratch_shapes=held_codes,
            compiler_params=vmem_limit(16),
        )(codes, coeffs, *[in_vmem(piece) for piece in (*next_own, next_other, near, early_sums)])
    arrived, taken = [], 2
    for peer in reversed(range(tm_count - 1)):
        with jax.named_scope("sum_over_columns"):
            arrived.append(lax.ppermute(summed, "tm", across(peer + 1)))
            if peer >= early:
                early_sums, _ = lax.optimization_barrier((early_sums, summed))
            else:
                late_sums, _ = lax.optimization_barrier((late_sums, summed))
        with jax.named_scope("edge_terms"):
            inner_sums = early_sums if peer >= early else late_sums
            edge_cost = pl.CostEstimate(flops=10**8, bytes_accessed=10**5, transcendentals=0)
            if peer > 1:
                summed, next_picked = pl.pallas_call(
                    functools.partial(edge_kernel, peer=peer, sizes=(chips, share, bits)),
                    out_shape=[pltpu.VMEM((block, modes), F32), picked],
                    in_specs=[vmem] * 6,
                    out_specs=[vmem] * 2,
                    scratch_shapes=held_codes,
                    compiler_params=vmem_limit(16),
                    cost_estimate=edge_cost,
                )(codes, *[in_vmem(table) for table in (*tables, inner_sums, next_picked)])
            elif peer:
                summed = pl.pallas_call(
                    functools.partial(picked_edge_kernel, peer=peer),
                    out_shape=pltpu.VMEM((block, modes), F32),
                    in_specs=[vmem] * 3,
                    out_specs=vmem,
                    compiler_params=vmem_limit(16),
                    cost_estimate=edge_cost,
                )(*[in_vmem(table) for table in (tables[2], inner_sums, next_picked)])
            else:
                summed = pl.pallas_call(
                    functools.partial(own_edge_kernel, sizes=(chips, share, bits)),
                    out_shape=pltpu.VMEM((block, modes), F32),
                    in_specs=[vmem] * 6,
                    out_specs=vmem,
                    scratch_shapes=[picked] + held_codes,
                    compiler_params=vmem_limit(16),
                    cost_estimate=edge_cost,
                )(codes, *[in_vmem(table) for table in (*tables, inner_sums, summed)])
                summed = pl.pallas_call(
                    add_kernel,
                    out_shape=pltpu.VMEM((block, modes), F32),
                    in_specs=[vmem] * (1 + taken),
                    out_specs=vmem,
                )(*[in_vmem(table) for table in (summed, *arrived[:taken])])
    with jax.named_scope("sum_over_columns"):
        for part in arrived[taken:]:
            summed = summed + part
    with jax.named_scope("sum_over_chips"):
        shares = summed.reshape(chips, share, modes)
        parts = None
        for step in reversed(range(1, chips)):
            pairing = [(2 * chip + c, 2 * (chip ^ step) + c) for chip in range(chips) for c in range(2)]
            part = lax.ppermute(shares[step], "space", pairing)
            parts = part if parts is None else part + parts
        result = shares[0] + parts
        return result * factor


def solution(mesh):
    placed = (P("tm", None, "space", None, None), P(), P())
    return jax.shard_map(
        shards, mesh=mesh, in_specs=placed, out_specs=P(("tm", "space"), None), check_vma=False
    )
```

```python
import functools
import itertools
import math

import jax
import jax.numpy as jnp
from jax import lax
from jax.experimental import pallas as pl
from jax.experimental.pallas import tpu as pltpu
from jax.sharding import PartitionSpec as P

F32 = jnp.float32
BF16 = jnp.bfloat16


def place_of_device():
    place = lax.axis_index("space")
    return lax.axis_index("tm"), lax.shift_right_logical(place, 1), jnp.bitwise_and(place, 1)


def split_high_low(values):
    high = values.astype(BF16)
    low = (values - high.astype(F32)).astype(BF16)
    return high, low


def border_layout(rows_y, lanes, width):
    per_run = (width + 1) // rows_y
    if per_run:
        run = width + 1 + per_run * rows_y
        firsts = [c // per_run * run + c % per_run * rows_y for c in range(3)]
        if firsts[2] + width + 1 + rows_y <= lanes:
            return [(0, first) for first in firsts], width + 1, 1
    per_slab = lanes // (2 * rows_y)
    places = [(c // per_slab, c % per_slab * 2 * rows_y) for c in range(3)]
    return places, rows_y, places[2][0] + 1


def exchange_blocks(rows, lane, width, lanes):
    rows = list(rows)
    step = len(rows) // 2
    while step:
        keeps = jnp.bitwise_and(lane, step * width) == 0
        for low in range(len(rows)):
            if low & step == 0:
                first, second = rows[low], rows[low + step]
                rows[low] = jnp.where(keeps, first, pltpu.roll(second, step * width, 1))
                rows[low + step] = jnp.where(keeps, pltpu.roll(first, lanes - step * width, 1), second)
        step //= 2
    return rows


def pack_kernel(field_ref, pairs_ref, coeffs_ref, *refs, sizes):
    *out_refs, codes_ref, held_coeffs_ref, sorted_ref, held_ref, held_pairs_ref, sems = refs
    local_s, rows_y, tm_count = sizes
    lanes = field_ref.shape[3]
    copies = [pltpu.make_async_copy(field_ref.at[:, c], held_ref.at[c], sems.at[c]) for c in range(3)]
    copies.append(pltpu.make_async_copy(pairs_ref, held_pairs_ref, sems.at[3]))
    copies.append(pltpu.make_async_copy(coeffs_ref, held_coeffs_ref, sems.at[4]))
    for copy in copies:
        copy.start()
    rows_ref = held_ref.reshape(3 * local_s * rows_y, lanes)
    t, _, core = place_of_device()
    width, groups = lanes // tm_count, rows_y // tm_count
    lane = lax.broadcasted_iota(jnp.int32, (local_s, lanes), 1)
    places, offset, border_slabs = border_layout(rows_y, lanes, width)
    borders = [[jnp.zeros((local_s, lanes), F32) for _ in range(tm_count)] for _ in range(border_slabs)]
    for c, (slab, first_lane) in enumerate(places):
        copies[c].wait()

        def one_group(g, border, c=c, first_lane=first_lane):
            border = list(border)
            rows = []
            for q in range(tm_count):
                y = q * groups + g
                row = rows_ref[pl.ds(c * local_s * rows_y + y, local_s, stride=rows_y), :]
                rows.append(row)
                before = first_lane + y
                after = before + offset - (width + 1)
                moved = pltpu.roll(row, jnp.bitwise_and(before, lanes - 1), 1)
                moved_after = moved if offset == width + 1 else pltpu.roll(row, jnp.bitwise_and(after, lanes - 1), 1)
                for block in range(tm_count):
                    at_before = lane == jnp.bitwise_and(before + block * width - 1, lanes - 1)
                    at_after = lane == jnp.bitwise_and(after + (block + 1) * width, lanes - 1)
                    if moved is moved_after:
                        border[block] = jnp.where(jnp.logical_or(at_before, at_after), moved, border[block])
                    else:
                        border[block] = jnp.where(at_before, moved, jnp.where(at_after, moved_after, border[block]))
            for block, main in enumerate(exchange_blocks(rows, lane, width, lanes)):
                sorted_ref[block, g * 3 + c] = main
            return tuple(border)

        borders[slab] = lax.fori_loop(0, groups, one_group, tuple(borders[slab]), unroll=True)
    half = groups // 2 * 3
    for slab, border in enumerate(borders):
        for block in range(tm_count):
            sorted_ref[block, groups * 3 + slab] = border[block]
    for peer in range(tm_count):
        block = jnp.bitwise_xor(t, peer)
        out_refs[peer][...] = sorted_ref[block]
        out_refs[tm_count][peer] = sorted_ref[block, pl.ds(core * half, half)]
    copies[3].wait()
    copies[4].wait()
    for first in range(0, codes_ref.shape[0], lanes):
        here = pl.ds(first, lanes)
        codes_ref[here] = held_pairs_ref[0, here] * held_coeffs_ref.shape[1] + held_pairs_ref[1, here]


def mode_weights(coeffs_ref, local_s, tm_count):
    t, _, _ = place_of_device()
    ordered = jnp.concatenate(
        [
            coeffs_ref[pl.ds(pl.multiple_of(jnp.bitwise_xor(t, peer) * local_s, 8), local_s), :]
            for peer in range(tm_count)
        ],
        axis=0,
    )
    high, low = split_high_low(ordered.T)
    return jnp.concatenate([high, low, high, low], axis=1)


def modes_of(weights, slab):
    high, low = split_high_low(slab)
    return jnp.dot(weights, jnp.concatenate([high, high, low, low], axis=0), preferred_element_type=F32)


def store_projection(rhs_ref, place, mode_slab):
    high, low = split_high_low(mode_slab.T)
    modes, lanes = mode_slab.shape
    rhs_ref[place * lanes : (place + 1) * lanes, 0:modes] = high
    rhs_ref[place * lanes : (place + 1) * lanes, modes : 2 * modes] = low


def project(conv_ref, rhs_ref, block, places, lanes):
    both = None
    for place in range(0, places, 2):
        highs, lows = zip(
            *(split_high_low(conv_ref[pl.ds(place + k, block, stride=places), :]) for k in range(2))
        )
        lhs = jnp.concatenate([jnp.concatenate(highs, axis=1), jnp.concatenate(lows, axis=1)], axis=0)
        part = jnp.dot(lhs, rhs_ref[place * lanes : (place + 2) * lanes, :], preferred_element_type=F32)
        both = part if both is None else both + part
    modes = both.shape[1] // 2
    return (both[:block, :modes] + both[:block, modes:]) + (both[block:, :modes] + both[block:, modes:])


def for_pairs_of(codes_ref, peer, sizes, one_pair):
    chips, share, bits = sizes
    t, chip, core = place_of_device()
    first_chip = jnp.bitwise_xor(t, peer) * chips

    def one_share(ahead, _):
        base = ((first_chip + jnp.bitwise_xor(chip, ahead)) * 2 + core) * share

        def one(q, _):
            code = codes_ref[base + q]
            one_pair(ahead * share + q, lax.shift_right_logical(code, bits), jnp.bitwise_and(code, 2**bits - 1))
            return 0

        return lax.fori_loop(0, share, one, 0, unroll=True)

    lax.fori_loop(0, chips, one_share, 0)


def copy_of_codes(codes_ref, held_codes_ref, sem):
    copy = pltpu.make_async_copy(codes_ref, held_codes_ref, sem)
    copy.start()
    return copy


def inner_kernel(codes_ref, coeffs_ref, *refs, first_peer, sizes):
    local_s, block_rows, tm_count, chips, share, bits = sizes
    own, other = refs[:tm_count], refs[tm_count : 2 * tm_count]
    near_ref, carry_ref, slope_ref, rhs_ref, out_ref, conv_ref, slab_ref, held_codes_ref, sem = refs[2 * tm_count :]
    codes = copy_of_codes(codes_ref, held_codes_ref, sem)
    t, _, core = place_of_device()
    modes, lanes = coeffs_ref.shape[1], own[0].shape[2]
    height = 2 * block_rows
    weights = mode_weights(coeffs_ref, local_s, tm_count)

    def one_slab(index, _):
        own_slab = jnp.concatenate([piece[index] for piece in own], axis=0)
        other_slab = jnp.concatenate([piece[index] for piece in other], axis=0)
        is_first = core == 0
        both = jnp.concatenate(
            [jnp.where(is_first, own_slab, other_slab), jnp.where(is_first, other_slab, own_slab)], axis=1
        )
        result = modes_of(weights, both)
        slab_ref[0, index] = result[:, :lanes]
        slab_ref[1, index] = result[:, lanes:]
        return 0

    slabs = own[0].shape[0]
    lax.fori_loop(0, slabs, one_slab, 0, unroll=True)
    width, rows_y = lanes // tm_count, block_rows * tm_count
    lane = lax.broadcasted_iota(jnp.int32, (1, lanes), 1)
    part, column = lax.div(lane, width), lax.rem(lane, width)
    has_border = jnp.where(column == 0, -0.5, jnp.where(column == width - 1, 0.5, 0.0))
    places, offset, _ = border_layout(rows_y, lanes, width)
    border_of = jnp.where(column == 0, 0, offset) + t * width - 1 + part * block_rows
    border_lanes = lax.broadcasted_iota(jnp.int32, (2 * lanes, lanes), 0)
    border_lanes = jnp.where(border_lanes >= lanes, border_lanes - lanes, border_lanes)
    borders = []
    for slab in range(3 * block_rows, slabs):
        both = jnp.concatenate([slab_ref[0, slab], slab_ref[1, slab]], axis=0)
        borders.append(jnp.concatenate(split_high_low(both), axis=1))
    some = math.gcd(modes, 32)
    for c, (slab, first_lane) in enumerate(places):
        for row in range(block_rows):
            center = row * 3 + c
            if row % 2 == 0:
                picks = [
                    jnp.where(
                        border_lanes == jnp.bitwise_and(border_of + (first_lane + row + k), lanes - 1), has_border, 0.0
                    ).astype(BF16)
                    for k in range(2)
                ]
                border = jnp.dot(borders[slab], jnp.concatenate(picks, axis=1), preferred_element_type=F32)
            for plane, first in itertools.product(range(2), range(0, modes, some)):
                place = plane * block_rows + row
                here = pl.ds(first, some)
                value = slab_ref[plane, center, here, :]
                stream = slab_ref[1 - plane, center, here, :] * (0.5 if plane == 0 else -0.5)
                if row + 1 < block_rows:
                    above = slab_ref[plane, center + 3, here, :]
                else:
                    above = pltpu.roll(slab_ref[plane, c, here, :], lanes - width, 1)
                    above = jnp.where(lane < lanes - width, above, 0.0)
                if row > 0:
                    below = slab_ref[plane, center - 3, here, :]
                else:
                    below = pltpu.roll(slab_ref[plane, 3 * (block_rows - 1) + c, here, :], width, 1)
                    below = jnp.where(lane >= width, below, 0.0)
                normal = (above - below) * 0.5
                after = jnp.where(column < width - 1, pltpu.roll(value, lanes - 1, 1), 0.0)
                before = jnp.where(column > 0, pltpu.roll(value, 1, 1), 0.0)
                beside = border[plane * modes + first :, row % 2 * lanes :][:some, :lanes]
                span = (after - before) * 0.5 + beside
                carry_ref[pl.ds(first * (3 * height) + c * height + place, some, stride=3 * height), :] = value
                for d, slope in enumerate((stream, normal, span)):
                    start = first * (9 * height) + (d * 3 + c) * height + place
                    slope_ref[pl.ds(start, some, stride=9 * height), :] = slope
                if (plane == 1) == (row < block_rows // 2):
                    near_ref[center, here, :] = value
            for plane in range(2):
                store_projection(rhs_ref, c * height + plane * block_rows + row, slab_ref[plane, center])
    codes.wait()

    def one_peer(number, _):
        @pl.when(number > 0)
        def _():
            out_ref[number - 1] = project(conv_ref, rhs_ref, chips * share, 3 * height, lanes)

        following = lax.rem(first_peer + number, tm_count)
        pick_inner(held_codes_ref, carry_ref, slope_ref, conv_ref, following, (chips, share, bits))
        return 0

    lax.fori_loop(0, out_ref.shape[0] + 1, one_peer, 0)


def pick_inner(codes_ref, carry_ref, slope_ref, conv_ref, peer, sizes):
    places = conv_ref.shape[0] // (sizes[0] * sizes[1])
    height = places // 3

    def one_pair(slot, i, j):
        carry = carry_ref[pl.ds(pl.multiple_of(i * places, 8), places), :]
        slope = slope_ref[pl.ds(pl.multiple_of(j * (3 * places), 8), 3 * places), :]
        rows = [
            sum(
                carry[d * height : (d + 1) * height] * slope[(d * 3 + c) * height : (d * 3 + c + 1) * height]
                for d in range(3)
            )
            for c in range(3)
        ]
        conv_ref[pl.ds(pl.multiple_of(slot * places, 8), places), :] = jnp.concatenate(rows, axis=0)

    for_pairs_of(codes_ref, peer, sizes, one_pair)


def rest_kernel(
    codes_ref, carry_ref, slope_ref, rhs_ref, picked_ref, out_ref, conv_ref, held_codes_ref, sem, *, sizes
):
    del picked_ref
    chips, share, _ = sizes
    codes = copy_of_codes(codes_ref, held_codes_ref, sem)
    block, lanes = chips * share, conv_ref.shape[1]
    places = conv_ref.shape[0] // block

    def one_peer(peer, _):
        out_ref[peer] = project(conv_ref, rhs_ref, block, places, lanes)

        @pl.when(peer == 0)
        def _():
            codes.wait()

        @pl.when(peer + 1 < out_ref.shape[0])
        def _():
            pick_inner(held_codes_ref, carry_ref, slope_ref, conv_ref, peer + 1, sizes)

        return 0

    lax.fori_loop(0, out_ref.shape[0], one_peer, 0)


def far_kernel(codes_ref, coeffs_ref, *refs, peer, sizes):
    local_s, block_rows, tm_count, chips, share, bits = sizes
    next_own, next_other, near_ref, inner_ref = refs[:tm_count], *refs[tm_count : tm_count + 3]
    carry_ref, slope_ref, rhs_ref, out_ref, conv_ref, held_codes_ref, sem = refs[tm_count + 3 :]
    codes = copy_of_codes(codes_ref, held_codes_ref, sem)
    _, _, core = place_of_device()
    is_first = core == 0
    modes, lanes = near_ref.shape[1:]
    height = 2 * block_rows
    half = block_rows // 2 * 3
    some = math.gcd(modes, 32)
    weights = mode_weights(coeffs_ref, local_s, tm_count)
    for slab in range(half):
        mine = jnp.concatenate([next_own[peer][slab] for peer in range(tm_count)], axis=0)
        theirs = jnp.concatenate([next_other[peer, slab] for peer in range(tm_count)], axis=0)
        after, before = jnp.where(is_first, theirs, mine), jnp.where(is_first, mine, theirs)
        result = modes_of(weights, jnp.concatenate([after, before], axis=1))
        row, c = divmod(slab, 3)
        edges = ((near_ref[slab], result[:, :lanes]), (result[:, lanes:], near_ref[half + slab]))
        for number, (low, high) in enumerate(edges):
            place = number * block_rows + 2 * row
            for first in range(0, modes, some):
                one, two = low[first : first + some], high[first : first + some]
                for at, value, across in ((place, one, two * 0.5), (place + 1, two, one * -0.5)):
                    if c == 0:
                        carry_ref[pl.ds(first * height + at, some, stride=height), :] = value
                    start = first * (3 * height) + c * height + at
                    slope_ref[pl.ds(start, some, stride=3 * height), :] = across
            store_projection(rhs_ref, c * height + place, low)
            store_projection(rhs_ref, c * height + place + 1, high)
    codes.wait()
    pick_edge(held_codes_ref, carry_ref, slope_ref, conv_ref, peer, (chips, share, bits))
    out_ref[...] = edge_sum(conv_ref, rhs_ref, inner_ref, peer)
    pick_edge(held_codes_ref, carry_ref, slope_ref, conv_ref, peer - 1, (chips, share, bits))


def pick_edge(codes_ref, carry_ref, slope_ref, conv_ref, peer, sizes):
    places = conv_ref.shape[0] // (sizes[0] * sizes[1])
    height = places // 3

    def one_pair(slot, i, j):
        carry = carry_ref[pl.ds(pl.multiple_of(i * height, 8), height), :]
        slope = slope_ref[pl.ds(pl.multiple_of(j * places, 8), places), :]
        rows = [carry * slope[c * height : (c + 1) * height] for c in range(3)]
        conv_ref[pl.ds(pl.multiple_of(slot * places, 8), places), :] = jnp.concatenate(rows, axis=0)

    for_pairs_of(codes_ref, peer, sizes, one_pair)


def edge_sum(picked_ref, rhs_ref, inner_ref, peer):
    block = inner_ref.shape[1]
    places = picked_ref.shape[0] // block
    return inner_ref[peer % inner_ref.shape[0]] + project(picked_ref, rhs_ref, block, places, picked_ref.shape[1])


def edge_kernel(
    codes_ref, carry_ref, slope_ref, rhs_ref, inner_ref, picked_ref, out_ref, conv_ref, held_codes_ref, sem, *,
    peer, sizes
):
    codes = copy_of_codes(codes_ref, held_codes_ref, sem)
    out_ref[...] = edge_sum(picked_ref, rhs_ref, inner_ref, peer)
    codes.wait()
    pick_edge(held_codes_ref, carry_ref, slope_ref, conv_ref, peer - 1, sizes)


def picked_edge_kernel(rhs_ref, inner_ref, picked_ref, out_ref, *, peer):
    out_ref[...] = edge_sum(picked_ref, rhs_ref, inner_ref, peer)


def own_edge_kernel(
    codes_ref, carry_ref, slope_ref, rhs_ref, inner_ref, after_ref, out_ref, conv_ref, held_codes_ref, sem, *, sizes
):
    del after_ref
    copy_of_codes(codes_ref, held_codes_ref, sem).wait()
    pick_edge(held_codes_ref, carry_ref, slope_ref, conv_ref, 0, sizes)
    out_ref[...] = edge_sum(conv_ref, rhs_ref, inner_ref, 0)


def add_kernel(own_ref, *refs):
    *arrived_refs, out_ref = refs
    total = own_ref[...]
    for arrived_ref in arrived_refs:
        total = total + arrived_ref[...]
    out_ref[...] = total


def vmem_limit(mebibytes):
    return pltpu.CompilerParams(vmem_limit_bytes=mebibytes * 2**20)


def in_vmem(array):
    return pltpu.with_memory_space_constraint(array, pltpu.VMEM)


def shards(snapshots, coeffs, pair_table):
    tm_count, space_count = lax.axis_size("tm"), lax.axis_size("space")
    chips = space_count // 2
    local_s, _, _, rows_y, lanes = snapshots.shape
    modes = coeffs.shape[1]
    block_rows = rows_y // tm_count
    slabs = 3 * block_rows + border_layout(rows_y, lanes, lanes // tm_count)[2]
    share = pair_table.shape[0] // (tm_count * space_count)
    factor = float(space_count * rows_y * lanes) ** (-0.5)
    bits = modes.bit_length() - 1
    assert modes == 2**bits
    vmem = pl.BlockSpec(memory_space=pltpu.VMEM)
    block = chips * share
    height = 2 * block_rows
    depth = 3 * height * lanes

    swap = [(2 * chip + c, 2 * chip + 1 - c) for chip in range(chips) for c in range(2)]

    def across(peer):
        return [(i, i ^ peer) for i in range(tm_count)]

    with jax.named_scope("pack"):
        *packed, codes, held_coeffs = pl.pallas_call(
            functools.partial(pack_kernel, sizes=(local_s, rows_y, tm_count)),
            out_shape=[pltpu.VMEM((slabs, local_s, lanes), F32)] * tm_count
            + [
                pltpu.VMEM((tm_count, block_rows // 2 * 3, local_s, lanes), F32),
                pltpu.VMEM((pair_table.shape[0],), jnp.int32),
                pltpu.VMEM(coeffs.shape, F32),
            ],
            in_specs=[pl.BlockSpec(memory_space=pltpu.HBM)] * 3,
            out_specs=[vmem] * (tm_count + 3),
            scratch_shapes=[
                pltpu.VMEM((tm_count, slabs, local_s, lanes), F32),
                pltpu.VMEM((3, local_s, rows_y, lanes), F32),
                pltpu.VMEM((2, pair_table.shape[0]), jnp.int32),
                pltpu.SemaphoreType.DMA((5,)),
            ],
            compiler_params=vmem_limit(16),
        )(
            *[
                pltpu.with_memory_space_constraint(array, pltpu.HBM)
                for array in (snapshots.reshape(local_s, 3, rows_y, lanes), pair_table.T, coeffs)
            ]
        )
        codes, coeffs = in_vmem(codes), in_vmem(held_coeffs)
    with jax.named_scope("to_next_plane"):
        ring = [(place, (place + (1 if place % 2 else -1)) % space_count) for place in range(space_count)]
        across_edge = lax.ppermute(packed[tm_count], "space", ring)
    order = [0, tm_count - 1, *range(1, tm_count - 1)]
    with jax.named_scope("to_columns"):
        sent = [packed[peer] if peer == 0 else lax.ppermute(packed[peer], "tm", across(peer)) for peer in order]
    with jax.named_scope("to_other_core"):
        swapped = [lax.ppermute(piece, "space", swap) for piece in sent[:3]]
    with jax.named_scope("next_to_columns"):
        across_edge, sent[:3] = lax.optimization_barrier((across_edge, sent[:3]))
        parts = [across_edge[peer] for peer in range(tm_count)]
        parts, sent[3:] = lax.optimization_barrier((parts, sent[3:]))
        next_own = [parts[0]] + [lax.ppermute(parts[peer], "tm", across(peer)) for peer in range(1, tm_count)]
    with jax.named_scope("to_other_core"):
        swapped = swapped + [lax.ppermute(piece, "space", swap) for piece in sent[3:]]
    own, other = ([pieces[order.index(peer)] for peer in range(tm_count)] for pieces in (sent, swapped))
    early = tm_count // 2
    picked = pltpu.VMEM((block * 3 * height, lanes), F32)
    held_codes = [pltpu.SMEM(codes.shape, jnp.int32), pltpu.SemaphoreType.DMA]
    groups = pltpu.VMEM((early, block, modes), F32)
    with jax.named_scope("inner_terms"):
        near, *inner_tables, early_sums, first_picked = pl.pallas_call(
            functools.partial(inner_kernel, first_peer=early, sizes=(local_s, block_rows, tm_count, chips, share, bits)),
            out_shape=[
                pltpu.VMEM((block_rows * 3, modes, lanes), F32),
                pltpu.VMEM((modes * 3 * height, lanes), F32),
                pltpu.VMEM((modes * 9 * height, lanes), F32),
                pltpu.VMEM((depth, 2 * modes), BF16),
                groups,
                picked,
            ],
            in_specs=[vmem] * (2 * tm_count + 2),
            out_specs=[vmem] * 6,
            scratch_shapes=[pltpu.VMEM((2, slabs, modes, lanes), F32)] + held_codes,
            compiler_params=vmem_limit(24),
            cost_estimate=pl.CostEstimate(flops=12 * 10**9, bytes_accessed=10**7, transcendentals=0),
        )(codes, coeffs, *[in_vmem(piece) for piece in (*own, *other)])
    with jax.named_scope("next_to_other_core"):
        next_own, inner_tables = lax.optimization_barrier((next_own, inner_tables))
        next_other = lax.ppermute(jnp.stack(next_own), "space", swap)
    with jax.named_scope("inner_terms"):
        late_sums, _ = pl.pallas_call(
            functools.partial(rest_kernel, sizes=(chips, share, bits)),
            out_shape=[groups, picked],
            in_specs=[vmem] * 5,
            out_specs=[vmem] * 2,
            input_output_aliases={4: 1},
            scratch_shapes=held_codes,
            compiler_params=vmem_limit(16),
            cost_estimate=pl.CostEstimate(flops=8 * 10**9, bytes_accessed=10**7, transcendentals=0),
        )(codes, *[in_vmem(table) for table in (*inner_tables, first_picked)])
    with jax.named_scope("edge_terms"):
        *tables, summed, next_picked = pl.pallas_call(
            functools.partial(
                far_kernel, peer=tm_count - 1, sizes=(local_s, block_rows, tm_count, chips, share, bits)
            ),
            out_shape=[
                pltpu.VMEM((modes * height, lanes), F32),
                pltpu.VMEM((modes * 3 * height, lanes), F32),
                pltpu.VMEM((depth, 2 * modes), BF16),
                pltpu.VMEM((block, modes), F32),
                picked,
            ],
            in_specs=[vmem] * (tm_count + 5),
            out_specs=[vmem] * 5,
            scratch_shapes=held_codes,
            compiler_params=vmem_limit(16),
        )(codes, coeffs, *[in_vmem(piece) for piece in (*next_own, next_other, near, early_sums)])
    arrived, taken = [], 2
    for peer in reversed(range(tm_count - 1)):
        with jax.named_scope("sum_over_columns"):
            arrived.append(lax.ppermute(summed, "tm", across(peer + 1)))
            if peer >= early:
                early_sums, _ = lax.optimization_barrier((early_sums, summed))
            else:
                late_sums, _ = lax.optimization_barrier((late_sums, summed))
        with jax.named_scope("edge_terms"):
            inner_sums = early_sums if peer >= early else late_sums
            edge_cost = pl.CostEstimate(flops=10**8, bytes_accessed=10**5, transcendentals=0)
            if peer > 1:
                summed, next_picked = pl.pallas_call(
                    functools.partial(edge_kernel, peer=peer, sizes=(chips, share, bits)),
                    out_shape=[pltpu.VMEM((block, modes), F32), picked],
                    in_specs=[vmem] * 6,
                    out_specs=[vmem] * 2,
                    scratch_shapes=held_codes,
                    compiler_params=vmem_limit(16),
                    cost_estimate=edge_cost,
                )(codes, *[in_vmem(table) for table in (*tables, inner_sums, next_picked)])
            elif peer:
                summed = pl.pallas_call(
                    functools.partial(picked_edge_kernel, peer=peer),
                    out_shape=pltpu.VMEM((block, modes), F32),
                    in_specs=[vmem] * 3,
                    out_specs=vmem,
                    compiler_params=vmem_limit(16),
                    cost_estimate=edge_cost,
                )(*[in_vmem(table) for table in (tables[2], inner_sums, next_picked)])
            else:
                summed = pl.pallas_call(
                    functools.partial(own_edge_kernel, sizes=(chips, share, bits)),
                    out_shape=pltpu.VMEM((block, modes), F32),
                    in_specs=[vmem] * 6,
                    out_specs=vmem,
                    scratch_shapes=[picked] + held_codes,
                    compiler_params=vmem_limit(16),
                    cost_estimate=edge_cost,
                )(codes, *[in_vmem(table) for table in (*tables, inner_sums, summed)])
                summed = pl.pallas_call(
                    add_kernel,
                    out_shape=pltpu.VMEM((block, modes), F32),
                    in_specs=[vmem] * (1 + taken),
                    out_specs=vmem,
                )(*[in_vmem(table) for table in (summed, *arrived[:taken])])
    with jax.named_scope("sum_over_columns"):
        for part in arrived[taken:]:
            summed = summed + part
    with jax.named_scope("sum_over_chips"):
        shares = summed.reshape(chips, share, modes)
        parts = None
        for step in reversed(range(1, chips)):
            pairing = [(2 * chip + c, 2 * (chip ^ step) + c) for chip in range(chips) for c in range(2)]
            part = lax.ppermute(shares[step], "space", pairing)
            parts = part if parts is None else part + parts
        result = shares[0] + parts
        return result * factor


def solution(mesh):
    placed = (P("tm", None, "space", None, None), P(), P())
    return jax.shard_map(
        shards, mesh=mesh, in_specs=placed, out_specs=P(("tm", "space"), None), check_vma=False
    )
```

```python
import functools
import itertools
import math

import jax
import jax.numpy as jnp
from jax import lax
from jax.experimental import pallas as pl
from jax.experimental.pallas import tpu as pltpu
from jax.sharding import PartitionSpec as P

F32 = jnp.float32
BF16 = jnp.bfloat16


def place_of_device():
    place = lax.axis_index("space")
    return lax.axis_index("tm"), lax.shift_right_logical(place, 1), jnp.bitwise_and(place, 1)


def split_high_low(values):
    high = values.astype(BF16)
    low = (values - high.astype(F32)).astype(BF16)
    return high, low


def border_layout(rows_y, lanes, width):
    per_run = (width + 1) // rows_y
    if per_run:
        run = width + 1 + per_run * rows_y
        firsts = [c // per_run * run + c % per_run * rows_y for c in range(3)]
        if firsts[2] + width + 1 + rows_y <= lanes:
            return [(0, first) for first in firsts], width + 1, 1
    per_slab = lanes // (2 * rows_y)
    places = [(c // per_slab, c % per_slab * 2 * rows_y) for c in range(3)]
    return places, rows_y, places[2][0] + 1


def exchange_blocks(rows, lane, width, lanes):
    rows = list(rows)
    step = len(rows) // 2
    while step:
        keeps = jnp.bitwise_and(lane, step * width) == 0
        for low in range(len(rows)):
            if low & step == 0:
                first, second = rows[low], rows[low + step]
                rows[low] = jnp.where(keeps, first, pltpu.roll(second, step * width, 1))
                rows[low + step] = jnp.where(keeps, pltpu.roll(first, lanes - step * width, 1), second)
        step //= 2
    return rows


def pack_kernel(field_ref, pairs_ref, coeffs_ref, *refs, sizes):
    *out_refs, codes_ref, held_coeffs_ref, sorted_ref, held_ref, held_pairs_ref, sems = refs
    local_s, rows_y, tm_count = sizes
    lanes = field_ref.shape[3]
    copies = [pltpu.make_async_copy(field_ref.at[:, c], held_ref.at[c], sems.at[c]) for c in range(3)]
    copies.append(pltpu.make_async_copy(pairs_ref, held_pairs_ref, sems.at[3]))
    copies.append(pltpu.make_async_copy(coeffs_ref, held_coeffs_ref, sems.at[4]))
    for copy in copies:
        copy.start()
    rows_ref = held_ref.reshape(3 * local_s * rows_y, lanes)
    t, _, core = place_of_device()
    width, groups = lanes // tm_count, rows_y // tm_count
    lane = lax.broadcasted_iota(jnp.int32, (local_s, lanes), 1)
    places, offset, border_slabs = border_layout(rows_y, lanes, width)
    borders = [[jnp.zeros((local_s, lanes), F32) for _ in range(tm_count)] for _ in range(border_slabs)]
    for c, (slab, first_lane) in enumerate(places):
        copies[c].wait()

        def one_group(g, border, c=c, first_lane=first_lane):
            border = list(border)
            rows = []
            for q in range(tm_count):
                y = q * groups + g
                row = rows_ref[pl.ds(c * local_s * rows_y + y, local_s, stride=rows_y), :]
                rows.append(row)
                before = first_lane + y
                after = before + offset - (width + 1)
                moved = pltpu.roll(row, jnp.bitwise_and(before, lanes - 1), 1)
                moved_after = moved if offset == width + 1 else pltpu.roll(row, jnp.bitwise_and(after, lanes - 1), 1)
                for block in range(tm_count):
                    at_before = lane == jnp.bitwise_and(before + block * width - 1, lanes - 1)
                    at_after = lane == jnp.bitwise_and(after + (block + 1) * width, lanes - 1)
                    if moved is moved_after:
                        border[block] = jnp.where(jnp.logical_or(at_before, at_after), moved, border[block])
                    else:
                        border[block] = jnp.where(at_before, moved, jnp.where(at_after, moved_after, border[block]))
            for block, main in enumerate(exchange_blocks(rows, lane, width, lanes)):
                sorted_ref[block, g * 3 + c] = main
            return tuple(border)

        borders[slab] = lax.fori_loop(0, groups, one_group, tuple(borders[slab]), unroll=True)
    half = groups // 2 * 3
    for slab, border in enumerate(borders):
        for block in range(tm_count):
            sorted_ref[block, groups * 3 + slab] = border[block]
    for peer in range(tm_count):
        block = jnp.bitwise_xor(t, peer)
        out_refs[peer][...] = sorted_ref[block]
        out_refs[tm_count][peer] = sorted_ref[block, pl.ds(core * half, half)]
    copies[3].wait()
    copies[4].wait()
    for first in range(0, codes_ref.shape[0], lanes):
        here = pl.ds(first, lanes)
        codes_ref[here] = held_pairs_ref[0, here] * held_coeffs_ref.shape[1] + held_pairs_ref[1, here]


def mode_weights(coeffs_ref, local_s, tm_count):
    t, _, _ = place_of_device()
    ordered = jnp.concatenate(
        [
            coeffs_ref[pl.ds(pl.multiple_of(jnp.bitwise_xor(t, peer) * local_s, 8), local_s), :]
            for peer in range(tm_count)
        ],
        axis=0,
    )
    high, low = split_high_low(ordered.T)
    return jnp.concatenate([high, low, high, low], axis=1)


def modes_of(weights, slab):
    high, low = split_high_low(slab)
    return jnp.dot(weights, jnp.concatenate([high, high, low, low], axis=0), preferred_element_type=F32)


def store_projection(rhs_ref, place, mode_slab):
    high, low = split_high_low(mode_slab.T)
    modes, lanes = mode_slab.shape
    rhs_ref[place * lanes : (place + 1) * lanes, 0:modes] = high
    rhs_ref[place * lanes : (place + 1) * lanes, modes : 2 * modes] = low


def project(conv_ref, rhs_ref, block, places, lanes):
    both = None
    for place in range(0, places, 2):
        highs, lows = zip(
            *(split_high_low(conv_ref[pl.ds(place + k, block, stride=places), :]) for k in range(2))
        )
        lhs = jnp.concatenate([jnp.concatenate(highs, axis=1), jnp.concatenate(lows, axis=1)], axis=0)
        part = jnp.dot(lhs, rhs_ref[place * lanes : (place + 2) * lanes, :], preferred_element_type=F32)
        both = part if both is None else both + part
    modes = both.shape[1] // 2
    return (both[:block, :modes] + both[:block, modes:]) + (both[block:, :modes] + both[block:, modes:])


def for_pairs_of(codes_ref, peer, sizes, one_pair):
    chips, share, bits = sizes
    t, chip, core = place_of_device()
    first_chip = jnp.bitwise_xor(t, peer) * chips

    def one_share(ahead, _):
        base = ((first_chip + jnp.bitwise_xor(chip, ahead)) * 2 + core) * share

        def one(q, _):
            code = codes_ref[base + q]
            one_pair(ahead * share + q, lax.shift_right_logical(code, bits), jnp.bitwise_and(code, 2**bits - 1))
            return 0

        return lax.fori_loop(0, share, one, 0, unroll=True)

    lax.fori_loop(0, chips, one_share, 0, unroll=2)


def copy_of_codes(codes_ref, held_codes_ref, sem):
    copy = pltpu.make_async_copy(codes_ref, held_codes_ref, sem)
    copy.start()
    return copy


def inner_kernel(codes_ref, coeffs_ref, *refs, first_peer, sizes):
    local_s, block_rows, tm_count, chips, share, bits = sizes
    own, other = refs[:tm_count], refs[tm_count : 2 * tm_count]
    near_ref, carry_ref, slope_ref, rhs_ref, out_ref, conv_ref, slab_ref, held_codes_ref, sem = refs[2 * tm_count :]
    codes = copy_of_codes(codes_ref, held_codes_ref, sem)
    t, _, core = place_of_device()
    modes, lanes = coeffs_ref.shape[1], own[0].shape[2]
    height = 2 * block_rows
    weights = mode_weights(coeffs_ref, local_s, tm_count)

    def one_slab(index, _):
        own_slab = jnp.concatenate([piece[index] for piece in own], axis=0)
        other_slab = jnp.concatenate([piece[index] for piece in other], axis=0)
        is_first = core == 0
        both = jnp.concatenate(
            [jnp.where(is_first, own_slab, other_slab), jnp.where(is_first, other_slab, own_slab)], axis=1
        )
        result = modes_of(weights, both)
        slab_ref[0, index] = result[:, :lanes]
        slab_ref[1, index] = result[:, lanes:]
        return 0

    slabs = own[0].shape[0]
    lax.fori_loop(0, slabs, one_slab, 0, unroll=True)
    width, rows_y = lanes // tm_count, block_rows * tm_count
    lane = lax.broadcasted_iota(jnp.int32, (1, lanes), 1)
    part, column = lax.div(lane, width), lax.rem(lane, width)
    has_border = jnp.where(column == 0, -0.5, jnp.where(column == width - 1, 0.5, 0.0))
    places, offset, _ = border_layout(rows_y, lanes, width)
    border_of = jnp.where(column == 0, 0, offset) + t * width - 1 + part * block_rows
    border_lanes = lax.broadcasted_iota(jnp.int32, (2 * lanes, lanes), 0)
    border_lanes = jnp.where(border_lanes >= lanes, border_lanes - lanes, border_lanes)
    borders = []
    for slab in range(3 * block_rows, slabs):
        both = jnp.concatenate([slab_ref[0, slab], slab_ref[1, slab]], axis=0)
        borders.append(jnp.concatenate(split_high_low(both), axis=1))
    some = math.gcd(modes, 32)
    for c, (slab, first_lane) in enumerate(places):
        for row in range(block_rows):
            center = row * 3 + c
            if row % 2 == 0:
                picks = [
                    jnp.where(
                        border_lanes == jnp.bitwise_and(border_of + (first_lane + row + k), lanes - 1), has_border, 0.0
                    ).astype(BF16)
                    for k in range(2)
                ]
                border = jnp.dot(borders[slab], jnp.concatenate(picks, axis=1), preferred_element_type=F32)
            for plane, first in itertools.product(range(2), range(0, modes, some)):
                place = plane * block_rows + row
                here = pl.ds(first, some)
                value = slab_ref[plane, center, here, :]
                stream = slab_ref[1 - plane, center, here, :] * (0.5 if plane == 0 else -0.5)
                if row + 1 < block_rows:
                    above = slab_ref[plane, center + 3, here, :]
                else:
                    above = pltpu.roll(slab_ref[plane, c, here, :], lanes - width, 1)
                    above = jnp.where(lane < lanes - width, above, 0.0)
                if row > 0:
                    below = slab_ref[plane, center - 3, here, :]
                else:
                    below = pltpu.roll(slab_ref[plane, 3 * (block_rows - 1) + c, here, :], width, 1)
                    below = jnp.where(lane >= width, below, 0.0)
                normal = (above - below) * 0.5
                after = jnp.where(column < width - 1, pltpu.roll(value, lanes - 1, 1), 0.0)
                before = jnp.where(column > 0, pltpu.roll(value, 1, 1), 0.0)
                beside = border[plane * modes + first :, row % 2 * lanes :][:some, :lanes]
                span = (after - before) * 0.5 + beside
                carry_ref[pl.ds(first * (3 * height) + c * height + place, some, stride=3 * height), :] = value
                for d, slope in enumerate((stream, normal, span)):
                    start = first * (9 * height) + (d * 3 + c) * height + place
                    slope_ref[pl.ds(start, some, stride=9 * height), :] = slope
                if (plane == 1) == (row < block_rows // 2):
                    near_ref[center, here, :] = value
            for plane in range(2):
                store_projection(rhs_ref, c * height + plane * block_rows + row, slab_ref[plane, center])
    codes.wait()

    def one_peer(number, _):
        @pl.when(number > 0)
        def _():
            out_ref[number - 1] = project(conv_ref, rhs_ref, chips * share, 3 * height, lanes)

        following = lax.rem(first_peer + number, tm_count)
        pick_inner(held_codes_ref, carry_ref, slope_ref, conv_ref, following, (chips, share, bits))
        return 0

    lax.fori_loop(0, out_ref.shape[0] + 1, one_peer, 0)


def pick_inner(codes_ref, carry_ref, slope_ref, conv_ref, peer, sizes):
    places = conv_ref.shape[0] // (sizes[0] * sizes[1])
    height = places // 3

    def one_pair(slot, i, j):
        carry = carry_ref[pl.ds(pl.multiple_of(i * places, 8), places), :]
        slope = slope_ref[pl.ds(pl.multiple_of(j * (3 * places), 8), 3 * places), :]
        rows = [
            sum(
                carry[d * height : (d + 1) * height] * slope[(d * 3 + c) * height : (d * 3 + c + 1) * height]
                for d in range(3)
            )
            for c in range(3)
        ]
        conv_ref[pl.ds(pl.multiple_of(slot * places, 8), places), :] = jnp.concatenate(rows, axis=0)

    for_pairs_of(codes_ref, peer, sizes, one_pair)


def rest_kernel(
    codes_ref, carry_ref, slope_ref, rhs_ref, picked_ref, out_ref, conv_ref, held_codes_ref, sem, *, sizes
):
    del picked_ref
    chips, share, _ = sizes
    codes = copy_of_codes(codes_ref, held_codes_ref, sem)
    block, lanes = chips * share, conv_ref.shape[1]
    places = conv_ref.shape[0] // block

    def one_peer(peer, _):
        out_ref[peer] = project(conv_ref, rhs_ref, block, places, lanes)

        @pl.when(peer == 0)
        def _():
            codes.wait()

        @pl.when(peer + 1 < out_ref.shape[0])
        def _():
            pick_inner(held_codes_ref, carry_ref, slope_ref, conv_ref, peer + 1, sizes)

        return 0

    lax.fori_loop(0, out_ref.shape[0], one_peer, 0)


def far_kernel(codes_ref, coeffs_ref, *refs, peer, sizes):
    local_s, block_rows, tm_count, chips, share, bits = sizes
    next_own, next_other, near_ref, inner_ref = refs[:tm_count], *refs[tm_count : tm_count + 3]
    carry_ref, slope_ref, rhs_ref, out_ref, conv_ref, held_codes_ref, sem = refs[tm_count + 3 :]
    codes = copy_of_codes(codes_ref, held_codes_ref, sem)
    _, _, core = place_of_device()
    is_first = core == 0
    modes, lanes = near_ref.shape[1:]
    height = 2 * block_rows
    half = block_rows // 2 * 3
    some = math.gcd(modes, 32)
    weights = mode_weights(coeffs_ref, local_s, tm_count)
    for slab in range(half):
        mine = jnp.concatenate([next_own[peer][slab] for peer in range(tm_count)], axis=0)
        theirs = jnp.concatenate([next_other[peer, slab] for peer in range(tm_count)], axis=0)
        after, before = jnp.where(is_first, theirs, mine), jnp.where(is_first, mine, theirs)
        result = modes_of(weights, jnp.concatenate([after, before], axis=1))
        row, c = divmod(slab, 3)
        edges = ((near_ref[slab], result[:, :lanes]), (result[:, lanes:], near_ref[half + slab]))
        for number, (low, high) in enumerate(edges):
            place = number * block_rows + 2 * row
            for first in range(0, modes, some):
                one, two = low[first : first + some], high[first : first + some]
                for at, value, across in ((place, one, two * 0.5), (place + 1, two, one * -0.5)):
                    if c == 0:
                        carry_ref[pl.ds(first * height + at, some, stride=height), :] = value
                    start = first * (3 * height) + c * height + at
                    slope_ref[pl.ds(start, some, stride=3 * height), :] = across
            store_projection(rhs_ref, c * height + place, low)
            store_projection(rhs_ref, c * height + place + 1, high)
    codes.wait()
    pick_edge(held_codes_ref, carry_ref, slope_ref, conv_ref, peer, (chips, share, bits))
    out_ref[...] = edge_sum(conv_ref, rhs_ref, inner_ref, peer)
    pick_edge(held_codes_ref, carry_ref, slope_ref, conv_ref, peer - 1, (chips, share, bits))


def pick_edge(codes_ref, carry_ref, slope_ref, conv_ref, peer, sizes):
    places = conv_ref.shape[0] // (sizes[0] * sizes[1])
    height = places // 3

    def one_pair(slot, i, j):
        carry = carry_ref[pl.ds(pl.multiple_of(i * height, 8), height), :]
        slope = slope_ref[pl.ds(pl.multiple_of(j * places, 8), places), :]
        rows = [carry * slope[c * height : (c + 1) * height] for c in range(3)]
        conv_ref[pl.ds(pl.multiple_of(slot * places, 8), places), :] = jnp.concatenate(rows, axis=0)

    for_pairs_of(codes_ref, peer, sizes, one_pair)


def edge_sum(picked_ref, rhs_ref, inner_ref, peer):
    block = inner_ref.shape[1]
    places = picked_ref.shape[0] // block
    return inner_ref[peer % inner_ref.shape[0]] + project(picked_ref, rhs_ref, block, places, picked_ref.shape[1])


def edge_kernel(
    codes_ref, carry_ref, slope_ref, rhs_ref, inner_ref, picked_ref, out_ref, conv_ref, held_codes_ref, sem, *,
    peer, sizes
):
    codes = copy_of_codes(codes_ref, held_codes_ref, sem)
    out_ref[...] = edge_sum(picked_ref, rhs_ref, inner_ref, peer)
    codes.wait()
    pick_edge(held_codes_ref, carry_ref, slope_ref, conv_ref, peer - 1, sizes)


def picked_edge_kernel(rhs_ref, inner_ref, picked_ref, out_ref, *, peer):
    out_ref[...] = edge_sum(picked_ref, rhs_ref, inner_ref, peer)


def own_edge_kernel(
    codes_ref, carry_ref, slope_ref, rhs_ref, inner_ref, after_ref, out_ref, conv_ref, held_codes_ref, sem, *, sizes
):
    del after_ref
    copy_of_codes(codes_ref, held_codes_ref, sem).wait()
    pick_edge(held_codes_ref, carry_ref, slope_ref, conv_ref, 0, sizes)
    out_ref[...] = edge_sum(conv_ref, rhs_ref, inner_ref, 0)


def add_kernel(own_ref, *refs):
    *arrived_refs, out_ref = refs
    total = own_ref[...]
    for arrived_ref in arrived_refs:
        total = total + arrived_ref[...]
    out_ref[...] = total


def vmem_limit(mebibytes):
    return pltpu.CompilerParams(vmem_limit_bytes=mebibytes * 2**20)


def in_vmem(array):
    return pltpu.with_memory_space_constraint(array, pltpu.VMEM)


def shards(snapshots, coeffs, pair_table):
    tm_count, space_count = lax.axis_size("tm"), lax.axis_size("space")
    chips = space_count // 2
    local_s, _, _, rows_y, lanes = snapshots.shape
    modes = coeffs.shape[1]
    block_rows = rows_y // tm_count
    slabs = 3 * block_rows + border_layout(rows_y, lanes, lanes // tm_count)[2]
    share = pair_table.shape[0] // (tm_count * space_count)
    factor = float(space_count * rows_y * lanes) ** (-0.5)
    bits = modes.bit_length() - 1
    assert modes == 2**bits
    vmem = pl.BlockSpec(memory_space=pltpu.VMEM)
    block = chips * share
    height = 2 * block_rows
    depth = 3 * height * lanes

    swap = [(2 * chip + c, 2 * chip + 1 - c) for chip in range(chips) for c in range(2)]

    def across(peer):
        return [(i, i ^ peer) for i in range(tm_count)]

    with jax.named_scope("pack"):
        *packed, codes, held_coeffs = pl.pallas_call(
            functools.partial(pack_kernel, sizes=(local_s, rows_y, tm_count)),
            out_shape=[pltpu.VMEM((slabs, local_s, lanes), F32)] * tm_count
            + [
                pltpu.VMEM((tm_count, block_rows // 2 * 3, local_s, lanes), F32),
                pltpu.VMEM((pair_table.shape[0],), jnp.int32),
                pltpu.VMEM(coeffs.shape, F32),
            ],
            in_specs=[pl.BlockSpec(memory_space=pltpu.HBM)] * 3,
            out_specs=[vmem] * (tm_count + 3),
            scratch_shapes=[
                pltpu.VMEM((tm_count, slabs, local_s, lanes), F32),
                pltpu.VMEM((3, local_s, rows_y, lanes), F32),
                pltpu.VMEM((2, pair_table.shape[0]), jnp.int32),
                pltpu.SemaphoreType.DMA((5,)),
            ],
            compiler_params=vmem_limit(16),
        )(
            *[
                pltpu.with_memory_space_constraint(array, pltpu.HBM)
                for array in (snapshots.reshape(local_s, 3, rows_y, lanes), pair_table.T, coeffs)
            ]
        )
        codes, coeffs = in_vmem(codes), in_vmem(held_coeffs)
    with jax.named_scope("to_next_plane"):
        ring = [(place, (place + (1 if place % 2 else -1)) % space_count) for place in range(space_count)]
        across_edge = lax.ppermute(packed[tm_count], "space", ring)
    with jax.named_scope("to_columns"):
        own = [packed[0]] + [lax.ppermute(packed[peer], "tm", across(peer)) for peer in range(1, tm_count)]
    with jax.named_scope("next_to_columns"):
        early_other = [lax.ppermute(piece, "space", swap) for piece in own[:3]]
        across_edge, own[:3] = lax.optimization_barrier((across_edge, own[:3]))
        parts = [across_edge[peer] for peer in range(tm_count)]
        parts, own[3:] = lax.optimization_barrier((parts, own[3:]))
        next_own = [parts[0]] + [lax.ppermute(parts[peer], "tm", across(peer)) for peer in range(1, tm_count)]
    with jax.named_scope("to_other_core"):
        other = early_other + [lax.ppermute(piece, "space", swap) for piece in own[3:]]
    early = tm_count // 2
    picked = pltpu.VMEM((block * 3 * height, lanes), F32)
    held_codes = [pltpu.SMEM(codes.shape, jnp.int32), pltpu.SemaphoreType.DMA]
    groups = pltpu.VMEM((early, block, modes), F32)
    with jax.named_scope("inner_terms"):
        near, *inner_tables, early_sums, first_picked = pl.pallas_call(
            functools.partial(inner_kernel, first_peer=early, sizes=(local_s, block_rows, tm_count, chips, share, bits)),
            out_shape=[
                pltpu.VMEM((block_rows * 3, modes, lanes), F32),
                pltpu.VMEM((modes * 3 * height, lanes), F32),
                pltpu.VMEM((modes * 9 * height, lanes), F32),
                pltpu.VMEM((depth, 2 * modes), BF16),
                groups,
                picked,
            ],
            in_specs=[vmem] * (2 * tm_count + 2),
            out_specs=[vmem] * 6,
            scratch_shapes=[pltpu.VMEM((2, slabs, modes, lanes), F32)] + held_codes,
            compiler_params=vmem_limit(24),
            cost_estimate=pl.CostEstimate(flops=12 * 10**9, bytes_accessed=10**7, transcendentals=0),
        )(codes, coeffs, *[in_vmem(piece) for piece in (*own, *other)])
    with jax.named_scope("next_to_other_core"):
        next_own, inner_tables = lax.optimization_barrier((next_own, inner_tables))
        next_other = lax.ppermute(jnp.stack(next_own), "space", swap)
    with jax.named_scope("inner_terms"):
        late_sums, _ = pl.pallas_call(
            functools.partial(rest_kernel, sizes=(chips, share, bits)),
            out_shape=[groups, picked],
            in_specs=[vmem] * 5,
            out_specs=[vmem] * 2,
            input_output_aliases={4: 1},
            scratch_shapes=held_codes,
            compiler_params=vmem_limit(16),
            cost_estimate=pl.CostEstimate(flops=8 * 10**9, bytes_accessed=10**7, transcendentals=0),
        )(codes, *[in_vmem(table) for table in (*inner_tables, first_picked)])
    with jax.named_scope("edge_terms"):
        *tables, summed, next_picked = pl.pallas_call(
            functools.partial(
                far_kernel, peer=tm_count - 1, sizes=(local_s, block_rows, tm_count, chips, share, bits)
            ),
            out_shape=[
                pltpu.VMEM((modes * height, lanes), F32),
                pltpu.VMEM((modes * 3 * height, lanes), F32),
                pltpu.VMEM((depth, 2 * modes), BF16),
                pltpu.VMEM((block, modes), F32),
                picked,
            ],
            in_specs=[vmem] * (tm_count + 5),
            out_specs=[vmem] * 5,
            scratch_shapes=held_codes,
            compiler_params=vmem_limit(16),
        )(codes, coeffs, *[in_vmem(piece) for piece in (*next_own, next_other, near, early_sums)])
    arrived, taken = [], 2
    for peer in reversed(range(tm_count - 1)):
        with jax.named_scope("sum_over_columns"):
            arrived.append(lax.ppermute(summed, "tm", across(peer + 1)))
            if peer >= early:
                early_sums, _ = lax.optimization_barrier((early_sums, summed))
            else:
                late_sums, _ = lax.optimization_barrier((late_sums, summed))
        with jax.named_scope("edge_terms"):
            inner_sums = early_sums if peer >= early else late_sums
            edge_cost = pl.CostEstimate(flops=10**8, bytes_accessed=10**5, transcendentals=0)
            if peer > 1:
                summed, next_picked = pl.pallas_call(
                    functools.partial(edge_kernel, peer=peer, sizes=(chips, share, bits)),
                    out_shape=[pltpu.VMEM((block, modes), F32), picked],
                    in_specs=[vmem] * 6,
                    out_specs=[vmem] * 2,
                    scratch_shapes=held_codes,
                    compiler_params=vmem_limit(16),
                    cost_estimate=edge_cost,
                )(codes, *[in_vmem(table) for table in (*tables, inner_sums, next_picked)])
            elif peer:
                summed = pl.pallas_call(
                    functools.partial(picked_edge_kernel, peer=peer),
                    out_shape=pltpu.VMEM((block, modes), F32),
                    in_specs=[vmem] * 3,
                    out_specs=vmem,
                    compiler_params=vmem_limit(16),
                    cost_estimate=edge_cost,
                )(*[in_vmem(table) for table in (tables[2], inner_sums, next_picked)])
            else:
                summed = pl.pallas_call(
                    functools.partial(own_edge_kernel, sizes=(chips, share, bits)),
                    out_shape=pltpu.VMEM((block, modes), F32),
                    in_specs=[vmem] * 6,
                    out_specs=vmem,
                    scratch_shapes=[picked] + held_codes,
                    compiler_params=vmem_limit(16),
                    cost_estimate=edge_cost,
                )(codes, *[in_vmem(table) for table in (*tables, inner_sums, summed)])
                summed = pl.pallas_call(
                    add_kernel,
                    out_shape=pltpu.VMEM((block, modes), F32),
                    in_specs=[vmem] * (1 + taken),
                    out_specs=vmem,
                )(*[in_vmem(table) for table in (summed, *arrived[:taken])])
    with jax.named_scope("sum_over_columns"):
        for part in arrived[taken:]:
            summed = summed + part
    with jax.named_scope("sum_over_chips"):
        shares = summed.reshape(chips, share, modes)
        parts = None
        for step in reversed(range(1, chips)):
            pairing = [(2 * chip + c, 2 * (chip ^ step) + c) for chip in range(chips) for c in range(2)]
            part = lax.ppermute(shares[step], "space", pairing)
            parts = part if parts is None else part + parts
        result = shares[0] + parts
        return result * factor


def solution(mesh):
    placed = (P("tm", None, "space", None, None), P(), P())
    return jax.shard_map(
        shards, mesh=mesh, in_specs=placed, out_specs=P(("tm", "space"), None), check_vma=False
    )
```
